128 devices in a mesh: seq: 64 (over z, x, y), tensor: 2 (over core).
Axes of the slice: x: 4, y: 4, z: 4, core: 2. Of those that a mesh axis runs over, the one named last changes fastest.
Arguments:
- tokens: bfloat16 [8192, 1536], P('seq'), may hold values from -6 to 6
- cotangent: bfloat16 [8192, 1536], P('seq'), may hold values from -6 to 6
- lengths: int32 [8], replicated, may hold values from 200 to 4096, as said below
- norm1_gain: float32 [1536], replicated, may hold values from 0.5 to 1.5
- w_query: bfloat16 [1536, 12, 128], P(None, 'tensor'), may hold values from -0.15625 to 0.15625
- b_query: bfloat16 [12, 128], P('tensor'), may hold values from -3 to 3
- w_key: bfloat16 [1536, 2, 128], P(None, 'tensor'), may hold values from -0.15625 to 0.15625
- b_key: bfloat16 [2, 128], P('tensor'), may hold values from -3 to 3
- w_value: bfloat16 [1536, 2, 128], P(None, 'tensor'), may hold values from -0.15625 to 0.15625
- b_value: bfloat16 [2, 128], P('tensor'), may hold values from -3 to 3
- w_out: bfloat16 [12, 128, 1536], P('tensor'), may hold values from -1.25 to 1.25
- norm2_gain: float32 [1536], replicated, may hold values from 0.5 to 1.5
- w_gate: bfloat16 [1536, 8960], P(None, 'tensor'), may hold values from -0.15625 to 0.15625
- w_up: bfloat16 [1536, 8960], P(None, 'tensor'), may hold values from -0.15625 to 0.15625
- w_down: bfloat16 [8960, 1536], P('tensor'), may hold values from -0.25 to 0.25
Outputs:
- output: float32 [8192, 1536], P('seq')
- grad_tokens: float32 [8192, 1536], P('seq')
- grad_norm1: float32 [1536], P('seq')
- grad_w_query: float32 [1536, 12, 128], P('seq', 'tensor')
- grad_b_query: float32 [12, 128], P('tensor', 'seq')
- grad_w_key: float32 [1536, 2, 128], P('seq', 'tensor')
- grad_b_key: float32 [2, 128], P('tensor', 'seq')
- grad_w_value: float32 [1536, 2, 128], P('seq', 'tensor')
- grad_b_value: float32 [2, 128], P('tensor', 'seq')
- grad_w_out: float32 [12, 128, 1536], P('tensor', None, 'seq')
- grad_norm2: float32 [1536], P('seq')
- grad_w_gate: float32 [1536, 8960], P('seq', 'tensor')
- grad_w_up: float32 [1536, 8960], P('seq', 'tensor')
- grad_w_down: float32 [8960, 1536], P('tensor', 'seq')
The draws below stay inside these ranges and needn't reach their ends.
Inputs may be any that keep to these rules, and one draw needn't show every extreme that they name: The 8 lengths sum to 8192; each is at least 200; exactly one, at a place in the pack drawn from the seed, is 4096 long, and all others are shorter.
All inputs are finite; a program needn't handle non-finite values.
Results may differ from the reference program's by a relative error of at most 0.035.
Values may be sent and summed in bfloat16 or wider, within the bound.
A program may use at most 320 MiB of HBM per device.

```python
import math
import jax
import jax.numpy as jnp
from jax import lax

D = 1536
QH = 12
KVH = 2
HD = 128
FF = 8960
TOK_DEV = 128
NDOCS = 8
TOKENS = 8192
N_SEQ = 64


def draw_cotangent(key, part):
    key = jax.random.fold_in(key, 23)
    values = jnp.clip(jax.random.normal(key, (TOKENS, D), jnp.float32), -6.0, 6.0)
    return values.astype(jnp.bfloat16)


def draw_lengths(key, part):
    key = jax.random.fold_in(key, 11)
    key_weights, key_place = jax.random.split(key)
    longest = TOKENS // 2
    shortest = min(200, TOKENS // (4 * NDOCS))
    other_count = NDOCS - 1
    spare_tokens = TOKENS - longest - other_count * shortest
    weights = jax.random.randint(key_weights, (other_count,), 1, 1001).astype(jnp.int32)
    weight_sum = jnp.sum(weights)
    extras = weights * spare_tokens // weight_sum
    extras = extras.at[0].add(spare_tokens - jnp.sum(extras))
    others = (shortest + extras).astype(jnp.int32)
    place_at = jax.random.randint(key_place, (), 0, NDOCS).astype(jnp.int32)
    places = jnp.arange(NDOCS, dtype=jnp.int32)
    source = jnp.clip(places - (places > place_at).astype(jnp.int32), 0, other_count - 1)
    return jnp.where(places == place_at, longest, others[source]).astype(jnp.int32)


def block_scale(stream_key, extent, cuts, smallest, high):
    loudness = 1.0
    for position, parts in cuts:
        heights = jax.random.uniform(jax.random.fold_in(jax.random.fold_in(stream_key, 6), position), (parts,), jnp.float32, smallest / len(cuts), high / len(cuts))
        loudness = loudness * jnp.repeat(jnp.exp(heights), extent[position] // parts).reshape((-1,) + (1,) * (len(extent) - 1 - position))
    return loudness


def noise(stream_key, shape, spread, most, cuts=(), held_as=jnp.bfloat16):
    entries = spread * jax.random.normal(stream_key, shape, jnp.float32)
    if cuts:
        entries = entries * block_scale(stream_key, shape, cuts, -0.22, 0.18)
    return jnp.clip(entries, -most, most).astype(held_as)


def setup_inputs(seed: int = 0) -> dict:
    splits = jax.random.split(jax.random.key(seed), 16)
    return {
        "tokens": noise(splits[0], (TOKENS, D), 1.0, 6.0, ((0, 64),)),
        "cotangent": draw_cotangent(jax.random.fold_in(splits[15], 71), 0),
        "lengths": draw_lengths(jax.random.fold_in(splits[15], 71), 0),
        "norm1_gain": jnp.clip(1.0 + 0.1 * jax.random.normal(splits[3], (D,), jnp.float32), 0.5, 1.5),
        "w_query": noise(splits[4], (D, QH, HD), D ** -0.5, 0.15625, ((1, 2),)),
        "b_query": noise(splits[5], (QH, HD), 0.5, 3.0, ((0, 2),)),
        "w_key": noise(splits[6], (D, KVH, HD), D ** -0.5, 0.15625, ((1, 2),)),
        "b_key": noise(splits[7], (KVH, HD), 0.5, 3.0, ((0, 2),)),
        "w_value": noise(splits[8], (D, KVH, HD), D ** -0.5, 0.15625, ((1, 2),)),
        "b_value": noise(splits[9], (KVH, HD), 0.5, 3.0, ((0, 2),)),
        "w_out": noise(splits[10], (QH, HD, D), (QH * HD // 64) ** -0.5, 1.25, ((0, 2),)),
        "norm2_gain": jnp.clip(1.0 + 0.1 * jax.random.normal(splits[11], (D,), jnp.float32), 0.5, 1.5),
        "w_gate": noise(splits[12], (D, FF), D ** -0.5, 0.15625, ((1, 2),)),
        "w_up": noise(splits[13], (D, FF), D ** -0.5, 0.15625, ((1, 2),)),
        "w_down": noise(splits[14], (FF, D), (FF // 16) ** -0.5, 0.25, ((0, 2),)),
    }


@jax.custom_vjp
def low(v):
    return lax.optimization_barrier(v.astype(jnp.bfloat16)).astype(jnp.float32)

@jax.custom_vjp
def low_back(v):
    return v

def low_keep(v):
    return (low(v), None)

def low_pass(kept, grad):
    return (grad,)

def back_keep(v):
    return (v, None)

def back_low(kept, grad):
    return (low(grad),)
low.defvjp(low_keep, low_pass)
low_back.defvjp(back_keep, back_low)

def inverse_rms(values):
    return lax.rsqrt(lax.optimization_barrier(jnp.mean(values * values, axis=-1, keepdims=True)) + 1e-06)

def rotate(values, cos_table, sin_table):
    half_dim = values.shape[-1] // 2
    front = values[..., :half_dim]
    back_half = values[..., half_dim:]
    return jnp.concatenate([front * cos_table - back_half * sin_table, back_half * cos_table + front * sin_table], axis=-1)

def attend(query_blk, key_rows, value_rows, query_doc, query_pos, key_doc, key_pos):
    highest = lax.Precision.HIGHEST
    head_dim = query_blk.shape[-1]
    scores = jnp.einsum('tkgd,skd->tkgs', query_blk, key_rows, precision=highest) * (1.0 / math.sqrt(head_dim))
    scores = low_back(scores)
    visible = (key_doc[None, :] == query_doc[:, None]) & (key_pos[None, :] <= query_pos[:, None])
    scores = jnp.where(visible[:, None, None, :], scores, -1e+30)
    row_max = lax.optimization_barrier(jnp.max(scores, axis=-1, keepdims=True))
    expon = jnp.exp(scores - row_max)
    probs = expon / lax.optimization_barrier(jnp.sum(expon, axis=-1, keepdims=True))
    return jnp.einsum('tkgs,skd->tkgd', low(probs), value_rows, precision=highest)

def reference(tokens, cotangent, lengths, norm1_gain, w_query, b_query, w_key, b_key, w_value, b_value, w_out, norm2_gain, w_gate, w_up, w_down):
    highest = lax.Precision.HIGHEST
    tok_total = tokens.shape[0]
    positions = jnp.arange(tok_total, dtype=jnp.int32)
    row_of_pos = (positions % N_SEQ * TOK_DEV + positions // N_SEQ).astype(jnp.int32)
    pos_of_row = (positions % TOK_DEV * N_SEQ + positions // TOK_DEV).astype(jnp.int32)
    doc_ends = jnp.cumsum(lengths).astype(jnp.int32)
    is_past = positions[:, None] >= doc_ends[None, :]
    doc_ids = lax.optimization_barrier(jnp.sum(is_past.astype(jnp.int32), axis=1)).astype(jnp.int32)
    doc_start = lax.optimization_barrier(jnp.sum(jnp.where(is_past, lengths[None, :], 0), axis=1)).astype(jnp.int32)
    rel_pos = (positions - doc_start).astype(jnp.float32)
    half_dim = HD // 2
    inv_freq = jnp.exp(-(2.0 * jnp.arange(half_dim, dtype=jnp.float32) / HD) * math.log(10000.0))
    angles = rel_pos[:, None] * inv_freq[None, :]
    cos_table = jnp.cos(angles)[:, None, :]
    sin_table = jnp.sin(angles)[:, None, :]
    group = QH // KVH
    query_block = min(512, tok_total)
    attend_block = jax.checkpoint(attend)

    def forward(inputs, gain_one, wq, bq, wk, bk, wv, bv, wo, gain_two, wg, wu, wd):
        normed_first = low(inputs * inverse_rms(inputs) * gain_one)
        q_pre = jnp.einsum('td,dhe->the', normed_first, wq, precision=highest) + bq
        k_pre = jnp.einsum('td,dhe->the', normed_first, wk, precision=highest) + bk
        v_pre = jnp.einsum('td,dhe->the', normed_first, wv, precision=highest) + bv
        queries = low(rotate(low_back(q_pre), cos_table, sin_table)).reshape(tok_total, KVH, group, HD)
        keys = low(rotate(low_back(k_pre), cos_table, sin_table))
        values = low(low_back(v_pre))
        pieces = []
        for blk_index in range(tok_total // query_block):
            lower = blk_index * query_block
            upper = lower + query_block
            pieces.append(attend_block(queries[lower:upper], keys[:upper], values[:upper], doc_ids[lower:upper], positions[lower:upper], doc_ids[:upper], positions[:upper]))
        attn = jnp.concatenate(pieces, axis=0).reshape(tok_total, QH, HD)
        attn_low = low_back(low(attn))
        branch = jnp.einsum('the,hed->td', attn_low, wo, precision=highest)
        mid_stream = inputs + low_back(branch)
        normed_second = low(mid_stream * inverse_rms(mid_stream) * gain_two)
        gate_act = low_back(jnp.dot(normed_second, wg, precision=highest))
        up_act = low_back(jnp.dot(normed_second, wu, precision=highest))
        hidden = low(jax.nn.silu(gate_act) * up_act)
        return mid_stream + low_back(jnp.dot(hidden, wd, precision=highest))
    tokens_pack = jnp.take(tokens.astype(jnp.float32), row_of_pos, axis=0)
    cotangent_pack = jnp.take(cotangent.astype(jnp.float32), row_of_pos, axis=0)
    arguments = (tokens_pack, norm1_gain, w_query.astype(jnp.float32), b_query.astype(jnp.float32), w_key.astype(jnp.float32), b_key.astype(jnp.float32), w_value.astype(jnp.float32), b_value.astype(jnp.float32), w_out.astype(jnp.float32), norm2_gain, w_gate.astype(jnp.float32), w_up.astype(jnp.float32), w_down.astype(jnp.float32))
    result, pullback = jax.vjp(forward, *arguments)
    gradients = pullback(cotangent_pack)
    output_rows = jnp.take(result, pos_of_row, axis=0)
    grad_rows = jnp.take(gradients[0], pos_of_row, axis=0)
    return (output_rows, grad_rows, gradients[1], gradients[2], gradients[3], gradients[4], gradients[5], gradients[6], gradients[7], gradients[8], gradients[9], gradients[10], gradients[11], gradients[12])
```

```python
import math

import jax
import jax.numpy as jnp
from jax import lax
from jax.experimental import pallas as pl
from jax.experimental.pallas import tpu as pltpu
from jax.sharding import PartitionSpec as P

MESH = pl.DeviceIdType.MESH
F32 = jnp.float32
BF16 = jnp.bfloat16
VMEM_BYTES = 60 * 1024 * 1024
AXES = ("z", "x", "y")
STRIDE = {"z": 16, "x": 4, "y": 1}


def coords():
    s = lax.axis_index("seq")
    return {"z": s // 16, "x": (s // 4) % 4, "y": s % 4}


def peer(axis, k):
    s = lax.axis_index("seq")
    c = coords()[axis]
    return (s + STRIDE[axis] * ((c + k) % 4 - c), lax.axis_index("tensor"))


def partner():
    return (lax.axis_index("seq"), 1 - lax.axis_index("tensor"))


def barrier(axes=AXES, core=False):
    bar = pltpu.get_barrier_semaphore()
    ids = [peer(a, k) for a in axes for k in (1, 2, 3)]
    if core:
        ids.append(partner())
    for d in ids:
        pl.semaphore_signal(bar, inc=1, device_id=d, device_id_type=MESH)
    pl.semaphore_wait(bar, len(ids))


def remote(src, dst, send, recv, device):
    return pltpu.make_async_remote_copy(
        src_ref=src, dst_ref=dst, send_sem=send, recv_sem=recv, device_id=device, device_id_type=MESH
    )


def comm_call(body, outs, ins, scratch, cid, name):
    vm = pl.BlockSpec(memory_space=pltpu.VMEM)
    return pl.pallas_call(
        body,
        out_shape=outs,
        in_specs=[vm] * ins,
        out_specs=jax.tree.map(lambda _: vm, outs),
        scratch_shapes=scratch,
        compiler_params=pltpu.CompilerParams(
            collective_id=cid, has_side_effects=True, vmem_limit_bytes=VMEM_BYTES
        ),
        name=name,
    )


DMA = pltpu.SemaphoreType.DMA


def core_sum(cid, *parts):
    n = len(parts)

    def body(*refs):
        ins, outs, bufs, send, recv = refs[:n], refs[n : 2 * n], refs[2 * n : 3 * n], refs[3 * n], refs[3 * n + 1]
        barrier((), True)
        copies = []
        for i in range(n):
            c = remote(ins[i], bufs[i], send.at[i], recv.at[i], partner())
            c.start()
            copies.append(c)
        for i in range(n):
            copies[i].wait()
            outs[i][...] = ins[i][...] + bufs[i][...]

    shapes = tuple(jax.ShapeDtypeStruct(p.shape, p.dtype) for p in parts)
    scratch = [pltpu.VMEM(p.shape, p.dtype) for p in parts] + [DMA((n,)), DMA((n,))]
    return comm_call(body, shapes, n, scratch, cid, "core_sum")(*parts)


KV_PARTS = (
    (0, 96, ("z", "x", "y")),
    (96, 80, ("x", "y", "z")),
    (176, 80, ("y", "z", "x")),
)


def kv_index(done, c, r0, rn):
    return tuple(slice(None) if a in done else c[a] for a in AXES) + (pl.ds(r0, rn), slice(None))


def gather_kv(kv):
    def body(kv_ref, out, send, recv):
        c = coords()
        out[c["z"], c["x"], c["y"]] = kv_ref[...]
        barrier()
        pending = [[] for _ in KV_PARTS]
        for stage in range(3):
            for p, (r0, rn, order) in enumerate(KV_PARTS):
                for copy in pending[p]:
                    copy.wait()
                pending[p] = []
                idx = kv_index(order[:stage], c, r0, rn)
                for k in (1, 2, 3):
                    src = kv_ref.at[pl.ds(r0, rn), :] if stage == 0 else out.at[idx]
                    n = (p * 3 + stage) * 3 + k - 1
                    copy = remote(src, out.at[idx], send.at[n], recv.at[n], peer(order[stage], k))
                    copy.start()
                    pending[p].append(copy)
        for copies in pending:
            for copy in copies:
                copy.wait()

    shape = jax.ShapeDtypeStruct((4, 4, 4, 256, 128), BF16)
    return comm_call(body, shape, 1, [DMA((27,)), DMA((27,))], 0, "gather_kv")(kv)


def scatter_kv(partial):
    def body(*refs):
        ins, out = refs[0], refs[1]
        got1, got2, got3 = refs[2:5], refs[5:8], refs[8:11]
        acc1, acc2 = refs[11:14], refs[14:17]
        send, recv = refs[17], refs[18]
        c = coords()
        barrier()
        pending = [[] for _ in KV_PARTS]
        for stage in range(3):
            for p, (r0, rn, order) in enumerate(KV_PARTS):
                for copy in pending[p]:
                    copy.wait()
                pending[p] = []
                rest = [a for a in AXES if a not in order[:1]]
                if stage == 1:
                    own = ins[kv_index(rest, c, r0, rn)].astype(F32)
                    for k in range(3):
                        own = own + got1[p][k].astype(F32)
                    acc1[p][...] = own.astype(BF16)
                if stage == 2:
                    own = acc1[p][pick1(rest, order, c[order[1]])].astype(F32)
                    for k in range(3):
                        own = own + got2[p][k].astype(F32)
                    acc2[p][...] = own.astype(BF16)
                for k in (1, 2, 3):
                    there = (c[order[stage]] + k) % 4
                    if stage == 0:
                        cc = dict(c)
                        cc[order[0]] = there
                        src, dst = ins.at[kv_index(rest, cc, r0, rn)], got1[p].at[k - 1]
                    elif stage == 1:
                        src, dst = acc1[p].at[pick1(rest, order, there)], got2[p].at[k - 1]
                    else:
                        src, dst = acc2[p].at[there], got3[p].at[k - 1]
                    n = (p * 3 + stage) * 3 + k - 1
                    copy = remote(src, dst, send.at[n], recv.at[n], peer(order[stage], k))
                    copy.start()
                    pending[p].append(copy)
        for p, (r0, rn, order) in enumerate(KV_PARTS):
            for copy in pending[p]:
                copy.wait()
            own = acc2[p][c[order[2]]].astype(F32)
            for k in range(3):
                own = own + got3[p][k].astype(F32)
            out[pl.ds(r0, rn), :] = own

    def pick1(rest, order, where):
        return (where,) if rest[0] == order[1] else (slice(None), where)

    rows = [rn for _, rn, _ in KV_PARTS]
    scratch = (
        [pltpu.VMEM((3, 4, 4, r, 128), BF16) for r in rows]
        + [pltpu.VMEM((3, 4, r, 128), BF16) for r in rows]
        + [pltpu.VMEM((3, r, 128), BF16) for r in rows]
        + [pltpu.VMEM((4, 4, r, 128), BF16) for r in rows]
        + [pltpu.VMEM((4, r, 128), BF16) for r in rows]
        + [DMA((27,)), DMA((27,))]
    )
    shape = jax.ShapeDtypeStruct((256, 128), F32)
    return comm_call(body, shape, 1, scratch, 1, "scatter_kv")(partial)


Q_BLK = 16
BLK = Q_BLK * 64
SCALE = 1.0 / math.sqrt(128)


def doc_bounds(pos, len_ref):
    start = jnp.zeros_like(pos)
    end = jnp.int32(0)
    for j in range(8):
        end = end + len_ref[j]
        start = jnp.where(pos >= end, end, start)
    return start


def doc_start_scalar(pos, len_ref):
    start, end = jnp.int32(0), jnp.int32(0)
    for j in range(8):
        end = end + len_ref[j]
        start = jnp.where(pos >= end, end, start)
    return start


def doc_end_scalar(pos, len_ref):
    end, result = jnp.int32(0), jnp.int32(0)
    for j in range(8):
        result = jnp.where(pos >= end, end + len_ref[j], result)
        end = end + len_ref[j]
    return result


def attn_forward(q, kv, lengths):
    def body(len_ref, q_ref, kv_ref, out_ref, lse_ref):
        dev = lax.axis_index("seq")
        col = lax.broadcasted_iota(jnp.int32, (96, BLK), 1)
        key_off = (col % Q_BLK) * 64 + col // Q_BLK
        row_off = (lax.broadcasted_iota(jnp.int32, (96, 1), 0) % Q_BLK) * 64 + dev

        def q_step(qb, _):
            q_blk = q_ref[qb]
            pos_q = row_off + qb * BLK
            start_q = doc_bounds(pos_q, len_ref)
            lo = doc_start_scalar(qb * BLK + dev, len_ref) // BLK

            def k_step(kb, carry):
                m, l, acc = carry
                rows = pl.ds(pl.multiple_of(kb * Q_BLK, Q_BLK), Q_BLK)
                vrows = pl.ds(pl.multiple_of(128 + kb * Q_BLK, Q_BLK), Q_BLK)
                k_blk = kv_ref[:, rows, :].reshape(BLK, 128)
                v_blk = kv_ref[:, vrows, :].reshape(BLK, 128)
                s = lax.dot_general(q_blk, k_blk, (((1,), (1,)), ((), ())), preferred_element_type=F32)
                pos_k = key_off + kb * BLK
                vis = (pos_k <= pos_q) & (pos_k >= start_q)
                s = jnp.where(vis, s * SCALE, -1e30)
                m_new = jnp.maximum(m, jnp.max(s, axis=1, keepdims=True))
                p = jnp.where(vis, jnp.exp(s - m_new), 0.0)
                a = jnp.exp(m - m_new)
                l = l * a + jnp.sum(p, axis=1, keepdims=True)
                acc = acc * a + jnp.dot(p.astype(BF16), v_blk, preferred_element_type=F32)
                return m_new, l, acc

            init = (jnp.full((96, 1), -1e30, F32), jnp.zeros((96, 1), F32), jnp.zeros((96, 128), F32))
            m, l, acc = lax.fori_loop(lo, qb + 1, k_step, init)
            out_ref[qb] = acc / l
            lse_ref[qb] = m + jnp.log(l)
            return 0

        lax.fori_loop(0, 8, q_step, 0)

    vm = pl.BlockSpec(memory_space=pltpu.VMEM)
    return pl.pallas_call(
        body,
        out_shape=(jax.ShapeDtypeStruct((8, 96, 128), F32), jax.ShapeDtypeStruct((8, 96, 1), F32)),
        in_specs=[pl.BlockSpec(memory_space=pltpu.SMEM), vm, vm],
        out_specs=(vm, vm),
        compiler_params=pltpu.CompilerParams(vmem_limit_bytes=VMEM_BYTES),
        name="attn_forward",
    )(lengths, q, kv)


def attn_backward(q, g, kv, lse, delta, lengths):
    def body(len_ref, q_ref, g_ref, kv_ref, lse_ref, delta_ref, dq_ref, dkv_ref):
        dev = lax.axis_index("seq")
        row = lax.broadcasted_iota(jnp.int32, (BLK, 96), 0)
        key_off = (row % Q_BLK) * 64 + row // Q_BLK
        q_off = (lax.broadcasted_iota(jnp.int32, (1, 96), 1) % Q_BLK) * 64 + dev
        dq_ref[...] = jnp.zeros_like(dq_ref)

        def k_step(kb, _):
            rows = pl.ds(pl.multiple_of(kb * Q_BLK, Q_BLK), Q_BLK)
            vrows = pl.ds(pl.multiple_of(128 + kb * Q_BLK, Q_BLK), Q_BLK)
            k_blk = kv_ref[:, rows, :].reshape(BLK, 128)
            v_blk = kv_ref[:, vrows, :].reshape(BLK, 128)
            k_t = k_blk.T
            pos_k = key_off + kb * BLK
            hi = (doc_end_scalar(kb * BLK + BLK - 1, len_ref) - 1) // BLK

            def q_step(qb, carry):
                dk, dv = carry
                q_blk, g_blk = q_ref[qb], g_ref[qb]
                pos_q = q_off + qb * BLK
                start_q = doc_bounds(pos_q, len_ref)
                s = lax.dot_general(k_blk, q_blk, (((1,), (1,)), ((), ())), preferred_element_type=F32)
                vis = (pos_k <= pos_q) & (pos_k >= start_q)
                p = jnp.where(vis, jnp.exp(s * SCALE - lse_ref[qb]), 0.0)
                gp = lax.dot_general(v_blk, g_blk, (((1,), (1,)), ((), ())), preferred_element_type=F32)
                gs = (p * (gp - delta_ref[qb])).astype(BF16)
                dq_ref[qb] += jnp.dot(k_t, gs, preferred_element_type=F32)
                dk = dk + jnp.dot(gs, q_blk, preferred_element_type=F32)
                dv = dv + jnp.dot(p.astype(BF16), g_blk, preferred_element_type=F32)
                return dk, dv

            zero = jnp.zeros((BLK, 128), F32)
            dk, dv = lax.fori_loop(kb, hi + 1, q_step, (zero, zero))
            dkv_ref[:, rows, :] = (dk * SCALE).astype(BF16).reshape(64, Q_BLK, 128)
            dkv_ref[:, vrows, :] = dv.astype(BF16).reshape(64, Q_BLK, 128)
            return 0

        lax.fori_loop(0, 8, k_step, 0)

    vm = pl.BlockSpec(memory_space=pltpu.VMEM)
    return pl.pallas_call(
        body,
        out_shape=(jax.ShapeDtypeStruct((8, 128, 96), F32), jax.ShapeDtypeStruct((64, 256, 128), BF16)),
        in_specs=[pl.BlockSpec(memory_space=pltpu.SMEM)] + [vm] * 5,
        out_specs=(vm, vm),
        compiler_params=pltpu.CompilerParams(vmem_limit_bytes=VMEM_BYTES),
        name="attn_backward",
    )(lengths, q, g, kv, lse, delta)


def to_blocks(v):
    return v.reshape(8, Q_BLK, 6, 128).transpose(0, 2, 1, 3).reshape(8, 96, 128)


def from_blocks(v):
    return v.reshape(8, 6, Q_BLK, 128).transpose(0, 2, 1, 3).reshape(128, 768)


FF_BLK = 640


def nt(a, b):
    return lax.dot_general(a, b, (((1,), (1,)), ((), ())), preferred_element_type=F32)


def feed_forward(normed, cot, w_gate, w_up, w_down):
    ff = w_gate.shape[1]

    def body(n_ref, c_ref, wg_ref, wu_ref, wd_ref, out_ref, gn_ref, h_ref, gg_ref, gu_ref):
        n, c = n_ref[...], c_ref[...]
        gate = jnp.dot(n, wg_ref[...], preferred_element_type=F32)
        up = jnp.dot(n, wu_ref[...], preferred_element_type=F32)
        gh = nt(c, wd_ref[...])
        sig = 1.0 / (1.0 + jnp.exp(-gate))
        silu = gate * sig
        hidden = (silu * up).astype(BF16)
        g_gate = (gh * up * sig * (1.0 + gate * (1.0 - sig))).astype(BF16)
        g_up = (gh * silu).astype(BF16)
        h_ref[...], gg_ref[...], gu_ref[...] = hidden, g_gate, g_up
        first = pl.program_id(0) == 0
        add_o = jnp.dot(hidden, wd_ref[...], preferred_element_type=F32)
        add_g = nt(g_gate, wg_ref[...]) + nt(g_up, wu_ref[...])

        @pl.when(first)
        def _():
            out_ref[...] = add_o
            gn_ref[...] = add_g

        @pl.when(jnp.logical_not(first))
        def _():
            out_ref[...] += add_o
            gn_ref[...] += add_g

    rows = normed.shape[0]
    whole = pl.BlockSpec((rows, 1536), lambda i: (0, 0))
    cols = pl.BlockSpec((1536, FF_BLK), lambda i: (0, i))
    act = pl.BlockSpec((rows, FF_BLK), lambda i: (0, i))
    return pl.pallas_call(
        body,
        grid=(ff // FF_BLK,),
        out_shape=(
            jax.ShapeDtypeStruct((rows, 1536), F32),
            jax.ShapeDtypeStruct((rows, 1536), F32),
        )
        + (jax.ShapeDtypeStruct((rows, ff), BF16),) * 3,
        in_specs=[whole, whole, cols, cols, pl.BlockSpec((FF_BLK, 1536), lambda i: (i, 0))],
        out_specs=(whole, whole, act, act, act),
        compiler_params=pltpu.CompilerParams(vmem_limit_bytes=VMEM_BYTES),
        name="feed_forward",
    )(normed, cot, w_gate, w_up, w_down)


FC = 1152


def col_start(c):
    return pl.multiple_of(jnp.minimum(c * FC, 4480 - FC), 128)


MLP_AXES = (("z", "x", "y"), ("x", "y", "z"), ("y", "z", "x"))


def mlp_weight_grads(norm_t, cot_t, g_gate, g_up, hidden):
    def body(*refs):
        nt_ref, ct_ref = refs[0], refs[1]
        grads = refs[2:5]
        outs = refs[5:8]
        xs, gs = refs[8:11], refs[11:14]
        sendbuf, got1, got2, acc2, got3 = refs[14:17], refs[17:20], refs[20:23], refs[23:26], refs[26:29]
        loc, send, recv = refs[29], refs[30], refs[31]
        c = coords()
        barrier()
        left = (nt_ref, nt_ref, ct_ref)
        first = []
        for m in range(3):
            w = MLP_AXES[m][0]
            copies = []
            for k in (1, 2, 3):
                n = (m * 4) * 6 + (k - 1) * 2
                a = remote(left[m], xs[m].at[:, pl.ds(k * 128, 128)], send.at[n], recv.at[n], peer(w, k))
                b = remote(
                    grads[m].at[:, pl.ds(col_start((c[w] + k) % 4), FC)],
                    gs[m].at[pl.ds(k * 128, 128), :],
                    send.at[n + 1],
                    recv.at[n + 1],
                    peer(w, k),
                )
                a.start()
                b.start()
                copies += [a, b]
            a = pltpu.make_async_copy(left[m], xs[m].at[:, pl.ds(0, 128)], loc.at[2 * m])
            b = pltpu.make_async_copy(
                grads[m].at[:, pl.ds(col_start(c[w]), FC)], gs[m].at[pl.ds(0, 128), :], loc.at[2 * m + 1]
            )
            a.start()
            b.start()
            first.append(copies + [a, b])

        pending = [[], [], []]

        def send_slab(m, stage, k, src, dst):
            n = (m * 4 + stage) * 6 + k - 1
            copy = remote(src, dst, send.at[n], recv.at[n], peer(MLP_AXES[m][stage % 3], k))
            copy.start()
            pending[m].append(copy)

        def dot(x, g):
            return jnp.dot(x, g, preferred_element_type=F32)

        def regroup(v, outer, inner):
            return jnp.concatenate(
                [v[(o * inner + i) * 24 : (o * inner + i + 1) * 24] for i in range(inner) for o in range(outer)], axis=0
            )

        m = 0
        for copy in first[m]:
            copy.wait()
        for k in (1, 2, 3, 0):
            u = (c["x"] + k) % 4
            rows = [pl.ds(pl.multiple_of(z * 384 + u * 96, 32), 96) for z in range(4)]
            x = jnp.concatenate([xs[m][r, :] for r in rows], axis=0)
            sendbuf[m][k] = regroup(dot(x, gs[m][...]), 4, 4).astype(BF16)
            if k:
                send_slab(m, 1, k, sendbuf[m].at[k], got1[m].at[k - 1])
        m = 2
        for copy in first[m]:
            copy.wait()
        for k in (1, 2, 3, 0):
            u = (c["z"] + k) % 4
            x = xs[m][pl.ds(pl.multiple_of(u * 384, 128), 384), :]
            sendbuf[m][k] = dot(x, gs[m][...]).astype(BF16)
            if k:
                send_slab(m, 1, k, sendbuf[m].at[k], got1[m].at[k - 1])
        m = 1
        for copy in first[m]:
            copy.wait()
        for z in range(4):
            v = regroup(dot(xs[m][z * 384 : (z + 1) * 384, :], gs[m][...]), 4, 4).astype(BF16)
            for y in range(4):
                sendbuf[m][y, z * 96 : (z + 1) * 96] = v[y * 96 : (y + 1) * 96]
        for k in (1, 2, 3):
            send_slab(m, 1, k, sendbuf[m].at[(c["y"] + k) % 4], got1[m].at[k - 1])

        for m in (0, 2, 1):
            for copy in pending[m]:
                copy.wait()
            pending[m] = []
            own = c["y"] if m == 1 else 0
            total = sendbuf[m][own].astype(F32)
            for k in range(3):
                total = total + got1[m][k].astype(F32)
            sendbuf[m][own] = total.astype(BF16)
            axis = MLP_AXES[m][2]
            for k in (1, 2, 3):
                rows = pl.ds(pl.multiple_of(((c[axis] + k) % 4) * 96, 32), 96)
                send_slab(m, 2, k, sendbuf[m].at[own, rows, :], got2[m].at[k - 1])
        for m in (0, 2, 1):
            for copy in pending[m]:
                copy.wait()
            pending[m] = []
            own = c["y"] if m == 1 else 0
            rows = pl.ds(pl.multiple_of(c[MLP_AXES[m][2]] * 96, 32), 96)
            total = sendbuf[m][own, rows, :].astype(F32)
            for k in range(3):
                total = total + got2[m][k].astype(F32)
            acc2[m][...] = total
            axis = MLP_AXES[m][0]
            for k in (1, 2, 3):
                rows = pl.ds(pl.multiple_of(((c[axis] + k) % 4) * 24, 8), 24)
                send_slab(m, 3, k, acc2[m].at[rows, :], got3[m].at[k - 1])
        for m in (0, 2, 1):
            for copy in pending[m]:
                copy.wait()
            here = c[MLP_AXES[m][0]]
            outs[m][:, pl.ds(col_start(here), FC)] = acc2[m][pl.ds(pl.multiple_of(here * 24, 8), 24), :]
            for k in (1, 2, 3):
                outs[m][:, pl.ds(col_start((here + 4 - k) % 4), FC)] = got3[m][k - 1]

    scratch = (
        [pltpu.VMEM((1536, 512), BF16)] * 3
        + [pltpu.VMEM((512, FC), BF16)] * 3
        + [pltpu.VMEM((4, 384, FC), BF16)] * 3
        + [pltpu.VMEM((3, 384, FC), BF16)] * 3
        + [pltpu.VMEM((3, 96, FC), BF16)] * 3
        + [pltpu.VMEM((96, FC), F32)] * 3
        + [pltpu.VMEM((3, 24, FC), F32)] * 3
        + [DMA((6,)), DMA((72,)), DMA((72,))]
    )
    shape = tuple(jax.ShapeDtypeStruct((24, 4480), F32) for _ in range(3))
    return comm_call(body, shape, 5, scratch, 2, "mlp_weight_grads")(norm_t, cot_t, g_gate, g_up, hidden)


ATTN_PARTS = ((640, ("z", "x", "y")), (640, ("x", "y", "z")), (512, ("y", "z", "x")))
SMALL = 40


def attn_weight_grads(norm_t, branch_t, g_qkv, attn_low, small):
    def body(*refs):
        nt_ref, bt_ref, g_ref, a_ref, s_ref = refs[:5]
        outs, s_out = refs[5:8], refs[8]
        sendbuf, got1, got2, acc2, got3 = refs[9:12], refs[12:15], refs[15:18], refs[18:21], refs[21:24]
        s_acc, s_got, send, recv = refs[24:28]
        c = coords()
        barrier(core=True)
        s_copy = remote(s_ref, s_got.at[0], send.at[36], recv.at[36], partner())
        s_copy.start()
        pending = [[], [], []]

        def send_slab(p, stage, k, src, dst):
            n = (p * 3 + stage) * 3 + k - 1
            copy = remote(src, dst, send.at[n], recv.at[n], peer(ATTN_PARTS[p][1][stage], k))
            copy.start()
            pending[p].append(copy)

        def product(rows, p):
            x, b = nt_ref[rows, :], bt_ref[rows, :]
            if p == 0:
                return jnp.dot(x, g_ref[:, :640], preferred_element_type=F32)
            if p == 1:
                left = jnp.dot(x, g_ref[:, 640:], preferred_element_type=F32)
                return jnp.concatenate([left, jnp.dot(b, a_ref[:, :256], preferred_element_type=F32)], axis=1)
            return jnp.dot(b, a_ref[:, 256:], preferred_element_type=F32)

        def blocks(v, order):
            return jnp.concatenate([v[o * 24 : (o + 1) * 24] for o in order], axis=0)

        for z in range(4):
            rows = slice(z * 384, (z + 1) * 384)
            sendbuf[0][z] = product(rows, 0).astype(BF16)
        for z in range(4):
            rows = slice(z * 384, (z + 1) * 384)
            v = product(rows, 2)
            v = blocks(v, [x * 4 + y for y in range(4) for x in range(4)]).astype(BF16)
            for y in range(4):
                sendbuf[2][y, z * 96 : (z + 1) * 96] = v[y * 96 : (y + 1) * 96]
        for x in range(4):
            v = jnp.concatenate([product(slice(z * 384 + x * 96, z * 384 + (x + 1) * 96), 1) for z in range(4)], axis=0)
            sendbuf[1][x] = blocks(v, [z * 4 + y for y in range(4) for z in range(4)]).astype(BF16)
        for p in range(3):
            for k in (1, 2, 3):
                there = (c[ATTN_PARTS[p][1][0]] + k) % 4
                send_slab(p, 0, k, sendbuf[p].at[there], got1[p].at[k - 1])
        s_copy.wait()
        s_acc[0] = s_ref[...] + s_got[0]
        s_pending = []

        def send_small(stage):
            for k in (1, 2, 3):
                n = 27 + stage * 3 + k - 1
                copy = remote(
                    s_acc.at[stage], s_got.at[1 + stage * 3 + k - 1], send.at[n], recv.at[n], peer(AXES[stage], k)
                )
                copy.start()
                s_pending.append(copy)

        def sum_small(stage):
            for copy in s_pending:
                copy.wait()
            s_pending.clear()
            axis = AXES[stage]
            parts = [s_acc[stage]] + [s_got[1 + stage * 3 + k] for k in range(3)]
            total = jnp.zeros_like(parts[0])
            for w in range(4):
                term = jnp.zeros_like(total)
                for k in range(4):
                    term = jnp.where((c[axis] + 4 - k) % 4 == w, parts[k], term)
                total = total + term
            return total

        send_small(0)
        for p in range(3):
            for copy in pending[p]:
                copy.wait()
            pending[p] = []
            order = ATTN_PARTS[p][1]
            own = c[order[0]]
            total = sendbuf[p][own].astype(F32)
            for k in range(3):
                total = total + got1[p][k].astype(F32)
            sendbuf[p][own] = total.astype(BF16)
            for k in (1, 2, 3):
                rows = pl.ds(pl.multiple_of(((c[order[1]] + k) % 4) * 96, 32), 96)
                send_slab(p, 1, k, sendbuf[p].at[own, rows, :], got2[p].at[k - 1])
        s_acc[1] = sum_small(0)
        send_small(1)
        for p in range(3):
            for copy in pending[p]:
                copy.wait()
            pending[p] = []
            order = ATTN_PARTS[p][1]
            own = c[order[0]]
            rows = pl.ds(pl.multiple_of(c[order[1]] * 96, 32), 96)
            total = sendbuf[p][own, rows, :].astype(F32)
            for k in range(3):
                total = total + got2[p][k].astype(F32)
            acc2[p][...] = total
            for k in (1, 2, 3):
                rows = pl.ds(pl.multiple_of(((c[order[2]] + k) % 4) * 24, 8), 24)
                send_slab(p, 2, k, acc2[p].at[rows, :], got3[p].at[k - 1])
        s_acc[2] = sum_small(1)
        send_small(2)
        for p in range(3):
            for copy in pending[p]:
                copy.wait()
            rows = pl.ds(pl.multiple_of(c[ATTN_PARTS[p][1][2]] * 24, 8), 24)
            total = acc2[p][rows, :]
            for k in range(3):
                total = total + got3[p][k]
            outs[p][...] = total
        s_out[...] = sum_small(2)

    cols = [n for n, _ in ATTN_PARTS]
    scratch = (
        [pltpu.VMEM((4, 384, n), BF16) for n in cols]
        + [pltpu.VMEM((3, 384, n), BF16) for n in cols]
        + [pltpu.VMEM((3, 96, n), BF16) for n in cols]
        + [pltpu.VMEM((96, n), F32) for n in cols]
        + [pltpu.VMEM((3, 24, n), F32) for n in cols]
        + [pltpu.VMEM((3, SMALL, 128), F32), pltpu.VMEM((10, SMALL, 128), F32), DMA((37,)), DMA((37,))]
    )
    shape = tuple(jax.ShapeDtypeStruct((24, n), F32) for n in cols) + (jax.ShapeDtypeStruct((SMALL, 128), F32),)
    return comm_call(body, shape, 5, scratch, 3, "attn_weight_grads")(norm_t, branch_t, g_qkv, attn_low, small)


def inverse_rms(values):
    return lax.rsqrt(jnp.mean(values * values, axis=-1, keepdims=True) + 1e-06)


def rotate(values, cos_table, sin_table):
    front, back_half = values[..., :64], values[..., 64:]
    return jnp.concatenate(
        [front * cos_table - back_half * sin_table, back_half * cos_table + front * sin_table], axis=-1
    )


def rotate_back(gradient, cos_table, sin_table):
    front, back_half = gradient[..., :64], gradient[..., 64:]
    return jnp.concatenate(
        [front * cos_table + back_half * sin_table, back_half * cos_table - front * sin_table], axis=-1
    )


def norm_back(gradient, source, inverse, gain):
    scaled = gradient * gain
    return inverse * scaled - source * inverse**3 * jnp.mean(scaled * source, axis=-1, keepdims=True)


def dot(a, b):
    return jnp.dot(a, b, preferred_element_type=F32)


def local(
    tokens, cotangent, lengths, norm1_gain, w_query, b_query, w_key, b_key, w_value, b_value, w_out,
    norm2_gain, w_gate, w_up, w_down,
):
    device = lax.axis_index("seq")
    core = lax.axis_index("tensor")
    positions = jnp.arange(128, dtype=jnp.int32) * 64 + device
    doc_ends = jnp.cumsum(lengths)
    is_past = positions[:, None] >= doc_ends[None, :]
    doc_start = jnp.sum(jnp.where(is_past, lengths[None, :], 0), axis=1)
    inv_freq = jnp.exp(-(2.0 * jnp.arange(64, dtype=F32) / 128) * math.log(10000.0))
    angles = (positions - doc_start).astype(F32)[:, None] * inv_freq[None, :]
    cos_table, sin_table = jnp.cos(angles)[:, None, :], jnp.sin(angles)[:, None, :]

    inputs = tokens.astype(F32)
    inv_first = inverse_rms(inputs)
    normed_first = (inputs * inv_first * norm1_gain).astype(BF16)
    wq, wk, wv = w_query.reshape(1536, 768), w_key.reshape(1536, 128), w_value.reshape(1536, 128)
    q_pre = dot(normed_first, wq).reshape(128, 6, 128) + b_query.astype(F32)
    k_pre = dot(normed_first, wk).reshape(128, 1, 128) + b_key.astype(F32)
    v_pre = dot(normed_first, wv) + b_value.astype(F32)
    q_blocks = to_blocks(rotate(q_pre, cos_table, sin_table).astype(BF16).reshape(128, 768))
    key_rows = rotate(k_pre, cos_table, sin_table).astype(BF16).reshape(128, 128)
    kv = gather_kv(jnp.concatenate([key_rows, v_pre.astype(BF16)], axis=0)).reshape(64, 256, 128)

    attn_blocks, lse = attn_forward(q_blocks, kv, lengths)
    attn_low = from_blocks(attn_blocks.astype(BF16))
    wo = w_out.reshape(768, 1536)
    (branch,) = core_sum(4, dot(attn_low, wo))
    mid_stream = inputs + branch
    inv_second = inverse_rms(mid_stream)
    normed_second = (mid_stream * inv_second * norm2_gain).astype(BF16)

    mlp_part, g_normed2_part, hidden, g_gate, g_up = feed_forward(normed_second, cotangent, w_gate, w_up, w_down)
    d_norm2 = jnp.sum(g_normed2_part * mid_stream * inv_second, axis=0)
    mlp_out, g_normed2 = core_sum(5, mlp_part, g_normed2_part)
    output = mid_stream + mlp_out
    g_mid = cotangent.astype(F32) + norm_back(g_normed2, mid_stream, inv_second, norm2_gain)
    g_branch = g_mid.astype(BF16)

    grad_gate, grad_up, grad_down = mlp_weight_grads(normed_second.T, cotangent.T, g_gate, g_up, hidden)

    g_attn = nt(g_branch, wo)
    g_blocks = to_blocks(g_attn.astype(BF16))
    delta = jnp.sum(g_blocks.astype(F32) * attn_blocks, axis=-1)
    dq_t, dkv = attn_backward(
        q_blocks, g_blocks, kv, lse.reshape(8, 1, 96), delta.reshape(8, 1, 96), lengths
    )
    dkv_own = scatter_kv(dkv.reshape(4, 4, 4, 256, 128))
    dq = from_blocks(dq_t.transpose(0, 2, 1)).reshape(128, 6, 128) * SCALE
    g_q_pre = rotate_back(dq, cos_table, sin_table).astype(BF16).reshape(128, 768)
    g_k_pre = rotate_back(dkv_own[:128].reshape(128, 1, 128), cos_table, sin_table).astype(BF16).reshape(128, 128)
    g_v_pre = dkv_own[128:].astype(BF16)
    g_qkv = jnp.concatenate([g_q_pre, g_k_pre, g_v_pre], axis=1)
    d_bias = jnp.sum(g_qkv.astype(F32), axis=0)
    g_normed1_part = nt(g_q_pre, wq) + nt(g_k_pre, wk) + nt(g_v_pre, wv)
    d_norm1 = jnp.sum(g_normed1_part * inputs * inv_first, axis=0)
    (g_normed1,) = core_sum(6, g_normed1_part)
    grad_tokens = g_mid + norm_back(g_normed1, inputs, inv_first, norm1_gain)

    part0, part1, part2, sums = attn_weight_grads(
        normed_first.T, g_branch.T, g_qkv, attn_low, pack_small(d_norm1, d_norm2, d_bias, core)
    )
    sums = sums.reshape(-1)
    grad_wq = jnp.concatenate([part0, part1[:, :128]], axis=1).reshape(24, 6, 128)
    grad_wk = part1[:, 128:256].reshape(24, 1, 128)
    grad_wv = part1[:, 256:384].reshape(24, 1, 128)
    grad_wo = jnp.concatenate([part1[:, 384:], part2], axis=1).T.reshape(6, 128, 24)
    grad_norm1 = lax.dynamic_slice(sums, (device * 24,), (24,))
    grad_norm2 = lax.dynamic_slice(sums, (1536 + device * 24,), (24,))
    bias = lax.dynamic_slice(sums, (3072 + core * 1024,), (1024,)).reshape(8, 128)
    bias = lax.dynamic_slice(bias, (0, device * 2), (8, 2))
    return (
        output,
        grad_tokens,
        grad_norm1,
        grad_wq,
        bias[:6],
        grad_wk,
        bias[6:7],
        grad_wv,
        bias[7:8],
        grad_wo,
        grad_norm2,
        grad_gate,
        grad_up,
        grad_down.T,
    )


def pack_small(d_norm1, d_norm2, d_bias, core):
    zero = jnp.zeros_like(d_bias)
    return jnp.concatenate(
        [d_norm1, d_norm2, jnp.where(core == 0, d_bias, zero), jnp.where(core == 1, d_bias, zero)]
    ).reshape(SMALL, 128)


def solution(mesh):
    in_specs = (
        P("seq", None), P("seq", None), P(), P(), P(None, "tensor", None), P("tensor", None),
        P(None, "tensor", None), P("tensor", None), P(None, "tensor", None), P("tensor", None),
        P("tensor", None, None), P(), P(None, "tensor"), P(None, "tensor"), P("tensor", None),
    )
    out_specs = (
        P("seq", None), P("seq", None), P("seq"), P("seq", "tensor", None), P("tensor", "seq"),
        P("seq", "tensor", None), P("tensor", "seq"), P("seq", "tensor", None), P("tensor", "seq"),
        P("tensor", None, "seq"), P("seq"), P("seq", "tensor"), P("seq", "tensor"), P("tensor", "seq"),
    )
    return jax.shard_map(local, mesh=mesh, in_specs=in_specs, out_specs=out_specs, check_vma=False)
```

```python
import math

import jax
import jax.numpy as jnp
from jax import lax
from jax.experimental import pallas as pl
from jax.experimental.pallas import tpu as pltpu
from jax.sharding import PartitionSpec as P

MESH = pl.DeviceIdType.MESH
F32 = jnp.float32
BF16 = jnp.bfloat16
VMEM_BYTES = 60 * 1024 * 1024
AXES = ("z", "x", "y")
STRIDE = {"z": 16, "x": 4, "y": 1}


def coords():
    s = lax.axis_index("seq")
    return {"z": s // 16, "x": (s // 4) % 4, "y": s % 4}


def peer(axis, k):
    s = lax.axis_index("seq")
    c = coords()[axis]
    return (s + STRIDE[axis] * ((c + k) % 4 - c), lax.axis_index("tensor"))


def partner():
    return (lax.axis_index("seq"), 1 - lax.axis_index("tensor"))


def barrier(axes=AXES, core=False):
    bar = pltpu.get_barrier_semaphore()
    ids = [peer(a, k) for a in axes for k in (1, 2, 3)]
    if core:
        ids.append(partner())
    for d in ids:
        pl.semaphore_signal(bar, inc=1, device_id=d, device_id_type=MESH)
    pl.semaphore_wait(bar, len(ids))


def remote(src, dst, send, recv, device):
    return pltpu.make_async_remote_copy(
        src_ref=src, dst_ref=dst, send_sem=send, recv_sem=recv, device_id=device, device_id_type=MESH
    )


def comm_call(body, outs, ins, scratch, cid, name):
    vm = pl.BlockSpec(memory_space=pltpu.VMEM)
    return pl.pallas_call(
        body,
        out_shape=outs,
        in_specs=[vm] * ins,
        out_specs=jax.tree.map(lambda _: vm, outs),
        scratch_shapes=scratch,
        compiler_params=pltpu.CompilerParams(
            collective_id=cid, has_side_effects=True, vmem_limit_bytes=VMEM_BYTES
        ),
        name=name,
    )


DMA = pltpu.SemaphoreType.DMA


KV_PARTS = (
    (0, 96, ("z", "x", "y")),
    (96, 80, ("x", "y", "z")),
    (176, 80, ("y", "z", "x")),
)


def kv_index(done, c, r0, rn):
    return tuple(slice(None) if a in done else c[a] for a in AXES) + (pl.ds(r0, rn), slice(None))


def rope_tables(len_ref):
    lane = lax.broadcasted_iota(jnp.int32, (128, 128), 1)
    pos = lax.broadcasted_iota(jnp.int32, (128, 128), 0) * 64 + lax.axis_index("seq")
    rel = (pos - doc_bounds(pos, len_ref)).astype(F32)
    inv_freq = jnp.exp(-(2.0 * (lane % 64).astype(F32) / 128) * math.log(10000.0))
    angle = rel * inv_freq
    sin = jnp.sin(angle)
    return jnp.cos(angle), jnp.where(lane < 64, -sin, sin)


def swap_halves(v):
    return pltpu.roll(v, 64, 1)


def qkv_gather(tokens, gain, wq, wk, wv, bq, bk, bv, lengths):
    def body(len_ref, t_ref, g_ref, wq_ref, wk_ref, wv_ref, bq_ref, bk_ref, bv_ref,
             q_out, out, nt_out, cos_out, sin_out, send, recv):
        c = coords()
        x = t_ref[...].astype(F32)
        inv = lax.rsqrt(jnp.mean(x * x, axis=1, keepdims=True) + 1e-06)
        normed = (x * inv * g_ref[...]).astype(BF16)
        cos, sin = rope_tables(len_ref)
        cos_out[...], sin_out[...] = cos, sin
        k_pre = jnp.dot(normed, wk_ref[...], preferred_element_type=F32) + bk_ref[...].astype(F32)
        v_pre = jnp.dot(normed, wv_ref[...], preferred_element_type=F32) + bv_ref[...].astype(F32)
        k_rot = (k_pre * cos + swap_halves(k_pre) * sin).astype(BF16)
        out[c["z"], c["x"], c["y"]] = jnp.concatenate([k_rot, v_pre.astype(BF16)], axis=0)
        barrier()
        pending = [[] for _ in KV_PARTS]

        def send_stage(stage):
            for p, (r0, rn, order) in enumerate(KV_PARTS):
                for copy in pending[p]:
                    copy.wait()
                pending[p] = []
                idx = kv_index(order[:stage], c, r0, rn)
                for k in (1, 2, 3):
                    n = (p * 3 + stage) * 3 + k - 1
                    copy = remote(out.at[idx], out.at[idx], send.at[n], recv.at[n], peer(order[stage], k))
                    copy.start()
                    pending[p].append(copy)

        send_stage(0)
        for h in range(6):
            q = jnp.dot(normed, wq_ref[h], preferred_element_type=F32) + bq_ref[h : h + 1, :].astype(F32)
            q = (q * cos + swap_halves(q) * sin).astype(BF16)
            q_out[:, h * Q_BLK : (h + 1) * Q_BLK, :] = q.reshape(8, Q_BLK, 128)
        send_stage(1)
        nt_out[...] = normed.T
        send_stage(2)
        for copies in pending:
            for copy in copies:
                copy.wait()

    vm, sm = pl.BlockSpec(memory_space=pltpu.VMEM), pl.BlockSpec(memory_space=pltpu.SMEM)
    return pl.pallas_call(
        body,
        out_shape=(
            jax.ShapeDtypeStruct((8, 96, 128), BF16),
            jax.ShapeDtypeStruct((4, 4, 4, 256, 128), BF16),
            jax.ShapeDtypeStruct((1536, 128), BF16),
            jax.ShapeDtypeStruct((128, 128), F32),
            jax.ShapeDtypeStruct((128, 128), F32),
        ),
        in_specs=[sm] + [vm] * 8,
        out_specs=(vm,) * 5,
        scratch_shapes=[DMA((27,)), DMA((27,))],
        compiler_params=pltpu.CompilerParams(collective_id=0, has_side_effects=True, vmem_limit_bytes=VMEM_BYTES),
        name="qkv_gather",
    )(lengths, tokens, gain, wq, wk, wv, bq, bk, bv)


Q_BLK = 16
BLK = Q_BLK * 64
SCALE = 1.0 / math.sqrt(128)


def doc_bounds(pos, len_ref):
    start = jnp.zeros_like(pos)
    end = jnp.int32(0)
    for j in range(8):
        end = end + len_ref[j]
        start = jnp.where(pos >= end, end, start)
    return start


def doc_start_scalar(pos, len_ref):
    start, end = jnp.int32(0), jnp.int32(0)
    for j in range(8):
        end = end + len_ref[j]
        start = jnp.where(pos >= end, end, start)
    return start


def attn_forward(q, kv, w_out, lengths):
    def body(len_ref, q_ref, kv_ref, wo_ref, part_ref, out_ref, low_ref, lse_ref):
        dev = lax.axis_index("seq")
        col = lax.broadcasted_iota(jnp.int32, (96, BLK), 1)
        key_off = (col % Q_BLK) * 64 + col // Q_BLK
        row_off = (lax.broadcasted_iota(jnp.int32, (96, 1), 0) % Q_BLK) * 64 + dev

        def q_step(qb, _):
            q_blk = q_ref[qb]
            pos_q = row_off + qb * BLK
            start_q = doc_bounds(pos_q, len_ref)
            lo = doc_start_scalar(qb * BLK + dev, len_ref) // BLK

            def k_step(kb, carry):
                m, l, acc = carry
                rows = pl.ds(pl.multiple_of(kb * Q_BLK, Q_BLK), Q_BLK)
                vrows = pl.ds(pl.multiple_of(128 + kb * Q_BLK, Q_BLK), Q_BLK)
                k_blk = kv_ref[:, rows, :].reshape(BLK, 128)
                v_blk = kv_ref[:, vrows, :].reshape(BLK, 128)
                s = lax.dot_general(q_blk, k_blk, (((1,), (1,)), ((), ())), preferred_element_type=F32)
                pos_k = key_off + kb * BLK
                vis = (pos_k <= pos_q) & (pos_k >= start_q)
                s = jnp.where(vis, s * SCALE, -1e30)
                m_new = jnp.maximum(m, jnp.max(s, axis=1, keepdims=True))
                p = jnp.where(vis, jnp.exp(s - m_new), 0.0)
                a = jnp.exp(m - m_new)
                l = l * a + jnp.sum(p, axis=1, keepdims=True)
                acc = acc * a + jnp.dot(p.astype(BF16), v_blk, preferred_element_type=F32)
                return m_new, l, acc

            init = (jnp.full((96, 1), -1e30, F32), jnp.zeros((96, 1), F32), jnp.zeros((96, 128), F32))
            m, l, acc = lax.fori_loop(lo, qb + 1, k_step, init)
            attn = acc / l
            out_ref[qb] = attn
            low = attn.astype(BF16)
            for h in range(6):
                rows = pl.ds(pl.multiple_of(qb * Q_BLK, Q_BLK), Q_BLK)
                low_ref[rows, h * 128 : (h + 1) * 128] = low[h * Q_BLK : (h + 1) * Q_BLK]
            lse_ref[qb] = jnp.broadcast_to(m + jnp.log(l), (96, 128)).T[0:1]
            return 0

        lax.fori_loop(0, 8, q_step, 0)
        part_ref[...] = jnp.dot(low_ref[...], wo_ref[...], preferred_element_type=F32)

    vm = pl.BlockSpec(memory_space=pltpu.VMEM)
    return pl.pallas_call(
        body,
        out_shape=(
            jax.ShapeDtypeStruct((128, 1536), F32),
            jax.ShapeDtypeStruct((8, 96, 128), F32),
            jax.ShapeDtypeStruct((128, 768), BF16),
            jax.ShapeDtypeStruct((8, 1, 96), F32),
        ),
        in_specs=[pl.BlockSpec(memory_space=pltpu.SMEM), vm, vm, vm],
        out_specs=(vm,) * 4,
        compiler_params=pltpu.CompilerParams(vmem_limit_bytes=VMEM_BYTES),
        name="attn_forward",
    )(lengths, q, kv, w_out)


FC = 1152


def nt(a, b):
    return lax.dot_general(a, b, (((1,), (1,)), ((), ())), preferred_element_type=F32)


def mm(a, b):
    return jnp.dot(a, b, preferred_element_type=F32)


def col_start(c):
    return pl.multiple_of(jnp.minimum(c * FC, 4480 - FC), 128)


MLP_AXES = (("z", "x", "y"), ("x", "y", "z"), ("y", "z", "x"))


def feed_forward(branch, attn, tokens, cot, gain, w_out, w_gate, w_up, w_down):
    def body(br_ref, at_ref, t_ref, c_ref, g_ref, wo_ref, wg_hbm, wu_hbm, wd_hbm,
             out_ref, gmid_ref, bt_ref, ga_ref, delta_ref, dn_ref, x0, x1, x2, g0, g1, g2,
             wg, wu, wd, got_br, acc, got, mid_ref, norm_ref, nt_ref, act, w_sem, loc, send, recv):
        xs, gs = (x0, x1, x2), (g0, g1, g2)
        c = coords()
        turn = c["z"] + c["x"] + c["y"]
        sems = iter(range(64))

        def load(j):
            cols = pl.ds(col_start((turn + j) % 4), FC)
            b = j % 2
            copies = [
                pltpu.make_async_copy(wg_hbm.at[:, cols], wg.at[b], w_sem.at[b, 0]),
                pltpu.make_async_copy(wu_hbm.at[:, cols], wu.at[b], w_sem.at[b, 1]),
                pltpu.make_async_copy(wd_hbm.at[cols, :], wd.at[b], w_sem.at[b, 2]),
            ]
            for copy in copies:
                copy.start()
            return copies

        loads = [load(0), load(1)]
        barrier(core=True)

        def push(src, dst, device):
            n = next(sems)
            copy = remote(src, dst, send.at[n], recv.at[n], device)
            copy.start()
            return copy

        later = []
        ex = push(br_ref, got_br, partner())
        x2[:, 0:128] = c_ref[...].T
        for k in (1, 2, 3):
            later.append(push(x2.at[:, pl.ds(0, 128)], x2.at[:, pl.ds(k * 128, 128)], peer("y", k)))
        ex.wait()
        mid = t_ref[...].astype(F32) + (br_ref[...] + got_br[...])
        mid_ref[...] = mid
        inv = lax.rsqrt(jnp.mean(mid * mid, axis=1, keepdims=True) + 1e-06)
        normed = (mid * inv * g_ref[...]).astype(BF16)
        norm_ref[...] = normed
        nt_ref[...] = normed.T
        x0[:, 0:128] = nt_ref[...]
        x1[:, 0:128] = nt_ref[...]
        for k in (1, 2, 3):
            for m, w in ((0, "z"), (1, "x")):
                later.append(push(nt_ref, xs[m].at[:, pl.ds(k * 128, 128)], peer(w, k)))

        lane = lax.broadcasted_iota(jnp.int32, (128, FC), 1)
        for j in range(4):
            b = j % 2
            d = (turn + j) % 4
            for copy in loads[j]:
                copy.wait()
            n = norm_ref[...]
            gate = mm(n, wg[b])
            up = mm(n, wu[b])
            gh = nt(c_ref[...], wd[b])
            sig = 1.0 / (1.0 + jnp.exp(-gate))
            silu = gate * sig
            hidden = (silu * up).astype(BF16)
            g_gate = (gh * up * sig * (1.0 + gate * (1.0 - sig))).astype(BF16)
            g_up = (gh * silu).astype(BF16)
            vals = (g_gate, g_up, hidden)
            for m in range(3):
                act[m, j] = vals[m]
            twice = (lane < 128) & (d == 3)
            zero = jnp.zeros((128, FC), BF16)
            hidden, g_gate, g_up = (jnp.where(twice, zero, v) for v in (hidden, g_gate, g_up))
            add_o = mm(hidden, wd[b])
            add_g = nt(g_gate, wg[b]) + nt(g_up, wu[b])
            if j == 0:
                acc[0], acc[1] = add_o, add_g
            else:
                acc[0] += add_o
                acc[1] += add_g
            if j + 2 < 4:
                loads.append(load(j + 2))
            for m in range(3):
                w = MLP_AXES[m][0]
                k = (d + 4 - c[w]) % 4
                slot = pl.ds(pl.multiple_of(k * 128, 128), 128)

                @pl.when(k == 0)
                def _():
                    copy = pltpu.make_async_copy(act.at[m, j], gs[m].at[pl.ds(0, 128), :], loc.at[m])
                    copy.start()
                    copy.wait()

                @pl.when(k != 0)
                def _():
                    remote(
                        act.at[m, j], gs[m].at[slot, :], send.at[32 + m * 4 + j], recv.at[32 + m * 4 + k], peer(w, k)
                    ).start()

        dn_ref[...] = jnp.sum(acc[1] * mid_ref[...] * inv, axis=0, keepdims=True)
        ex = [push(acc.at[1], got.at[1], partner()), push(acc.at[0], got.at[0], partner())]
        cot_f = c_ref[...].astype(F32)
        ex[0].wait()
        gn = acc[1] + got[1]
        mid = mid_ref[...]
        scaled = gn * g_ref[...]
        g_mid = cot_f + (inv * scaled - mid * (inv * inv * inv) * jnp.mean(scaled * mid, axis=1, keepdims=True))
        gmid_ref[...] = g_mid
        branch_low = g_mid.astype(BF16)
        bt_ref[...] = branch_low.T
        g_attn = nt(branch_low, wo_ref[...]).astype(BF16)
        for h in range(6):
            ga_ref[:, h * Q_BLK : (h + 1) * Q_BLK, :] = g_attn[:, h * 128 : (h + 1) * 128].reshape(8, Q_BLK, 128)
        for qb in range(8):
            delta_ref[qb] = jnp.sum((ga_ref[qb].astype(F32) * at_ref[qb]).T, axis=0, keepdims=True)
        ex[1].wait()
        out_ref[...] = mid_ref[...] + (acc[0] + got[0])
        for copy in later:
            copy.wait()
        for m in range(3):
            w = MLP_AXES[m][0]
            for j in range(4):
                k = ((turn + j) % 4 + 4 - c[w]) % 4

                @pl.when(k != 0)
                def _():
                    slot = pl.ds(pl.multiple_of(k * 128, 128), 128)
                    remote(
                        act.at[m, j], gs[m].at[slot, :], send.at[32 + m * 4 + j], recv.at[32 + m * 4 + k], peer(w, k)
                    ).wait()

    f32 = lambda *s: jax.ShapeDtypeStruct(s, F32)
    b16 = lambda *s: jax.ShapeDtypeStruct(s, BF16)
    vm, hbm = pl.BlockSpec(memory_space=pltpu.VMEM), pl.BlockSpec(memory_space=pl.ANY)
    return pl.pallas_call(
        body,
        out_shape=(f32(128, 1536), f32(128, 1536), b16(1536, 128), b16(8, 96, 128), f32(8, 1, 96), f32(1, 1536))
        + (b16(1536, 512),) * 3
        + (b16(512, FC),) * 3,
        in_specs=[vm] * 6 + [hbm] * 3,
        out_specs=(vm,) * 12,
        scratch_shapes=[
            pltpu.VMEM((2, 1536, FC), BF16),
            pltpu.VMEM((2, 1536, FC), BF16),
            pltpu.VMEM((2, FC, 1536), BF16),
            pltpu.VMEM((128, 1536), F32),
            pltpu.VMEM((2, 128, 1536), F32),
            pltpu.VMEM((2, 128, 1536), F32),
            pltpu.VMEM((128, 1536), F32),
            pltpu.VMEM((128, 1536), BF16),
            pltpu.VMEM((1536, 128), BF16),
            pltpu.VMEM((3, 4, 128, FC), BF16),
            DMA((2, 3)),
            DMA((3,)),
            DMA((64,)),
            DMA((64,)),
        ],
        compiler_params=pltpu.CompilerParams(collective_id=4, has_side_effects=True, vmem_limit_bytes=VMEM_BYTES),
        name="feed_forward",
    )(branch, attn, tokens, cot, gain, w_out, w_gate, w_up, w_down)


def backward(xs_in, gs_in, q, g, kv, lse, delta, lengths):
    def body(*refs):
        len_ref = refs[0]
        xs, gs = refs[1:4], refs[4:7]
        q_ref, g_ref, kv_ref, lse_ref, delta_ref = refs[7:12]
        outs, dq_ref, own_ref = refs[12:15], refs[15], refs[16]
        sendbuf, got1, got2, acc2, got3 = refs[17:20], refs[20:23], refs[23:26], refs[26:29], refs[29:32]
        dkv = refs[32]
        kv1, kv2, kv3, kva1, kva2 = refs[33:36], refs[36:39], refs[39:42], refs[42:45], refs[45:48]
        send, recv = refs[48], refs[49]
        c = coords()
        barrier()
        pending = [[], [], []]

        def send_slab(m, stage, k, src, dst):
            n = (m * 3 + stage - 1) * 3 + k - 1
            copy = remote(src, dst, send.at[n], recv.at[n], peer(MLP_AXES[m][stage % 3], k))
            copy.start()
            pending[m].append(copy)

        def regroup(v, outer, inner):
            return jnp.concatenate(
                [v[(o * inner + i) * 24 : (o * inner + i + 1) * 24] for i in range(inner) for o in range(outer)], axis=0
            )

        m = 0
        for k in (1, 2, 3, 0):
            u = (c["x"] + k) % 4
            rows = [pl.ds(pl.multiple_of(z * 384 + u * 96, 32), 96) for z in range(4)]
            x = jnp.concatenate([xs[m][r, :] for r in rows], axis=0)
            sendbuf[m][k] = regroup(mm(x, gs[m][...]), 4, 4).astype(BF16)
            if k:
                send_slab(m, 1, k, sendbuf[m].at[k], got1[m].at[k - 1])
        m = 2
        for k in (1, 2, 3, 0):
            u = (c["z"] + k) % 4
            x = xs[m][pl.ds(pl.multiple_of(u * 384, 128), 384), :]
            sendbuf[m][k] = mm(x, gs[m][...]).astype(BF16)
            if k:
                send_slab(m, 1, k, sendbuf[m].at[k], got1[m].at[k - 1])
        m = 1
        for z in range(4):
            v = regroup(mm(xs[m][z * 384 : (z + 1) * 384, :], gs[m][...]), 4, 4).astype(BF16)
            for y in range(4):
                sendbuf[m][y, z * 96 : (z + 1) * 96] = v[y * 96 : (y + 1) * 96]
        for k in (1, 2, 3):
            send_slab(m, 1, k, sendbuf[m].at[(c["y"] + k) % 4], got1[m].at[k - 1])

        dev = lax.axis_index("seq")
        row = lax.broadcasted_iota(jnp.int32, (BLK, 96), 0)
        key_off = (row % Q_BLK) * 64 + row // Q_BLK
        q_off = (lax.broadcasted_iota(jnp.int32, (1, 96), 1) % Q_BLK) * 64 + dev
        dq_ref[...] = jnp.zeros_like(dq_ref)

        def k_step(kb, _):
            rows = pl.ds(pl.multiple_of(kb * Q_BLK, Q_BLK), Q_BLK)
            vrows = pl.ds(pl.multiple_of(128 + kb * Q_BLK, Q_BLK), Q_BLK)
            k_blk = kv_ref[:, rows, :].reshape(BLK, 128)
            v_blk = kv_ref[:, vrows, :].reshape(BLK, 128)
            k_t = k_blk.T
            pos_k = key_off + kb * BLK

            def q_step(qb, carry):
                dk, dv = carry
                q_blk, g_blk = q_ref[qb], g_ref[qb]
                pos_q = q_off + qb * BLK
                start_q = doc_bounds(pos_q, len_ref)
                s = nt(k_blk, q_blk)
                vis = (pos_k <= pos_q) & (pos_k >= start_q)
                p = jnp.where(vis, jnp.exp(s * SCALE - lse_ref[qb]), 0.0)
                gp = nt(v_blk, g_blk)
                ds = (p * (gp - delta_ref[qb])).astype(BF16)
                dq_ref[qb] += mm(k_t, ds)
                dk = dk + mm(ds, q_blk)
                dv = dv + mm(p.astype(BF16), g_blk)
                return dk, dv

            zero = jnp.zeros((BLK, 128), F32)
            dk, dv = lax.fori_loop(kb, 8, q_step, (zero, zero))
            dkv[:, :, :, rows, :] = (dk * SCALE).astype(BF16).reshape(4, 4, 4, Q_BLK, 128)
            dkv[:, :, :, vrows, :] = dv.astype(BF16).reshape(4, 4, 4, Q_BLK, 128)
            return 0

        lax.fori_loop(0, 8, k_step, 0)

        kv_pending = [[] for _ in KV_PARTS]

        def pick1(rest, order, where):
            return (where,) if rest[0] == order[1] else (slice(None), where)

        def kv_stage(stage):
            for p, (r0, rn, order) in enumerate(KV_PARTS):
                for copy in kv_pending[p]:
                    copy.wait()
                kv_pending[p] = []
                rest = [a for a in AXES if a not in order[:1]]
                if stage == 1:
                    own = dkv[kv_index(rest, c, r0, rn)].astype(F32)
                    for k in range(3):
                        own = own + kv1[p][k].astype(F32)
                    kva1[p][...] = own.astype(BF16)
                if stage == 2:
                    own = kva1[p][pick1(rest, order, c[order[1]])].astype(F32)
                    for k in range(3):
                        own = own + kv2[p][k].astype(F32)
                    kva2[p][...] = own.astype(BF16)
                for k in (1, 2, 3):
                    there = (c[order[stage]] + k) % 4
                    if stage == 0:
                        cc = dict(c)
                        cc[order[0]] = there
                        src, dst = dkv.at[kv_index(rest, cc, r0, rn)], kv1[p].at[k - 1]
                    elif stage == 1:
                        src, dst = kva1[p].at[pick1(rest, order, there)], kv2[p].at[k - 1]
                    else:
                        src, dst = kva2[p].at[there], kv3[p].at[k - 1]
                    n = 27 + (p * 3 + stage) * 3 + k - 1
                    copy = remote(src, dst, send.at[n], recv.at[n], peer(order[stage], k))
                    copy.start()
                    kv_pending[p].append(copy)

        def mlp_second():
            for m in (0, 2, 1):
                for copy in pending[m]:
                    copy.wait()
                pending[m] = []
                own = c["y"] if m == 1 else 0
                total = sendbuf[m][own].astype(F32)
                for k in range(3):
                    total = total + got1[m][k].astype(F32)
                sendbuf[m][own] = total.astype(BF16)
                axis = MLP_AXES[m][2]
                for k in (1, 2, 3):
                    rows = pl.ds(pl.multiple_of(((c[axis] + k) % 4) * 96, 32), 96)
                    send_slab(m, 2, k, sendbuf[m].at[own, rows, :], got2[m].at[k - 1])

        def mlp_third():
            for m in (0, 2, 1):
                for copy in pending[m]:
                    copy.wait()
                pending[m] = []
                own = c["y"] if m == 1 else 0
                rows = pl.ds(pl.multiple_of(c[MLP_AXES[m][2]] * 96, 32), 96)
                total = sendbuf[m][own, rows, :].astype(F32)
                for k in range(3):
                    total = total + got2[m][k].astype(F32)
                acc2[m][...] = total
                axis = MLP_AXES[m][0]
                for k in (1, 2, 3):
                    rows = pl.ds(pl.multiple_of(((c[axis] + k) % 4) * 24, 8), 24)
                    send_slab(m, 3, k, acc2[m].at[rows, :], got3[m].at[k - 1])

        kv_stage(0)
        mlp_second()
        kv_stage(1)
        mlp_third()
        kv_stage(2)
        for p, (r0, rn, order) in enumerate(KV_PARTS):
            for copy in kv_pending[p]:
                copy.wait()
            own = kva2[p][c[order[2]]].astype(F32)
            for k in range(3):
                own = own + kv3[p][k].astype(F32)
            own_ref[pl.ds(r0, rn), :] = own
        for m in (0, 2, 1):
            for copy in pending[m]:
                copy.wait()
            here = c[MLP_AXES[m][0]]
            outs[m][:, pl.ds(col_start(here), FC)] = acc2[m][pl.ds(pl.multiple_of(here * 24, 8), 24), :]
            for k in (1, 2, 3):
                outs[m][:, pl.ds(col_start((here + 4 - k) % 4), FC)] = got3[m][k - 1]

    rows = [rn for _, rn, _ in KV_PARTS]
    scratch = (
        [pltpu.VMEM((4, 384, FC), BF16)] * 3
        + [pltpu.VMEM((3, 384, FC), BF16)] * 3
        + [pltpu.VMEM((3, 96, FC), BF16)] * 3
        + [pltpu.VMEM((96, FC), F32)] * 3
        + [pltpu.VMEM((3, 24, FC), F32)] * 3
        + [pltpu.VMEM((4, 4, 4, 256, 128), BF16)]
        + [pltpu.VMEM((3, 4, 4, r, 128), BF16) for r in rows]
        + [pltpu.VMEM((3, 4, r, 128), BF16) for r in rows]
        + [pltpu.VMEM((3, r, 128), BF16) for r in rows]
        + [pltpu.VMEM((4, 4, r, 128), BF16) for r in rows]
        + [pltpu.VMEM((4, r, 128), BF16) for r in rows]
        + [DMA((54,)), DMA((54,))]
    )
    vm, sm = pl.BlockSpec(memory_space=pltpu.VMEM), pl.BlockSpec(memory_space=pltpu.SMEM)
    return pl.pallas_call(
        body,
        out_shape=tuple(jax.ShapeDtypeStruct((24, 4480), F32) for _ in range(3))
        + (jax.ShapeDtypeStruct((8, 128, 96), F32), jax.ShapeDtypeStruct((256, 128), F32)),
        in_specs=[sm] + [vm] * 11,
        out_specs=(vm,) * 5,
        scratch_shapes=scratch,
        compiler_params=pltpu.CompilerParams(collective_id=2, has_side_effects=True, vmem_limit_bytes=VMEM_BYTES),
        name="backward",
    )(lengths, *xs_in, *gs_in, q, g, kv, lse, delta)


ATTN_PARTS = (
    ("o", 0, 256, ("z", "x", "y")),
    ("o", 256, 512, ("x", "y", "z")),
    ("o", 512, 768, ("y", "z", "x")),
    ("g", 0, 384, ("z", "x", "y")),
    ("g", 384, 768, ("x", "y", "z")),
    ("g", 768, 1024, ("y", "z", "x")),
)
SMALL = 40


def finish(dq_t, dkv, cos, sin, norm_t, branch_t, attn_low, wq, wk, wv, tokens, gain, g_mid, d_norm2):
    np_ = len(ATTN_PARTS)

    def body(*refs):
        (dq_ref, dkv_ref, cos_ref, sin_ref, nt_ref, bt_ref, a_ref, wq_ref, wk_ref, wv_ref, t_ref, gain_ref,
         gmid_ref, dn2_ref) = refs[:14]
        gt_ref, gq_ref, gk_ref, gv_ref, go_ref, s_out = refs[14:20]
        r = refs[20:]
        sendbuf, got1, got2, acc2, got3 = (r[i * np_ : (i + 1) * np_] for i in range(5))
        s_acc, s_got, g_ref, part, got_part, send, recv = r[5 * np_ :]
        c = coords()
        core = lax.axis_index("tensor")
        barrier(core=True)
        pending = [[] for _ in ATTN_PARTS]

        def send_slab(p, stage, k, src, dst):
            n = (p * 3 + stage) * 3 + k - 1
            copy = remote(src, dst, send.at[n], recv.at[n], peer(ATTN_PARTS[p][3][stage], k))
            copy.start()
            pending[p].append(copy)

        def blocks(v, order):
            return jnp.concatenate([v[o * 24 : (o + 1) * 24] for o in order], axis=0)

        def first(p):
            side, lo, hi, order = ATTN_PARTS[p]
            left, right = (bt_ref, a_ref) if side == "o" else (nt_ref, g_ref)
            rhs = right[:, lo:hi]
            if order[0] == "z":
                for z in range(4):
                    sendbuf[p][z] = mm(left[z * 384 : (z + 1) * 384, :], rhs).astype(BF16)
            elif order[0] == "x":
                for x in range(4):
                    lhs = jnp.concatenate([left[z * 384 + x * 96 : z * 384 + (x + 1) * 96, :] for z in range(4)], axis=0)
                    sendbuf[p][x] = blocks(mm(lhs, rhs), [z * 4 + y for y in range(4) for z in range(4)]).astype(BF16)
            else:
                for z in range(4):
                    v = mm(left[z * 384 : (z + 1) * 384, :], rhs)
                    v = blocks(v, [x * 4 + y for y in range(4) for x in range(4)]).astype(BF16)
                    for y in range(4):
                        sendbuf[p][y, z * 96 : (z + 1) * 96] = v[y * 96 : (y + 1) * 96]
            for k in (1, 2, 3):
                there = (c[order[0]] + k) % 4
                send_slab(p, 0, k, sendbuf[p].at[there], got1[p].at[k - 1])

        for p in range(3):
            first(p)

        cos_t, sin_t = cos_ref[...], sin_ref[...]
        for qb in range(8):
            dq = dq_ref[qb].T * SCALE
            rows = slice(qb * Q_BLK, (qb + 1) * Q_BLK)
            cs, sn = cos_t[rows], sin_t[rows]
            for h in range(6):
                v = dq[h * Q_BLK : (h + 1) * Q_BLK]
                g_ref[rows, h * 128 : (h + 1) * 128] = (v * cs - swap_halves(v) * sn).astype(BF16)
        dk = dkv_ref[:128, :]
        g_ref[:, 768:896] = (dk * cos_t - swap_halves(dk) * sin_t).astype(BF16)
        g_ref[:, 896:] = dkv_ref[128:, :].astype(BF16)
        total = nt(g_ref[:, 768:896], wk_ref[...]) + nt(g_ref[:, 896:], wv_ref[...])
        for h in range(6):
            total = total + nt(g_ref[:, h * 128 : (h + 1) * 128], wq_ref[h])
        part[...] = total
        n = 9 * np_
        swap = remote(part, got_part, send.at[n], recv.at[n], partner())
        swap.start()
        for p in range(3, np_):
            first(p)

        inputs = t_ref[...].astype(F32)
        inv = lax.rsqrt(jnp.mean(inputs * inputs, axis=1, keepdims=True) + 1e-06)
        d_norm1 = jnp.sum(part[...] * inputs * inv, axis=0, keepdims=True)
        d_bias = jnp.sum(g_ref[...].astype(F32), axis=0, keepdims=True)
        for j in range(12):
            s_acc[0, j : j + 1, :] = d_norm1[:, j * 128 : (j + 1) * 128]
            s_acc[0, 12 + j : 13 + j, :] = dn2_ref[:, j * 128 : (j + 1) * 128]
        for j in range(8):
            v = d_bias[:, j * 128 : (j + 1) * 128]
            s_acc[0, 24 + j : 25 + j, :] = jnp.where(core == 0, v, 0.0)
            s_acc[0, 32 + j : 33 + j, :] = jnp.where(core == 1, v, 0.0)
        s_pending = []

        def send_small(stage):
            peers = [partner()] if stage == 0 else [peer(AXES[stage - 1], k) for k in (1, 2, 3)]
            for i, d in enumerate(peers):
                n = 9 * np_ + 1 + stage * 3 + i
                copy = remote(s_acc.at[stage], s_got.at[stage * 3 + i], send.at[n], recv.at[n], d)
                copy.start()
                s_pending.append(copy)

        def sum_small(stage):
            for copy in s_pending:
                copy.wait()
            s_pending.clear()
            if stage == 0:
                return s_acc[0] + s_got[0]
            axis = AXES[stage - 1]
            parts = [s_acc[stage]] + [s_got[stage * 3 + k] for k in range(3)]
            total = jnp.zeros_like(parts[0])
            for w in range(4):
                term = jnp.zeros_like(total)
                for k in range(4):
                    term = jnp.where((c[axis] + 4 - k) % 4 == w, parts[k], term)
                total = total + term
            return total

        send_small(0)
        swap.wait()
        g_norm = part[...] + got_part[...]
        scaled = g_norm * gain_ref[...]
        gt_ref[...] = gmid_ref[...] + (
            inv * scaled - inputs * (inv * inv * inv) * jnp.mean(scaled * inputs, axis=1, keepdims=True)
        )
        s_acc[1] = sum_small(0)
        send_small(1)
        for p in range(np_):
            for copy in pending[p]:
                copy.wait()
            pending[p] = []
            order = ATTN_PARTS[p][3]
            own = c[order[0]]
            total = sendbuf[p][own].astype(F32)
            for k in range(3):
                total = total + got1[p][k].astype(F32)
            sendbuf[p][own] = total.astype(BF16)
            for k in (1, 2, 3):
                rows = pl.ds(pl.multiple_of(((c[order[1]] + k) % 4) * 96, 32), 96)
                send_slab(p, 1, k, sendbuf[p].at[own, rows, :], got2[p].at[k - 1])
        s_acc[2] = sum_small(1)
        send_small(2)
        for p in range(np_):
            for copy in pending[p]:
                copy.wait()
            pending[p] = []
            order = ATTN_PARTS[p][3]
            own = c[order[0]]
            rows = pl.ds(pl.multiple_of(c[order[1]] * 96, 32), 96)
            total = sendbuf[p][own, rows, :].astype(F32)
            for k in range(3):
                total = total + got2[p][k].astype(F32)
            acc2[p][...] = total
            for k in (1, 2, 3):
                rows = pl.ds(pl.multiple_of(((c[order[2]] + k) % 4) * 24, 8), 24)
                send_slab(p, 2, k, acc2[p].at[rows, :], got3[p].at[k - 1])
        s_acc[3] = sum_small(2)
        send_small(3)
        for p in range(np_):
            for copy in pending[p]:
                copy.wait()
            side, lo, hi, order = ATTN_PARTS[p]
            rows = pl.ds(pl.multiple_of(c[order[2]] * 24, 8), 24)
            total = acc2[p][rows, :]
            for k in range(3):
                total = total + got3[p][k]
            for j in range(lo // 128, hi // 128):
                v = total[:, j * 128 - lo : (j + 1) * 128 - lo]
                if side == "o":
                    go_ref[j] = v
                elif j < 6:
                    gq_ref[j] = v
                elif j == 6:
                    gk_ref[...] = v
                else:
                    gv_ref[...] = v
        s_out[...] = sum_small(3)

    cols = [hi - lo for _, lo, hi, _ in ATTN_PARTS]
    n_sem = 9 * np_ + 1 + 12
    scratch = (
        [pltpu.VMEM((4, 384, n), BF16) for n in cols]
        + [pltpu.VMEM((3, 384, n), BF16) for n in cols]
        + [pltpu.VMEM((3, 96, n), BF16) for n in cols]
        + [pltpu.VMEM((96, n), F32) for n in cols]
        + [pltpu.VMEM((3, 24, n), F32) for n in cols]
        + [
            pltpu.VMEM((4, SMALL, 128), F32),
            pltpu.VMEM((12, SMALL, 128), F32),
            pltpu.VMEM((128, 1024), BF16),
            pltpu.VMEM((128, 1536), F32),
            pltpu.VMEM((128, 1536), F32),
            DMA((n_sem,)),
            DMA((n_sem,)),
        ]
    )
    f32 = lambda *s: jax.ShapeDtypeStruct(s, F32)
    shape = (f32(128, 1536), f32(6, 24, 128), f32(24, 128), f32(24, 128), f32(6, 24, 128), f32(SMALL, 128))
    return comm_call(body, shape, 14, scratch, 3, "finish")(
        dq_t, dkv, cos, sin, norm_t, branch_t, attn_low, wq, wk, wv, tokens, gain, g_mid, d_norm2
    )


def local(
    tokens, cotangent, lengths, norm1_gain, w_query, b_query, w_key, b_key, w_value, b_value, w_out,
    norm2_gain, w_gate, w_up, w_down,
):
    device = lax.axis_index("seq")
    core = lax.axis_index("tensor")
    wq = w_query.transpose(1, 0, 2)
    wk, wv = w_key.reshape(1536, 128), w_value.reshape(1536, 128)
    wo = w_out.reshape(768, 1536)
    gain1, gain2 = norm1_gain.reshape(1, 1536), norm2_gain.reshape(1, 1536)

    q, kv, norm_t, cos, sin = qkv_gather(tokens, gain1, wq, wk, wv, b_query, b_key, b_value, lengths)
    kv = kv.reshape(64, 256, 128)
    branch, attn, attn_low, lse = attn_forward(q, kv, wo, lengths)
    output, g_mid, branch_t, g_attn, delta, d_norm2, *shared = feed_forward(
        branch, attn, tokens, cotangent, gain2, wo, w_gate, w_up, w_down
    )
    grad_gate, grad_up, grad_down, dq_t, dkv = backward(
        shared[:3], shared[3:], q, g_attn, kv, lse, delta, lengths
    )
    grad_tokens, grad_wq, grad_wk, grad_wv, grad_wo, sums = finish(
        dq_t, dkv, cos, sin, norm_t, branch_t, attn_low, wq, wk, wv, tokens, gain1, g_mid, d_norm2
    )
    sums = sums.reshape(-1)
    grad_norm1 = lax.dynamic_slice(sums, (device * 24,), (24,))
    grad_norm2 = lax.dynamic_slice(sums, (1536 + device * 24,), (24,))
    bias = lax.dynamic_slice(sums.reshape(SMALL, 128), (24 + core * 8, device * 2), (8, 2))
    return (
        output,
        grad_tokens,
        grad_norm1,
        grad_wq.transpose(1, 0, 2),
        bias[:6],
        grad_wk.reshape(24, 1, 128),
        bias[6:7],
        grad_wv.reshape(24, 1, 128),
        bias[7:8],
        grad_wo.transpose(0, 2, 1),
        grad_norm2,
        grad_gate,
        grad_up,
        grad_down.T,
    )


def solution(mesh):
    in_specs = (
        P("seq", None), P("seq", None), P(), P(), P(None, "tensor", None), P("tensor", None),
        P(None, "tensor", None), P("tensor", None), P(None, "tensor", None), P("tensor", None),
        P("tensor", None, None), P(), P(None, "tensor"), P(None, "tensor"), P("tensor", None),
    )
    out_specs = (
        P("seq", None), P("seq", None), P("seq"), P("seq", "tensor", None), P("tensor", "seq"),
        P("seq", "tensor", None), P("tensor", "seq"), P("seq", "tensor", None), P("tensor", "seq"),
        P("tensor", None, "seq"), P("seq"), P("seq", "tensor"), P("seq", "tensor"), P("tensor", "seq"),
    )
    return jax.shard_map(local, mesh=mesh, in_specs=in_specs, out_specs=out_specs, check_vma=False)
```

```python
import math

import jax
import jax.numpy as jnp
from jax import lax
from jax.experimental import pallas as pl
from jax.experimental.pallas import tpu as pltpu
from jax.sharding import PartitionSpec as P

MESH = pl.DeviceIdType.MESH
F32 = jnp.float32
BF16 = jnp.bfloat16
VMEM_BYTES = 60 * 1024 * 1024
AXES = ("z", "x", "y")
STRIDE = {"z": 16, "x": 4, "y": 1}


def coords():
    s = lax.axis_index("seq")
    return {"z": s // 16, "x": (s // 4) % 4, "y": s % 4}


def peer(axis, k):
    s = lax.axis_index("seq")
    c = coords()[axis]
    return (s + STRIDE[axis] * ((c + k) % 4 - c), lax.axis_index("tensor"))


def partner():
    return (lax.axis_index("seq"), 1 - lax.axis_index("tensor"))


def barrier(axes=AXES, core=False):
    bar = pltpu.get_barrier_semaphore()
    ids = [peer(a, k) for a in axes for k in (1, 2, 3)]
    if core:
        ids.append(partner())
    for d in ids:
        pl.semaphore_signal(bar, inc=1, device_id=d, device_id_type=MESH)
    pl.semaphore_wait(bar, len(ids))


def remote(src, dst, send, recv, device):
    return pltpu.make_async_remote_copy(
        src_ref=src, dst_ref=dst, send_sem=send, recv_sem=recv, device_id=device, device_id_type=MESH
    )


def comm_call(body, outs, ins, scratch, cid, name):
    vm = pl.BlockSpec(memory_space=pltpu.VMEM)
    return pl.pallas_call(
        body,
        out_shape=outs,
        in_specs=[vm] * ins,
        out_specs=jax.tree.map(lambda _: vm, outs),
        scratch_shapes=scratch,
        compiler_params=pltpu.CompilerParams(
            collective_id=cid, has_side_effects=True, vmem_limit_bytes=VMEM_BYTES
        ),
        name=name,
    )


DMA = pltpu.SemaphoreType.DMA


KV_CHUNK = (
    (0, 48, ("z", "x", "y")),
    (48, 48, ("x", "y", "z")),
    (96, 32, ("y", "z", "x")),
)


def kv_rows(kb, v):
    return pl.ds(pl.multiple_of((kb // 4) * 128 + v * 64 + (kb % 4) * Q_BLK, Q_BLK), Q_BLK)


def kv_index(done, c, r0, rn):
    return tuple(slice(None) if a in done else c[a] for a in AXES) + (pl.ds(r0, rn), slice(None))


def rope_tables(len_ref):
    lane = lax.broadcasted_iota(jnp.int32, (128, 128), 1)
    pos = lax.broadcasted_iota(jnp.int32, (128, 128), 0) * 64 + lax.axis_index("seq")
    rel = (pos - doc_bounds(pos, len_ref)).astype(F32)
    inv_freq = jnp.exp(-(2.0 * (lane % 64).astype(F32) / 128) * math.log(10000.0))
    angle = rel * inv_freq
    sin = jnp.sin(angle)
    return jnp.cos(angle), jnp.where(lane < 64, -sin, sin)


def swap_halves(v):
    return pltpu.roll(v, 64, 1)


def qkv_gather(tokens, gain, wq, wk, wv, bq, bk, bv, lengths):
    def body(len_ref, t_ref, g_ref, wq_ref, wk_ref, wv_ref, bq_ref, bk_ref, bv_ref,
             q_out, out, nt_out, cos_out, sin_out, send, recv):
        c = coords()
        x = t_ref[...].astype(F32)
        inv = lax.rsqrt(jnp.mean(x * x, axis=1, keepdims=True) + 1e-06)
        normed = (x * inv * g_ref[...]).astype(BF16)
        cos, sin = rope_tables(len_ref)
        cos_out[...], sin_out[...] = cos, sin
        k_pre = jnp.dot(normed, wk_ref[...], preferred_element_type=F32) + bk_ref[...].astype(F32)
        v_pre = jnp.dot(normed, wv_ref[...], preferred_element_type=F32) + bv_ref[...].astype(F32)
        k_rot = (k_pre * cos + swap_halves(k_pre) * sin).astype(BF16)
        v_low = v_pre.astype(BF16)
        out[c["z"], c["x"], c["y"]] = jnp.concatenate([k_rot[:64], v_low[:64], k_rot[64:], v_low[64:]], axis=0)
        barrier()
        parts = [(r0 + 128 * chunk, rn, order) for chunk in range(2) for r0, rn, order in KV_CHUNK]
        pending = [[] for _ in parts]

        def send_stage(stage):
            for p, (r0, rn, order) in enumerate(parts):
                for copy in pending[p]:
                    copy.wait()
                pending[p] = []
                idx = kv_index(order[:stage], c, r0, rn)
                for k in (1, 2, 3):
                    n = (p * 3 + stage) * 3 + k - 1
                    copy = remote(out.at[idx], out.at[idx], send.at[n], recv.at[n], peer(order[stage], k))
                    copy.start()
                    pending[p].append(copy)

        send_stage(0)
        for h in range(6):
            q = jnp.dot(normed, wq_ref[h], preferred_element_type=F32) + bq_ref[h : h + 1, :].astype(F32)
            q = (q * cos + swap_halves(q) * sin).astype(BF16)
            q_out[:, h * Q_BLK : (h + 1) * Q_BLK, :] = q.reshape(8, Q_BLK, 128)
        send_stage(1)
        nt_out[...] = normed.T
        send_stage(2)
        for copies in pending:
            for copy in copies:
                copy.wait()

    vm, sm = pl.BlockSpec(memory_space=pltpu.VMEM), pl.BlockSpec(memory_space=pltpu.SMEM)
    return pl.pallas_call(
        body,
        out_shape=(
            jax.ShapeDtypeStruct((8, 96, 128), BF16),
            jax.ShapeDtypeStruct((4, 4, 4, 256, 128), BF16),
            jax.ShapeDtypeStruct((1536, 128), BF16),
            jax.ShapeDtypeStruct((128, 128), F32),
            jax.ShapeDtypeStruct((128, 128), F32),
        ),
        in_specs=[sm] + [vm] * 8,
        out_specs=(vm,) * 5,
        scratch_shapes=[DMA((54,)), DMA((54,))],
        compiler_params=pltpu.CompilerParams(collective_id=0, has_side_effects=True, vmem_limit_bytes=VMEM_BYTES),
        name="qkv_gather",
    )(lengths, tokens, gain, wq, wk, wv, bq, bk, bv)


Q_BLK = 16
BLK = Q_BLK * 64
SCALE = 1.0 / math.sqrt(128)
SCALE2 = SCALE / math.log(2.0)


def doc_bounds(pos, len_ref):
    start = jnp.zeros_like(pos)
    end = jnp.int32(0)
    for j in range(8):
        end = end + len_ref[j]
        start = jnp.where(pos >= end, end, start)
    return start


def doc_start_scalar(pos, len_ref):
    start, end = jnp.int32(0), jnp.int32(0)
    for j in range(8):
        end = end + len_ref[j]
        start = jnp.where(pos >= end, end, start)
    return start


def attn_forward(q, kv, w_out, lengths):
    def body(len_ref, q_ref, kv_ref, wo_ref, part_ref, out_ref, low_ref, lse_ref):
        dev = lax.axis_index("seq")
        col = lax.broadcasted_iota(jnp.int32, (96, BLK), 1)
        key_off = (col % Q_BLK) * 64 + col // Q_BLK
        row_off = (lax.broadcasted_iota(jnp.int32, (96, 1), 0) % Q_BLK) * 64 + dev

        def q_step(qb, _):
            q_blk = q_ref[qb]
            pos_q = row_off + qb * BLK
            start_q = doc_bounds(pos_q, len_ref)
            lo = doc_start_scalar(qb * BLK + dev, len_ref) // BLK

            def k_step(kb, carry):
                m, l, acc = carry
                k_blk = kv_ref[:, kv_rows(kb, 0), :].reshape(BLK, 128)
                v_blk = kv_ref[:, kv_rows(kb, 1), :].reshape(BLK, 128)
                s = lax.dot_general(q_blk, k_blk, (((1,), (1,)), ((), ())), preferred_element_type=F32)
                pos_k = key_off + kb * BLK
                vis = (pos_k <= pos_q) & (pos_k >= start_q)
                s = jnp.where(vis, s * SCALE2, -1e30)
                m_new = jnp.maximum(m, jnp.max(s, axis=1, keepdims=True))
                p = jnp.where(vis, jnp.exp2(s - m_new), 0.0)
                a = jnp.exp2(m - m_new)
                l = l * a + jnp.sum(p, axis=1, keepdims=True)
                acc = acc * a + jnp.dot(p.astype(BF16), v_blk, preferred_element_type=F32)
                return m_new, l, acc

            init = (jnp.full((96, 1), -1e30, F32), jnp.zeros((96, 1), F32), jnp.zeros((96, 128), F32))
            m, l, acc = lax.fori_loop(lo, qb + 1, k_step, init)
            attn = acc / l
            out_ref[qb] = attn
            low = attn.astype(BF16)
            for h in range(6):
                rows = pl.ds(pl.multiple_of(qb * Q_BLK, Q_BLK), Q_BLK)
                low_ref[rows, h * 128 : (h + 1) * 128] = low[h * Q_BLK : (h + 1) * Q_BLK]
            lse_ref[qb] = jnp.broadcast_to(m + jnp.log2(l), (96, 128)).T[0:1]
            return 0

        lax.fori_loop(0, 8, q_step, 0)
        part_ref[...] = jnp.dot(low_ref[...], wo_ref[...], preferred_element_type=F32)

    vm = pl.BlockSpec(memory_space=pltpu.VMEM)
    return pl.pallas_call(
        body,
        out_shape=(
            jax.ShapeDtypeStruct((128, 1536), F32),
            jax.ShapeDtypeStruct((8, 96, 128), F32),
            jax.ShapeDtypeStruct((128, 768), BF16),
            jax.ShapeDtypeStruct((8, 1, 96), F32),
        ),
        in_specs=[pl.BlockSpec(memory_space=pltpu.SMEM), vm, vm, vm],
        out_specs=(vm,) * 4,
        compiler_params=pltpu.CompilerParams(vmem_limit_bytes=VMEM_BYTES),
        name="attn_forward",
    )(lengths, q, kv, w_out)


FC = 1152


def nt(a, b):
    return lax.dot_general(a, b, (((1,), (1,)), ((), ())), preferred_element_type=F32)


def mm(a, b):
    return jnp.dot(a, b, preferred_element_type=F32)


def col_start(c):
    return pl.multiple_of(jnp.minimum(c * FC, 4480 - FC), 128)


MLP_AXES = (("z", "x", "y"), ("x", "y", "z"), ("y", "z", "x"))


def feed_forward(branch, attn, tokens, cot, gain, w_out, w_gate, w_up, w_down):
    def body(br_ref, at_ref, t_ref, c_ref, g_ref, wo_ref, wg_hbm, wu_hbm, wd_hbm,
             out_ref, gmid_ref, bt_ref, ga_ref, delta_ref, dn_ref, x0, x1, x2, g0, g1, g2,
             wg, wu, wd, got_br, acc, got, mid_ref, norm_ref, nt_ref, act, w_sem, loc, send, recv):
        xs, gs = (x0, x1, x2), (g0, g1, g2)
        c = coords()
        turn = c["z"] + c["x"] + c["y"]
        sems = iter(range(64))

        def load(j):
            cols = pl.ds(col_start((turn + j) % 4), FC)
            b = j % 2
            copies = [
                pltpu.make_async_copy(wg_hbm.at[:, cols], wg.at[b], w_sem.at[b, 0]),
                pltpu.make_async_copy(wu_hbm.at[:, cols], wu.at[b], w_sem.at[b, 1]),
                pltpu.make_async_copy(wd_hbm.at[cols, :], wd.at[b], w_sem.at[b, 2]),
            ]
            for copy in copies:
                copy.start()
            return copies

        loads = [load(0), load(1)]
        barrier(core=True)

        def push(src, dst, device):
            n = next(sems)
            copy = remote(src, dst, send.at[n], recv.at[n], device)
            copy.start()
            return copy

        later = []
        ex = push(br_ref, got_br, partner())
        x2[:, 0:128] = c_ref[...].T
        for k in (1, 2, 3):
            later.append(push(x2.at[:, pl.ds(0, 128)], x2.at[:, pl.ds(k * 128, 128)], peer("y", k)))
        ex.wait()
        mid = t_ref[...].astype(F32) + (br_ref[...] + got_br[...])
        mid_ref[...] = mid
        inv = lax.rsqrt(jnp.mean(mid * mid, axis=1, keepdims=True) + 1e-06)
        normed = (mid * inv * g_ref[...]).astype(BF16)
        norm_ref[...] = normed
        nt_ref[...] = normed.T
        x0[:, 0:128] = nt_ref[...]
        x1[:, 0:128] = nt_ref[...]
        for k in (1, 2, 3):
            for m, w in ((0, "z"), (1, "x")):
                later.append(push(nt_ref, xs[m].at[:, pl.ds(k * 128, 128)], peer(w, k)))

        lane = lax.broadcasted_iota(jnp.int32, (128, FC), 1)
        for j in range(4):
            b = j % 2
            d = (turn + j) % 4
            for copy in loads[j]:
                copy.wait()
            n = norm_ref[...]
            gate = mm(n, wg[b])
            up = mm(n, wu[b])
            gh = nt(c_ref[...], wd[b])
            sig = 1.0 / (1.0 + jnp.exp(-gate))
            silu = gate * sig
            hidden = (silu * up).astype(BF16)
            g_gate = (gh * up * sig * (1.0 + gate * (1.0 - sig))).astype(BF16)
            g_up = (gh * silu).astype(BF16)
            vals = (g_gate, g_up, hidden)
            for m in range(3):
                act[m, j] = vals[m]
            twice = (lane < 128) & (d == 3)
            zero = jnp.zeros((128, FC), BF16)
            hidden, g_gate, g_up = (jnp.where(twice, zero, v) for v in (hidden, g_gate, g_up))
            add_o = mm(hidden, wd[b])
            add_g = nt(g_gate, wg[b]) + nt(g_up, wu[b])
            if j == 0:
                acc[0], acc[1] = add_o, add_g
            else:
                acc[0] += add_o
                acc[1] += add_g
            if j + 2 < 4:
                loads.append(load(j + 2))
            for m in range(3):
                w = MLP_AXES[m][0]
                k = (d + 4 - c[w]) % 4
                slot = pl.ds(pl.multiple_of(k * 128, 128), 128)

                @pl.when(k == 0)
                def _():
                    copy = pltpu.make_async_copy(act.at[m, j], gs[m].at[pl.ds(0, 128), :], loc.at[m])
                    copy.start()
                    copy.wait()

                @pl.when(k != 0)
                def _():
                    remote(
                        act.at[m, j], gs[m].at[slot, :], send.at[32 + m * 4 + j], recv.at[32 + m * 4 + k], peer(w, k)
                    ).start()

        dn_ref[...] = jnp.sum(acc[1] * mid_ref[...] * inv, axis=0, keepdims=True)
        ex = [push(acc.at[1], got.at[1], partner()), push(acc.at[0], got.at[0], partner())]
        cot_f = c_ref[...].astype(F32)
        ex[0].wait()
        gn = acc[1] + got[1]
        mid = mid_ref[...]
        scaled = gn * g_ref[...]
        g_mid = cot_f + (inv * scaled - mid * (inv * inv * inv) * jnp.mean(scaled * mid, axis=1, keepdims=True))
        gmid_ref[...] = g_mid
        branch_low = g_mid.astype(BF16)
        bt_ref[...] = branch_low.T
        g_attn = nt(branch_low, wo_ref[...]).astype(BF16)
        for h in range(6):
            ga_ref[:, h * Q_BLK : (h + 1) * Q_BLK, :] = g_attn[:, h * 128 : (h + 1) * 128].reshape(8, Q_BLK, 128)
        for qb in range(8):
            delta_ref[qb] = jnp.sum((ga_ref[qb].astype(F32) * at_ref[qb]).T, axis=0, keepdims=True)
        ex[1].wait()
        out_ref[...] = mid_ref[...] + (acc[0] + got[0])
        for copy in later:
            copy.wait()
        for m in range(3):
            w = MLP_AXES[m][0]
            for j in range(4):
                k = ((turn + j) % 4 + 4 - c[w]) % 4

                @pl.when(k != 0)
                def _():
                    slot = pl.ds(pl.multiple_of(k * 128, 128), 128)
                    remote(
                        act.at[m, j], gs[m].at[slot, :], send.at[32 + m * 4 + j], recv.at[32 + m * 4 + k], peer(w, k)
                    ).wait()

    f32 = lambda *s: jax.ShapeDtypeStruct(s, F32)
    b16 = lambda *s: jax.ShapeDtypeStruct(s, BF16)
    vm, hbm = pl.BlockSpec(memory_space=pltpu.VMEM), pl.BlockSpec(memory_space=pl.ANY)
    return pl.pallas_call(
        body,
        out_shape=(f32(128, 1536), f32(128, 1536), b16(1536, 128), b16(8, 96, 128), f32(8, 1, 96), f32(1, 1536))
        + (b16(1536, 512),) * 3
        + (b16(512, FC),) * 3,
        in_specs=[vm] * 6 + [hbm] * 3,
        out_specs=(vm,) * 12,
        scratch_shapes=[
            pltpu.VMEM((2, 1536, FC), BF16),
            pltpu.VMEM((2, 1536, FC), BF16),
            pltpu.VMEM((2, FC, 1536), BF16),
            pltpu.VMEM((128, 1536), F32),
            pltpu.VMEM((2, 128, 1536), F32),
            pltpu.VMEM((2, 128, 1536), F32),
            pltpu.VMEM((128, 1536), F32),
            pltpu.VMEM((128, 1536), BF16),
            pltpu.VMEM((1536, 128), BF16),
            pltpu.VMEM((3, 4, 128, FC), BF16),
            DMA((2, 3)),
            DMA((3,)),
            DMA((64,)),
            DMA((64,)),
        ],
        compiler_params=pltpu.CompilerParams(collective_id=4, has_side_effects=True, vmem_limit_bytes=VMEM_BYTES),
        name="feed_forward",
    )(branch, attn, tokens, cot, gain, w_out, w_gate, w_up, w_down)


OUT_ORDERS = (("z", "x", "y"), ("x", "y", "z"), ("y", "z", "x"))
QKV_PARTS = ((0, 384, ("z", "x", "y")), (384, 768, ("x", "y", "z")), (768, 1024, ("y", "z", "x")))


def slab_products(buf, left, rhs, order):
    def blocks(v, places):
        return jnp.concatenate([v[o * 24 : (o + 1) * 24] for o in places], axis=0)

    if order[0] == "z":
        for z in range(4):
            buf[z] = mm(left[z * 384 : (z + 1) * 384, :], rhs).astype(BF16)
    elif order[0] == "x":
        for x in range(4):
            lhs = jnp.concatenate([left[z * 384 + x * 96 : z * 384 + (x + 1) * 96, :] for z in range(4)], axis=0)
            buf[x] = blocks(mm(lhs, rhs), [z * 4 + y for y in range(4) for z in range(4)]).astype(BF16)
    else:
        for z in range(4):
            v = blocks(mm(left[z * 384 : (z + 1) * 384, :], rhs), [x * 4 + y for y in range(4) for x in range(4)])
            v = v.astype(BF16)
            for y in range(4):
                buf[y, z * 96 : (z + 1) * 96] = v[y * 96 : (y + 1) * 96]


def sum_first(buf, got, copies, own):
    for copy in copies:
        copy.wait()
    total = buf[own].astype(F32)
    for k in range(3):
        total = total + got[k].astype(F32)
    buf[own] = total.astype(BF16)


def backward(xs_in, gs_in, q, g, kv, lse, delta, branch_t, attn_low, lengths):
    def body(*refs):
        len_ref, xs_hbm, gs_hbm, kv_hbm = refs[0], refs[1:4], refs[4:7], refs[7]
        q_ref, g_ref, lse_ref, delta_ref, bt_ref, a_ref = refs[8:14]
        acc2, o_acc2, dq_ref, own_ref = refs[14:17], refs[17:20], refs[20], refs[21]
        r = list(refs[22:])
        take = lambda n: [r.pop(0) for _ in range(n)]
        xs, gs, (kv_ref,) = take(3), take(3), take(1)
        sendbuf, r1a, r1b, r2, got2 = take(3), take(3), take(3), take(3), take(3)
        o_buf, o_got1, o_got2 = take(3), take(3), take(3)
        (dkv,) = take(1)
        kv1, kv2, kv3, kva1, kva2 = take(6), take(6), take(6), take(6), take(6)
        loc, send, recv = take(3)
        c = coords()
        loads = [pltpu.make_async_copy(a, b, loc.at[i]) for i, (a, b) in enumerate(
            ((xs_hbm[0], xs[0]), (gs_hbm[0], gs[0]), (xs_hbm[2], xs[2]), (gs_hbm[2], gs[2]),
             (xs_hbm[1], xs[1]), (gs_hbm[1], gs[1]), (kv_hbm, kv_ref)))]
        for copy in loads:
            copy.start()
        barrier()
        sems = iter(range(256))

        def push(src, dst, device):
            n = next(sems)
            copy = remote(src, dst, send.at[n], recv.at[n], device)
            copy.start()
            return copy

        def regroup(v, outer, inner):
            return jnp.concatenate(
                [v[(o * inner + i) * 24 : (o * inner + i + 1) * 24] for i in range(inner) for o in range(outer)], axis=0
            )

        near = lambda u: u + 1 - 2 * (u % 2)
        far = lambda u: 3 - u
        over = lambda u: (u + 2) % 4
        top, low = pl.ds(0, 192), pl.ds(192, 192)
        first, second = [[], [], []], [[], [], []]

        def neighbour(axis, u):
            return peer(axis, u + 4 - c[axis])

        def slab(m, u):
            return sendbuf[m].at[u]

        def ready(m, which):
            axis = MLP_AXES[m][1]
            u = c[axis]
            if which == "over":
                first[m].append(push(slab(m, over(u)).at[top, :], r1a[m].at[0], neighbour(axis, near(u))))
                first[m].append(push(slab(m, over(u)).at[low, :], r1b[m].at[0], neighbour(axis, far(u))))
            elif which == "near":
                first[m].append(push(slab(m, near(u)).at[top, :], r1a[m].at[1], neighbour(axis, near(u))))
            elif which == "far":
                first[m].append(push(slab(m, far(u)).at[low, :], r1b[m].at[1], neighbour(axis, far(u))))

        def second_step(m):
            axis = MLP_AXES[m][1]
            u = c[axis]
            first[m][0].wait()
            at = slab(m, far(u)).at[top, :]
            at[...] = (at[...].astype(F32) + r1a[m][0].astype(F32)).astype(BF16)
            second[m].append(push(at, r2[m].at[0], neighbour(axis, far(u))))
            first[m][1].wait()
            at = slab(m, near(u)).at[low, :]
            at[...] = (at[...].astype(F32) + r1b[m][0].astype(F32)).astype(BF16)
            second[m].append(push(at, r2[m].at[1], neighbour(axis, near(u))))

        second_axis = [[], [], []]

        def second_axis_step(m):
            axis = MLP_AXES[m][1]
            own = slab(m, c[axis])
            for copy in first[m][2:] + second[m]:
                copy.wait()
            own[top, :] = (own[top, :].astype(F32) + r1a[m][1].astype(F32) + r2[m][0].astype(F32)).astype(BF16)
            own[low, :] = (own[low, :].astype(F32) + r1b[m][1].astype(F32) + r2[m][1].astype(F32)).astype(BF16)
            axis = MLP_AXES[m][2]
            for k in (1, 2, 3):
                rows = pl.ds(pl.multiple_of(((c[axis] + k) % 4) * 96, 32), 96)
                second_axis[m].append(push(own.at[rows, :], got2[m].at[k - 1], peer(axis, k)))

        def second_axis_sum(m):
            for copy in second_axis[m]:
                copy.wait()
            rows = pl.ds(pl.multiple_of(c[MLP_AXES[m][2]] * 96, 32), 96)
            total = slab(m, c[MLP_AXES[m][1]])[rows, :].astype(F32)
            for k in range(3):
                total = total + got2[m][k].astype(F32)
            acc2[m][...] = total

        places = (("over", over), ("near", near), ("far", far), ("own", lambda u: u))
        loads[0].wait()
        loads[1].wait()
        for name, place in places:
            u = place(c["x"])
            rows = [pl.ds(pl.multiple_of(z * 384 + u * 96, 32), 96) for z in range(4)]
            x = jnp.concatenate([xs[0][r, :] for r in rows], axis=0)
            sendbuf[0][u] = regroup(mm(x, gs[0][...]), 4, 4).astype(BF16)
            ready(0, name)
        loads[2].wait()
        loads[3].wait()
        for name, place in places:
            u = place(c["z"])
            x = xs[2][pl.ds(pl.multiple_of(u * 384, 128), 384), :]
            sendbuf[2][u] = mm(x, gs[2][...]).astype(BF16)
            ready(2, name)
        loads[4].wait()
        loads[5].wait()
        for z in range(4):
            v = regroup(mm(xs[1][z * 384 : (z + 1) * 384, :], gs[1][...]), 4, 4).astype(BF16)
            for y in range(4):
                sendbuf[1][y, z * 96 : (z + 1) * 96] = v[y * 96 : (y + 1) * 96]
        for name, _ in places:
            ready(1, name)

        o_first, o_second = [[], [], []], [[], [], []]
        for p, order in enumerate(OUT_ORDERS):
            slab_products(o_buf[p], bt_ref, a_ref[:, p * 256 : (p + 1) * 256], order)
            for k in (1, 2, 3):
                there = (c[order[0]] + k) % 4
                o_first[p].append(push(o_buf[p].at[there], o_got1[p].at[k - 1], peer(order[0], k)))

        def out_second(p):
            order = OUT_ORDERS[p]
            sum_first(o_buf[p], o_got1[p], o_first[p], c[order[0]])
            for k in (1, 2, 3):
                rows = pl.ds(pl.multiple_of(((c[order[1]] + k) % 4) * 96, 32), 96)
                o_second[p].append(push(o_buf[p].at[c[order[0]], rows, :], o_got2[p].at[k - 1], peer(order[1], k)))

        def out_sum(p):
            order = OUT_ORDERS[p]
            for copy in o_second[p]:
                copy.wait()
            rows = pl.ds(pl.multiple_of(c[order[1]] * 96, 32), 96)
            total = o_buf[p][c[order[0]], rows, :].astype(F32)
            for k in range(3):
                total = total + o_got2[p][k].astype(F32)
            o_acc2[p][...] = total

        loads[6].wait()
        dev = lax.axis_index("seq")
        row = lax.broadcasted_iota(jnp.int32, (BLK, 96), 0)
        key_off = (row % Q_BLK) * 64 + row // Q_BLK
        q_off = (lax.broadcasted_iota(jnp.int32, (1, 96), 1) % Q_BLK) * 64 + dev
        dq_ref[...] = jnp.zeros_like(dq_ref)

        def k_step(kb, _):
            k_blk = kv_ref[:, kv_rows(kb, 0), :].reshape(BLK, 128)
            v_blk = kv_ref[:, kv_rows(kb, 1), :].reshape(BLK, 128)
            k_t = k_blk.T
            pos_k = key_off + kb * BLK

            def pair(qb, carry, causal):
                dk, dv = carry
                q_blk, g_blk = q_ref[qb], g_ref[qb]
                pos_q = q_off + qb * BLK
                vis = pos_k >= doc_bounds(pos_q, len_ref)
                if causal:
                    vis = vis & (pos_k <= pos_q)
                s = nt(k_blk, q_blk)
                p = jnp.where(vis, jnp.exp2(s * SCALE2 - lse_ref[qb]), 0.0)
                gp = nt(v_blk, g_blk)
                ds = (p * (gp - delta_ref[qb])).astype(BF16)
                dq_ref[qb] += mm(k_t, ds)
                dk = dk + mm(ds, q_blk)
                dv = dv + mm(p.astype(BF16), g_blk)
                return dk, dv

            zero = jnp.zeros((BLK, 128), F32)
            carry = pair(kb, (zero, zero), True)
            dk, dv = lax.fori_loop(kb + 1, 8, lambda qb, carry: pair(qb, carry, False), carry)
            dkv[:, :, :, kv_rows(kb, 0), :] = (dk * SCALE).astype(BF16).reshape(4, 4, 4, Q_BLK, 128)
            dkv[:, :, :, kv_rows(kb, 1), :] = dv.astype(BF16).reshape(4, 4, 4, Q_BLK, 128)
            return 0

        kv_pending = [[] for _ in range(6)]

        def pick1(rest, order, where):
            return (where,) if rest[0] == order[1] else (slice(None), where)

        def kv_stage(chunk, stage):
            for i, (r0, rn, order) in enumerate(KV_CHUNK):
                p, r0 = chunk * 3 + i, r0 + chunk * 128
                for copy in kv_pending[p]:
                    copy.wait()
                kv_pending[p] = []
                rest = [a for a in AXES if a not in order[:1]]
                if stage == 1:
                    own = dkv[kv_index(rest, c, r0, rn)].astype(F32)
                    for k in range(3):
                        own = own + kv1[p][k].astype(F32)
                    kva1[p][...] = own.astype(BF16)
                if stage == 2:
                    own = kva1[p][pick1(rest, order, c[order[1]])].astype(F32)
                    for k in range(3):
                        own = own + kv2[p][k].astype(F32)
                    kva2[p][...] = own.astype(BF16)
                if stage == 3:
                    own = kva2[p][c[order[2]]].astype(F32)
                    for k in range(3):
                        own = own + kv3[p][k].astype(F32)
                    own_ref[pl.ds(r0, rn), :] = own
                    continue
                for k in (1, 2, 3):
                    there = (c[order[stage]] + k) % 4
                    if stage == 0:
                        cc = dict(c)
                        cc[order[0]] = there
                        src, dst = dkv.at[kv_index(rest, cc, r0, rn)], kv1[p].at[k - 1]
                    elif stage == 1:
                        src, dst = kva1[p].at[pick1(rest, order, there)], kv2[p].at[k - 1]
                    else:
                        src, dst = kva2[p].at[there], kv3[p].at[k - 1]
                    kv_pending[p].append(push(src, dst, peer(order[stage], k)))

        lax.fori_loop(0, 4, k_step, 0)
        for m in (0, 2, 1):
            second_step(m)
        kv_stage(0, 0)
        lax.fori_loop(4, 8, k_step, 0)
        kv_stage(1, 0)
        kv_stage(0, 1)
        for p in range(3):
            out_second(p)
        for m in (0, 2, 1):
            second_axis_step(m)
        kv_stage(1, 1)
        kv_stage(0, 2)
        for p in range(3):
            out_sum(p)
        kv_stage(1, 2)
        for m in (0, 2, 1):
            second_axis_sum(m)
        kv_stage(0, 3)
        kv_stage(1, 3)

    rows = [rn for _, rn, _ in KV_CHUNK] * 2
    scratch = (
        [pltpu.VMEM((1536, 512), BF16)] * 3
        + [pltpu.VMEM((512, FC), BF16)] * 3
        + [pltpu.VMEM((64, 256, 128), BF16)]
        + [pltpu.VMEM((4, 384, FC), BF16)] * 3
        + [pltpu.VMEM((2, 192, FC), BF16)] * 3
        + [pltpu.VMEM((2, 192, FC), BF16)] * 3
        + [pltpu.VMEM((2, 192, FC), BF16)] * 3
        + [pltpu.VMEM((3, 96, FC), BF16)] * 3
        + [pltpu.VMEM((4, 384, 256), BF16)] * 3
        + [pltpu.VMEM((3, 384, 256), BF16)] * 3
        + [pltpu.VMEM((3, 96, 256), BF16)] * 3
        + [pltpu.VMEM((4, 4, 4, 256, 128), BF16)]
        + [pltpu.VMEM((3, 4, 4, r, 128), BF16) for r in rows]
        + [pltpu.VMEM((3, 4, r, 128), BF16) for r in rows]
        + [pltpu.VMEM((3, r, 128), BF16) for r in rows]
        + [pltpu.VMEM((4, 4, r, 128), BF16) for r in rows]
        + [pltpu.VMEM((4, r, 128), BF16) for r in rows]
        + [DMA((7,)), DMA((128,)), DMA((128,))]
    )
    vm, sm = pl.BlockSpec(memory_space=pltpu.VMEM), pl.BlockSpec(memory_space=pltpu.SMEM)
    f32 = lambda *s: jax.ShapeDtypeStruct(s, F32)
    return pl.pallas_call(
        body,
        out_shape=(f32(96, FC),) * 3 + (f32(96, 256),) * 3 + (f32(8, 128, 96), f32(256, 128)),
        in_specs=[sm] + [pl.BlockSpec(memory_space=pl.ANY)] * 7 + [vm] * 6,
        out_specs=(vm,) * 8,
        scratch_shapes=scratch,
        compiler_params=pltpu.CompilerParams(collective_id=2, has_side_effects=True, vmem_limit_bytes=VMEM_BYTES),
        name="backward",
    )(lengths, *xs_in, *gs_in, kv, q, g, lse, delta, branch_t, attn_low)


SMALL = 40


def finish(mlp_acc, out_acc, dq_t, dkv, cos, sin, norm_t, wq, wk, wv, tokens, gain, g_mid, d_norm2):
    def body(*refs):
        m_acc, o_acc = refs[0:3], refs[3:6]
        (dq_ref, dkv_ref, cos_ref, sin_ref, nt_ref, wq_ref, wk_ref, wv_ref, t_ref, gain_ref,
         gmid_ref, dn2_ref) = refs[6:18]
        gt_ref, gq_ref, gk_ref, gv_ref, go_ref, s_out = refs[18:24]
        m_outs = refs[24:27]
        r = list(refs[27:])
        take = lambda n: [r.pop(0) for _ in range(n)]
        m_got, o_got = take(3), take(3)
        sendbuf, got1, got2, acc2, got3 = take(3), take(3), take(3), take(3), take(3)
        s_acc, s_got, g_ref, part, got_part, send, recv = take(7)
        c = coords()
        core = lax.axis_index("tensor")
        barrier(core=True)
        sems = iter(range(256))

        def push(src, dst, device):
            n = next(sems)
            copy = remote(src, dst, send.at[n], recv.at[n], device)
            copy.start()
            return copy

        def share(acc, got, axis):
            copies = []
            for k in (1, 2, 3):
                rows = pl.ds(pl.multiple_of(((c[axis] + k) % 4) * 24, 8), 24)
                copies.append(push(acc.at[rows, :], got.at[k - 1], peer(axis, k)))
            return copies

        o_copies = [share(o_acc[p], o_got[p], OUT_ORDERS[p][2]) for p in range(3)]
        m_copies = [share(m_acc[m], m_got[m], MLP_AXES[m][0]) for m in range(3)]

        cos_t, sin_t = cos_ref[...], sin_ref[...]
        for qb in range(8):
            dq = dq_ref[qb].T * SCALE
            rows = slice(qb * Q_BLK, (qb + 1) * Q_BLK)
            cs, sn = cos_t[rows], sin_t[rows]
            for h in range(6):
                v = dq[h * Q_BLK : (h + 1) * Q_BLK]
                g_ref[rows, h * 128 : (h + 1) * 128] = (v * cs - swap_halves(v) * sn).astype(BF16)
        dk = jnp.concatenate([dkv_ref[0:64, :], dkv_ref[128:192, :]], axis=0)
        g_ref[:, 768:896] = (dk * cos_t - swap_halves(dk) * sin_t).astype(BF16)
        g_ref[:, 896:] = jnp.concatenate([dkv_ref[64:128, :], dkv_ref[192:256, :]], axis=0).astype(BF16)

        pending = [[], [], []]
        for p, (lo, hi, order) in enumerate(QKV_PARTS):
            slab_products(sendbuf[p], nt_ref, g_ref[:, lo:hi], order)
            for k in (1, 2, 3):
                there = (c[order[0]] + k) % 4
                pending[p].append(push(sendbuf[p].at[there], got1[p].at[k - 1], peer(order[0], k)))

        total = nt(g_ref[:, 768:896], wk_ref[...]) + nt(g_ref[:, 896:], wv_ref[...])
        for h in range(6):
            total = total + nt(g_ref[:, h * 128 : (h + 1) * 128], wq_ref[h])
        part[...] = total
        swap = push(part, got_part, partner())

        inputs = t_ref[...].astype(F32)
        inv = lax.rsqrt(jnp.mean(inputs * inputs, axis=1, keepdims=True) + 1e-06)
        d_norm1 = jnp.sum(part[...] * inputs * inv, axis=0, keepdims=True)
        d_bias = jnp.sum(g_ref[...].astype(F32), axis=0, keepdims=True)
        for j in range(12):
            s_acc[0, j : j + 1, :] = d_norm1[:, j * 128 : (j + 1) * 128]
            s_acc[0, 12 + j : 13 + j, :] = dn2_ref[:, j * 128 : (j + 1) * 128]
        for j in range(8):
            v = d_bias[:, j * 128 : (j + 1) * 128]
            s_acc[0, 24 + j : 25 + j, :] = jnp.where(core == 0, v, 0.0)
            s_acc[0, 32 + j : 33 + j, :] = jnp.where(core == 1, v, 0.0)
        s_pending = []

        def send_small(stage):
            peers = [partner()] if stage == 0 else [peer(AXES[stage - 1], k) for k in (1, 2, 3)]
            for i, d in enumerate(peers):
                s_pending.append(push(s_acc.at[stage], s_got.at[stage * 3 + i], d))

        def sum_small(stage):
            for copy in s_pending:
                copy.wait()
            s_pending.clear()
            if stage == 0:
                return s_acc[0] + s_got[0]
            axis = AXES[stage - 1]
            parts = [s_acc[stage]] + [s_got[stage * 3 + k] for k in range(3)]
            total = jnp.zeros_like(parts[0])
            for w in range(4):
                term = jnp.zeros_like(total)
                for k in range(4):
                    term = jnp.where((c[axis] + 4 - k) % 4 == w, parts[k], term)
                total = total + term
            return total

        send_small(0)
        for p in range(3):
            for copy in o_copies[p]:
                copy.wait()
            rows = pl.ds(pl.multiple_of(c[OUT_ORDERS[p][2]] * 24, 8), 24)
            total = o_acc[p][rows, :]
            for k in range(3):
                total = total + o_got[p][k]
            for j in range(2):
                go_ref[p * 2 + j] = total[:, j * 128 : (j + 1) * 128]
        s_acc[1] = sum_small(0)
        send_small(1)
        swap.wait()
        g_norm = part[...] + got_part[...]
        scaled = g_norm * gain_ref[...]
        gt_ref[...] = gmid_ref[...] + (
            inv * scaled - inputs * (inv * inv * inv) * jnp.mean(scaled * inputs, axis=1, keepdims=True)
        )
        for p, (lo, hi, order) in enumerate(QKV_PARTS):
            own = c[order[0]]
            sum_first(sendbuf[p], got1[p], pending[p], own)
            pending[p] = []
            for k in (1, 2, 3):
                rows = pl.ds(pl.multiple_of(((c[order[1]] + k) % 4) * 96, 32), 96)
                pending[p].append(push(sendbuf[p].at[own, rows, :], got2[p].at[k - 1], peer(order[1], k)))
        s_acc[2] = sum_small(1)
        send_small(2)
        for m in range(3):
            for copy in m_copies[m]:
                copy.wait()
            here = c[MLP_AXES[m][0]]
            m_outs[m][:, pl.ds(col_start(here), FC)] = m_acc[m][pl.ds(pl.multiple_of(here * 24, 8), 24), :]
            for k in (1, 2, 3):
                m_outs[m][:, pl.ds(col_start((here + 4 - k) % 4), FC)] = m_got[m][k - 1]
        for p, (lo, hi, order) in enumerate(QKV_PARTS):
            for copy in pending[p]:
                copy.wait()
            own = c[order[0]]
            rows = pl.ds(pl.multiple_of(c[order[1]] * 96, 32), 96)
            total = sendbuf[p][own, rows, :].astype(F32)
            for k in range(3):
                total = total + got2[p][k].astype(F32)
            acc2[p][...] = total
            pending[p] = share(acc2[p], got3[p], order[2])
        s_acc[3] = sum_small(2)
        send_small(3)
        for p, (lo, hi, order) in enumerate(QKV_PARTS):
            for copy in pending[p]:
                copy.wait()
            rows = pl.ds(pl.multiple_of(c[order[2]] * 24, 8), 24)
            total = acc2[p][rows, :]
            for k in range(3):
                total = total + got3[p][k]
            for j in range(lo // 128, hi // 128):
                v = total[:, j * 128 - lo : (j + 1) * 128 - lo]
                if j < 6:
                    gq_ref[j] = v
                elif j == 6:
                    gk_ref[...] = v
                else:
                    gv_ref[...] = v
        s_out[...] = sum_small(3)

    cols = [hi - lo for lo, hi, _ in QKV_PARTS]
    scratch = (
        [pltpu.VMEM((3, 24, FC), F32)] * 3
        + [pltpu.VMEM((3, 24, 256), F32)] * 3
        + [pltpu.VMEM((4, 384, n), BF16) for n in cols]
        + [pltpu.VMEM((3, 384, n), BF16) for n in cols]
        + [pltpu.VMEM((3, 96, n), BF16) for n in cols]
        + [pltpu.VMEM((96, n), F32) for n in cols]
        + [pltpu.VMEM((3, 24, n), F32) for n in cols]
        + [
            pltpu.VMEM((4, SMALL, 128), F32),
            pltpu.VMEM((12, SMALL, 128), F32),
            pltpu.VMEM((128, 1024), BF16),
            pltpu.VMEM((128, 1536), F32),
            pltpu.VMEM((128, 1536), F32),
            DMA((64,)),
            DMA((64,)),
        ]
    )
    f32 = lambda *s: jax.ShapeDtypeStruct(s, F32)
    shape = (f32(128, 1536), f32(6, 24, 128), f32(24, 128), f32(24, 128), f32(6, 24, 128), f32(SMALL, 128))
    shape = shape + (f32(24, 4480),) * 3
    return comm_call(body, shape, 18, scratch, 3, "finish")(
        *mlp_acc, *out_acc, dq_t, dkv, cos, sin, norm_t, wq, wk, wv, tokens, gain, g_mid, d_norm2
    )


def local(
    tokens, cotangent, lengths, norm1_gain, w_query, b_query, w_key, b_key, w_value, b_value, w_out,
    norm2_gain, w_gate, w_up, w_down,
):
    device = lax.axis_index("seq")
    core = lax.axis_index("tensor")
    wq = w_query.transpose(1, 0, 2)
    wk, wv = w_key.reshape(1536, 128), w_value.reshape(1536, 128)
    wo = w_out.reshape(768, 1536)
    gain1, gain2 = norm1_gain.reshape(1, 1536), norm2_gain.reshape(1, 1536)

    q, kv, norm_t, cos, sin = qkv_gather(tokens, gain1, wq, wk, wv, b_query, b_key, b_value, lengths)
    kv = kv.reshape(64, 256, 128)
    branch, attn, attn_low, lse = attn_forward(q, kv, wo, lengths)
    output, g_mid, branch_t, g_attn, delta, d_norm2, *shared = feed_forward(
        branch, attn, tokens, cotangent, gain2, wo, w_gate, w_up, w_down
    )
    *acc, dq_t, dkv = backward(shared[:3], shared[3:], q, g_attn, kv, lse, delta, branch_t, attn_low, lengths)
    grad_tokens, grad_wq, grad_wk, grad_wv, grad_wo, sums, grad_gate, grad_up, grad_down = finish(
        acc[:3], acc[3:], dq_t, dkv, cos, sin, norm_t, wq, wk, wv, tokens, gain1, g_mid, d_norm2
    )
    sums = sums.reshape(-1)
    grad_norm1 = lax.dynamic_slice(sums, (device * 24,), (24,))
    grad_norm2 = lax.dynamic_slice(sums, (1536 + device * 24,), (24,))
    bias = lax.dynamic_slice(sums.reshape(SMALL, 128), (24 + core * 8, device * 2), (8, 2))
    return (
        output,
        grad_tokens,
        grad_norm1,
        grad_wq.transpose(1, 0, 2),
        bias[:6],
        grad_wk.reshape(24, 1, 128),
        bias[6:7],
        grad_wv.reshape(24, 1, 128),
        bias[7:8],
        grad_wo.transpose(0, 2, 1),
        grad_norm2,
        grad_gate,
        grad_up,
        grad_down.T,
    )


def solution(mesh):
    in_specs = (
        P("seq", None), P("seq", None), P(), P(), P(None, "tensor", None), P("tensor", None),
        P(None, "tensor", None), P("tensor", None), P(None, "tensor", None), P("tensor", None),
        P("tensor", None, None), P(), P(None, "tensor"), P(None, "tensor"), P("tensor", None),
    )
    out_specs = (
        P("seq", None), P("seq", None), P("seq"), P("seq", "tensor", None), P("tensor", "seq"),
        P("seq", "tensor", None), P("tensor", "seq"), P("seq", "tensor", None), P("tensor", "seq"),
        P("tensor", None, "seq"), P("seq"), P("seq", "tensor"), P("seq", "tensor"), P("tensor", "seq"),
    )
    return jax.shard_map(local, mesh=mesh, in_specs=in_specs, out_specs=out_specs, check_vma=False)
```

```python
import math

import jax
import jax.numpy as jnp
from jax import lax
from jax.experimental import pallas as pl
from jax.experimental.pallas import tpu as pltpu
from jax.sharding import PartitionSpec as P

MESH = pl.DeviceIdType.MESH
F32 = jnp.float32
BF16 = jnp.bfloat16
VMEM_BYTES = 60 * 1024 * 1024
AXES = ("z", "x", "y")
STRIDE = {"z": 16, "x": 4, "y": 1}


def coords():
    s = lax.axis_index("seq")
    return {"z": s // 16, "x": (s // 4) % 4, "y": s % 4}


def peer(axis, k):
    s = lax.axis_index("seq")
    c = coords()[axis]
    return (s + STRIDE[axis] * ((c + k) % 4 - c), lax.axis_index("tensor"))


def partner():
    return (lax.axis_index("seq"), 1 - lax.axis_index("tensor"))


def barrier(axes=AXES, core=False):
    bar = pltpu.get_barrier_semaphore()
    ids = [peer(a, k) for a in axes for k in (1, 2, 3)]
    if core:
        ids.append(partner())
    for d in ids:
        pl.semaphore_signal(bar, inc=1, device_id=d, device_id_type=MESH)
    pl.semaphore_wait(bar, len(ids))


def remote(src, dst, send, recv, device):
    return pltpu.make_async_remote_copy(
        src_ref=src, dst_ref=dst, send_sem=send, recv_sem=recv, device_id=device, device_id_type=MESH
    )


DMA = pltpu.SemaphoreType.DMA


KV_CHUNK = (
    (0, 48, ("z", "x", "y")),
    (48, 48, ("x", "y", "z")),
    (96, 32, ("y", "z", "x")),
)


def kv_rows(kb, v):
    return pl.ds(pl.multiple_of((kb // 4) * 128 + v * 64 + (kb % 4) * Q_BLK, Q_BLK), Q_BLK)


def kv_index(done, c, r0, rn):
    return tuple(slice(None) if a in done else c[a] for a in AXES) + (pl.ds(r0, rn), slice(None))


def rope_tables(len_ref):
    lane = lax.broadcasted_iota(jnp.int32, (128, 128), 1)
    pos = lax.broadcasted_iota(jnp.int32, (128, 128), 0) * 64 + lax.axis_index("seq")
    rel = (pos - doc_bounds(pos, len_ref)).astype(F32)
    inv_freq = jnp.exp(-(2.0 * (lane % 64).astype(F32) / 128) * math.log(10000.0))
    angle = rel * inv_freq
    sin = jnp.sin(angle)
    return jnp.cos(angle), jnp.where(lane < 64, -sin, sin)


def swap_halves(v):
    return pltpu.roll(v, 64, 1)


def qkv_gather(tokens, gain, wq, wk, wv, bq, bk, bv, lengths):
    def body(len_ref, t_ref, g_ref, wq_ref, wk_ref, wv_ref, bq_ref, bk_ref, bv_ref,
             q_out, out, nt_out, cos_out, sin_out, wq_buf, loc, send, recv):
        c = coords()
        load = pltpu.make_async_copy(wq_ref, wq_buf, loc)
        load.start()
        x = t_ref[...].astype(F32)
        inv = lax.rsqrt(jnp.mean(x * x, axis=1, keepdims=True) + 1e-06)
        normed = (x * inv * g_ref[0:1, :]).astype(BF16)
        cos, sin = rope_tables(len_ref)
        cos_out[...], sin_out[...] = cos, sin
        k_pre = jnp.dot(normed, wk_ref[...], preferred_element_type=F32) + bk_ref[...].astype(F32)
        v_pre = jnp.dot(normed, wv_ref[...], preferred_element_type=F32) + bv_ref[...].astype(F32)
        k_rot = (k_pre * cos + swap_halves(k_pre) * sin).astype(BF16)
        v_low = v_pre.astype(BF16)
        out[c["z"], c["x"], c["y"]] = jnp.concatenate([k_rot[:64], v_low[:64], k_rot[64:], v_low[64:]], axis=0)
        barrier()
        parts = [(r0 + 128 * chunk, rn, order) for chunk in range(2) for r0, rn, order in KV_CHUNK]
        pending = [[] for _ in parts]

        def send_stage(stage):
            for p, (r0, rn, order) in enumerate(parts):
                for copy in pending[p]:
                    copy.wait()
                pending[p] = []
                idx = kv_index(order[:stage], c, r0, rn)
                for k in (1, 2, 3):
                    n = (p * 3 + stage) * 3 + k - 1
                    copy = remote(out.at[idx], out.at[idx], send.at[n], recv.at[n], peer(order[stage], k))
                    copy.start()
                    pending[p].append(copy)

        send_stage(0)
        load.wait()
        for h in range(6):
            q = jnp.dot(normed, wq_buf[h], preferred_element_type=F32) + bq_ref[h : h + 1, :].astype(F32)
            q = (q * cos + swap_halves(q) * sin).astype(BF16)
            q_out[:, h * Q_BLK : (h + 1) * Q_BLK, :] = q.reshape(8, Q_BLK, 128)
        send_stage(1)
        nt_out[...] = normed.T
        send_stage(2)
        for copies in pending:
            for copy in copies:
                copy.wait()

    vm, sm = pl.BlockSpec(memory_space=pltpu.VMEM), pl.BlockSpec(memory_space=pltpu.SMEM)
    return pl.pallas_call(
        body,
        out_shape=(
            jax.ShapeDtypeStruct((8, 96, 128), BF16),
            jax.ShapeDtypeStruct((4, 4, 4, 256, 128), BF16),
            jax.ShapeDtypeStruct((1536, 128), BF16),
            jax.ShapeDtypeStruct((128, 128), F32),
            jax.ShapeDtypeStruct((128, 128), F32),
        ),
        in_specs=[sm, vm, vm, pl.BlockSpec(memory_space=pl.ANY)] + [vm] * 5,
        out_specs=(vm,) * 5,
        scratch_shapes=[pltpu.VMEM((6, 1536, 128), BF16), DMA, DMA((54,)), DMA((54,))],
        compiler_params=pltpu.CompilerParams(collective_id=0, has_side_effects=True, vmem_limit_bytes=VMEM_BYTES),
        name="qkv_gather",
    )(lengths, tokens, gain, wq, wk, wv, bq, bk, bv)


Q_BLK = 16
BLK = Q_BLK * 64
SCALE = 1.0 / math.sqrt(128)
SCALE2 = SCALE / math.log(2.0)


def doc_bounds(pos, len_ref):
    start = jnp.zeros_like(pos)
    end = jnp.int32(0)
    for j in range(8):
        end = end + len_ref[j]
        start = jnp.where(pos >= end, end, start)
    return start


def doc_start_scalar(pos, len_ref):
    start, end = jnp.int32(0), jnp.int32(0)
    for j in range(8):
        end = end + len_ref[j]
        start = jnp.where(pos >= end, end, start)
    return start


def attn_forward(q, kv, w_out, lengths):
    def body(len_ref, q_ref, kv_hbm, wo_hbm, part_ref, out_ref, low_ref, lse_ref, kv_ref, wo_ref, loc):
        loads = [
            pltpu.make_async_copy(kv_hbm.at[:, pl.ds(0, 128), :], kv_ref.at[:, pl.ds(0, 128), :], loc.at[0]),
            pltpu.make_async_copy(kv_hbm.at[:, pl.ds(128, 128), :], kv_ref.at[:, pl.ds(128, 128), :], loc.at[1]),
            pltpu.make_async_copy(wo_hbm, wo_ref, loc.at[2]),
        ]
        for copy in loads:
            copy.start()
        dev = lax.axis_index("seq")
        col = lax.broadcasted_iota(jnp.int32, (96, BLK), 1)
        key_off = (col % Q_BLK) * 64 + col // Q_BLK
        row_off = (lax.broadcasted_iota(jnp.int32, (96, 1), 0) % Q_BLK) * 64 + dev

        def q_step(qb, _):
            q_blk = q_ref[qb]
            pos_q = row_off + qb * BLK
            start_q = doc_bounds(pos_q, len_ref)
            lo = doc_start_scalar(qb * BLK + dev, len_ref) // BLK

            def k_step(kb, carry):
                m, l, acc = carry
                k_blk = kv_ref[:, kv_rows(kb, 0), :].reshape(BLK, 128)
                v_blk = kv_ref[:, kv_rows(kb, 1), :].reshape(BLK, 128)
                s = lax.dot_general(q_blk, k_blk, (((1,), (1,)), ((), ())), preferred_element_type=F32)
                pos_k = key_off + kb * BLK
                vis = (pos_k <= pos_q) & (pos_k >= start_q)
                s = jnp.where(vis, s * SCALE2, -1e30)
                m_new = jnp.maximum(m, jnp.max(s, axis=1, keepdims=True))
                p = jnp.where(vis, jnp.exp2(s - m_new), 0.0)
                a = jnp.exp2(m - m_new)
                l = l * a + jnp.sum(p, axis=1, keepdims=True)
                acc = acc * a + jnp.dot(p.astype(BF16), v_blk, preferred_element_type=F32)
                return m_new, l, acc

            init = (jnp.full((96, 1), -1e30, F32), jnp.zeros((96, 1), F32), jnp.zeros((96, 128), F32))
            m, l, acc = lax.fori_loop(lo, qb + 1, k_step, init)
            attn = acc / l
            out_ref[qb] = attn
            low = attn.astype(BF16)
            for h in range(6):
                rows = pl.ds(pl.multiple_of(qb * Q_BLK, Q_BLK), Q_BLK)
                low_ref[rows, h * 128 : (h + 1) * 128] = low[h * Q_BLK : (h + 1) * Q_BLK]
            lse_ref[qb] = jnp.broadcast_to(m + jnp.log2(l), (96, 128)).T[0:1]
            return 0

        loads[0].wait()
        lax.fori_loop(0, 4, q_step, 0)
        loads[1].wait()
        lax.fori_loop(4, 8, q_step, 0)
        loads[2].wait()
        part_ref[...] = jnp.dot(low_ref[...], wo_ref[...], preferred_element_type=F32)

    vm = pl.BlockSpec(memory_space=pltpu.VMEM)
    return pl.pallas_call(
        body,
        out_shape=(
            jax.ShapeDtypeStruct((128, 1536), F32),
            jax.ShapeDtypeStruct((8, 96, 128), F32),
            jax.ShapeDtypeStruct((128, 768), BF16),
            jax.ShapeDtypeStruct((8, 1, 96), F32),
        ),
        in_specs=[pl.BlockSpec(memory_space=pltpu.SMEM), vm] + [pl.BlockSpec(memory_space=pl.ANY)] * 2,
        out_specs=(vm,) * 4,
        scratch_shapes=[pltpu.VMEM((64, 256, 128), BF16), pltpu.VMEM((768, 1536), BF16), DMA((3,))],
        compiler_params=pltpu.CompilerParams(vmem_limit_bytes=VMEM_BYTES),
        name="attn_forward",
    )(lengths, q, kv, w_out)


FC = 1152


def nt(a, b):
    return lax.dot_general(a, b, (((1,), (1,)), ((), ())), preferred_element_type=F32)


def mm(a, b):
    return jnp.dot(a, b, preferred_element_type=F32)


def col_start(c):
    return pl.multiple_of(jnp.minimum(c * FC, 4480 - FC), 128)


MLP_AXES = (("z", "x", "y"), ("x", "y", "z"), ("y", "z", "x"))


def feed_forward(branch, attn, tokens, cot, gain, w_out, w_gate, w_up, w_down):
    def body(br_ref, at_ref, t_ref, c_ref, g_ref, wo_hbm, wg_hbm, wu_hbm, wd_hbm,
             out_ref, gmid_ref, bt_ref, ga_ref, delta_ref, dn_ref, x0, x1, x2, g0, g1, g2,
             wo_ref, wg, wu, wd, got_br, acc, got, mid_ref, norm_ref, nt_ref, ct_ref, act, w_sem, loc, send, recv):
        xs, gs = (x0, x1, x2), (g0, g1, g2)
        c = coords()
        turn = c["z"] + c["x"] + c["y"]
        sems = iter(range(64))

        def load(j):
            cols = pl.ds(col_start((turn + j) % 4), FC)
            b = j % 2
            copies = [
                pltpu.make_async_copy(wg_hbm.at[:, cols], wg.at[b], w_sem.at[b, 0]),
                pltpu.make_async_copy(wu_hbm.at[:, cols], wu.at[b], w_sem.at[b, 1]),
                pltpu.make_async_copy(wd_hbm.at[cols, :], wd.at[b], w_sem.at[b, 2]),
            ]
            for copy in copies:
                copy.start()
            return copies

        loads = [load(0), load(1)]
        barrier(core=True)

        def push(src, dst, device):
            n = next(sems)
            copy = remote(src, dst, send.at[n], recv.at[n], device)
            copy.start()
            return copy

        later = []
        ex = push(br_ref, got_br, partner())
        ct_ref[...] = c_ref[...].T
        own = [pltpu.make_async_copy(ct_ref, x2.at[:, pl.ds(0, 128)], loc.at[3])]
        own[0].start()
        for k in (1, 2, 3):
            later.append(push(ct_ref, x2.at[:, pl.ds(k * 128, 128)], peer("y", k)))
        ex.wait()
        mid = t_ref[...].astype(F32) + (br_ref[...] + got_br[...])
        mid_ref[...] = mid
        inv = lax.rsqrt(jnp.mean(mid * mid, axis=1, keepdims=True) + 1e-06)
        normed = (mid * inv * g_ref[1:2, :]).astype(BF16)
        norm_ref[...] = normed
        nt_ref[...] = normed.T
        own.append(pltpu.make_async_copy(nt_ref, x0.at[:, pl.ds(0, 128)], loc.at[4]))
        own.append(pltpu.make_async_copy(nt_ref, x1.at[:, pl.ds(0, 128)], loc.at[5]))
        own.append(pltpu.make_async_copy(wo_hbm, wo_ref, loc.at[6]))
        for copy in own[1:]:
            copy.start()
        for k in (1, 2, 3):
            for m, w in ((0, "z"), (1, "x")):
                later.append(push(nt_ref, xs[m].at[:, pl.ds(k * 128, 128)], peer(w, k)))

        lane = lax.broadcasted_iota(jnp.int32, (128, FC), 1)
        for j in range(4):
            b = j % 2
            d = (turn + j) % 4
            for copy in loads[j]:
                copy.wait()
            n = norm_ref[...]
            gate = mm(n, wg[b])
            up = mm(n, wu[b])
            gh = nt(c_ref[...], wd[b])
            sig = 1.0 / (1.0 + jnp.exp(-gate))
            silu = gate * sig
            hidden = (silu * up).astype(BF16)
            g_gate = (gh * up * sig * (1.0 + gate * (1.0 - sig))).astype(BF16)
            g_up = (gh * silu).astype(BF16)
            vals = (g_gate, g_up, hidden)
            for m in range(3):
                act[m, j] = vals[m]
            twice = (lane < 128) & (d == 3)
            zero = jnp.zeros((128, FC), BF16)
            hidden, g_gate, g_up = (jnp.where(twice, zero, v) for v in (hidden, g_gate, g_up))
            add_o = mm(hidden, wd[b])
            add_g = nt(g_gate, wg[b]) + nt(g_up, wu[b])
            if j == 0:
                acc[0], acc[1] = add_o, add_g
            else:
                acc[0] += add_o
                acc[1] += add_g
            if j + 2 < 4:
                loads.append(load(j + 2))
            for m in range(3):
                w = MLP_AXES[m][0]
                k = (d + 4 - c[w]) % 4
                slot = pl.ds(pl.multiple_of(k * 128, 128), 128)

                @pl.when(k == 0)
                def _():
                    pltpu.make_async_copy(act.at[m, j], gs[m].at[pl.ds(0, 128), :], loc.at[m]).start()

                @pl.when(k != 0)
                def _():
                    remote(
                        act.at[m, j], gs[m].at[slot, :], send.at[32 + m * 4 + j], recv.at[32 + m * 4 + k], peer(w, k)
                    ).start()

        dn_ref[...] = jnp.sum(acc[1] * mid_ref[...] * inv, axis=0, keepdims=True)
        ex = [push(acc.at[1], got.at[1], partner()), push(acc.at[0], got.at[0], partner())]
        cot_f = c_ref[...].astype(F32)
        ex[0].wait()
        gn = acc[1] + got[1]
        mid = mid_ref[...]
        scaled = gn * g_ref[1:2, :]
        g_mid = cot_f + (inv * scaled - mid * (inv * inv * inv) * jnp.mean(scaled * mid, axis=1, keepdims=True))
        gmid_ref[...] = g_mid
        own[3].wait()
        branch_low = g_mid.astype(BF16)
        bt_ref[...] = branch_low.T
        g_attn = nt(branch_low, wo_ref[...]).astype(BF16)
        for h in range(6):
            ga_ref[:, h * Q_BLK : (h + 1) * Q_BLK, :] = g_attn[:, h * 128 : (h + 1) * 128].reshape(8, Q_BLK, 128)
        for qb in range(8):
            delta_ref[qb] = jnp.sum((ga_ref[qb].astype(F32) * at_ref[qb]).T, axis=0, keepdims=True)
        ex[1].wait()
        out_ref[...] = mid_ref[...] + (acc[0] + got[0])
        for copy in later + own[:3]:
            copy.wait()
        for m in range(3):
            w = MLP_AXES[m][0]
            pltpu.make_async_copy(act.at[m, 0], gs[m].at[pl.ds(0, 128), :], loc.at[m]).wait()
            for j in range(4):
                k = ((turn + j) % 4 + 4 - c[w]) % 4

                @pl.when(k != 0)
                def _():
                    slot = pl.ds(pl.multiple_of(k * 128, 128), 128)
                    remote(
                        act.at[m, j], gs[m].at[slot, :], send.at[32 + m * 4 + j], recv.at[32 + m * 4 + k], peer(w, k)
                    ).wait()

    f32 = lambda *s: jax.ShapeDtypeStruct(s, F32)
    b16 = lambda *s: jax.ShapeDtypeStruct(s, BF16)
    vm, hbm = pl.BlockSpec(memory_space=pltpu.VMEM), pl.BlockSpec(memory_space=pl.ANY)
    return pl.pallas_call(
        body,
        out_shape=(f32(128, 1536), f32(128, 1536), b16(1536, 128), b16(8, 96, 128), f32(8, 1, 96), f32(1, 1536))
        + (b16(1536, 512),) * 3
        + (b16(512, FC),) * 3,
        in_specs=[vm] * 5 + [hbm] * 4,
        out_specs=(vm,) * 6 + (hbm,) * 6,
        scratch_shapes=[
            pltpu.VMEM((768, 1536), BF16),
            pltpu.VMEM((2, 1536, FC), BF16),
            pltpu.VMEM((2, 1536, FC), BF16),
            pltpu.VMEM((2, FC, 1536), BF16),
            pltpu.VMEM((128, 1536), F32),
            pltpu.VMEM((2, 128, 1536), F32),
            pltpu.VMEM((2, 128, 1536), F32),
            pltpu.VMEM((128, 1536), F32),
            pltpu.VMEM((128, 1536), BF16),
            pltpu.VMEM((1536, 128), BF16),
            pltpu.VMEM((1536, 128), BF16),
            pltpu.VMEM((3, 4, 128, FC), BF16),
            DMA((2, 3)),
            DMA((7,)),
            DMA((64,)),
            DMA((64,)),
        ],
        compiler_params=pltpu.CompilerParams(collective_id=4, has_side_effects=True, vmem_limit_bytes=VMEM_BYTES),
        name="feed_forward",
    )(branch, attn, tokens, cot, gain, w_out, w_gate, w_up, w_down)


OUT_ORDERS = (("z", "x", "y"), ("x", "y", "z"), ("y", "z", "x"))
QKV_PARTS = ((0, 384, ("z", "x", "y")), (384, 768, ("x", "y", "z")), (768, 1024, ("y", "z", "x")))


def slab_products(buf, left, rhs, order):
    def blocks(v, places):
        return jnp.concatenate([v[o * 24 : (o + 1) * 24] for o in places], axis=0)

    if order[0] == "z":
        for z in range(4):
            buf[z] = mm(left[z * 384 : (z + 1) * 384, :], rhs).astype(BF16)
    elif order[0] == "x":
        for x in range(4):
            lhs = jnp.concatenate([left[z * 384 + x * 96 : z * 384 + (x + 1) * 96, :] for z in range(4)], axis=0)
            buf[x] = blocks(mm(lhs, rhs), [z * 4 + y for y in range(4) for z in range(4)]).astype(BF16)
    else:
        for z in range(4):
            v = blocks(mm(left[z * 384 : (z + 1) * 384, :], rhs), [x * 4 + y for y in range(4) for x in range(4)])
            v = v.astype(BF16)
            for y in range(4):
                buf[y, z * 96 : (z + 1) * 96] = v[y * 96 : (y + 1) * 96]


def sum_first(buf, got, copies, own):
    for copy in copies:
        copy.wait()
    total = buf[own].astype(F32)
    for k in range(3):
        total = total + got[k].astype(F32)
    buf[own] = total.astype(BF16)


def backward(xs_in, gs_in, q, g, kv, lse, delta, branch_t, attn_low, lengths):
    def body(*refs):
        len_ref, xs_hbm, gs_hbm, kv_hbm = refs[0], refs[1:4], refs[4:7], refs[7]
        q_ref, g_ref, lse_ref, delta_ref, bt_ref, a_ref = refs[8:14]
        acc2, o_acc2, dq_ref, own_ref = refs[14:17], refs[17:20], refs[20], refs[21]
        r = list(refs[22:])
        take = lambda n: [r.pop(0) for _ in range(n)]
        xs, gs, (kv_ref,) = take(3), take(3), take(1)
        sendbuf, r1a, r1b, r2, got2 = take(3), take(3), take(3), take(3), take(3)
        o_buf, o_got1, o_got2 = take(3), take(3), take(3)
        (dkv,) = take(1)
        kv1, kv2, kv3, kva1, kva2 = take(6), take(6), take(6), take(6), take(6)
        loc, send, recv = take(3)
        c = coords()
        loads = [pltpu.make_async_copy(a, b, loc.at[i]) for i, (a, b) in enumerate(
            ((xs_hbm[0], xs[0]), (gs_hbm[0], gs[0]), (xs_hbm[2], xs[2]), (gs_hbm[2], gs[2]),
             (xs_hbm[1], xs[1]), (gs_hbm[1], gs[1]), (kv_hbm, kv_ref)))]
        for copy in loads:
            copy.start()
        barrier()
        sems = iter(range(256))

        def push(src, dst, device):
            n = next(sems)
            copy = remote(src, dst, send.at[n], recv.at[n], device)
            copy.start()
            return copy

        def regroup(v, outer, inner):
            return jnp.concatenate(
                [v[(o * inner + i) * 24 : (o * inner + i + 1) * 24] for i in range(inner) for o in range(outer)], axis=0
            )

        near = lambda u: u + 1 - 2 * (u % 2)
        far = lambda u: 3 - u
        over = lambda u: (u + 2) % 4
        top, low = pl.ds(0, 192), pl.ds(192, 192)
        first, second = [[], [], []], [[], [], []]

        def neighbour(axis, u):
            return peer(axis, u + 4 - c[axis])

        def slab(m, u):
            return sendbuf[m].at[u]

        def ready(m, which):
            axis = MLP_AXES[m][1]
            u = c[axis]
            if which == "over":
                first[m].append(push(slab(m, over(u)).at[top, :], r1a[m].at[0], neighbour(axis, near(u))))
                first[m].append(push(slab(m, over(u)).at[low, :], r1b[m].at[0], neighbour(axis, far(u))))
            elif which == "near":
                first[m].append(push(slab(m, near(u)).at[top, :], r1a[m].at[1], neighbour(axis, near(u))))
            elif which == "far":
                first[m].append(push(slab(m, far(u)).at[low, :], r1b[m].at[1], neighbour(axis, far(u))))

        def second_step(m):
            axis = MLP_AXES[m][1]
            u = c[axis]
            first[m][0].wait()
            at = slab(m, far(u)).at[top, :]
            at[...] = (at[...].astype(F32) + r1a[m][0].astype(F32)).astype(BF16)
            second[m].append(push(at, r2[m].at[0], neighbour(axis, far(u))))
            first[m][1].wait()
            at = slab(m, near(u)).at[low, :]
            at[...] = (at[...].astype(F32) + r1b[m][0].astype(F32)).astype(BF16)
            second[m].append(push(at, r2[m].at[1], neighbour(axis, near(u))))

        second_axis = [[], [], []]

        def second_axis_step(m):
            axis = MLP_AXES[m][1]
            own = slab(m, c[axis])
            for copy in first[m][2:] + second[m]:
                copy.wait()
            own[top, :] = (own[top, :].astype(F32) + r1a[m][1].astype(F32) + r2[m][0].astype(F32)).astype(BF16)
            own[low, :] = (own[low, :].astype(F32) + r1b[m][1].astype(F32) + r2[m][1].astype(F32)).astype(BF16)
            axis = MLP_AXES[m][2]
            for k in (1, 2, 3):
                rows = pl.ds(pl.multiple_of(((c[axis] + k) % 4) * 96, 32), 96)
                second_axis[m].append(push(own.at[rows, :], got2[m].at[k - 1], peer(axis, k)))

        def second_axis_sum(m):
            for copy in second_axis[m]:
                copy.wait()
            rows = pl.ds(pl.multiple_of(c[MLP_AXES[m][2]] * 96, 32), 96)
            total = slab(m, c[MLP_AXES[m][1]])[rows, :].astype(F32)
            for k in range(3):
                total = total + got2[m][k].astype(F32)
            acc2[m][...] = total

        places = (("over", over), ("near", near), ("far", far), ("own", lambda u: u))
        loads[0].wait()
        loads[1].wait()
        for name, place in places:
            u = place(c["x"])
            rows = [pl.ds(pl.multiple_of(z * 384 + u * 96, 32), 96) for z in range(4)]
            x = jnp.concatenate([xs[0][r, :] for r in rows], axis=0)
            sendbuf[0][u] = regroup(mm(x, gs[0][...]), 4, 4).astype(BF16)
            ready(0, name)
        loads[2].wait()
        loads[3].wait()
        for name, place in places:
            u = place(c["z"])
            x = xs[2][pl.ds(pl.multiple_of(u * 384, 128), 384), :]
            sendbuf[2][u] = mm(x, gs[2][...]).astype(BF16)
            ready(2, name)
        loads[4].wait()
        loads[5].wait()
        for z in range(4):
            v = regroup(mm(xs[1][z * 384 : (z + 1) * 384, :], gs[1][...]), 4, 4).astype(BF16)
            for y in range(4):
                sendbuf[1][y, z * 96 : (z + 1) * 96] = v[y * 96 : (y + 1) * 96]
        for name, _ in places:
            ready(1, name)

        o_first, o_second = [[], [], []], [[], [], []]
        for p, order in enumerate(OUT_ORDERS):
            slab_products(o_buf[p], bt_ref, a_ref[:, p * 256 : (p + 1) * 256], order)
            for k in (1, 2, 3):
                there = (c[order[0]] + k) % 4
                o_first[p].append(push(o_buf[p].at[there], o_got1[p].at[k - 1], peer(order[0], k)))

        def out_second(p):
            order = OUT_ORDERS[p]
            sum_first(o_buf[p], o_got1[p], o_first[p], c[order[0]])
            for k in (1, 2, 3):
                rows = pl.ds(pl.multiple_of(((c[order[1]] + k) % 4) * 96, 32), 96)
                o_second[p].append(push(o_buf[p].at[c[order[0]], rows, :], o_got2[p].at[k - 1], peer(order[1], k)))

        def out_sum(p):
            order = OUT_ORDERS[p]
            for copy in o_second[p]:
                copy.wait()
            rows = pl.ds(pl.multiple_of(c[order[1]] * 96, 32), 96)
            total = o_buf[p][c[order[0]], rows, :].astype(F32)
            for k in range(3):
                total = total + o_got2[p][k].astype(F32)
            o_acc2[p][...] = total

        loads[6].wait()
        dev = lax.axis_index("seq")
        row = lax.broadcasted_iota(jnp.int32, (BLK, 96), 0)
        key_off = (row % Q_BLK) * 64 + row // Q_BLK
        q_off = (lax.broadcasted_iota(jnp.int32, (1, 96), 1) % Q_BLK) * 64 + dev
        dq_ref[...] = jnp.zeros_like(dq_ref)

        def k_step(kb, _):
            k_blk = kv_ref[:, kv_rows(kb, 0), :].reshape(BLK, 128)
            v_blk = kv_ref[:, kv_rows(kb, 1), :].reshape(BLK, 128)
            k_t = k_blk.T
            pos_k = key_off + kb * BLK

            def pair(qb, carry, causal):
                dk, dv = carry
                q_blk, g_blk = q_ref[qb], g_ref[qb]
                pos_q = q_off + qb * BLK
                vis = pos_k >= doc_bounds(pos_q, len_ref)
                if causal:
                    vis = vis & (pos_k <= pos_q)
                s = nt(k_blk, q_blk)
                p = jnp.where(vis, jnp.exp2(s * SCALE2 - lse_ref[qb]), 0.0)
                gp = nt(v_blk, g_blk)
                ds = (p * (gp - delta_ref[qb])).astype(BF16)
                dq_ref[qb] += mm(k_t, ds)
                dk = dk + mm(ds, q_blk)
                dv = dv + mm(p.astype(BF16), g_blk)
                return dk, dv

            zero = jnp.zeros((BLK, 128), F32)
            carry = pair(kb, (zero, zero), True)
            dk, dv = lax.fori_loop(kb + 1, 8, lambda qb, carry: pair(qb, carry, False), carry)
            dkv[:, :, :, kv_rows(kb, 0), :] = (dk * SCALE).astype(BF16).reshape(4, 4, 4, Q_BLK, 128)
            dkv[:, :, :, kv_rows(kb, 1), :] = dv.astype(BF16).reshape(4, 4, 4, Q_BLK, 128)
            return 0

        kv_pending = [[] for _ in range(6)]

        def pick1(rest, order, where):
            return (where,) if rest[0] == order[1] else (slice(None), where)

        def kv_stage(chunk, stage):
            for i, (r0, rn, order) in enumerate(KV_CHUNK):
                p, r0 = chunk * 3 + i, r0 + chunk * 128
                for copy in kv_pending[p]:
                    copy.wait()
                kv_pending[p] = []
                rest = [a for a in AXES if a not in order[:1]]
                if stage == 1:
                    own = dkv[kv_index(rest, c, r0, rn)].astype(F32)
                    for k in range(3):
                        own = own + kv1[p][k].astype(F32)
                    kva1[p][...] = own.astype(BF16)
                if stage == 2:
                    own = kva1[p][pick1(rest, order, c[order[1]])].astype(F32)
                    for k in range(3):
                        own = own + kv2[p][k].astype(F32)
                    kva2[p][...] = own.astype(BF16)
                if stage == 3:
                    own = kva2[p][c[order[2]]].astype(F32)
                    for k in range(3):
                        own = own + kv3[p][k].astype(F32)
                    own_ref[pl.ds(r0, rn), :] = own
                    continue
                for k in (1, 2, 3):
                    there = (c[order[stage]] + k) % 4
                    if stage == 0:
                        cc = dict(c)
                        cc[order[0]] = there
                        src, dst = dkv.at[kv_index(rest, cc, r0, rn)], kv1[p].at[k - 1]
                    elif stage == 1:
                        src, dst = kva1[p].at[pick1(rest, order, there)], kv2[p].at[k - 1]
                    else:
                        src, dst = kva2[p].at[there], kv3[p].at[k - 1]
                    kv_pending[p].append(push(src, dst, peer(order[stage], k)))

        lax.fori_loop(4, 8, k_step, 0)
        kv_stage(1, 0)
        second_step(0)
        lax.fori_loop(0, 1, k_step, 0)
        second_step(2)
        second_step(1)
        lax.fori_loop(1, 2, k_step, 0)
        kv_stage(1, 1)
        second_axis_step(0)
        lax.fori_loop(2, 3, k_step, 0)
        kv_stage(1, 2)
        second_axis_step(2)
        second_axis_step(1)
        for p in range(3):
            out_second(p)
        lax.fori_loop(3, 4, k_step, 0)
        kv_stage(0, 0)
        kv_stage(1, 3)
        for m in (0, 2, 1):
            second_axis_sum(m)
        for p in range(3):
            out_sum(p)
        kv_stage(0, 1)
        kv_stage(0, 2)
        kv_stage(0, 3)

    rows = [rn for _, rn, _ in KV_CHUNK] * 2
    scratch = (
        [pltpu.VMEM((1536, 512), BF16)] * 3
        + [pltpu.VMEM((512, FC), BF16)] * 3
        + [pltpu.VMEM((64, 256, 128), BF16)]
        + [pltpu.VMEM((4, 384, FC), BF16)] * 3
        + [pltpu.VMEM((2, 192, FC), BF16)] * 3
        + [pltpu.VMEM((2, 192, FC), BF16)] * 3
        + [pltpu.VMEM((2, 192, FC), BF16)] * 3
        + [pltpu.VMEM((3, 96, FC), BF16)] * 3
        + [pltpu.VMEM((4, 384, 256), BF16)] * 3
        + [pltpu.VMEM((3, 384, 256), BF16)] * 3
        + [pltpu.VMEM((3, 96, 256), BF16)] * 3
        + [pltpu.VMEM((4, 4, 4, 256, 128), BF16)]
        + [pltpu.VMEM((3, 4, 4, r, 128), BF16) for r in rows]
        + [pltpu.VMEM((3, 4, r, 128), BF16) for r in rows]
        + [pltpu.VMEM((3, r, 128), BF16) for r in rows]
        + [pltpu.VMEM((4, 4, r, 128), BF16) for r in rows]
        + [pltpu.VMEM((4, r, 128), BF16) for r in rows]
        + [DMA((7,)), DMA((128,)), DMA((128,))]
    )
    vm, sm = pl.BlockSpec(memory_space=pltpu.VMEM), pl.BlockSpec(memory_space=pltpu.SMEM)
    f32 = lambda *s: jax.ShapeDtypeStruct(s, F32)
    return pl.pallas_call(
        body,
        out_shape=(f32(96, FC),) * 3 + (f32(96, 256),) * 3 + (f32(8, 128, 96), f32(256, 128)),
        in_specs=[sm] + [pl.BlockSpec(memory_space=pl.ANY)] * 7 + [vm] * 6,
        out_specs=(vm,) * 8,
        scratch_shapes=scratch,
        compiler_params=pltpu.CompilerParams(collective_id=2, has_side_effects=True, vmem_limit_bytes=VMEM_BYTES),
        name="backward",
    )(lengths, *xs_in, *gs_in, kv, q, g, lse, delta, branch_t, attn_low)


SMALL = 40


def finish(mlp_acc, out_acc, dq_t, dkv, cos, sin, norm_t, wq, wk, wv, tokens, gain, g_mid, d_norm2):
    def body(*refs):
        late = refs[0:11]
        dq_ref, dkv_ref, cos_ref, sin_ref, nt_ref, gain_ref, dn2_ref = refs[11:18]
        gt_ref, gq_ref, gk_ref, gv_ref, go_ref, s_out = refs[18:24]
        m_outs = refs[24:27]
        r = list(refs[27:])
        take = lambda n: [r.pop(0) for _ in range(n)]
        held = take(11)
        m_acc, o_acc, (wq_ref, wk_ref, wv_ref, t_ref, gmid_ref) = held[0:3], held[3:6], held[6:11]
        m_got, o_got = take(3), take(3)
        sendbuf, got1, got2, acc2, got3 = take(3), take(3), take(3), take(3), take(3)
        s_acc, s_got, g_ref, part, got_part, loc, send, recv = take(8)
        c = coords()
        loads = [pltpu.make_async_copy(a, b, loc.at[i]) for i, (a, b) in enumerate(zip(late, held))]
        for copy in loads:
            copy.start()
        core = lax.axis_index("tensor")
        barrier(core=True)
        sems = iter(range(256))

        def push(src, dst, device):
            n = next(sems)
            copy = remote(src, dst, send.at[n], recv.at[n], device)
            copy.start()
            return copy

        def share(acc, got, axis):
            copies = []
            for k in (1, 2, 3):
                rows = pl.ds(pl.multiple_of(((c[axis] + k) % 4) * 24, 8), 24)
                copies.append(push(acc.at[rows, :], got.at[k - 1], peer(axis, k)))
            return copies

        cos_t, sin_t = cos_ref[...], sin_ref[...]
        for qb in range(8):
            dq = dq_ref[qb].T * SCALE
            rows = slice(qb * Q_BLK, (qb + 1) * Q_BLK)
            cs, sn = cos_t[rows], sin_t[rows]
            for h in range(6):
                v = dq[h * Q_BLK : (h + 1) * Q_BLK]
                g_ref[rows, h * 128 : (h + 1) * 128] = (v * cs - swap_halves(v) * sn).astype(BF16)
        dk = jnp.concatenate([dkv_ref[0:64, :], dkv_ref[128:192, :]], axis=0)
        g_ref[:, 768:896] = (dk * cos_t - swap_halves(dk) * sin_t).astype(BF16)
        g_ref[:, 896:] = jnp.concatenate([dkv_ref[64:128, :], dkv_ref[192:256, :]], axis=0).astype(BF16)

        pending = [[], [], []]
        for p, (lo, hi, order) in enumerate(QKV_PARTS):
            slab_products(sendbuf[p], nt_ref, g_ref[:, lo:hi], order)
            for k in (1, 2, 3):
                there = (c[order[0]] + k) % 4
                pending[p].append(push(sendbuf[p].at[there], got1[p].at[k - 1], peer(order[0], k)))

        for copy in loads:
            copy.wait()
        o_copies = [share(o_acc[p], o_got[p], OUT_ORDERS[p][2]) for p in range(3)]
        m_copies = [share(m_acc[m], m_got[m], MLP_AXES[m][0]) for m in range(3)]
        total = nt(g_ref[:, 768:896], wk_ref[...]) + nt(g_ref[:, 896:], wv_ref[...])
        for h in range(6):
            total = total + nt(g_ref[:, h * 128 : (h + 1) * 128], wq_ref[h])
        part[...] = total
        swap = push(part, got_part, partner())

        inputs = t_ref[...].astype(F32)
        inv = lax.rsqrt(jnp.mean(inputs * inputs, axis=1, keepdims=True) + 1e-06)
        d_norm1 = jnp.sum(part[...] * inputs * inv, axis=0, keepdims=True)
        d_bias = jnp.sum(g_ref[...].astype(F32), axis=0, keepdims=True)
        for j in range(12):
            s_acc[0, j : j + 1, :] = d_norm1[:, j * 128 : (j + 1) * 128]
            s_acc[0, 12 + j : 13 + j, :] = dn2_ref[:, j * 128 : (j + 1) * 128]
        for j in range(8):
            v = d_bias[:, j * 128 : (j + 1) * 128]
            s_acc[0, 24 + j : 25 + j, :] = jnp.where(core == 0, v, 0.0)
            s_acc[0, 32 + j : 33 + j, :] = jnp.where(core == 1, v, 0.0)
        s_pending = []

        def send_small(stage):
            peers = [partner()] if stage == 0 else [peer(AXES[stage - 1], k) for k in (1, 2, 3)]
            for i, d in enumerate(peers):
                s_pending.append(push(s_acc.at[stage], s_got.at[stage * 3 + i], d))

        def sum_small(stage):
            for copy in s_pending:
                copy.wait()
            s_pending.clear()
            if stage == 0:
                return s_acc[0] + s_got[0]
            axis = AXES[stage - 1]
            parts = [s_acc[stage]] + [s_got[stage * 3 + k] for k in range(3)]
            total = jnp.zeros_like(parts[0])
            for w in range(4):
                term = jnp.zeros_like(total)
                for k in range(4):
                    term = jnp.where((c[axis] + 4 - k) % 4 == w, parts[k], term)
                total = total + term
            return total

        send_small(0)
        for p in range(3):
            for copy in o_copies[p]:
                copy.wait()
            rows = pl.ds(pl.multiple_of(c[OUT_ORDERS[p][2]] * 24, 8), 24)
            total = o_acc[p][rows, :]
            for k in range(3):
                total = total + o_got[p][k]
            for j in range(2):
                go_ref[p * 2 + j] = total[:, j * 128 : (j + 1) * 128]
        s_acc[1] = sum_small(0)
        send_small(1)
        swap.wait()
        g_norm = part[...] + got_part[...]
        scaled = g_norm * gain_ref[0:1, :]
        gt_ref[...] = gmid_ref[...] + (
            inv * scaled - inputs * (inv * inv * inv) * jnp.mean(scaled * inputs, axis=1, keepdims=True)
        )
        for p, (lo, hi, order) in enumerate(QKV_PARTS):
            own = c[order[0]]
            sum_first(sendbuf[p], got1[p], pending[p], own)
            pending[p] = []
            for k in (1, 2, 3):
                rows = pl.ds(pl.multiple_of(((c[order[1]] + k) % 4) * 96, 32), 96)
                pending[p].append(push(sendbuf[p].at[own, rows, :], got2[p].at[k - 1], peer(order[1], k)))
        s_acc[2] = sum_small(1)
        send_small(2)
        for m in range(3):
            for copy in m_copies[m]:
                copy.wait()
            here = c[MLP_AXES[m][0]]
            m_outs[m][:, pl.ds(col_start(here), FC)] = m_acc[m][pl.ds(pl.multiple_of(here * 24, 8), 24), :]
            for k in (1, 2, 3):
                m_outs[m][:, pl.ds(col_start((here + 4 - k) % 4), FC)] = m_got[m][k - 1]
        for p, (lo, hi, order) in enumerate(QKV_PARTS):
            for copy in pending[p]:
                copy.wait()
            own = c[order[0]]
            rows = pl.ds(pl.multiple_of(c[order[1]] * 96, 32), 96)
            total = sendbuf[p][own, rows, :].astype(F32)
            for k in range(3):
                total = total + got2[p][k].astype(F32)
            acc2[p][...] = total
            pending[p] = share(acc2[p], got3[p], order[2])
        s_acc[3] = sum_small(2)
        send_small(3)
        for p, (lo, hi, order) in enumerate(QKV_PARTS):
            for copy in pending[p]:
                copy.wait()
            rows = pl.ds(pl.multiple_of(c[order[2]] * 24, 8), 24)
            total = acc2[p][rows, :]
            for k in range(3):
                total = total + got3[p][k]
            for j in range(lo // 128, hi // 128):
                v = total[:, j * 128 - lo : (j + 1) * 128 - lo]
                if j < 6:
                    gq_ref[j] = v
                elif j == 6:
                    gk_ref[...] = v
                else:
                    gv_ref[...] = v
        s_out[...] = sum_small(3)

    cols = [hi - lo for lo, hi, _ in QKV_PARTS]
    late = (*mlp_acc, *out_acc, wq, wk, wv, tokens, g_mid)
    scratch = (
        [pltpu.VMEM(v.shape, v.dtype) for v in late]
        + [pltpu.VMEM((3, 24, FC), F32)] * 3
        + [pltpu.VMEM((3, 24, 256), F32)] * 3
        + [pltpu.VMEM((4, 384, n), BF16) for n in cols]
        + [pltpu.VMEM((3, 384, n), BF16) for n in cols]
        + [pltpu.VMEM((3, 96, n), BF16) for n in cols]
        + [pltpu.VMEM((96, n), F32) for n in cols]
        + [pltpu.VMEM((3, 24, n), F32) for n in cols]
        + [
            pltpu.VMEM((4, SMALL, 128), F32),
            pltpu.VMEM((12, SMALL, 128), F32),
            pltpu.VMEM((128, 1024), BF16),
            pltpu.VMEM((128, 1536), F32),
            pltpu.VMEM((128, 1536), F32),
            DMA((11,)),
            DMA((64,)),
            DMA((64,)),
        ]
    )
    f32 = lambda *s: jax.ShapeDtypeStruct(s, F32)
    shape = (f32(128, 1536), f32(6, 24, 128), f32(24, 128), f32(24, 128), f32(6, 24, 128), f32(SMALL, 128))
    shape = shape + (f32(24, 4480),) * 3
    vm, hbm = pl.BlockSpec(memory_space=pltpu.VMEM), pl.BlockSpec(memory_space=pl.ANY)
    return pl.pallas_call(
        body,
        out_shape=shape,
        in_specs=[hbm] * 11 + [vm] * 7,
        out_specs=(vm,) * 9,
        scratch_shapes=scratch,
        compiler_params=pltpu.CompilerParams(collective_id=3, has_side_effects=True, vmem_limit_bytes=VMEM_BYTES),
        name="finish",
    )(*late, dq_t, dkv, cos, sin, norm_t, gain, d_norm2)


def hand_out(*arrays):
    n = len(arrays)

    def body(*refs):
        ins, outs, sem = refs[:n], refs[n : 2 * n], refs[2 * n]
        copies = [pltpu.make_async_copy(a, b, sem.at[i]) for i, (a, b) in enumerate(zip(ins, outs))]
        for copy in copies:
            copy.start()
        for copy in copies:
            copy.wait()

    hbm = pl.BlockSpec(memory_space=pl.ANY)
    return pl.pallas_call(
        body,
        out_shape=tuple(jax.ShapeDtypeStruct(v.shape, v.dtype) for v in arrays),
        in_specs=[hbm] * n,
        out_specs=(hbm,) * n,
        scratch_shapes=[DMA((n,))],
        name="hand_out",
    )(*arrays)


def local(
    tokens, cotangent, lengths, norm1_gain, w_query, b_query, w_key, b_key, w_value, b_value, w_out,
    norm2_gain, w_gate, w_up, w_down,
):
    device = lax.axis_index("seq")
    core = lax.axis_index("tensor")
    wq = w_query.transpose(1, 0, 2)
    wk, wv = w_key.reshape(1536, 128), w_value.reshape(1536, 128)
    wo = w_out.reshape(768, 1536)
    gains = jnp.stack([norm1_gain, norm2_gain])

    q, kv, norm_t, cos, sin = qkv_gather(tokens, gains, wq, wk, wv, b_query, b_key, b_value, lengths)
    kv = kv.reshape(64, 256, 128)
    branch, attn, attn_low, lse = attn_forward(q, kv, wo, lengths)
    output, g_mid, branch_t, g_attn, delta, d_norm2, *shared = feed_forward(
        branch, attn, tokens, cotangent, gains, wo, w_gate, w_up, w_down
    )
    *acc, dq_t, dkv = backward(shared[:3], shared[3:], q, g_attn, kv, lse, delta, branch_t, attn_low, lengths)
    grad_tokens, grad_wq, grad_wk, grad_wv, grad_wo, sums, grad_gate, grad_up, grad_down = finish(
        acc[:3], acc[3:], dq_t, dkv, cos, sin, norm_t, wq, wk, wv, tokens, gains, g_mid, d_norm2
    )
    output, grad_tokens, grad_wq, grad_wk, grad_wv, grad_wo, grad_gate, grad_up, grad_down = hand_out(
        output, grad_tokens, grad_wq, grad_wk, grad_wv, grad_wo, grad_gate, grad_up, grad_down
    )
    sums = sums.reshape(-1)
    grad_norm1 = lax.dynamic_slice(sums, (device * 24,), (24,))
    grad_norm2 = lax.dynamic_slice(sums, (1536 + device * 24,), (24,))
    bias = lax.dynamic_slice(sums.reshape(SMALL, 128), (24 + core * 8, device * 2), (8, 2))
    return (
        output,
        grad_tokens,
        grad_norm1,
        grad_wq.transpose(1, 0, 2),
        bias[:6],
        grad_wk.reshape(24, 1, 128),
        bias[6:7],
        grad_wv.reshape(24, 1, 128),
        bias[7:8],
        grad_wo.transpose(0, 2, 1),
        grad_norm2,
        grad_gate,
        grad_up,
        grad_down.T,
    )


def solution(mesh):
    in_specs = (
        P("seq", None), P("seq", None), P(), P(), P(None, "tensor", None), P("tensor", None),
        P(None, "tensor", None), P("tensor", None), P(None, "tensor", None), P("tensor", None),
        P("tensor", None, None), P(), P(None, "tensor"), P(None, "tensor"), P("tensor", None),
    )
    out_specs = (
        P("seq", None), P("seq", None), P("seq"), P("seq", "tensor", None), P("tensor", "seq"),
        P("seq", "tensor", None), P("tensor", "seq"), P("seq", "tensor", None), P("tensor", "seq"),
        P("tensor", None, "seq"), P("seq"), P("seq", "tensor"), P("seq", "tensor"), P("tensor", "seq"),
    )
    return jax.shard_map(local, mesh=mesh, in_specs=in_specs, out_specs=out_specs, check_vma=False)
```

```python
import math

import jax
import jax.numpy as jnp
from jax import lax
from jax.experimental import pallas as pl
from jax.experimental.pallas import tpu as pltpu
from jax.sharding import PartitionSpec as P

MESH = pl.DeviceIdType.MESH
F32 = jnp.float32
BF16 = jnp.bfloat16
VMEM_BYTES = 60 * 1024 * 1024
AXES = ("z", "x", "y")
STRIDE = {"z": 16, "x": 4, "y": 1}


def coords():
    s = lax.axis_index("seq")
    return {"z": s // 16, "x": (s // 4) % 4, "y": s % 4}


def peer(axis, k):
    s = lax.axis_index("seq")
    c = coords()[axis]
    return (s + STRIDE[axis] * ((c + k) % 4 - c), lax.axis_index("tensor"))


def partner():
    return (lax.axis_index("seq"), 1 - lax.axis_index("tensor"))


def barrier(axes=AXES, core=False):
    bar = pltpu.get_barrier_semaphore()
    ids = [peer(a, k) for a in axes for k in (1, 2, 3)]
    if core:
        ids.append(partner())
    for d in ids:
        pl.semaphore_signal(bar, inc=1, device_id=d, device_id_type=MESH)
    pl.semaphore_wait(bar, len(ids))


def remote(src, dst, send, recv, device):
    return pltpu.make_async_remote_copy(
        src_ref=src, dst_ref=dst, send_sem=send, recv_sem=recv, device_id=device, device_id_type=MESH
    )


DMA = pltpu.SemaphoreType.DMA


KV_CHUNK = (
    (0, 48, ("z", "x", "y")),
    (48, 48, ("x", "y", "z")),
    (96, 32, ("y", "z", "x")),
)


def kv_rows(kb, v):
    return pl.ds(pl.multiple_of((kb // 4) * 128 + v * 64 + (kb % 4) * Q_BLK, Q_BLK), Q_BLK)


def kv_index(done, c, r0, rn):
    return tuple(slice(None) if a in done else c[a] for a in AXES) + (pl.ds(r0, rn), slice(None))


def rope_tables(len_ref):
    lane = lax.broadcasted_iota(jnp.int32, (128, 128), 1)
    pos = lax.broadcasted_iota(jnp.int32, (128, 128), 0) * 64 + lax.axis_index("seq")
    rel = (pos - doc_bounds(pos, len_ref)).astype(F32)
    inv_freq = jnp.exp(-(2.0 * (lane % 64).astype(F32) / 128) * math.log(10000.0))
    angle = rel * inv_freq
    sin = jnp.sin(angle)
    return jnp.cos(angle), jnp.where(lane < 64, -sin, sin)


def swap_halves(v):
    return pltpu.roll(v, 64, 1)


def qkv_gather(tokens, gain, wq, wk, wv, bq, bk, bv, lengths):
    def body(len_ref, t_ref, g_ref, wq_ref, wk_ref, wv_ref, bq_ref, bk_ref, bv_ref,
             q_out, out, nt_out, cos_out, sin_out, wq_buf, loc, send, recv):
        c = coords()
        load = pltpu.make_async_copy(wq_ref, wq_buf, loc)
        load.start()
        x = t_ref[...].astype(F32)
        inv = lax.rsqrt(jnp.mean(x * x, axis=1, keepdims=True) + 1e-06)
        normed = (x * inv * g_ref[0:1, :]).astype(BF16)
        cos, sin = rope_tables(len_ref)
        cos_out[...], sin_out[...] = cos, sin
        k_pre = jnp.dot(normed, wk_ref[...], preferred_element_type=F32) + bk_ref[...].astype(F32)
        v_pre = jnp.dot(normed, wv_ref[...], preferred_element_type=F32) + bv_ref[...].astype(F32)
        k_rot = (k_pre * cos + swap_halves(k_pre) * sin).astype(BF16)
        v_low = v_pre.astype(BF16)
        out[c["z"], c["x"], c["y"]] = jnp.concatenate([k_rot[:64], v_low[:64], k_rot[64:], v_low[64:]], axis=0)
        barrier()
        parts = [(r0 + 128 * chunk, rn, order) for chunk in range(2) for r0, rn, order in KV_CHUNK]
        pending = [[] for _ in parts]

        def send_stage(stage):
            for p, (r0, rn, order) in enumerate(parts):
                for copy in pending[p]:
                    copy.wait()
                pending[p] = []
                idx = kv_index(order[:stage], c, r0, rn)
                for k in (1, 2, 3):
                    n = (p * 3 + stage) * 3 + k - 1
                    copy = remote(out.at[idx], out.at[idx], send.at[n], recv.at[n], peer(order[stage], k))
                    copy.start()
                    pending[p].append(copy)

        send_stage(0)
        load.wait()
        for h in range(6):
            q = jnp.dot(normed, wq_buf[h], preferred_element_type=F32) + bq_ref[h : h + 1, :].astype(F32)
            q = (q * cos + swap_halves(q) * sin).astype(BF16)
            q_out[:, h * Q_BLK : (h + 1) * Q_BLK, :] = q.reshape(8, Q_BLK, 128)
        send_stage(1)
        nt_out[...] = normed.T
        send_stage(2)
        for copies in pending:
            for copy in copies:
                copy.wait()

    vm, sm = pl.BlockSpec(memory_space=pltpu.VMEM), pl.BlockSpec(memory_space=pltpu.SMEM)
    return pl.pallas_call(
        body,
        out_shape=(
            jax.ShapeDtypeStruct((8, 96, 128), BF16),
            jax.ShapeDtypeStruct((4, 4, 4, 256, 128), BF16),
            jax.ShapeDtypeStruct((1536, 128), BF16),
            jax.ShapeDtypeStruct((128, 128), F32),
            jax.ShapeDtypeStruct((128, 128), F32),
        ),
        in_specs=[sm, vm, vm, pl.BlockSpec(memory_space=pl.ANY)] + [vm] * 5,
        out_specs=(vm,) * 5,
        scratch_shapes=[pltpu.VMEM((6, 1536, 128), BF16), DMA, DMA((54,)), DMA((54,))],
        compiler_params=pltpu.CompilerParams(collective_id=0, has_side_effects=True, vmem_limit_bytes=VMEM_BYTES),
        name="qkv_gather",
    )(lengths, tokens, gain, wq, wk, wv, bq, bk, bv)


Q_BLK = 16
BLK = Q_BLK * 64
SCALE = 1.0 / math.sqrt(128)
SCALE2 = SCALE / math.log(2.0)


def doc_bounds(pos, len_ref):
    start = jnp.zeros_like(pos)
    end = jnp.int32(0)
    for j in range(8):
        end = end + len_ref[j]
        start = jnp.where(pos >= end, end, start)
    return start


def doc_start_scalar(pos, len_ref):
    start, end = jnp.int32(0), jnp.int32(0)
    for j in range(8):
        end = end + len_ref[j]
        start = jnp.where(pos >= end, end, start)
    return start


def attn_forward(q, kv, w_out, lengths):
    def body(len_ref, q_ref, kv_hbm, wo_hbm, part_ref, out_ref, low_ref, lse_ref, kv_ref, wo_ref, loc):
        loads = [
            pltpu.make_async_copy(kv_hbm.at[:, pl.ds(0, 128), :], kv_ref.at[:, pl.ds(0, 128), :], loc.at[0]),
            pltpu.make_async_copy(kv_hbm.at[:, pl.ds(128, 128), :], kv_ref.at[:, pl.ds(128, 128), :], loc.at[1]),
            pltpu.make_async_copy(wo_hbm, wo_ref, loc.at[2]),
        ]
        for copy in loads:
            copy.start()
        dev = lax.axis_index("seq")
        col = lax.broadcasted_iota(jnp.int32, (96, BLK), 1)
        key_off = (col % Q_BLK) * 64 + col // Q_BLK
        row_off = (lax.broadcasted_iota(jnp.int32, (96, 1), 0) % Q_BLK) * 64 + dev

        def q_step(qb, _):
            q_blk = q_ref[qb]
            pos_q = row_off + qb * BLK
            start_q = doc_bounds(pos_q, len_ref)
            lo = doc_start_scalar(qb * BLK + dev, len_ref) // BLK

            def k_step(kb, carry):
                m, l, acc = carry
                k_blk = kv_ref[:, kv_rows(kb, 0), :].reshape(BLK, 128)
                v_blk = kv_ref[:, kv_rows(kb, 1), :].reshape(BLK, 128)
                s = lax.dot_general(q_blk, k_blk, (((1,), (1,)), ((), ())), preferred_element_type=F32)
                pos_k = key_off + kb * BLK
                vis = (pos_k <= pos_q) & (pos_k >= start_q)
                s = jnp.where(vis, s * SCALE2, -1e30)
                m_new = jnp.maximum(m, jnp.max(s, axis=1, keepdims=True))
                p = jnp.where(vis, jnp.exp2(s - m_new), 0.0)
                a = jnp.exp2(m - m_new)
                l = l * a + jnp.sum(p, axis=1, keepdims=True)
                acc = acc * a + jnp.dot(p.astype(BF16), v_blk, preferred_element_type=F32)
                return m_new, l, acc

            init = (jnp.full((96, 1), -1e30, F32), jnp.zeros((96, 1), F32), jnp.zeros((96, 128), F32))
            m, l, acc = lax.fori_loop(lo, qb + 1, k_step, init)
            attn = acc / l
            out_ref[qb] = attn
            low = attn.astype(BF16)
            for h in range(6):
                rows = pl.ds(pl.multiple_of(qb * Q_BLK, Q_BLK), Q_BLK)
                low_ref[rows, h * 128 : (h + 1) * 128] = low[h * Q_BLK : (h + 1) * Q_BLK]
            lse_ref[qb] = jnp.broadcast_to(m + jnp.log2(l), (96, 128)).T[0:1]
            return 0

        loads[0].wait()
        lax.fori_loop(0, 4, q_step, 0)
        loads[1].wait()
        lax.fori_loop(4, 8, q_step, 0)
        loads[2].wait()
        part_ref[...] = jnp.dot(low_ref[...], wo_ref[...], preferred_element_type=F32)

    vm = pl.BlockSpec(memory_space=pltpu.VMEM)
    return pl.pallas_call(
        body,
        out_shape=(
            jax.ShapeDtypeStruct((128, 1536), F32),
            jax.ShapeDtypeStruct((8, 96, 128), F32),
            jax.ShapeDtypeStruct((128, 768), BF16),
            jax.ShapeDtypeStruct((8, 1, 96), F32),
        ),
        in_specs=[pl.BlockSpec(memory_space=pltpu.SMEM), vm] + [pl.BlockSpec(memory_space=pl.ANY)] * 2,
        out_specs=(vm,) * 4,
        scratch_shapes=[pltpu.VMEM((64, 256, 128), BF16), pltpu.VMEM((768, 1536), BF16), DMA((3,))],
        compiler_params=pltpu.CompilerParams(vmem_limit_bytes=VMEM_BYTES),
        name="attn_forward",
    )(lengths, q, kv, w_out)


FC = 1152


def nt(a, b):
    return lax.dot_general(a, b, (((1,), (1,)), ((), ())), preferred_element_type=F32)


def mm(a, b):
    return jnp.dot(a, b, preferred_element_type=F32)


def col_start(c):
    return pl.multiple_of(jnp.minimum(c * FC, 4480 - FC), 128)


MLP_AXES = (("z", "x", "y"), ("x", "y", "z"), ("y", "z", "x"))


def in_order(v, order):
    place = {}
    rows = []
    for i in range(64):
        for n, a in enumerate(order):
            place[a] = (i // (16, 4, 1)[n]) % 4
        o = place["z"] * 16 + place["x"] * 4 + place["y"]
        rows.append(v[o * 24 : (o + 1) * 24])
    return jnp.concatenate(rows, axis=0)


def feed_forward(branch, attn, tokens, cot, gain, w_out, w_gate, w_up, w_down):
    def body(br_ref, at_ref, t_ref, c_ref, g_ref, wo_hbm, wg_hbm, wu_hbm, wd_hbm,
             out_ref, gmid_ref, bt_ref, ga_ref, delta_ref, dn_ref, x0, x1, x2, g0, g1, g2,
             wo_ref, wg, wu, wd, got_br, acc, got, mid_ref, norm_ref, nt_ref, ct_ref, act, w_sem, loc, send, recv):
        xs, gs = (x0, x1, x2), (g0, g1, g2)
        c = coords()
        turn = c["z"] + c["x"] + c["y"]
        sems = iter(range(64))

        def load(j):
            cols = pl.ds(col_start((turn + j) % 4), FC)
            b = j % 2
            copies = [
                pltpu.make_async_copy(wg_hbm.at[:, cols], wg.at[b], w_sem.at[b, 0]),
                pltpu.make_async_copy(wu_hbm.at[:, cols], wu.at[b], w_sem.at[b, 1]),
                pltpu.make_async_copy(wd_hbm.at[cols, :], wd.at[b], w_sem.at[b, 2]),
            ]
            for copy in copies:
                copy.start()
            return copies

        loads = [load(0), load(1)]
        barrier(core=True)

        def push(src, dst, device):
            n = next(sems)
            copy = remote(src, dst, send.at[n], recv.at[n], device)
            copy.start()
            return copy

        later = []
        ex = push(br_ref, got_br, partner())
        ct_ref[...] = c_ref[...].T.reshape(4, 384, 128)
        own = [pltpu.make_async_copy(ct_ref, x2.at[:, :, pl.ds(0, 128)], loc.at[3])]
        own[0].start()
        for k in (1, 2, 3):
            later.append(push(ct_ref, x2.at[:, :, pl.ds(k * 128, 128)], peer("y", k)))
        ex.wait()
        mid = t_ref[...].astype(F32) + (br_ref[...] + got_br[...])
        mid_ref[...] = mid
        inv = lax.rsqrt(jnp.mean(mid * mid, axis=1, keepdims=True) + 1e-06)
        normed = (mid * inv * g_ref[1:2, :]).astype(BF16)
        norm_ref[...] = normed
        turned = normed.astype(F32).T
        for m in range(2):
            nt_ref[m] = in_order(turned, MLP_AXES[m][1:] + MLP_AXES[m][:1]).astype(BF16).reshape(4, 384, 128)
        own.append(pltpu.make_async_copy(nt_ref.at[0], x0.at[:, :, pl.ds(0, 128)], loc.at[4]))
        own.append(pltpu.make_async_copy(nt_ref.at[1], x1.at[:, :, pl.ds(0, 128)], loc.at[5]))
        own.append(pltpu.make_async_copy(wo_hbm, wo_ref, loc.at[6]))
        for copy in own[1:]:
            copy.start()
        for k in (1, 2, 3):
            for m, w in ((0, "z"), (1, "x")):
                later.append(push(nt_ref.at[m], xs[m].at[:, :, pl.ds(k * 128, 128)], peer(w, k)))

        lane = lax.broadcasted_iota(jnp.int32, (128, FC), 1)
        for j in range(4):
            b = j % 2
            d = (turn + j) % 4
            for copy in loads[j]:
                copy.wait()
            n = norm_ref[...]
            gate = mm(n, wg[b])
            up = mm(n, wu[b])
            gh = nt(c_ref[...], wd[b])
            sig = 1.0 / (1.0 + jnp.exp(-gate))
            silu = gate * sig
            hidden = (silu * up).astype(BF16)
            g_gate = (gh * up * sig * (1.0 + gate * (1.0 - sig))).astype(BF16)
            g_up = (gh * silu).astype(BF16)
            vals = (g_gate, g_up, hidden)
            for m in range(3):
                act[m, j] = vals[m]
            twice = (lane < 128) & (d == 3)
            zero = jnp.zeros((128, FC), BF16)
            hidden, g_gate, g_up = (jnp.where(twice, zero, v) for v in (hidden, g_gate, g_up))
            add_o = mm(hidden, wd[b])
            add_g = nt(g_gate, wg[b]) + nt(g_up, wu[b])
            if j == 0:
                acc[0], acc[1] = add_o, add_g
            else:
                acc[0] += add_o
                acc[1] += add_g
            if j + 2 < 4:
                loads.append(load(j + 2))
            for m in range(3):
                w = MLP_AXES[m][0]
                k = (d + 4 - c[w]) % 4
                slot = pl.ds(pl.multiple_of(k * 128, 128), 128)

                @pl.when(k == 0)
                def _():
                    pltpu.make_async_copy(act.at[m, j], gs[m].at[pl.ds(0, 128), :], loc.at[m]).start()

                @pl.when(k != 0)
                def _():
                    remote(
                        act.at[m, j], gs[m].at[slot, :], send.at[32 + m * 4 + j], recv.at[32 + m * 4 + k], peer(w, k)
                    ).start()

        dn_ref[...] = jnp.sum(acc[1] * mid_ref[...] * inv, axis=0, keepdims=True)
        ex = [push(acc.at[1], got.at[1], partner()), push(acc.at[0], got.at[0], partner())]
        cot_f = c_ref[...].astype(F32)
        ex[0].wait()
        gn = acc[1] + got[1]
        mid = mid_ref[...]
        scaled = gn * g_ref[1:2, :]
        g_mid = cot_f + (inv * scaled - mid * (inv * inv * inv) * jnp.mean(scaled * mid, axis=1, keepdims=True))
        gmid_ref[...] = g_mid
        own[3].wait()
        branch_low = g_mid.astype(BF16)
        bt_ref[...] = branch_low.T
        g_attn = nt(branch_low, wo_ref[...]).astype(BF16)
        for h in range(6):
            ga_ref[:, h * Q_BLK : (h + 1) * Q_BLK, :] = g_attn[:, h * 128 : (h + 1) * 128].reshape(8, Q_BLK, 128)
        for qb in range(8):
            delta_ref[qb] = jnp.sum((ga_ref[qb].astype(F32) * at_ref[qb]).T, axis=0, keepdims=True)
        ex[1].wait()
        out_ref[...] = mid_ref[...] + (acc[0] + got[0])
        for copy in later + own[:3]:
            copy.wait()
        for m in range(3):
            w = MLP_AXES[m][0]
            pltpu.make_async_copy(act.at[m, 0], gs[m].at[pl.ds(0, 128), :], loc.at[m]).wait()
            for j in range(4):
                k = ((turn + j) % 4 + 4 - c[w]) % 4

                @pl.when(k != 0)
                def _():
                    slot = pl.ds(pl.multiple_of(k * 128, 128), 128)
                    remote(
                        act.at[m, j], gs[m].at[slot, :], send.at[32 + m * 4 + j], recv.at[32 + m * 4 + k], peer(w, k)
                    ).wait()

    f32 = lambda *s: jax.ShapeDtypeStruct(s, F32)
    b16 = lambda *s: jax.ShapeDtypeStruct(s, BF16)
    vm, hbm = pl.BlockSpec(memory_space=pltpu.VMEM), pl.BlockSpec(memory_space=pl.ANY)
    return pl.pallas_call(
        body,
        out_shape=(f32(128, 1536), f32(128, 1536), b16(1536, 128), b16(8, 96, 128), f32(8, 1, 96), f32(1, 1536))
        + (b16(4, 384, 512),) * 3
        + (b16(512, FC),) * 3,
        in_specs=[vm] * 5 + [hbm] * 4,
        out_specs=(vm,) * 6 + (hbm,) * 6,
        scratch_shapes=[
            pltpu.VMEM((768, 1536), BF16),
            pltpu.VMEM((2, 1536, FC), BF16),
            pltpu.VMEM((2, 1536, FC), BF16),
            pltpu.VMEM((2, FC, 1536), BF16),
            pltpu.VMEM((128, 1536), F32),
            pltpu.VMEM((2, 128, 1536), F32),
            pltpu.VMEM((2, 128, 1536), F32),
            pltpu.VMEM((128, 1536), F32),
            pltpu.VMEM((128, 1536), BF16),
            pltpu.VMEM((2, 4, 384, 128), BF16),
            pltpu.VMEM((4, 384, 128), BF16),
            pltpu.VMEM((3, 4, 128, FC), BF16),
            DMA((2, 3)),
            DMA((7,)),
            DMA((64,)),
            DMA((64,)),
        ],
        compiler_params=pltpu.CompilerParams(collective_id=4, has_side_effects=True, vmem_limit_bytes=VMEM_BYTES),
        name="feed_forward",
    )(branch, attn, tokens, cot, gain, w_out, w_gate, w_up, w_down)


OUT_ORDERS = (("z", "x", "y"), ("x", "y", "z"), ("y", "z", "x"))
QKV_PARTS = (
    (0, 256, ("z", "x", "y")),
    (256, 512, ("x", "y", "z")),
    (512, 768, ("y", "z", "x")),
    (768, 896, ("z", "x", "y")),
    (896, 1024, ("x", "y", "z")),
)
SMALL = 40


def slab_products(buf, left, rhs, order):
    def blocks(v, places):
        return jnp.concatenate([v[o * 24 : (o + 1) * 24] for o in places], axis=0)

    if order[0] == "z":
        for z in range(4):
            buf[z] = mm(left[z * 384 : (z + 1) * 384, :], rhs).astype(BF16)
    elif order[0] == "x":
        for x in range(4):
            lhs = jnp.concatenate([left[z * 384 + x * 96 : z * 384 + (x + 1) * 96, :] for z in range(4)], axis=0)
            buf[x] = blocks(mm(lhs, rhs), [z * 4 + y for y in range(4) for z in range(4)]).astype(BF16)
    else:
        for z in range(4):
            v = blocks(mm(left[z * 384 : (z + 1) * 384, :], rhs), [x * 4 + y for y in range(4) for x in range(4)])
            v = v.astype(BF16)
            for y in range(4):
                buf[y, z * 96 : (z + 1) * 96] = v[y * 96 : (y + 1) * 96]


def sum_first(buf, got, copies, own):
    for copy in copies:
        copy.wait()
    total = buf[own].astype(F32)
    for k in range(3):
        total = total + got[k][...].astype(F32)
    buf[own] = total.astype(BF16)


def backward(xs_in, gs_in, q, g, kv, lse, delta, branch_t, attn_low, lengths,
             cos, sin, norm_t, wq, wk, wv, tokens, gain, g_mid, d_norm2):
    n_late = 2

    def body(*refs):
        r = list(refs)
        take = lambda n: [r.pop(0) for _ in range(n)]
        (len_ref,), xs_hbm, gs_hbm, (kv_hbm, *w_hbm), late = take(1), take(3), take(3), take(4), take(n_late)
        q_ref, g_ref, lse_ref, delta_ref, bt_ref, a_ref, cos_ref, sin_ref, nt_ref, gain_ref, dn2_ref = take(11)
        gt_ref, gq_ref, gk_ref, gv_ref, go_ref, s_out = take(6)
        m_outs = take(3)
        xs, gs, (dkv,), (t_ref,) = take(3), take(3), take(1), take(1)
        held = (t_ref, gt_ref)
        acc2, o_acc2, (dq_ref, own_ref) = take(3), take(3), take(2)
        sendbuf, r1a, r1b, r2, got2 = take(3), take(3), take(3), take(3), take(3)
        o_buf, o_got1, o_got2 = take(1), take(3), take(3)
        kv1, kv2, kv3 = take(6), take(6), take(6)
        m_got, o_got = take(3), take(3)
        n_parts = len(QKV_PARTS)
        q_got2, q_acc2, q_got3 = (take(n_parts) for _ in range(3))
        o_buf = [xs[2].at[:, :, 0:256], xs[2].at[:, :, 256:512], o_buf[0]]
        room = ((0, 0, 256), (0, 256, 512), (1, 0, 256), (1, 256, 384), (1, 384, 512))
        q_buf = [xs[m].at[:, :, lo:hi] for m, lo, hi in room]
        room = ((0, 0, 256), (1, 0, 256), (2, 0, 256), (0, 768, 128), (1, 768, 128))
        q_got1 = [[gs[m].at[0:384, lo + k * n : lo + (k + 1) * n] for k in range(3)] for m, lo, n in room]
        s_acc, s_got, gp_ref, part, got_part = take(5)
        loc, send, recv = take(3)
        c = coords()
        loads = [pltpu.make_async_copy(a, b, loc.at[i]) for i, (a, b) in enumerate(
            ((xs_hbm[0], xs[0]), (gs_hbm[0], gs[0]), (xs_hbm[2], xs[2]), (gs_hbm[2], gs[2]),
             (xs_hbm[1], xs[1]), (gs_hbm[1], gs[1]), (kv_hbm, dkv), *zip(late, held)))]
        for copy in loads:
            copy.start()
        barrier(core=True)
        sems = iter(range(256))

        def push(src, dst, device):
            n = next(sems)
            copy = remote(src, dst, send.at[n], recv.at[n], device)
            copy.start()
            return copy

        near = lambda u: u + 1 - 2 * (u % 2)
        far = lambda u: 3 - u
        over = lambda u: (u + 2) % 4
        top, low = pl.ds(0, 192), pl.ds(192, 192)
        first, second = [[], [], []], [[], [], []]

        def neighbour(axis, u):
            return peer(axis, u + 4 - c[axis])

        def slab(m, u):
            return sendbuf[m].at[u]

        def ready(m, which):
            axis = MLP_AXES[m][1]
            u = c[axis]
            if which == "over":
                first[m].append(push(slab(m, over(u)).at[top, :], r1a[m].at[0], neighbour(axis, near(u))))
                first[m].append(push(slab(m, over(u)).at[low, :], r1b[m].at[0], neighbour(axis, far(u))))
            elif which == "near":
                first[m].append(push(slab(m, near(u)).at[top, :], r1a[m].at[1], neighbour(axis, near(u))))
            elif which == "far":
                first[m].append(push(slab(m, far(u)).at[low, :], r1b[m].at[1], neighbour(axis, far(u))))

        def second_step(m):
            axis = MLP_AXES[m][1]
            u = c[axis]
            first[m][0].wait()
            at = slab(m, far(u)).at[top, :]
            at[...] = (at[...].astype(F32) + r1a[m][0].astype(F32)).astype(BF16)
            second[m].append(push(at, r2[m].at[0], neighbour(axis, far(u))))
            first[m][1].wait()
            at = slab(m, near(u)).at[low, :]
            at[...] = (at[...].astype(F32) + r1b[m][0].astype(F32)).astype(BF16)
            second[m].append(push(at, r2[m].at[1], neighbour(axis, near(u))))

        second_axis = [[], [], []]

        def second_axis_step(m):
            axis = MLP_AXES[m][1]
            own = slab(m, c[axis])
            for copy in first[m][2:] + second[m]:
                copy.wait()
            own[top, :] = (own[top, :].astype(F32) + r1a[m][1].astype(F32) + r2[m][0].astype(F32)).astype(BF16)
            own[low, :] = (own[low, :].astype(F32) + r1b[m][1].astype(F32) + r2[m][1].astype(F32)).astype(BF16)
            axis = MLP_AXES[m][2]
            for k in (1, 2, 3):
                rows = pl.ds(pl.multiple_of(((c[axis] + k) % 4) * 96, 32), 96)
                second_axis[m].append(push(own.at[rows, :], got2[m].at[k - 1], peer(axis, k)))

        def second_axis_sum(m):
            for copy in second_axis[m]:
                copy.wait()
            rows = pl.ds(pl.multiple_of(c[MLP_AXES[m][2]] * 96, 32), 96)
            total = slab(m, c[MLP_AXES[m][1]])[rows, :].astype(F32)
            for k in range(3):
                total = total + got2[m][k].astype(F32)
            acc2[m][...] = total

        for name, place in (("over", over), ("near", near), ("far", far), ("own", lambda u: u)):
            for i, m in enumerate((0, 2, 1)):
                if name == "over":
                    loads[2 * i].wait()
                    loads[2 * i + 1].wait()
                u = place(c[MLP_AXES[m][1]])
                x = xs[m][u]
                sendbuf[m][u] = mm(x, gs[m][...]).astype(BF16)
                ready(m, name)

        o_first, o_second = [[], [], []], [[], [], []]
        def out_first(p):
            order = OUT_ORDERS[p]
            slab_products(o_buf[p], bt_ref, a_ref[:, p * 256 : (p + 1) * 256], order)
            for k in (1, 2, 3):
                there = (c[order[0]] + k) % 4
                o_first[p].append(push(o_buf[p].at[there], o_got1[p].at[k - 1], peer(order[0], k)))

        def out_second(p):
            order = OUT_ORDERS[p]
            sum_first(o_buf[p], [o_got1[p].at[k] for k in range(3)], o_first[p], c[order[0]])
            for k in (1, 2, 3):
                rows = pl.ds(pl.multiple_of(((c[order[1]] + k) % 4) * 96, 32), 96)
                o_second[p].append(push(o_buf[p].at[c[order[0]], rows, :], o_got2[p].at[k - 1], peer(order[1], k)))

        def out_sum(p):
            order = OUT_ORDERS[p]
            for copy in o_second[p]:
                copy.wait()
            rows = pl.ds(pl.multiple_of(c[order[1]] * 96, 32), 96)
            total = o_buf[p][c[order[0]], rows, :].astype(F32)
            for k in range(3):
                total = total + o_got2[p][k].astype(F32)
            o_acc2[p][...] = total

        loads[6].wait()
        dev = lax.axis_index("seq")
        row = lax.broadcasted_iota(jnp.int32, (BLK, 96), 0)
        key_off = (row % Q_BLK) * 64 + row // Q_BLK
        q_off = (lax.broadcasted_iota(jnp.int32, (1, 96), 1) % Q_BLK) * 64 + dev
        dq_ref[...] = jnp.zeros_like(dq_ref)

        def k_step(kb, _):
            k_blk = dkv[:, :, :, kv_rows(kb, 0), :].reshape(BLK, 128)
            v_blk = dkv[:, :, :, kv_rows(kb, 1), :].reshape(BLK, 128)
            k_t = k_blk.T
            pos_k = key_off + kb * BLK

            def pair(qb, carry, causal):
                dk, dv = carry
                q_blk, g_blk = q_ref[qb], g_ref[qb]
                pos_q = q_off + qb * BLK
                vis = pos_k >= doc_bounds(pos_q, len_ref)
                if causal:
                    vis = vis & (pos_k <= pos_q)
                s = nt(k_blk, q_blk)
                p = jnp.where(vis, jnp.exp2(s * SCALE2 - lse_ref[qb]), 0.0)
                gp = nt(v_blk, g_blk)
                ds = (p * (gp - delta_ref[qb])).astype(BF16)
                dq_ref[qb] += mm(k_t, ds)
                dk = dk + mm(ds, q_blk)
                dv = dv + mm(p.astype(BF16), g_blk)
                return dk, dv

            zero = jnp.zeros((BLK, 128), F32)
            carry = pair(kb, (zero, zero), True)
            dk, dv = lax.fori_loop(kb + 1, 8, lambda qb, carry: pair(qb, carry, False), carry)
            dkv[:, :, :, kv_rows(kb, 0), :] = (dk * SCALE).astype(BF16).reshape(4, 4, 4, Q_BLK, 128)
            dkv[:, :, :, kv_rows(kb, 1), :] = dv.astype(BF16).reshape(4, 4, 4, Q_BLK, 128)
            return 0

        kv_pending = [[] for _ in range(6)]

        def kv_stage(chunk, stage):
            for i, (r0, rn, order) in enumerate(KV_CHUNK):
                p, r0 = chunk * 3 + i, r0 + chunk * 128
                for copy in kv_pending[p]:
                    copy.wait()
                kv_pending[p] = []
                got = (kv1, kv2, kv3)
                if stage:
                    mine = kv_index(order[stage:], c, r0, rn)
                    own = dkv[mine].astype(F32)
                    for k in range(3):
                        own = own + got[stage - 1][p][k].astype(F32)
                    if stage == 3:
                        own_ref[pl.ds(r0, rn), :] = own
                        continue
                    dkv[mine] = own.astype(BF16)
                for k in (1, 2, 3):
                    there = (c[order[stage]] + k) % 4
                    cc = dict(c)
                    cc[order[stage]] = there
                    src = dkv.at[kv_index(order[stage + 1 :], cc, r0, rn)]
                    kv_pending[p].append(push(src, got[stage][p].at[k - 1], peer(order[stage], k)))

        def share(acc, got, axis):
            copies = []
            for k in (1, 2, 3):
                rows = pl.ds(pl.multiple_of(((c[axis] + k) % 4) * 24, 8), 24)
                copies.append(push(acc.at[rows, :], got.at[k - 1], peer(axis, k)))
            return copies

        q_copies = [[] for _ in QKV_PARTS]

        def qkv_first(p):
            lo, hi, order = QKV_PARTS[p]
            slab_products(q_buf[p], nt_ref, gp_ref[:, lo:hi], order)
            for k in (1, 2, 3):
                there = (c[order[0]] + k) % 4
                q_copies[p].append(push(q_buf[p].at[there], q_got1[p][k - 1], peer(order[0], k)))

        def qkv_second(p):
            order = QKV_PARTS[p][2]
            sum_first(q_buf[p], q_got1[p], q_copies[p], c[order[0]])
            q_copies[p] = []
            for k in (1, 2, 3):
                rows = pl.ds(pl.multiple_of(((c[order[1]] + k) % 4) * 96, 32), 96)
                q_copies[p].append(push(q_buf[p].at[c[order[0]], rows, :], q_got2[p].at[k - 1], peer(order[1], k)))

        def qkv_third(p):
            order = QKV_PARTS[p][2]
            for copy in q_copies[p]:
                copy.wait()
            rows = pl.ds(pl.multiple_of(c[order[1]] * 96, 32), 96)
            total = q_buf[p][c[order[0]], rows, :].astype(F32)
            for k in range(3):
                total = total + q_got2[p][k].astype(F32)
            q_acc2[p][...] = total
            q_copies[p] = share(q_acc2[p], q_got3[p], order[2])

        def qkv_out(p):
            lo, hi, order = QKV_PARTS[p]
            for copy in q_copies[p]:
                copy.wait()
            total = q_acc2[p][pl.ds(pl.multiple_of(c[order[2]] * 24, 8), 24), :]
            for k in range(3):
                total = total + q_got3[p][k]
            for j in range(lo // 128, hi // 128):
                v = total[:, j * 128 - lo : (j + 1) * 128 - lo]
                if j < 6:
                    gq_ref[j] = v
                elif j == 6:
                    gk_ref[...] = v
                else:
                    gv_ref[...] = v

        lax.fori_loop(4, 8, k_step, 0)
        kv_stage(1, 0)
        second_step(0)
        lax.fori_loop(0, 1, k_step, 0)
        second_step(2)
        second_step(1)
        lax.fori_loop(1, 2, k_step, 0)
        kv_stage(1, 1)
        second_axis_step(0)
        for p in range(3):
            out_first(p)
        lax.fori_loop(2, 3, k_step, 0)
        kv_stage(1, 2)
        second_axis_step(2)
        second_axis_step(1)
        lax.fori_loop(3, 4, k_step, 0)
        kv_stage(0, 0)

        cos_t, sin_t = cos_ref[...], sin_ref[...]
        for qb in range(8):
            dq = dq_ref[qb].T * SCALE
            rows = slice(qb * Q_BLK, (qb + 1) * Q_BLK)
            cs, sn = cos_t[rows], sin_t[rows]
            for h in range(6):
                v = dq[h * Q_BLK : (h + 1) * Q_BLK]
                gp_ref[rows, h * 128 : (h + 1) * 128] = (v * cs - swap_halves(v) * sn).astype(BF16)
        for p in range(3):
            qkv_first(p)
        kv_stage(0, 1)
        m_copies = [None] * 3
        for m in (0, 2, 1):
            second_axis_sum(m)
            m_copies[m] = share(acc2[m], m_got[m], MLP_AXES[m][0])
        w_ref = [sendbuf[0].at[:, :, h * 128 : (h + 1) * 128] for h in range(8)]
        w_from = [w_hbm[0].at[h] for h in range(6)] + [w_hbm[1], w_hbm[2]]
        w_loads = [pltpu.make_async_copy(w_from[h], w_ref[h], loc.at[7 + n_late + h]) for h in range(8)]
        for copy in w_loads:
            copy.start()

        def back_through(lo, hi):
            total = nt(gp_ref[:, lo * 128 : (lo + 1) * 128], w_ref[lo][...].reshape(1536, 128))
            for h in range(lo + 1, hi):
                total = total + nt(gp_ref[:, h * 128 : (h + 1) * 128], w_ref[h][...].reshape(1536, 128))
            return total

        for p in range(3):
            out_second(p)
        kv_stage(0, 2)
        for copy in loads[7:] + w_loads:
            copy.wait()
        part[...] = back_through(0, 6)
        kv_stage(1, 3)
        kv_stage(0, 3)

        dk = jnp.concatenate([own_ref[0:64, :], own_ref[128:192, :]], axis=0)
        gp_ref[:, 768:896] = (dk * cos_t - swap_halves(dk) * sin_t).astype(BF16)
        gp_ref[:, 896:] = jnp.concatenate([own_ref[64:128, :], own_ref[192:256, :]], axis=0).astype(BF16)
        qkv_first(3)
        qkv_first(4)
        part[...] += back_through(6, 8)
        swap = push(part, got_part, partner())

        inputs = t_ref[...].astype(F32)
        inv = lax.rsqrt(jnp.mean(inputs * inputs, axis=1, keepdims=True) + 1e-06)
        d_norm1 = jnp.sum(part[...] * inputs * inv, axis=0, keepdims=True)
        d_bias = jnp.sum(gp_ref[...].astype(F32), axis=0, keepdims=True)
        core = lax.axis_index("tensor")
        for j in range(12):
            s_acc[0, j : j + 1, :] = d_norm1[:, j * 128 : (j + 1) * 128]
            s_acc[0, 12 + j : 13 + j, :] = dn2_ref[:, j * 128 : (j + 1) * 128]
        for j in range(8):
            v = d_bias[:, j * 128 : (j + 1) * 128]
            s_acc[0, 24 + j : 25 + j, :] = jnp.where(core == 0, v, 0.0)
            s_acc[0, 32 + j : 33 + j, :] = jnp.where(core == 1, v, 0.0)
        s_pending = []

        def send_small(stage):
            peers = [partner()] if stage == 0 else [peer(AXES[stage - 1], k) for k in (1, 2, 3)]
            for i, d in enumerate(peers):
                s_pending.append(push(s_acc.at[stage], s_got.at[stage * 3 + i], d))

        def sum_small(stage):
            for copy in s_pending:
                copy.wait()
            s_pending.clear()
            if stage == 0:
                return s_acc[0] + s_got[0]
            axis = AXES[stage - 1]
            parts = [s_acc[stage]] + [s_got[stage * 3 + k] for k in range(3)]
            total = jnp.zeros_like(parts[0])
            for w in range(4):
                term = jnp.zeros_like(total)
                for k in range(4):
                    term = jnp.where((c[axis] + 4 - k) % 4 == w, parts[k], term)
                total = total + term
            return total

        send_small(0)
        for p in range(3):
            qkv_second(p)
        o_copies = [None] * 3
        for p in range(3):
            out_sum(p)
            o_copies[p] = share(o_acc2[p], o_got[p], OUT_ORDERS[p][2])
        s_acc[1] = sum_small(0)
        send_small(1)
        qkv_second(3)
        qkv_second(4)
        swap.wait()
        g_norm = part[...] + got_part[...]
        scaled = g_norm * gain_ref[0:1, :]
        gt_ref[...] += (
            inv * scaled - inputs * (inv * inv * inv) * jnp.mean(scaled * inputs, axis=1, keepdims=True)
        )
        for p in range(3):
            qkv_third(p)
        s_acc[2] = sum_small(1)
        send_small(2)
        qkv_third(3)
        qkv_third(4)
        for p in range(3):
            for copy in o_copies[p]:
                copy.wait()
            rows = pl.ds(pl.multiple_of(c[OUT_ORDERS[p][2]] * 24, 8), 24)
            total = o_acc2[p][rows, :]
            for k in range(3):
                total = total + o_got[p][k]
            for j in range(2):
                go_ref[p * 2 + j] = total[:, j * 128 : (j + 1) * 128]
        for m in range(3):
            for copy in m_copies[m]:
                copy.wait()
            here = c[MLP_AXES[m][0]]
            m_outs[m][:, pl.ds(col_start(here), FC)] = acc2[m][pl.ds(pl.multiple_of(here * 24, 8), 24), :]
            for k in (1, 2, 3):
                m_outs[m][:, pl.ds(col_start((here + 4 - k) % 4), FC)] = m_got[m][k - 1]
        s_acc[3] = sum_small(2)
        send_small(3)
        for p in range(n_parts):
            qkv_out(p)
        s_out[...] = sum_small(3)

    rows = [rn for _, rn, _ in KV_CHUNK] * 2
    cols = [hi - lo for lo, hi, _ in QKV_PARTS]
    late = (tokens, g_mid)
    scratch = (
        [pltpu.VMEM((4, 384, 512), BF16)] * 3
        + [pltpu.VMEM((512, FC), BF16)] * 3
        + [pltpu.VMEM((4, 4, 4, 256, 128), BF16)]
        + [pltpu.VMEM((128, 1536), BF16)]
        + [pltpu.VMEM((96, FC), F32)] * 3
        + [pltpu.VMEM((96, 256), F32)] * 3
        + [pltpu.VMEM((8, 128, 96), F32), pltpu.VMEM((256, 128), F32)]
        + [pltpu.VMEM((4, 384, FC), BF16)] * 3
        + [pltpu.VMEM((2, 192, FC), BF16)] * 3
        + [pltpu.VMEM((2, 192, FC), BF16)] * 3
        + [pltpu.VMEM((2, 192, FC), BF16)] * 3
        + [pltpu.VMEM((3, 96, FC), BF16)] * 3
        + [pltpu.VMEM((4, 384, 256), BF16)]
        + [pltpu.VMEM((3, 384, 256), BF16)] * 3
        + [pltpu.VMEM((3, 96, 256), BF16)] * 3
        + [pltpu.VMEM((3, 4, 4, r, 128), BF16) for r in rows]
        + [pltpu.VMEM((3, 4, r, 128), BF16) for r in rows]
        + [pltpu.VMEM((3, r, 128), BF16) for r in rows]
        + [pltpu.VMEM((3, 24, FC), F32)] * 3
        + [pltpu.VMEM((3, 24, 256), F32)] * 3
        + [pltpu.VMEM((3, 96, n), BF16) for n in cols]
        + [pltpu.VMEM((96, n), F32) for n in cols]
        + [pltpu.VMEM((3, 24, n), F32) for n in cols]
        + [
            pltpu.VMEM((4, SMALL, 128), F32),
            pltpu.VMEM((12, SMALL, 128), F32),
            pltpu.VMEM((128, 1024), BF16),
            pltpu.VMEM((128, 1536), F32),
            pltpu.VMEM((128, 1536), F32),
            DMA((7 + n_late + 8,)),
            DMA((192,)),
            DMA((192,)),
        ]
    )
    vm, sm, hbm = (pl.BlockSpec(memory_space=m) for m in (pltpu.VMEM, pltpu.SMEM, pl.ANY))
    f32 = lambda *s: jax.ShapeDtypeStruct(s, F32)
    shape = (f32(128, 1536), f32(6, 24, 128), f32(24, 128), f32(24, 128), f32(6, 24, 128), f32(SMALL, 128))
    shape = shape + (f32(24, 4480),) * 3
    return pl.pallas_call(
        body,
        out_shape=shape,
        in_specs=[sm] + [hbm] * (10 + n_late) + [vm] * 11,
        out_specs=(vm,) * 9,
        scratch_shapes=scratch,
        compiler_params=pltpu.CompilerParams(collective_id=2, has_side_effects=True, vmem_limit_bytes=VMEM_BYTES),
        name="backward",
    )(lengths, *xs_in, *gs_in, kv, wq.reshape(6, 4, 384, 128), wk.reshape(4, 384, 128), wv.reshape(4, 384, 128), *late, q, g, lse, delta, branch_t, attn_low, cos, sin, norm_t, gain, d_norm2)


def hand_out(*arrays):
    n = len(arrays)

    def body(*refs):
        ins, outs, held, sem = refs[:n], refs[n : 2 * n], refs[2 * n : 3 * n], refs[3 * n]
        to = [pltpu.make_async_copy(a, b, sem.at[i]) for i, (a, b) in enumerate(zip(ins, held))]
        back = [pltpu.make_async_copy(a, b, sem.at[n + i]) for i, (a, b) in enumerate(zip(held, outs))]
        for copy in to:
            copy.start()
        for i in range(n):
            to[i].wait()
            back[i].start()
        for copy in back:
            copy.wait()

    hbm = pl.BlockSpec(memory_space=pl.ANY)
    return pl.pallas_call(
        body,
        out_shape=tuple(jax.ShapeDtypeStruct(v.shape, v.dtype) for v in arrays),
        in_specs=[hbm] * n,
        out_specs=(hbm,) * n,
        scratch_shapes=[pltpu.VMEM(v.shape, v.dtype) for v in arrays] + [DMA((2 * n,))],
        compiler_params=pltpu.CompilerParams(vmem_limit_bytes=VMEM_BYTES),
        name="hand_out",
    )(*arrays)


def local(
    tokens, cotangent, lengths, norm1_gain, w_query, b_query, w_key, b_key, w_value, b_value, w_out,
    norm2_gain, w_gate, w_up, w_down,
):
    device = lax.axis_index("seq")
    core = lax.axis_index("tensor")
    wq = w_query.transpose(1, 0, 2)
    wk, wv = w_key.reshape(1536, 128), w_value.reshape(1536, 128)
    wo = w_out.reshape(768, 1536)
    gains = jnp.stack([norm1_gain, norm2_gain])

    q, kv, norm_t, cos, sin = qkv_gather(tokens, gains, wq, wk, wv, b_query, b_key, b_value, lengths)
    kv = kv.reshape(64, 256, 128)
    branch, attn, attn_low, lse = attn_forward(q, kv, wo, lengths)
    output, g_mid, branch_t, g_attn, delta, d_norm2, *shared = feed_forward(
        branch, attn, tokens, cotangent, gains, wo, w_gate, w_up, w_down
    )
    grad_tokens, grad_wq, grad_wk, grad_wv, grad_wo, sums, grad_gate, grad_up, grad_down = backward(
        shared[:3], shared[3:], q, g_attn, kv.reshape(4, 4, 4, 256, 128), lse, delta, branch_t, attn_low, lengths,
        cos, sin, norm_t, wq, wk, wv, tokens, gains, g_mid, d_norm2,
    )
    output, grad_tokens, grad_wq, grad_wk, grad_wv, grad_wo, grad_gate, grad_up, grad_down = hand_out(
        output, grad_tokens, grad_wq, grad_wk, grad_wv, grad_wo, grad_gate, grad_up, grad_down
    )
    sums = sums.reshape(-1)
    grad_norm1 = lax.dynamic_slice(sums, (device * 24,), (24,))
    grad_norm2 = lax.dynamic_slice(sums, (1536 + device * 24,), (24,))
    bias = lax.dynamic_slice(sums.reshape(SMALL, 128), (24 + core * 8, device * 2), (8, 2))
    return (
        output,
        grad_tokens,
        grad_norm1,
        grad_wq.transpose(1, 0, 2),
        bias[:6],
        grad_wk.reshape(24, 1, 128),
        bias[6:7],
        grad_wv.reshape(24, 1, 128),
        bias[7:8],
        grad_wo.transpose(0, 2, 1),
        grad_norm2,
        grad_gate,
        grad_up,
        grad_down.T,
    )


def solution(mesh):
    in_specs = (
        P("seq", None), P("seq", None), P(), P(), P(None, "tensor", None), P("tensor", None),
        P(None, "tensor", None), P("tensor", None), P(None, "tensor", None), P("tensor", None),
        P("tensor", None, None), P(), P(None, "tensor"), P(None, "tensor"), P("tensor", None),
    )
    out_specs = (
        P("seq", None), P("seq", None), P("seq"), P("seq", "tensor", None), P("tensor", "seq"),
        P("seq", "tensor", None), P("tensor", "seq"), P("seq", "tensor", None), P("tensor", "seq"),
        P("tensor", None, "seq"), P("seq"), P("seq", "tensor"), P("seq", "tensor"), P("tensor", "seq"),
    )
    return jax.shard_map(local, mesh=mesh, in_specs=in_specs, out_specs=out_specs, check_vma=False)
```

```python
import math

import jax
import jax.numpy as jnp
from jax import lax
from jax.experimental import pallas as pl
from jax.experimental.pallas import tpu as pltpu
from jax.sharding import PartitionSpec as P

MESH = pl.DeviceIdType.MESH
F32 = jnp.float32
BF16 = jnp.bfloat16
VMEM_BYTES = 60 * 1024 * 1024
AXES = ("z", "x", "y")
STRIDE = {"z": 16, "x": 4, "y": 1}


def coords():
    s = lax.axis_index("seq")
    return {"z": s // 16, "x": (s // 4) % 4, "y": s % 4}


def peer(axis, k):
    s = lax.axis_index("seq")
    c = coords()[axis]
    return (s + STRIDE[axis] * ((c + k) % 4 - c), lax.axis_index("tensor"))


def partner():
    return (lax.axis_index("seq"), 1 - lax.axis_index("tensor"))


def barrier(axes=AXES, core=False):
    bar = pltpu.get_barrier_semaphore()
    ids = [peer(a, k) for a in axes for k in (1, 2, 3)]
    if core:
        ids.append(partner())
    for d in ids:
        pl.semaphore_signal(bar, inc=1, device_id=d, device_id_type=MESH)
    pl.semaphore_wait(bar, len(ids))


def remote(src, dst, send, recv, device):
    return pltpu.make_async_remote_copy(
        src_ref=src, dst_ref=dst, send_sem=send, recv_sem=recv, device_id=device, device_id_type=MESH
    )


DMA = pltpu.SemaphoreType.DMA


KV_CHUNK = (
    (0, 48, ("z", "x", "y")),
    (48, 48, ("x", "y", "z")),
    (96, 32, ("y", "z", "x")),
)


def kv_rows(kb, v):
    return pl.ds(pl.multiple_of((kb // 4) * 128 + v * 64 + (kb % 4) * Q_BLK, Q_BLK), Q_BLK)


def kv_index(done, c, r0, rn):
    return tuple(slice(None) if a in done else c[a] for a in AXES) + (pl.ds(r0, rn), slice(None))


def rope_tables(len_ref):
    lane = lax.broadcasted_iota(jnp.int32, (128, 128), 1)
    pos = lax.broadcasted_iota(jnp.int32, (128, 128), 0) * 64 + lax.axis_index("seq")
    rel = (pos - doc_bounds(pos, len_ref)).astype(F32)
    inv_freq = jnp.exp(-(2.0 * (lane % 64).astype(F32) / 128) * math.log(10000.0))
    angle = rel * inv_freq
    sin = jnp.sin(angle)
    return jnp.cos(angle), jnp.where(lane < 64, -sin, sin)


def swap_halves(v):
    return pltpu.roll(v, 64, 1)


Q_BLK = 16
BLK = Q_BLK * 64
SCALE = 1.0 / math.sqrt(128)
SCALE2 = SCALE / math.log(2.0)


def doc_bounds(pos, len_ref):
    start = jnp.zeros_like(pos)
    end = jnp.int32(0)
    for j in range(8):
        end = end + len_ref[j]
        start = jnp.where(pos >= end, end, start)
    return start


FC = 1152


def nt(a, b):
    return lax.dot_general(a, b, (((1,), (1,)), ((), ())), preferred_element_type=F32)


def mm(a, b):
    return jnp.dot(a, b, preferred_element_type=F32)


def col_start(c):
    return pl.multiple_of(jnp.minimum(c * FC, 4480 - FC), 128)


MLP_AXES = (("z", "x", "y"), ("x", "y", "z"), ("y", "z", "x"))


def in_order(v, order):
    place = {}
    rows = []
    for i in range(64):
        for n, a in enumerate(order):
            place[a] = (i // (16, 4, 1)[n]) % 4
        o = place["z"] * 16 + place["x"] * 4 + place["y"]
        rows.append(v[o * 24 : (o + 1) * 24])
    return jnp.concatenate(rows, axis=0)


def forward(tokens, cot, lengths, gains, wq, wk, wv, bq, bk, bv, w_out, w_gate, w_up, w_down):
    def body(len_ref, t_ref, c_ref, g_ref, wk_ref, wv_ref, bq_ref, bk_ref, bv_ref, wq_hbm, wo_hbm, wg_hbm, wu_hbm, wd_hbm,
             out_ref, gmid_ref, bt_ref, ga_ref, delta_ref, dn_ref, q_ref, nt1_ref, cos_out, sin_out, low_ref, lse_ref,
             x0, x1, x2, g0, g1, g2, kv_hbm,
             kv, wq_ref, at_ref, m_ref, l_ref, acc_ref, br_ref,
             wo_ref, wg, wu, wd, got_br, acc, got, mid_ref, norm_ref, nt_ref, ct_ref, act, w_sem, loc, send, recv):
        xs, gs = (x0, x1, x2), (g0, g1, g2)
        c = coords()
        dev = lax.axis_index("seq")
        turn = c["z"] + c["x"] + c["y"]
        sems = iter(range(128))

        def load(j):
            cols = pl.ds(col_start((turn + j) % 4), FC)
            b = j % 2
            copies = [
                pltpu.make_async_copy(wg_hbm.at[:, cols], wg.at[b], w_sem.at[b, 0]),
                pltpu.make_async_copy(wu_hbm.at[:, cols], wu.at[b], w_sem.at[b, 1]),
                pltpu.make_async_copy(wd_hbm.at[cols, :], wd.at[b], w_sem.at[b, 2]),
            ]
            for copy in copies:
                copy.start()
            return copies

        def push(src, dst, device):
            n = next(sems)
            copy = remote(src, dst, send.at[n], recv.at[n], device)
            copy.start()
            return copy

        def keep(src, dst, n):
            copy = pltpu.make_async_copy(src, dst, loc.at[n])
            copy.start()
            return copy

        wq_load = keep(wq_hbm, wq_ref, 6)
        wo_load = keep(wo_hbm, wo_ref, 7)

        x = t_ref[...].astype(F32)
        inv = lax.rsqrt(jnp.mean(x * x, axis=1, keepdims=True) + 1e-06)
        normed = (x * inv * g_ref[0:1, :]).astype(BF16)
        cos, sin = rope_tables(len_ref)
        cos_out[...], sin_out[...] = cos, sin
        k_pre = mm(normed, wk_ref[...]) + bk_ref[...].astype(F32)
        v_low = (mm(normed, wv_ref[...]) + bv_ref[...].astype(F32)).astype(BF16)
        k_rot = (k_pre * cos + swap_halves(k_pre) * sin).astype(BF16)
        kv[c["z"], c["x"], c["y"]] = jnp.concatenate([k_rot[:64], v_low[:64], k_rot[64:], v_low[64:]], axis=0)
        barrier(core=True)
        kv_pending = [[] for _ in range(6)]

        def kv_wait(chunk):
            for p in range(chunk * 3, chunk * 3 + 3):
                for copy in kv_pending[p]:
                    copy.wait()
                kv_pending[p] = []

        def kv_stage(chunk, stage):
            for i, (r0, rn, order) in enumerate(KV_CHUNK):
                p, r0 = chunk * 3 + i, r0 + chunk * 128
                for copy in kv_pending[p]:
                    copy.wait()
                idx = kv_index(order[:stage], c, r0, rn)
                kv_pending[p] = [push(kv.at[idx], kv.at[idx], peer(order[stage], k)) for k in (1, 2, 3)]

        kv_stage(0, 0)
        kv_stage(1, 0)
        wq_load.wait()
        for h in range(6):
            q = mm(normed, wq_ref[h]) + bq_ref[h : h + 1, :].astype(F32)
            q = (q * cos + swap_halves(q) * sin).astype(BF16)
            q_ref[:, h * Q_BLK : (h + 1) * Q_BLK, :] = q.reshape(8, Q_BLK, 128)
        kv_stage(0, 1)
        kv_stage(1, 1)
        nt1_ref[...] = normed.T
        kv_stage(0, 2)
        loads = [load(0), load(1)]
        ct_ref[...] = c_ref[...].T.reshape(4, 384, 128)
        own = [keep(ct_ref, x2.at[:, :, pl.ds(0, 128)], 3)]
        kv_wait(0)
        kv_stage(1, 2)
        later = [push(ct_ref, x2.at[:, :, pl.ds(k * 128, 128)], peer("y", k)) for k in (1, 2, 3)]

        row_off = (lax.broadcasted_iota(jnp.int32, (96, 1), 0) % Q_BLK) * 64 + dev
        col = lax.broadcasted_iota(jnp.int32, (96, BLK), 1)
        key_off = (col % Q_BLK) * 64 + col // Q_BLK

        def attend(qb, lo, hi, carry, diagonal):
            q_blk = q_ref[qb]
            pos_q = row_off + qb * BLK
            start_q = doc_bounds(pos_q, len_ref)

            def block(kb, carry, causal):
                m, l, acc = carry
                k_blk = kv[:, :, :, kv_rows(kb, 0), :].reshape(BLK, 128)
                v_blk = kv[:, :, :, kv_rows(kb, 1), :].reshape(BLK, 128)
                pos_k = key_off + kb * BLK
                vis = pos_k >= start_q
                if causal:
                    vis = vis & (pos_k <= pos_q)
                s = jnp.where(vis, nt(q_blk, k_blk) * SCALE2, -1e30)
                m_new = jnp.maximum(m, jnp.max(s, axis=1, keepdims=True))
                p = jnp.exp2(s - m_new)
                a = jnp.exp2(m - m_new)
                return m_new, l * a + jnp.sum(p, axis=1, keepdims=True), acc * a + mm(p.astype(BF16), v_blk)

            carry = lax.fori_loop(lo, hi, lambda kb, carry: block(kb, carry, False), carry)
            return block(qb, carry, True) if diagonal else carry

        def attend_end(qb, carry):
            m, l, acc = carry
            attn = acc / l
            at_ref[qb] = attn
            low = attn.astype(BF16)
            for h in range(6):
                rows = pl.ds(pl.multiple_of(qb * Q_BLK, Q_BLK), Q_BLK)
                low_ref[rows, h * 128 : (h + 1) * 128] = low[h * Q_BLK : (h + 1) * Q_BLK]
            lse_ref[qb] = jnp.broadcast_to(m + jnp.log2(l), (96, 128)).T[0:1]

        init = (jnp.full((96, 1), -1e30, F32), jnp.zeros((96, 1), F32), jnp.zeros((96, 128), F32))

        def upper(qb, _):
            m_ref[qb - 4], l_ref[qb - 4], acc_ref[qb - 4] = attend(qb, 0, 4, init, False)
            return 0

        def whole(qb, _):
            attend_end(qb, attend(qb, 0, qb, init, True))
            return 0

        def rest(qb, _):
            attend_end(qb, attend(qb, 4, qb, (m_ref[qb - 4], l_ref[qb - 4], acc_ref[qb - 4]), True))
            return 0

        out_kv = [keep(kv.at[:, :, :, pl.ds(0, 128), :], kv_hbm.at[:, :, :, pl.ds(0, 128), :], 8)]
        lax.fori_loop(0, 4, whole, 0)
        lax.fori_loop(4, 8, upper, 0)
        kv_wait(1)
        out_kv.append(keep(kv.at[:, :, :, pl.ds(128, 128), :], kv_hbm.at[:, :, :, pl.ds(128, 128), :], 9))
        lax.fori_loop(4, 8, rest, 0)
        wo_load.wait()
        ex = []
        for half in range(2):
            cols = slice(half * 768, (half + 1) * 768)
            br_ref[half] = mm(low_ref[...], wo_ref[:, cols])
            ex.append(push(br_ref.at[half], got_br.at[half], partner()))
        for copy in ex:
            copy.wait()
        mid = t_ref[...].astype(F32) + jnp.concatenate([br_ref[h] + got_br[h] for h in range(2)], axis=1)
        mid_ref[...] = mid
        inv = lax.rsqrt(jnp.mean(mid * mid, axis=1, keepdims=True) + 1e-06)
        normed = (mid * inv * g_ref[1:2, :]).astype(BF16)
        norm_ref[...] = normed
        turned = normed.astype(F32).T
        for m in range(2):
            nt_ref[m] = in_order(turned, MLP_AXES[m][1:] + MLP_AXES[m][:1]).astype(BF16).reshape(4, 384, 128)
        own.append(keep(nt_ref.at[0], x0.at[:, :, pl.ds(0, 128)], 4))
        own.append(keep(nt_ref.at[1], x1.at[:, :, pl.ds(0, 128)], 5))
        for k in (1, 2, 3):
            for m, w in ((0, "z"), (1, "x")):
                later.append(push(nt_ref.at[m], xs[m].at[:, :, pl.ds(k * 128, 128)], peer(w, k)))

        lane = lax.broadcasted_iota(jnp.int32, (128, FC), 1)
        for j in range(4):
            b = j % 2
            d = (turn + j) % 4
            for copy in loads[j]:
                copy.wait()
            n = norm_ref[...]
            gate = mm(n, wg[b])
            up = mm(n, wu[b])
            gh = nt(c_ref[...], wd[b])
            sig = 1.0 / (1.0 + jnp.exp(-gate))
            silu = gate * sig
            hidden = (silu * up).astype(BF16)
            g_gate = (gh * up * sig * (1.0 + gate * (1.0 - sig))).astype(BF16)
            g_up = (gh * silu).astype(BF16)
            vals = (g_gate, g_up, hidden)
            for m in range(3):
                act[m, j] = vals[m]
            twice = (lane < 128) & (d == 3)
            zero = jnp.zeros((128, FC), BF16)
            hidden, g_gate, g_up = (jnp.where(twice, zero, v) for v in (hidden, g_gate, g_up))
            add_g = nt(g_gate, wg[b]) + nt(g_up, wu[b])
            acc[1] = add_g if j == 0 else acc[1] + add_g
            if j == 3:
                ex = [push(acc.at[1], got.at[1], partner())]
            add_o = mm(hidden, wd[b])
            acc[0] = add_o if j == 0 else acc[0] + add_o
            if j + 2 < 4:
                loads.append(load(j + 2))
            for m in range(3):
                w = MLP_AXES[m][0]
                k = (d + 4 - c[w]) % 4
                slot = pl.ds(pl.multiple_of(k * 128, 128), 128)

                @pl.when(k == 0)
                def _():
                    pltpu.make_async_copy(act.at[m, j], gs[m].at[pl.ds(0, 128), :], loc.at[m]).start()

                @pl.when(k != 0)
                def _():
                    remote(
                        act.at[m, j], gs[m].at[slot, :], send.at[96 + m * 4 + j], recv.at[96 + m * 4 + k], peer(w, k)
                    ).start()

        ex.append(push(acc.at[0], got.at[0], partner()))
        dn_ref[...] = jnp.sum(acc[1] * mid_ref[...] * inv, axis=0, keepdims=True)
        cot_f = c_ref[...].astype(F32)
        ex[0].wait()
        gn = acc[1] + got[1]
        mid = mid_ref[...]
        scaled = gn * g_ref[1:2, :]
        g_mid = cot_f + (inv * scaled - mid * (inv * inv * inv) * jnp.mean(scaled * mid, axis=1, keepdims=True))
        gmid_ref[...] = g_mid
        branch_low = g_mid.astype(BF16)
        bt_ref[...] = branch_low.T
        g_attn = nt(branch_low, wo_ref[...]).astype(BF16)
        for h in range(6):
            ga_ref[:, h * Q_BLK : (h + 1) * Q_BLK, :] = g_attn[:, h * 128 : (h + 1) * 128].reshape(8, Q_BLK, 128)
        for qb in range(8):
            delta_ref[qb] = jnp.sum((ga_ref[qb].astype(F32) * at_ref[qb]).T, axis=0, keepdims=True)
        ex[1].wait()
        out_ref[...] = mid_ref[...] + (acc[0] + got[0])
        for copy in later + own + out_kv:
            copy.wait()
        for m in range(3):
            w = MLP_AXES[m][0]
            pltpu.make_async_copy(act.at[m, 0], gs[m].at[pl.ds(0, 128), :], loc.at[m]).wait()
            for j in range(4):
                k = ((turn + j) % 4 + 4 - c[w]) % 4

                @pl.when(k != 0)
                def _():
                    slot = pl.ds(pl.multiple_of(k * 128, 128), 128)
                    remote(
                        act.at[m, j], gs[m].at[slot, :], send.at[96 + m * 4 + j], recv.at[96 + m * 4 + k], peer(w, k)
                    ).wait()

    f32 = lambda *s: jax.ShapeDtypeStruct(s, F32)
    b16 = lambda *s: jax.ShapeDtypeStruct(s, BF16)
    vm, sm, hbm = (pl.BlockSpec(memory_space=m) for m in (pltpu.VMEM, pltpu.SMEM, pl.ANY))
    held = [(6, 1536, 128, BF16), (8, 96, 128, F32), (4, 96, 1, F32), (4, 96, 1, F32), (4, 96, 128, F32)]
    held += [(2, 128, 768, F32), (768, 1536, BF16), (2, 1536, FC, BF16), (2, 1536, FC, BF16), (2, FC, 1536, BF16)]
    held += [(2, 128, 768, F32), (2, 128, 1536, F32), (2, 128, 1536, F32), (128, 1536, F32), (128, 1536, BF16)]
    held += [(2, 4, 384, 128, BF16), (4, 384, 128, BF16), (3, 4, 128, FC, BF16)]
    return pl.pallas_call(
        body,
        out_shape=(f32(128, 1536), f32(128, 1536), b16(1536, 128), b16(8, 96, 128), f32(8, 1, 96), f32(1, 1536))
        + (b16(8, 96, 128), b16(1536, 128), f32(128, 128), f32(128, 128), b16(128, 768), f32(8, 1, 96))
        + (b16(4, 384, 512),) * 3
        + (b16(512, FC),) * 3
        + (b16(4, 4, 4, 256, 128),),
        in_specs=[sm] + [vm] * 8 + [hbm] * 5,
        out_specs=(vm,) * 12 + (hbm,) * 7,
        scratch_shapes=[pltpu.VMEM((4, 4, 4, 256, 128), BF16)]
        + [pltpu.VMEM(v[:-1], v[-1]) for v in held]
        + [DMA((2, 3)), DMA((10,)), DMA((112,)), DMA((112,))],
        compiler_params=pltpu.CompilerParams(collective_id=4, has_side_effects=True, vmem_limit_bytes=VMEM_BYTES),
        name="forward",
    )(lengths, tokens, cot, gains, wk, wv, bq, bk, bv, wq, w_out, w_gate, w_up, w_down)


OUT_ORDERS = (("z", "x", "y"), ("x", "y", "z"), ("y", "z", "x"))
QKV_PARTS = (
    (0, 256, ("z", "x", "y")),
    (256, 512, ("x", "y", "z")),
    (512, 768, ("y", "z", "x")),
    (768, 896, ("z", "x", "y")),
    (896, 1024, ("x", "y", "z")),
)
SMALL = 40


def slab_products(buf, left, rhs, order):
    def blocks(v, places):
        return jnp.concatenate([v[o * 24 : (o + 1) * 24] for o in places], axis=0)

    if order[0] == "z":
        for z in range(4):
            buf[z] = mm(left[z * 384 : (z + 1) * 384, :], rhs).astype(BF16)
    elif order[0] == "x":
        for x in range(4):
            lhs = jnp.concatenate([left[z * 384 + x * 96 : z * 384 + (x + 1) * 96, :] for z in range(4)], axis=0)
            buf[x] = blocks(mm(lhs, rhs), [z * 4 + y for y in range(4) for z in range(4)]).astype(BF16)
    else:
        for z in range(4):
            v = blocks(mm(left[z * 384 : (z + 1) * 384, :], rhs), [x * 4 + y for y in range(4) for x in range(4)])
            v = v.astype(BF16)
            for y in range(4):
                buf[y, z * 96 : (z + 1) * 96] = v[y * 96 : (y + 1) * 96]


def sum_first(buf, got, copies, own):
    for copy in copies:
        copy.wait()
    total = buf[own].astype(F32)
    for k in range(3):
        total = total + got[k][...].astype(F32)
    buf[own] = total.astype(BF16)


def backward(xs_in, gs_in, q, g, kv, lse, delta, branch_t, attn_low, lengths,
             cos, sin, norm_t, wq, wk, wv, tokens, gain, g_mid, d_norm2):
    n_late = 2

    def body(*refs):
        r = list(refs)
        take = lambda n: [r.pop(0) for _ in range(n)]
        (len_ref,), xs_hbm, gs_hbm, (kv_hbm, *w_hbm), late = take(1), take(3), take(3), take(4), take(n_late)
        q_ref, g_ref, lse_ref, delta_ref, bt_ref, a_ref, cos_ref, sin_ref, nt_ref, gain_ref, dn2_ref = take(11)
        gt_ref, gq_ref, gk_ref, gv_ref, go_ref, s_out = take(6)
        m_outs = take(3)
        xs, gs, (dkv,), (t_ref,) = take(3), take(3), take(1), take(1)
        held = (t_ref, gt_ref)
        acc2, o_acc2, (dq_ref, own_ref) = take(3), take(3), take(2)
        sendbuf, r1a, r1b, r2, got2 = take(3), take(3), take(3), take(3), take(3)
        o_buf, o_got1, o_got2 = take(1), take(3), take(3)
        kv1, kv2, kv3 = take(6), take(6), take(6)
        m_got, o_got = take(3), take(3)
        n_parts = len(QKV_PARTS)
        q_got2, q_acc2, q_got3 = (take(n_parts) for _ in range(3))
        o_buf = [xs[2].at[:, :, 0:256], xs[2].at[:, :, 256:512], o_buf[0]]
        room = ((0, 0, 256), (0, 256, 512), (1, 0, 256), (1, 256, 384), (1, 384, 512))
        q_buf = [xs[m].at[:, :, lo:hi] for m, lo, hi in room]
        room = ((0, 0, 256), (1, 0, 256), (2, 0, 256), (0, 768, 128), (1, 768, 128))
        q_got1 = [[gs[m].at[0:384, lo + k * n : lo + (k + 1) * n] for k in range(3)] for m, lo, n in room]
        s_acc, s_got, gp_ref, part, got_part = take(5)
        loc, send, recv = take(3)
        c = coords()
        loads = [pltpu.make_async_copy(a, b, loc.at[i]) for i, (a, b) in enumerate(
            ((xs_hbm[0], xs[0]), (gs_hbm[0], gs[0]), (xs_hbm[2], xs[2]), (gs_hbm[2], gs[2]),
             (xs_hbm[1], xs[1]), (gs_hbm[1], gs[1]), (kv_hbm, dkv), *zip(late, held)))]
        for copy in loads:
            copy.start()
        barrier(core=True)
        sems = iter(range(256))

        def push(src, dst, device):
            n = next(sems)
            copy = remote(src, dst, send.at[n], recv.at[n], device)
            copy.start()
            return copy

        near = lambda u: u + 1 - 2 * (u % 2)
        far = lambda u: 3 - u
        over = lambda u: (u + 2) % 4
        top, low = pl.ds(0, 192), pl.ds(192, 192)
        first, second = [[], [], []], [[], [], []]

        def neighbour(axis, u):
            return peer(axis, u + 4 - c[axis])

        def slab(m, u):
            return sendbuf[m].at[u]

        def ready(m, which):
            axis = MLP_AXES[m][1]
            u = c[axis]
            if which == "over":
                first[m].append(push(slab(m, over(u)).at[top, :], r1a[m].at[0], neighbour(axis, near(u))))
                first[m].append(push(slab(m, over(u)).at[low, :], r1b[m].at[0], neighbour(axis, far(u))))
            elif which == "near":
                first[m].append(push(slab(m, near(u)).at[top, :], r1a[m].at[1], neighbour(axis, near(u))))
            elif which == "far":
                first[m].append(push(slab(m, far(u)).at[low, :], r1b[m].at[1], neighbour(axis, far(u))))

        def second_step(m):
            axis = MLP_AXES[m][1]
            u = c[axis]
            first[m][0].wait()
            at = slab(m, far(u)).at[top, :]
            at[...] = (at[...].astype(F32) + r1a[m][0].astype(F32)).astype(BF16)
            second[m].append(push(at, r2[m].at[0], neighbour(axis, far(u))))
            first[m][1].wait()
            at = slab(m, near(u)).at[low, :]
            at[...] = (at[...].astype(F32) + r1b[m][0].astype(F32)).astype(BF16)
            second[m].append(push(at, r2[m].at[1], neighbour(axis, near(u))))

        second_axis = [[], [], []]

        def second_axis_step(m):
            axis = MLP_AXES[m][1]
            own = slab(m, c[axis])
            for copy in first[m][2:] + second[m]:
                copy.wait()
            own[top, :] = (own[top, :].astype(F32) + r1a[m][1].astype(F32) + r2[m][0].astype(F32)).astype(BF16)
            own[low, :] = (own[low, :].astype(F32) + r1b[m][1].astype(F32) + r2[m][1].astype(F32)).astype(BF16)
            axis = MLP_AXES[m][2]
            for k in (1, 2, 3):
                rows = pl.ds(pl.multiple_of(((c[axis] + k) % 4) * 96, 32), 96)
                second_axis[m].append(push(own.at[rows, :], got2[m].at[k - 1], peer(axis, k)))

        def second_axis_sum(m):
            for copy in second_axis[m]:
                copy.wait()
            rows = pl.ds(pl.multiple_of(c[MLP_AXES[m][2]] * 96, 32), 96)
            total = slab(m, c[MLP_AXES[m][1]])[rows, :].astype(F32)
            for k in range(3):
                total = total + got2[m][k].astype(F32)
            acc2[m][...] = total

        for name, place in (("over", over), ("near", near), ("far", far), ("own", lambda u: u)):
            for i, m in enumerate((0, 2, 1)):
                if name == "over":
                    loads[2 * i].wait()
                    loads[2 * i + 1].wait()
                u = place(c[MLP_AXES[m][1]])
                x = xs[m][u]
                sendbuf[m][u] = mm(x, gs[m][...]).astype(BF16)
                ready(m, name)

        o_first, o_second = [[], [], []], [[], [], []]
        def out_first(p):
            order = OUT_ORDERS[p]
            slab_products(o_buf[p], bt_ref, a_ref[:, p * 256 : (p + 1) * 256], order)
            for k in (1, 2, 3):
                there = (c[order[0]] + k) % 4
                o_first[p].append(push(o_buf[p].at[there], o_got1[p].at[k - 1], peer(order[0], k)))

        def out_second(p):
            order = OUT_ORDERS[p]
            sum_first(o_buf[p], [o_got1[p].at[k] for k in range(3)], o_first[p], c[order[0]])
            for k in (1, 2, 3):
                rows = pl.ds(pl.multiple_of(((c[order[1]] + k) % 4) * 96, 32), 96)
                o_second[p].append(push(o_buf[p].at[c[order[0]], rows, :], o_got2[p].at[k - 1], peer(order[1], k)))

        def out_sum(p):
            order = OUT_ORDERS[p]
            for copy in o_second[p]:
                copy.wait()
            rows = pl.ds(pl.multiple_of(c[order[1]] * 96, 32), 96)
            total = o_buf[p][c[order[0]], rows, :].astype(F32)
            for k in range(3):
                total = total + o_got2[p][k].astype(F32)
            o_acc2[p][...] = total

        loads[6].wait()
        dev = lax.axis_index("seq")
        row = lax.broadcasted_iota(jnp.int32, (BLK, 96), 0)
        key_off = (row % Q_BLK) * 64 + row // Q_BLK
        q_off = (lax.broadcasted_iota(jnp.int32, (1, 96), 1) % Q_BLK) * 64 + dev
        dq_ref[...] = jnp.zeros_like(dq_ref)

        def k_step(kb, _):
            k_blk = dkv[:, :, :, kv_rows(kb, 0), :].reshape(BLK, 128)
            v_blk = dkv[:, :, :, kv_rows(kb, 1), :].reshape(BLK, 128)
            k_t = k_blk.T
            pos_k = key_off + kb * BLK

            def pair(qb, carry, causal):
                dk, dv = carry
                q_blk, g_blk = q_ref[qb], g_ref[qb]
                pos_q = q_off + qb * BLK
                vis = pos_k >= doc_bounds(pos_q, len_ref)
                if causal:
                    vis = vis & (pos_k <= pos_q)
                s = nt(k_blk, q_blk)
                p = jnp.where(vis, jnp.exp2(s * SCALE2 - lse_ref[qb]), 0.0)
                gp = nt(v_blk, g_blk)
                ds = (p * (gp - delta_ref[qb])).astype(BF16)
                dq_ref[qb] += mm(k_t, ds)
                dk = dk + mm(ds, q_blk)
                dv = dv + mm(p.astype(BF16), g_blk)
                return dk, dv

            zero = jnp.zeros((BLK, 128), F32)
            carry = pair(kb, (zero, zero), True)
            dk, dv = lax.fori_loop(kb + 1, 8, lambda qb, carry: pair(qb, carry, False), carry)
            dkv[:, :, :, kv_rows(kb, 0), :] = (dk * SCALE).astype(BF16).reshape(4, 4, 4, Q_BLK, 128)
            dkv[:, :, :, kv_rows(kb, 1), :] = dv.astype(BF16).reshape(4, 4, 4, Q_BLK, 128)
            return 0

        kv_pending = [[] for _ in range(6)]

        def kv_stage(chunk, stage):
            for i, (r0, rn, order) in enumerate(KV_CHUNK):
                p, r0 = chunk * 3 + i, r0 + chunk * 128
                for copy in kv_pending[p]:
                    copy.wait()
                kv_pending[p] = []
                got = (kv1, kv2, kv3)
                if stage:
                    mine = kv_index(order[stage:], c, r0, rn)
                    own = dkv[mine].astype(F32)
                    for k in range(3):
                        own = own + got[stage - 1][p][k].astype(F32)
                    if stage == 3:
                        own_ref[pl.ds(r0, rn), :] = own
                        continue
                    dkv[mine] = own.astype(BF16)
                for k in (1, 2, 3):
                    there = (c[order[stage]] + k) % 4
                    cc = dict(c)
                    cc[order[stage]] = there
                    src = dkv.at[kv_index(order[stage + 1 :], cc, r0, rn)]
                    kv_pending[p].append(push(src, got[stage][p].at[k - 1], peer(order[stage], k)))

        def share(acc, got, axis):
            copies = []
            for k in (1, 2, 3):
                rows = pl.ds(pl.multiple_of(((c[axis] + k) % 4) * 24, 8), 24)
                copies.append(push(acc.at[rows, :], got.at[k - 1], peer(axis, k)))
            return copies

        q_copies = [[] for _ in QKV_PARTS]

        def qkv_first(p):
            lo, hi, order = QKV_PARTS[p]
            slab_products(q_buf[p], nt_ref, gp_ref[:, lo:hi], order)
            for k in (1, 2, 3):
                there = (c[order[0]] + k) % 4
                q_copies[p].append(push(q_buf[p].at[there], q_got1[p][k - 1], peer(order[0], k)))

        def qkv_second(p):
            order = QKV_PARTS[p][2]
            sum_first(q_buf[p], q_got1[p], q_copies[p], c[order[0]])
            q_copies[p] = []
            for k in (1, 2, 3):
                rows = pl.ds(pl.multiple_of(((c[order[1]] + k) % 4) * 96, 32), 96)
                q_copies[p].append(push(q_buf[p].at[c[order[0]], rows, :], q_got2[p].at[k - 1], peer(order[1], k)))

        def qkv_third(p):
            order = QKV_PARTS[p][2]
            for copy in q_copies[p]:
                copy.wait()
            rows = pl.ds(pl.multiple_of(c[order[1]] * 96, 32), 96)
            total = q_buf[p][c[order[0]], rows, :].astype(F32)
            for k in range(3):
                total = total + q_got2[p][k].astype(F32)
            q_acc2[p][...] = total
            q_copies[p] = share(q_acc2[p], q_got3[p], order[2])

        def qkv_out(p):
            lo, hi, order = QKV_PARTS[p]
            for copy in q_copies[p]:
                copy.wait()
            total = q_acc2[p][pl.ds(pl.multiple_of(c[order[2]] * 24, 8), 24), :]
            for k in range(3):
                total = total + q_got3[p][k]
            for j in range(lo // 128, hi // 128):
                v = total[:, j * 128 - lo : (j + 1) * 128 - lo]
                if j < 6:
                    gq_ref[j] = v
                elif j == 6:
                    gk_ref[...] = v
                else:
                    gv_ref[...] = v

        lax.fori_loop(4, 8, k_step, 0)
        kv_stage(1, 0)
        second_step(0)
        lax.fori_loop(0, 1, k_step, 0)
        second_step(2)
        second_step(1)
        lax.fori_loop(1, 2, k_step, 0)
        kv_stage(1, 1)
        second_axis_step(0)
        for p in range(3):
            out_first(p)
        lax.fori_loop(2, 3, k_step, 0)
        kv_stage(1, 2)
        second_axis_step(2)
        second_axis_step(1)
        lax.fori_loop(3, 4, k_step, 0)
        kv_stage(0, 0)

        cos_t, sin_t = cos_ref[...], sin_ref[...]
        for qb in range(8):
            dq = dq_ref[qb].T * SCALE
            rows = slice(qb * Q_BLK, (qb + 1) * Q_BLK)
            cs, sn = cos_t[rows], sin_t[rows]
            for h in range(6):
                v = dq[h * Q_BLK : (h + 1) * Q_BLK]
                gp_ref[rows, h * 128 : (h + 1) * 128] = (v * cs - swap_halves(v) * sn).astype(BF16)
        for p in range(3):
            qkv_first(p)
        kv_stage(0, 1)
        m_copies = [None] * 3
        for m in (0, 2, 1):
            second_axis_sum(m)
            m_copies[m] = share(acc2[m], m_got[m], MLP_AXES[m][0])
        w_ref = [sendbuf[0].at[:, :, h * 128 : (h + 1) * 128] for h in range(8)]
        w_from = [w_hbm[0].at[h] for h in range(6)] + [w_hbm[1], w_hbm[2]]
        w_loads = [pltpu.make_async_copy(w_from[h], w_ref[h], loc.at[7 + n_late + h]) for h in range(8)]
        for copy in w_loads:
            copy.start()

        def back_through(lo, hi):
            total = nt(gp_ref[:, lo * 128 : (lo + 1) * 128], w_ref[lo][...].reshape(1536, 128))
            for h in range(lo + 1, hi):
                total = total + nt(gp_ref[:, h * 128 : (h + 1) * 128], w_ref[h][...].reshape(1536, 128))
            return total

        for p in range(3):
            out_second(p)
        kv_stage(0, 2)
        for copy in loads[7:] + w_loads:
            copy.wait()
        part[...] = back_through(0, 6)
        kv_stage(1, 3)
        kv_stage(0, 3)

        dk = jnp.concatenate([own_ref[0:64, :], own_ref[128:192, :]], axis=0)
        gp_ref[:, 768:896] = (dk * cos_t - swap_halves(dk) * sin_t).astype(BF16)
        gp_ref[:, 896:] = jnp.concatenate([own_ref[64:128, :], own_ref[192:256, :]], axis=0).astype(BF16)
        qkv_first(3)
        qkv_first(4)
        part[...] += back_through(6, 8)
        swap = push(part, got_part, partner())

        inputs = t_ref[...].astype(F32)
        inv = lax.rsqrt(jnp.mean(inputs * inputs, axis=1, keepdims=True) + 1e-06)
        d_norm1 = jnp.sum(part[...] * inputs * inv, axis=0, keepdims=True)
        d_bias = jnp.sum(gp_ref[...].astype(F32), axis=0, keepdims=True)
        core = lax.axis_index("tensor")
        for j in range(12):
            s_acc[0, j : j + 1, :] = d_norm1[:, j * 128 : (j + 1) * 128]
            s_acc[0, 12 + j : 13 + j, :] = dn2_ref[:, j * 128 : (j + 1) * 128]
        for j in range(8):
            v = d_bias[:, j * 128 : (j + 1) * 128]
            s_acc[0, 24 + j : 25 + j, :] = jnp.where(core == 0, v, 0.0)
            s_acc[0, 32 + j : 33 + j, :] = jnp.where(core == 1, v, 0.0)
        s_pending = []

        def send_small(stage):
            peers = [partner()] if stage == 0 else [peer(AXES[stage - 1], k) for k in (1, 2, 3)]
            for i, d in enumerate(peers):
                s_pending.append(push(s_acc.at[stage], s_got.at[stage * 3 + i], d))

        def sum_small(stage):
            for copy in s_pending:
                copy.wait()
            s_pending.clear()
            if stage == 0:
                return s_acc[0] + s_got[0]
            axis = AXES[stage - 1]
            parts = [s_acc[stage]] + [s_got[stage * 3 + k] for k in range(3)]
            total = jnp.zeros_like(parts[0])
            for w in range(4):
                term = jnp.zeros_like(total)
                for k in range(4):
                    term = jnp.where((c[axis] + 4 - k) % 4 == w, parts[k], term)
                total = total + term
            return total

        send_small(0)
        for p in range(3):
            qkv_second(p)
        o_copies = [None] * 3
        for p in range(3):
            out_sum(p)
            o_copies[p] = share(o_acc2[p], o_got[p], OUT_ORDERS[p][2])
        s_acc[1] = sum_small(0)
        send_small(1)
        qkv_second(3)
        qkv_second(4)
        swap.wait()
        g_norm = part[...] + got_part[...]
        scaled = g_norm * gain_ref[0:1, :]
        gt_ref[...] += (
            inv * scaled - inputs * (inv * inv * inv) * jnp.mean(scaled * inputs, axis=1, keepdims=True)
        )
        for p in range(3):
            qkv_third(p)
        s_acc[2] = sum_small(1)
        send_small(2)
        qkv_third(3)
        qkv_third(4)
        for p in range(3):
            for copy in o_copies[p]:
                copy.wait()
            rows = pl.ds(pl.multiple_of(c[OUT_ORDERS[p][2]] * 24, 8), 24)
            total = o_acc2[p][rows, :]
            for k in range(3):
                total = total + o_got[p][k]
            for j in range(2):
                go_ref[p * 2 + j] = total[:, j * 128 : (j + 1) * 128]
        for m in range(3):
            for copy in m_copies[m]:
                copy.wait()
            here = c[MLP_AXES[m][0]]
            m_outs[m][:, pl.ds(col_start(here), FC)] = acc2[m][pl.ds(pl.multiple_of(here * 24, 8), 24), :]
            for k in (1, 2, 3):
                m_outs[m][:, pl.ds(col_start((here + 4 - k) % 4), FC)] = m_got[m][k - 1]
        s_acc[3] = sum_small(2)
        send_small(3)
        for p in range(n_parts):
            qkv_out(p)
        s_out[...] = sum_small(3)

    rows = [rn for _, rn, _ in KV_CHUNK] * 2
    cols = [hi - lo for lo, hi, _ in QKV_PARTS]
    late = (tokens, g_mid)
    scratch = (
        [pltpu.VMEM((4, 384, 512), BF16)] * 3
        + [pltpu.VMEM((512, FC), BF16)] * 3
        + [pltpu.VMEM((4, 4, 4, 256, 128), BF16)]
        + [pltpu.VMEM((128, 1536), BF16)]
        + [pltpu.VMEM((96, FC), F32)] * 3
        + [pltpu.VMEM((96, 256), F32)] * 3
        + [pltpu.VMEM((8, 128, 96), F32), pltpu.VMEM((256, 128), F32)]
        + [pltpu.VMEM((4, 384, FC), BF16)] * 3
        + [pltpu.VMEM((2, 192, FC), BF16)] * 3
        + [pltpu.VMEM((2, 192, FC), BF16)] * 3
        + [pltpu.VMEM((2, 192, FC), BF16)] * 3
        + [pltpu.VMEM((3, 96, FC), BF16)] * 3
        + [pltpu.VMEM((4, 384, 256), BF16)]
        + [pltpu.VMEM((3, 384, 256), BF16)] * 3
        + [pltpu.VMEM((3, 96, 256), BF16)] * 3
        + [pltpu.VMEM((3, 4, 4, r, 128), BF16) for r in rows]
        + [pltpu.VMEM((3, 4, r, 128), BF16) for r in rows]
        + [pltpu.VMEM((3, r, 128), BF16) for r in rows]
        + [pltpu.VMEM((3, 24, FC), F32)] * 3
        + [pltpu.VMEM((3, 24, 256), F32)] * 3
        + [pltpu.VMEM((3, 96, n), BF16) for n in cols]
        + [pltpu.VMEM((96, n), F32) for n in cols]
        + [pltpu.VMEM((3, 24, n), F32) for n in cols]
        + [
            pltpu.VMEM((4, SMALL, 128), F32),
            pltpu.VMEM((12, SMALL, 128), F32),
            pltpu.VMEM((128, 1024), BF16),
            pltpu.VMEM((128, 1536), F32),
            pltpu.VMEM((128, 1536), F32),
            DMA((7 + n_late + 8,)),
            DMA((192,)),
            DMA((192,)),
        ]
    )
    vm, sm, hbm = (pl.BlockSpec(memory_space=m) for m in (pltpu.VMEM, pltpu.SMEM, pl.ANY))
    f32 = lambda *s: jax.ShapeDtypeStruct(s, F32)
    shape = (f32(128, 1536), f32(6, 24, 128), f32(24, 128), f32(24, 128), f32(6, 24, 128), f32(SMALL, 128))
    shape = shape + (f32(24, 4480),) * 3
    return pl.pallas_call(
        body,
        out_shape=shape,
        in_specs=[sm] + [hbm] * (10 + n_late) + [vm] * 11,
        out_specs=(vm,) * 9,
        scratch_shapes=scratch,
        compiler_params=pltpu.CompilerParams(collective_id=2, has_side_effects=True, vmem_limit_bytes=VMEM_BYTES),
        name="backward",
    )(lengths, *xs_in, *gs_in, kv, wq.reshape(6, 4, 384, 128), wk.reshape(4, 384, 128), wv.reshape(4, 384, 128), *late, q, g, lse, delta, branch_t, attn_low, cos, sin, norm_t, gain, d_norm2)


def hand_out(*arrays):
    n = len(arrays)

    def body(*refs):
        ins, outs, held, sem = refs[:n], refs[n : 2 * n], refs[2 * n : 3 * n], refs[3 * n]
        to = [pltpu.make_async_copy(a, b, sem.at[i]) for i, (a, b) in enumerate(zip(ins, held))]
        back = [pltpu.make_async_copy(a, b, sem.at[n + i]) for i, (a, b) in enumerate(zip(held, outs))]
        for copy in to:
            copy.start()
        for i in range(n):
            to[i].wait()
            back[i].start()
        for copy in back:
            copy.wait()

    hbm = pl.BlockSpec(memory_space=pl.ANY)
    return pl.pallas_call(
        body,
        out_shape=tuple(jax.ShapeDtypeStruct(v.shape, v.dtype) for v in arrays),
        in_specs=[hbm] * n,
        out_specs=(hbm,) * n,
        scratch_shapes=[pltpu.VMEM(v.shape, v.dtype) for v in arrays] + [DMA((2 * n,))],
        compiler_params=pltpu.CompilerParams(vmem_limit_bytes=VMEM_BYTES),
        name="hand_out",
    )(*arrays)


def local(
    tokens, cotangent, lengths, norm1_gain, w_query, b_query, w_key, b_key, w_value, b_value, w_out,
    norm2_gain, w_gate, w_up, w_down,
):
    device = lax.axis_index("seq")
    core = lax.axis_index("tensor")
    wq = w_query.transpose(1, 0, 2)
    wk, wv = w_key.reshape(1536, 128), w_value.reshape(1536, 128)
    wo = w_out.reshape(768, 1536)
    gains = jnp.stack([norm1_gain, norm2_gain])

    (output, g_mid, branch_t, g_attn, delta, d_norm2, q, norm_t, cos, sin, attn_low, lse, *shared, kv) = forward(
        tokens, cotangent, lengths, gains, wq, wk, wv, b_query, b_key, b_value, wo, w_gate, w_up, w_down
    )
    grad_tokens, grad_wq, grad_wk, grad_wv, grad_wo, sums, grad_gate, grad_up, grad_down = backward(
        shared[:3], shared[3:], q, g_attn, kv, lse, delta, branch_t, attn_low, lengths,
        cos, sin, norm_t, wq, wk, wv, tokens, gains, g_mid, d_norm2,
    )
    output, grad_tokens, grad_wq, grad_wk, grad_wv, grad_wo, grad_gate, grad_up, grad_down = hand_out(
        output, grad_tokens, grad_wq, grad_wk, grad_wv, grad_wo, grad_gate, grad_up, grad_down
    )
    sums = sums.reshape(-1)
    grad_norm1 = lax.dynamic_slice(sums, (device * 24,), (24,))
    grad_norm2 = lax.dynamic_slice(sums, (1536 + device * 24,), (24,))
    bias = lax.dynamic_slice(sums.reshape(SMALL, 128), (24 + core * 8, device * 2), (8, 2))
    return (
        output,
        grad_tokens,
        grad_norm1,
        grad_wq.transpose(1, 0, 2),
        bias[:6],
        grad_wk.reshape(24, 1, 128),
        bias[6:7],
        grad_wv.reshape(24, 1, 128),
        bias[7:8],
        grad_wo.transpose(0, 2, 1),
        grad_norm2,
        grad_gate,
        grad_up,
        grad_down.T,
    )


def solution(mesh):
    in_specs = (
        P("seq", None), P("seq", None), P(), P(), P(None, "tensor", None), P("tensor", None),
        P(None, "tensor", None), P("tensor", None), P(None, "tensor", None), P("tensor", None),
        P("tensor", None, None), P(), P(None, "tensor"), P(None, "tensor"), P("tensor", None),
    )
    out_specs = (
        P("seq", None), P("seq", None), P("seq"), P("seq", "tensor", None), P("tensor", "seq"),
        P("seq", "tensor", None), P("tensor", "seq"), P("seq", "tensor", None), P("tensor", "seq"),
        P("tensor", None, "seq"), P("seq"), P("seq", "tensor"), P("seq", "tensor"), P("tensor", "seq"),
    )
    return jax.shard_map(local, mesh=mesh, in_specs=in_specs, out_specs=out_specs, check_vma=False)
```

```python
import math

import jax
import jax.numpy as jnp
from jax import lax
from jax.experimental import pallas as pl
from jax.experimental.pallas import tpu as pltpu
from jax.sharding import PartitionSpec as P

MESH = pl.DeviceIdType.MESH
F32 = jnp.float32
BF16 = jnp.bfloat16
VMEM_BYTES = 60 * 1024 * 1024
AXES = ("z", "x", "y")
STRIDE = {"z": 16, "x": 4, "y": 1}


def coords():
    s = lax.axis_index("seq")
    return {"z": s // 16, "x": (s // 4) % 4, "y": s % 4}


def peer(axis, k):
    s = lax.axis_index("seq")
    c = coords()[axis]
    return (s + STRIDE[axis] * ((c + k) % 4 - c), lax.axis_index("tensor"))


def partner():
    return (lax.axis_index("seq"), 1 - lax.axis_index("tensor"))


def barrier(axes=AXES, core=False):
    bar = pltpu.get_barrier_semaphore()
    ids = [peer(a, k) for a in axes for k in (1, 2, 3)]
    if core:
        ids.append(partner())
    for d in ids:
        pl.semaphore_signal(bar, inc=1, device_id=d, device_id_type=MESH)
    pl.semaphore_wait(bar, len(ids))


def remote(src, dst, send, recv, device):
    return pltpu.make_async_remote_copy(
        src_ref=src, dst_ref=dst, send_sem=send, recv_sem=recv, device_id=device, device_id_type=MESH
    )


DMA = pltpu.SemaphoreType.DMA


KV_CHUNK = (
    (0, 48, ("z", "x", "y")),
    (48, 48, ("x", "y", "z")),
    (96, 32, ("y", "z", "x")),
)


def kv_rows(kb, v):
    return pl.ds(pl.multiple_of((kb // 4) * 128 + v * 64 + (kb % 4) * Q_BLK, Q_BLK), Q_BLK)


def kv_index(done, c, r0, rn):
    return tuple(slice(None) if a in done else c[a] for a in AXES) + (pl.ds(r0, rn), slice(None))


def rope_tables(len_ref):
    lane = lax.broadcasted_iota(jnp.int32, (128, 128), 1)
    pos = lax.broadcasted_iota(jnp.int32, (128, 128), 0) * 64 + lax.axis_index("seq")
    rel = (pos - doc_bounds(pos, len_ref)).astype(F32)
    inv_freq = jnp.exp(-(2.0 * (lane % 64).astype(F32) / 128) * math.log(10000.0))
    angle = rel * inv_freq
    sin = jnp.sin(angle)
    return jnp.cos(angle), jnp.where(lane < 64, -sin, sin)


def swap_halves(v):
    return pltpu.roll(v, 64, 1)


Q_BLK = 16
BLK = Q_BLK * 64
SCALE = 1.0 / math.sqrt(128)
SCALE2 = SCALE / math.log(2.0)


def doc_bounds(pos, len_ref):
    start = jnp.zeros_like(pos)
    end = jnp.int32(0)
    for j in range(8):
        end = end + len_ref[j]
        start = jnp.where(pos >= end, end, start)
    return start


FC = 1152


def nt(a, b):
    return lax.dot_general(a, b, (((1,), (1,)), ((), ())), preferred_element_type=F32)


def mm(a, b):
    return jnp.dot(a, b, preferred_element_type=F32)


def col_start(c):
    return pl.multiple_of(jnp.minimum(c * FC, 4480 - FC), 128)


MLP_AXES = (("z", "x", "y"), ("x", "y", "z"), ("y", "z", "x"))


def in_order(v, order):
    place = {}
    rows = []
    for i in range(64):
        for n, a in enumerate(order):
            place[a] = (i // (16, 4, 1)[n]) % 4
        o = place["z"] * 16 + place["x"] * 4 + place["y"]
        rows.append(v[o * 24 : (o + 1) * 24])
    return jnp.concatenate(rows, axis=0)


def forward(tokens, cot, lengths, gains, wq, wk, wv, bq, bk, bv, w_out, w_gate, w_up, w_down):
    def body(len_ref, t_ref, c_ref, g_ref, wk_ref, wv_ref, bq_ref, bk_ref, bv_ref, wq_hbm, wo_hbm, wg_hbm, wu_hbm, wd_hbm,
             out_ref, gmid_ref, bt_ref, ga_ref, delta_ref, dn_ref, q_ref, nt1_ref, cos_out, sin_out, low_ref, lse_ref,
             x0, x1, x2, g0, g1, g2, kv_hbm,
             kv, wq_ref, at_ref, m_ref, l_ref, acc_ref, br_ref,
             wo_ref, wg, wu, wd, got_br, acc, got, mid_ref, norm_ref, nt_ref, ct_ref, act, w_sem, loc, send, recv):
        xs, gs = (x0, x1, x2), (g0, g1, g2)
        c = coords()
        dev = lax.axis_index("seq")
        turn = c["z"] + c["x"] + c["y"]
        sems = iter(range(128))

        def load(j):
            cols = pl.ds(col_start((turn + j) % 4), FC)
            b = j % 2
            copies = [
                pltpu.make_async_copy(wg_hbm.at[:, cols], wg.at[b], w_sem.at[b, 0]),
                pltpu.make_async_copy(wu_hbm.at[:, cols], wu.at[b], w_sem.at[b, 1]),
                pltpu.make_async_copy(wd_hbm.at[cols, :], wd.at[b], w_sem.at[b, 2]),
            ]
            for copy in copies:
                copy.start()
            return copies

        def push(src, dst, device):
            n = next(sems)
            copy = remote(src, dst, send.at[n], recv.at[n], device)
            copy.start()
            return copy

        def keep(src, dst, n):
            copy = pltpu.make_async_copy(src, dst, loc.at[n])
            copy.start()
            return copy

        wq_load = keep(wq_hbm, wq_ref, 6)
        wo_load = keep(wo_hbm, wo_ref, 7)

        x = t_ref[...].astype(F32)
        inv = lax.rsqrt(jnp.mean(x * x, axis=1, keepdims=True) + 1e-06)
        normed = (x * inv * g_ref[0:1, :]).astype(BF16)
        cos, sin = rope_tables(len_ref)
        cos_out[...], sin_out[...] = cos, sin
        k_pre = mm(normed, wk_ref[...]) + bk_ref[...].astype(F32)
        v_low = (mm(normed, wv_ref[...]) + bv_ref[...].astype(F32)).astype(BF16)
        k_rot = (k_pre * cos + swap_halves(k_pre) * sin).astype(BF16)
        kv[c["z"], c["x"], c["y"]] = jnp.concatenate([k_rot[:64], v_low[:64], k_rot[64:], v_low[64:]], axis=0)
        barrier(core=True)
        kv_pending = [[] for _ in range(6)]

        def kv_wait(chunk):
            for p in range(chunk * 3, chunk * 3 + 3):
                for copy in kv_pending[p]:
                    copy.wait()
                kv_pending[p] = []

        def kv_stage(chunk, stage):
            for i, (r0, rn, order) in enumerate(KV_CHUNK):
                p, r0 = chunk * 3 + i, r0 + chunk * 128
                for copy in kv_pending[p]:
                    copy.wait()
                idx = kv_index(order[:stage], c, r0, rn)
                kv_pending[p] = [push(kv.at[idx], kv.at[idx], peer(order[stage], k)) for k in (1, 2, 3)]

        kv_stage(0, 0)
        kv_stage(1, 0)
        wq_load.wait()
        for h in range(6):
            q = mm(normed, wq_ref[h]) + bq_ref[h : h + 1, :].astype(F32)
            q = (q * cos + swap_halves(q) * sin).astype(BF16)
            q_ref[:, h * Q_BLK : (h + 1) * Q_BLK, :] = q.reshape(8, Q_BLK, 128)
        kv_stage(0, 1)
        kv_stage(1, 1)
        nt1_ref[...] = normed.T
        kv_stage(0, 2)
        loads = [load(0), load(1)]
        ct_ref[...] = c_ref[...].T.reshape(4, 384, 128)
        own = [keep(ct_ref, x2.at[:, :, pl.ds(0, 128)], 3)]
        kv_wait(0)
        kv_stage(1, 2)
        later = [push(ct_ref, x2.at[:, :, pl.ds(k * 128, 128)], peer("y", k)) for k in (1, 2, 3)]

        row_off = (lax.broadcasted_iota(jnp.int32, (96, 1), 0) % Q_BLK) * 64 + dev
        col = lax.broadcasted_iota(jnp.int32, (96, BLK), 1)
        key_off = (col % Q_BLK) * 64 + col // Q_BLK

        def attend(qb, lo, hi, carry, diagonal):
            q_blk = q_ref[qb]
            pos_q = row_off + qb * BLK
            start_q = doc_bounds(pos_q, len_ref)

            def block(kb, carry, causal):
                m, l, acc = carry
                k_blk = kv[:, :, :, kv_rows(kb, 0), :].reshape(BLK, 128)
                v_blk = kv[:, :, :, kv_rows(kb, 1), :].reshape(BLK, 128)
                pos_k = key_off + kb * BLK
                vis = pos_k >= start_q
                if causal:
                    vis = vis & (pos_k <= pos_q)
                s = jnp.where(vis, nt(q_blk, k_blk) * SCALE2, -1e30)
                m_new = jnp.maximum(m, jnp.max(s, axis=1, keepdims=True))
                p = jnp.exp2(s - m_new)
                a = jnp.exp2(m - m_new)
                return m_new, l * a + jnp.sum(p, axis=1, keepdims=True), acc * a + mm(p.astype(BF16), v_blk)

            carry = lax.fori_loop(lo, hi, lambda kb, carry: block(kb, carry, False), carry)
            return block(qb, carry, True) if diagonal else carry

        def attend_end(qb, carry):
            m, l, acc = carry
            attn = acc / l
            at_ref[qb] = attn
            low = attn.astype(BF16)
            for h in range(6):
                rows = pl.ds(pl.multiple_of(qb * Q_BLK, Q_BLK), Q_BLK)
                low_ref[rows, h * 128 : (h + 1) * 128] = low[h * Q_BLK : (h + 1) * Q_BLK]
            lse_ref[qb] = jnp.broadcast_to(m + jnp.log2(l), (96, 128)).T[0:1]

        init = (jnp.full((96, 1), -1e30, F32), jnp.zeros((96, 1), F32), jnp.zeros((96, 128), F32))

        def upper(qb, _):
            m_ref[qb - 4], l_ref[qb - 4], acc_ref[qb - 4] = attend(qb, 0, 4, init, False)
            return 0

        def whole(qb, _):
            attend_end(qb, attend(qb, 0, qb, init, True))
            return 0

        def rest(qb, _):
            attend_end(qb, attend(qb, 4, qb, (m_ref[qb - 4], l_ref[qb - 4], acc_ref[qb - 4]), True))
            return 0

        out_kv = [keep(kv.at[:, :, :, pl.ds(0, 128), :], kv_hbm.at[:, :, :, pl.ds(0, 128), :], 8)]
        lax.fori_loop(0, 4, whole, 0)
        lax.fori_loop(4, 8, upper, 0)
        kv_wait(1)
        out_kv.append(keep(kv.at[:, :, :, pl.ds(128, 128), :], kv_hbm.at[:, :, :, pl.ds(128, 128), :], 9))
        lax.fori_loop(4, 8, rest, 0)
        wo_load.wait()
        ex = []
        for half in range(2):
            cols = slice(half * 768, (half + 1) * 768)
            br_ref[half] = mm(low_ref[...], wo_ref[:, cols])
            ex.append(push(br_ref.at[half], got_br.at[half], partner()))
        for copy in ex:
            copy.wait()
        mid = t_ref[...].astype(F32) + jnp.concatenate([br_ref[h] + got_br[h] for h in range(2)], axis=1)
        mid_ref[...] = mid
        inv = lax.rsqrt(jnp.mean(mid * mid, axis=1, keepdims=True) + 1e-06)
        normed = (mid * inv * g_ref[1:2, :]).astype(BF16)
        norm_ref[...] = normed
        turned = normed.astype(F32).T
        for m in range(2):
            nt_ref[m] = in_order(turned, MLP_AXES[m][1:] + MLP_AXES[m][:1]).astype(BF16).reshape(4, 384, 128)
        own.append(keep(nt_ref.at[0], x0.at[:, :, pl.ds(0, 128)], 4))
        own.append(keep(nt_ref.at[1], x1.at[:, :, pl.ds(0, 128)], 5))
        for k in (1, 2, 3):
            for m, w in ((0, "z"), (1, "x")):
                later.append(push(nt_ref.at[m], xs[m].at[:, :, pl.ds(k * 128, 128)], peer(w, k)))

        lane = lax.broadcasted_iota(jnp.int32, (128, FC), 1)
        for j in range(4):
            b = j % 2
            d = (turn + j) % 4
            for copy in loads[j]:
                copy.wait()
            n = norm_ref[...]
            gate = mm(n, wg[b])
            up = mm(n, wu[b])
            gh = nt(c_ref[...], wd[b])
            sig = 1.0 / (1.0 + jnp.exp(-gate))
            silu = gate * sig
            hidden = (silu * up).astype(BF16)
            g_gate = (gh * up * sig * (1.0 + gate * (1.0 - sig))).astype(BF16)
            g_up = (gh * silu).astype(BF16)
            vals = (g_gate, g_up, hidden)
            for m in range(3):
                act[m, j] = vals[m]
            twice = (lane < 128) & (d == 3)
            zero = jnp.zeros((128, FC), BF16)
            hidden, g_gate, g_up = (jnp.where(twice, zero, v) for v in (hidden, g_gate, g_up))
            add_g = nt(g_gate, wg[b]) + nt(g_up, wu[b])
            acc[1] = add_g if j == 0 else acc[1] + add_g
            if j == 3:
                ex = [push(acc.at[1], got.at[1], partner())]
            add_o = mm(hidden, wd[b])
            acc[0] = add_o if j == 0 else acc[0] + add_o
            if j + 2 < 4:
                loads.append(load(j + 2))
            for m in range(3):
                w = MLP_AXES[m][0]
                k = (d + 4 - c[w]) % 4
                slot = pl.ds(pl.multiple_of(k * 128, 128), 128)

                @pl.when(k == 0)
                def _():
                    pltpu.make_async_copy(act.at[m, j], gs[m].at[pl.ds(0, 128), :], loc.at[m]).start()

                @pl.when(k != 0)
                def _():
                    remote(
                        act.at[m, j], gs[m].at[slot, :], send.at[96 + m * 4 + j], recv.at[96 + m * 4 + k], peer(w, k)
                    ).start()

        ex.append(push(acc.at[0], got.at[0], partner()))
        dn_ref[...] = jnp.sum(acc[1] * mid_ref[...] * inv, axis=0, keepdims=True)
        cot_f = c_ref[...].astype(F32)
        ex[0].wait()
        gn = acc[1] + got[1]
        mid = mid_ref[...]
        scaled = gn * g_ref[1:2, :]
        g_mid = cot_f + (inv * scaled - mid * (inv * inv * inv) * jnp.mean(scaled * mid, axis=1, keepdims=True))
        gmid_ref[...] = g_mid
        branch_low = g_mid.astype(BF16)
        bt_ref[...] = branch_low.T
        g_attn = nt(branch_low, wo_ref[...]).astype(BF16)
        for h in range(6):
            ga_ref[:, h * Q_BLK : (h + 1) * Q_BLK, :] = g_attn[:, h * 128 : (h + 1) * 128].reshape(8, Q_BLK, 128)
        for qb in range(8):
            delta_ref[qb] = jnp.sum((ga_ref[qb].astype(F32) * at_ref[qb]).T, axis=0, keepdims=True)
        ex[1].wait()
        out_ref[...] = mid_ref[...] + (acc[0] + got[0])
        for copy in later + own + out_kv:
            copy.wait()
        for m in range(3):
            w = MLP_AXES[m][0]
            pltpu.make_async_copy(act.at[m, 0], gs[m].at[pl.ds(0, 128), :], loc.at[m]).wait()
            for j in range(4):
                k = ((turn + j) % 4 + 4 - c[w]) % 4

                @pl.when(k != 0)
                def _():
                    slot = pl.ds(pl.multiple_of(k * 128, 128), 128)
                    remote(
                        act.at[m, j], gs[m].at[slot, :], send.at[96 + m * 4 + j], recv.at[96 + m * 4 + k], peer(w, k)
                    ).wait()

    f32 = lambda *s: jax.ShapeDtypeStruct(s, F32)
    b16 = lambda *s: jax.ShapeDtypeStruct(s, BF16)
    vm, sm, hbm = (pl.BlockSpec(memory_space=m) for m in (pltpu.VMEM, pltpu.SMEM, pl.ANY))
    held = [(6, 1536, 128, BF16), (8, 96, 128, F32), (4, 96, 1, F32), (4, 96, 1, F32), (4, 96, 128, F32)]
    held += [(2, 128, 768, F32), (768, 1536, BF16), (2, 1536, FC, BF16), (2, 1536, FC, BF16), (2, FC, 1536, BF16)]
    held += [(2, 128, 768, F32), (2, 128, 1536, F32), (2, 128, 1536, F32), (128, 1536, F32), (128, 1536, BF16)]
    held += [(2, 4, 384, 128, BF16), (4, 384, 128, BF16), (3, 4, 128, FC, BF16)]
    return pl.pallas_call(
        body,
        out_shape=(f32(128, 1536), f32(128, 1536), b16(1536, 128), b16(8, 96, 128), f32(8, 1, 96), f32(1, 1536))
        + (b16(8, 96, 128), b16(1536, 128), f32(128, 128), f32(128, 128), b16(128, 768), f32(8, 1, 96))
        + (b16(4, 384, 512),) * 3
        + (b16(512, FC),) * 3
        + (b16(4, 4, 4, 256, 128),),
        in_specs=[sm] + [vm] * 8 + [hbm] * 5,
        out_specs=(vm,) * 12 + (hbm,) * 7,
        scratch_shapes=[pltpu.VMEM((4, 4, 4, 256, 128), BF16)]
        + [pltpu.VMEM(v[:-1], v[-1]) for v in held]
        + [DMA((2, 3)), DMA((10,)), DMA((112,)), DMA((112,))],
        compiler_params=pltpu.CompilerParams(collective_id=4, has_side_effects=True, vmem_limit_bytes=VMEM_BYTES),
        name="forward",
    )(lengths, tokens, cot, gains, wk, wv, bq, bk, bv, wq, w_out, w_gate, w_up, w_down)


OUT_ORDERS = (("z", "x", "y"), ("x", "y", "z"), ("y", "z", "x"))
QKV_PARTS = (
    (0, 256, ("z", "x", "y")),
    (256, 512, ("x", "y", "z")),
    (512, 768, ("y", "z", "x")),
    (768, 896, ("z", "x", "y")),
    (896, 1024, ("x", "y", "z")),
)
SMALL = 40


def slab_products(buf, left, rhs, order):
    def blocks(v, places):
        return jnp.concatenate([v[o * 24 : (o + 1) * 24] for o in places], axis=0)

    if order[0] == "z":
        for z in range(4):
            buf[z] = mm(left[z * 384 : (z + 1) * 384, :], rhs).astype(BF16)
    elif order[0] == "x":
        for x in range(4):
            lhs = jnp.concatenate([left[z * 384 + x * 96 : z * 384 + (x + 1) * 96, :] for z in range(4)], axis=0)
            buf[x] = blocks(mm(lhs, rhs), [z * 4 + y for y in range(4) for z in range(4)]).astype(BF16)
    else:
        for z in range(4):
            v = blocks(mm(left[z * 384 : (z + 1) * 384, :], rhs), [x * 4 + y for y in range(4) for x in range(4)])
            v = v.astype(BF16)
            for y in range(4):
                buf[y, z * 96 : (z + 1) * 96] = v[y * 96 : (y + 1) * 96]


def near(u):
    return u + 1 - 2 * (u % 2)


def far(u):
    return 3 - u


def over(u):
    return (u + 2) % 4


class Halves:
    def __init__(self, push, axis, c, slab, got_first, got_second):
        self.push, self.slab, self.u = push, slab, c[axis]
        self.got_first, self.got_second = got_first, got_second
        self.to = lambda place: peer(axis, place + 4 - c[axis])
        self.one, self.two = {}, []

    def ready(self, which):
        u = self.u
        if which == "over":
            self.one[0, 0] = self.push(self.slab(over(u), 0), self.got_first(0, 0), self.to(near(u)))
            self.one[1, 0] = self.push(self.slab(over(u), 1), self.got_first(1, 0), self.to(far(u)))
        elif which == "near":
            self.one[0, 1] = self.push(self.slab(near(u), 0), self.got_first(0, 1), self.to(near(u)))
        elif which == "far":
            self.one[1, 1] = self.push(self.slab(far(u), 1), self.got_first(1, 1), self.to(far(u)))

    def first(self):
        for which in ("over", "near", "far"):
            self.ready(which)

    def second(self):
        u = self.u
        for h, place in ((0, far(u)), (1, near(u))):
            self.one[h, 0].wait()
            at = self.slab(place, h)
            at[...] = (at[...].astype(F32) + self.got_first(h, 0)[...].astype(F32)).astype(BF16)
            self.two.append(self.push(at, self.got_second(h), self.to(place)))

    def final(self):
        for h in range(2):
            self.one[h, 1].wait()
            self.two[h].wait()
            at = self.slab(self.u, h)
            at[...] = (
                at[...].astype(F32) + self.got_first(h, 1)[...].astype(F32) + self.got_second(h)[...].astype(F32)
            ).astype(BF16)


def sum_first(buf, got, copies, own):
    for copy in copies:
        copy.wait()
    total = buf[own].astype(F32)
    for k in range(3):
        total = total + got[k][...].astype(F32)
    buf[own] = total.astype(BF16)


def backward(xs_in, gs_in, q, g, kv, lse, delta, branch_t, attn_low, lengths,
             cos, sin, norm_t, wq, wk, wv, tokens, gain, g_mid, d_norm2):
    n_late = 2

    def body(*refs):
        r = list(refs)
        take = lambda n: [r.pop(0) for _ in range(n)]
        (len_ref,), xs_hbm, gs_hbm, (kv_hbm, *w_hbm), late = take(1), take(3), take(3), take(4), take(n_late)
        q_ref, g_ref, lse_ref, delta_ref, bt_ref, a_ref, cos_ref, sin_ref, nt_ref, gain_ref, dn2_ref = take(11)
        gt_ref, gq_ref, gk_ref, gv_ref, go_ref, s_out = take(6)
        m_outs = take(3)
        xs, gs, (dkv,), (t_ref,) = take(3), take(3), take(1), take(1)
        held = (t_ref, gt_ref)
        acc2, o_acc2, (dq_ref, own_ref) = take(3), take(3), take(2)
        sendbuf, r1, r2, t1, t2 = take(3), take(3), take(3), take(3), take(3)
        o_buf, o_r1, o_r2, o_got2 = take(1), take(3), take(3), take(3)
        kv1, kv1b, kv2, kv3 = take(6), take(6), take(6), take(6)
        m_got, o_got = take(3), take(3)
        n_parts = len(QKV_PARTS)
        q_got2, q_acc2, q_got3 = (take(n_parts) for _ in range(3))
        o_buf = [xs[2].at[:, :, 0:256], xs[2].at[:, :, 256:512], o_buf[0]]
        room = ((0, 0, 256), (0, 256, 512), (1, 0, 256), (1, 256, 384), (1, 384, 512))
        q_buf = [xs[m].at[:, :, lo:hi] for m, lo, hi in room]
        room = ((0, 0, 256), (1, 0, 256), (2, 0, 256), (0, 768, 128), (1, 768, 128))
        q_got1 = [
            [gs[m].at[192 * (k % 2) : 192 * (k % 2) + 192, lo + k // 2 * n : lo + (k // 2 + 1) * n] for k in range(6)]
            for m, lo, n in room[:3]
        ] + [[gs[m].at[0:384, lo + k * n : lo + (k + 1) * n] for k in range(3)] for m, lo, n in room[3:]]
        s_acc, s_got, gp_ref, part, got_part = take(5)
        loc, send, recv = take(3)
        c = coords()
        loads = [pltpu.make_async_copy(a, b, loc.at[i]) for i, (a, b) in enumerate(
            ((xs_hbm[0], xs[0]), (gs_hbm[0], gs[0]), (xs_hbm[2], xs[2]), (gs_hbm[2], gs[2]),
             (xs_hbm[1], xs[1]), (gs_hbm[1], gs[1]), (kv_hbm, dkv), *zip(late, held)))]
        for copy in loads:
            copy.start()
        barrier(core=True)
        sems = iter(range(256))

        def push(src, dst, device):
            n = next(sems)
            copy = remote(src, dst, send.at[n], recv.at[n], device)
            copy.start()
            return copy

        def mlp_slab(m):
            return lambda u, h: sendbuf[m].at[u, pl.ds(192 * h, 192), :]

        mlp_one = [
            Halves(push, MLP_AXES[m][1], c, mlp_slab(m), lambda h, i, m=m: r1[m].at[h, i], lambda h, m=m: r2[m].at[h])
            for m in range(3)
        ]

        def mlp_rows(m):
            own = sendbuf[m].at[c[MLP_AXES[m][1]]]
            return lambda u, h: own.at[pl.ds(pl.multiple_of(u * 96 + h * 48, 16), 48), :]

        mlp_two = [
            Halves(push, MLP_AXES[m][2], c, mlp_rows(m), lambda h, i, m=m: t1[m].at[h, i], lambda h, m=m: t2[m].at[h])
            for m in range(3)
        ]

        for name, place in (("over", over), ("near", near), ("far", far), ("own", lambda v: v)):
            for i, m in enumerate((0, 2, 1)):
                if name == "over":
                    loads[2 * i].wait()
                    loads[2 * i + 1].wait()
                u = place(c[MLP_AXES[m][1]])
                x = xs[m][u]
                sendbuf[m][u] = mm(x, gs[m][...]).astype(BF16)
                mlp_one[m].ready(name)

        def buf_slab(buf):
            return lambda u, h: buf.at[u, pl.ds(192 * h, 192), :]

        out_one = [
            Halves(push, OUT_ORDERS[p][0], c, buf_slab(o_buf[p]), lambda h, i, p=p: o_r1[p].at[h, i], lambda h, p=p: o_r2[p].at[h])
            for p in range(3)
        ]
        o_second = [[], [], []]

        def out_second(p):
            order = OUT_ORDERS[p]
            out_one[p].final()
            for k in (1, 2, 3):
                rows = pl.ds(pl.multiple_of(((c[order[1]] + k) % 4) * 96, 32), 96)
                o_second[p].append(push(o_buf[p].at[c[order[0]], rows, :], o_got2[p].at[k - 1], peer(order[1], k)))

        def out_sum(p):
            order = OUT_ORDERS[p]
            for copy in o_second[p]:
                copy.wait()
            rows = pl.ds(pl.multiple_of(c[order[1]] * 96, 32), 96)
            total = o_buf[p][c[order[0]], rows, :].astype(F32)
            for k in range(3):
                total = total + o_got2[p][k].astype(F32)
            o_acc2[p][...] = total

        loads[6].wait()
        dev = lax.axis_index("seq")
        row = lax.broadcasted_iota(jnp.int32, (BLK, 96), 0)
        key_off = (row % Q_BLK) * 64 + row // Q_BLK
        q_off = (lax.broadcasted_iota(jnp.int32, (1, 96), 1) % Q_BLK) * 64 + dev
        dq_ref[...] = jnp.zeros_like(dq_ref)

        def k_step(kb, _):
            k_blk = dkv[:, :, :, kv_rows(kb, 0), :].reshape(BLK, 128)
            v_blk = dkv[:, :, :, kv_rows(kb, 1), :].reshape(BLK, 128)
            k_t = k_blk.T
            pos_k = key_off + kb * BLK

            def pair(qb, carry, causal):
                dk, dv = carry
                q_blk, g_blk = q_ref[qb], g_ref[qb]
                pos_q = q_off + qb * BLK
                vis = pos_k >= doc_bounds(pos_q, len_ref)
                if causal:
                    vis = vis & (pos_k <= pos_q)
                s = nt(k_blk, q_blk)
                p = jnp.where(vis, jnp.exp2(s * SCALE2 - lse_ref[qb]), 0.0)
                gp = nt(v_blk, g_blk)
                ds = (p * (gp - delta_ref[qb])).astype(BF16)
                dq_ref[qb] += mm(k_t, ds)
                dk = dk + mm(ds, q_blk)
                dv = dv + mm(p.astype(BF16), g_blk)
                return dk, dv

            zero = jnp.zeros((BLK, 128), F32)
            carry = pair(kb, (zero, zero), True)
            dk, dv = lax.fori_loop(kb + 1, 8, lambda qb, carry: pair(qb, carry, False), carry)
            dkv[:, :, :, kv_rows(kb, 0), :] = (dk * SCALE).astype(BF16).reshape(4, 4, 4, Q_BLK, 128)
            dkv[:, :, :, kv_rows(kb, 1), :] = dv.astype(BF16).reshape(4, 4, 4, Q_BLK, 128)
            return 0

        kv_pending = [[] for _ in range(6)]
        kv_parts = [(r0 + 128 * chunk, rn, order) for chunk in range(2) for r0, rn, order in KV_CHUNK]

        def kv_slab(p):
            r0, rn, order = kv_parts[p]
            rest = [a for a in AXES if a != order[0]]

            def slab(u, h):
                where = {order[0]: u, rest[0]: pl.ds(2 * h, 2), rest[1]: slice(None)}
                return dkv.at[where["z"], where["x"], where["y"], pl.ds(r0, rn), :]

            return slab

        kv_one = [
            Halves(push, kv_parts[p][2][0], c, kv_slab(p), lambda h, i, p=p: kv1[p].at[h, i], lambda h, p=p: kv1b[p].at[h])
            for p in range(6)
        ]

        def kv_halves(chunk, step):
            for p in range(chunk * 3, chunk * 3 + 3):
                getattr(kv_one[p], step)()

        def kv_stage(chunk, stage):
            got = (None, kv2, kv3)
            for p in range(chunk * 3, chunk * 3 + 3):
                r0, rn, order = kv_parts[p]
                if stage == 1:
                    kv_one[p].final()
                else:
                    for copy in kv_pending[p]:
                        copy.wait()
                    kv_pending[p] = []
                    mine = kv_index(order[stage:], c, r0, rn)
                    own = dkv[mine].astype(F32)
                    for k in range(3):
                        own = own + got[stage - 1][p][k].astype(F32)
                    if stage == 3:
                        own_ref[pl.ds(r0, rn), :] = own
                        continue
                    dkv[mine] = own.astype(BF16)
                for k in (1, 2, 3):
                    cc = dict(c)
                    cc[order[stage]] = (c[order[stage]] + k) % 4
                    src = dkv.at[kv_index(order[stage + 1 :], cc, r0, rn)]
                    kv_pending[p].append(push(src, got[stage][p].at[k - 1], peer(order[stage], k)))

        def share(acc, got, axis):
            copies = []
            for k in (1, 2, 3):
                rows = pl.ds(pl.multiple_of(((c[axis] + k) % 4) * 24, 8), 24)
                copies.append(push(acc.at[rows, :], got.at[k - 1], peer(axis, k)))
            return copies

        q_copies = [[] for _ in QKV_PARTS]
        q_one = [
            Halves(push, QKV_PARTS[p][2][0], c, buf_slab(q_buf[p]), lambda h, i, p=p: q_got1[p][2 * h + i], lambda h, p=p: q_got1[p][4 + h])
            for p in range(3)
        ]

        def qkv_first(p):
            lo, hi, order = QKV_PARTS[p]
            slab_products(q_buf[p], nt_ref, gp_ref[:, lo:hi], order)
            if p < 3:
                q_one[p].first()
                return
            for k in (1, 2, 3):
                there = (c[order[0]] + k) % 4
                q_copies[p].append(push(q_buf[p].at[there], q_got1[p][k - 1], peer(order[0], k)))

        def qkv_second(p):
            order = QKV_PARTS[p][2]
            if p < 3:
                q_one[p].final()
            else:
                sum_first(q_buf[p], q_got1[p], q_copies[p], c[order[0]])
            q_copies[p] = []
            for k in (1, 2, 3):
                rows = pl.ds(pl.multiple_of(((c[order[1]] + k) % 4) * 96, 32), 96)
                q_copies[p].append(push(q_buf[p].at[c[order[0]], rows, :], q_got2[p].at[k - 1], peer(order[1], k)))

        def qkv_third(p):
            order = QKV_PARTS[p][2]
            for copy in q_copies[p]:
                copy.wait()
            rows = pl.ds(pl.multiple_of(c[order[1]] * 96, 32), 96)
            total = q_buf[p][c[order[0]], rows, :].astype(F32)
            for k in range(3):
                total = total + q_got2[p][k].astype(F32)
            q_acc2[p][...] = total
            q_copies[p] = share(q_acc2[p], q_got3[p], order[2])

        def qkv_out(p):
            lo, hi, order = QKV_PARTS[p]
            for copy in q_copies[p]:
                copy.wait()
            total = q_acc2[p][pl.ds(pl.multiple_of(c[order[2]] * 24, 8), 24), :]
            for k in range(3):
                total = total + q_got3[p][k]
            for j in range(lo // 128, hi // 128):
                v = total[:, j * 128 - lo : (j + 1) * 128 - lo]
                if j < 6:
                    gq_ref[j] = v
                elif j == 6:
                    gk_ref[...] = v
                else:
                    gv_ref[...] = v

        m_copies = [None] * 3

        def mlp_third(m):
            mlp_two[m].final()
            rows = pl.ds(pl.multiple_of(c[MLP_AXES[m][2]] * 96, 32), 96)
            acc2[m][...] = sendbuf[m][c[MLP_AXES[m][1]], rows, :].astype(F32)
            m_copies[m] = share(acc2[m], m_got[m], MLP_AXES[m][0])

        lax.fori_loop(4, 8, k_step, 0)
        kv_halves(1, "first")
        mlp_one[0].second()
        lax.fori_loop(0, 1, k_step, 0)
        mlp_one[2].second()
        mlp_one[1].second()
        kv_halves(1, "second")
        lax.fori_loop(1, 2, k_step, 0)
        for p, order in enumerate(OUT_ORDERS):
            slab_products(o_buf[p], bt_ref, a_ref[:, p * 256 : (p + 1) * 256], order)
            out_one[p].first()
        mlp_one[0].final()
        mlp_two[0].first()
        lax.fori_loop(2, 3, k_step, 0)
        kv_stage(1, 1)
        for m in (2, 1):
            mlp_one[m].final()
            mlp_two[m].first()
        lax.fori_loop(3, 4, k_step, 0)
        kv_halves(0, "first")

        cos_t, sin_t = cos_ref[...], sin_ref[...]
        for qb in range(8):
            dq = dq_ref[qb].T * SCALE
            rows = slice(qb * Q_BLK, (qb + 1) * Q_BLK)
            cs, sn = cos_t[rows], sin_t[rows]
            for h in range(6):
                v = dq[h * Q_BLK : (h + 1) * Q_BLK]
                gp_ref[rows, h * 128 : (h + 1) * 128] = (v * cs - swap_halves(v) * sn).astype(BF16)
        mlp_two[0].second()
        kv_halves(0, "second")
        for p in range(3):
            out_one[p].second()
        for m in (2, 1):
            mlp_two[m].second()
        for p in range(3):
            qkv_first(p)
        kv_stage(1, 2)
        kv_stage(0, 1)
        for m in (0, 2, 1):
            mlp_third(m)
        w_ref = [sendbuf[0].at[:, :, h * 128 : (h + 1) * 128] for h in range(8)]
        w_from = [w_hbm[0].at[h] for h in range(6)] + [w_hbm[1], w_hbm[2]]
        w_loads = [pltpu.make_async_copy(w_from[h], w_ref[h], loc.at[7 + n_late + h]) for h in range(8)]
        for copy in w_loads:
            copy.start()

        def back_through(lo, hi):
            total = nt(gp_ref[:, lo * 128 : (lo + 1) * 128], w_ref[lo][...].reshape(1536, 128))
            for h in range(lo + 1, hi):
                total = total + nt(gp_ref[:, h * 128 : (h + 1) * 128], w_ref[h][...].reshape(1536, 128))
            return total

        kv_stage(0, 2)
        for p in range(3):
            out_second(p)
        for p in range(3):
            q_one[p].second()
        for copy in loads[7:] + w_loads:
            copy.wait()
        part[...] = back_through(0, 6)
        kv_stage(1, 3)
        kv_stage(0, 3)

        dk = jnp.concatenate([own_ref[0:64, :], own_ref[128:192, :]], axis=0)
        gp_ref[:, 768:896] = (dk * cos_t - swap_halves(dk) * sin_t).astype(BF16)
        gp_ref[:, 896:] = jnp.concatenate([own_ref[64:128, :], own_ref[192:256, :]], axis=0).astype(BF16)
        qkv_first(3)
        qkv_first(4)
        part[...] += back_through(6, 8)
        swap = push(part, got_part, partner())

        inputs = t_ref[...].astype(F32)
        inv = lax.rsqrt(jnp.mean(inputs * inputs, axis=1, keepdims=True) + 1e-06)
        d_norm1 = jnp.sum(part[...] * inputs * inv, axis=0, keepdims=True)
        d_bias = jnp.sum(gp_ref[...].astype(F32), axis=0, keepdims=True)
        core = lax.axis_index("tensor")
        for j in range(12):
            s_acc[0, j : j + 1, :] = d_norm1[:, j * 128 : (j + 1) * 128]
            s_acc[0, 12 + j : 13 + j, :] = dn2_ref[:, j * 128 : (j + 1) * 128]
        for j in range(8):
            v = d_bias[:, j * 128 : (j + 1) * 128]
            s_acc[0, 24 + j : 25 + j, :] = jnp.where(core == 0, v, 0.0)
            s_acc[0, 32 + j : 33 + j, :] = jnp.where(core == 1, v, 0.0)
        s_pending = []

        def send_small(stage):
            peers = [partner()] if stage == 0 else [peer(AXES[stage - 1], k) for k in (1, 2, 3)]
            for i, d in enumerate(peers):
                s_pending.append(push(s_acc.at[stage], s_got.at[stage * 3 + i], d))

        def sum_small(stage):
            for copy in s_pending:
                copy.wait()
            s_pending.clear()
            if stage == 0:
                return s_acc[0] + s_got[0]
            axis = AXES[stage - 1]
            parts = [s_acc[stage]] + [s_got[stage * 3 + k] for k in range(3)]
            total = jnp.zeros_like(parts[0])
            for w in range(4):
                term = jnp.zeros_like(total)
                for k in range(4):
                    term = jnp.where((c[axis] + 4 - k) % 4 == w, parts[k], term)
                total = total + term
            return total

        send_small(0)
        for p in range(3):
            qkv_second(p)
        o_copies = [None] * 3
        for p in range(3):
            out_sum(p)
            o_copies[p] = share(o_acc2[p], o_got[p], OUT_ORDERS[p][2])
        s_acc[1] = sum_small(0)
        send_small(1)
        qkv_second(3)
        qkv_second(4)
        swap.wait()
        g_norm = part[...] + got_part[...]
        scaled = g_norm * gain_ref[0:1, :]
        gt_ref[...] += (
            inv * scaled - inputs * (inv * inv * inv) * jnp.mean(scaled * inputs, axis=1, keepdims=True)
        )
        for p in range(3):
            qkv_third(p)
        s_acc[2] = sum_small(1)
        send_small(2)
        qkv_third(3)
        qkv_third(4)
        for p in range(3):
            for copy in o_copies[p]:
                copy.wait()
            rows = pl.ds(pl.multiple_of(c[OUT_ORDERS[p][2]] * 24, 8), 24)
            total = o_acc2[p][rows, :]
            for k in range(3):
                total = total + o_got[p][k]
            for j in range(2):
                go_ref[p * 2 + j] = total[:, j * 128 : (j + 1) * 128]
        for m in range(3):
            for copy in m_copies[m]:
                copy.wait()
            here = c[MLP_AXES[m][0]]
            m_outs[m][:, pl.ds(col_start(here), FC)] = acc2[m][pl.ds(pl.multiple_of(here * 24, 8), 24), :]
            for k in (1, 2, 3):
                m_outs[m][:, pl.ds(col_start((here + 4 - k) % 4), FC)] = m_got[m][k - 1]
        s_acc[3] = sum_small(2)
        send_small(3)
        for p in range(n_parts):
            qkv_out(p)
        s_out[...] = sum_small(3)

    rows = [rn for _, rn, _ in KV_CHUNK] * 2
    cols = [hi - lo for lo, hi, _ in QKV_PARTS]
    late = (tokens, g_mid)
    scratch = (
        [pltpu.VMEM((4, 384, 512), BF16)] * 3
        + [pltpu.VMEM((512, FC), BF16)] * 3
        + [pltpu.VMEM((4, 4, 4, 256, 128), BF16)]
        + [pltpu.VMEM((128, 1536), BF16)]
        + [pltpu.VMEM((96, FC), F32)] * 3
        + [pltpu.VMEM((96, 256), F32)] * 3
        + [pltpu.VMEM((8, 128, 96), F32), pltpu.VMEM((256, 128), F32)]
        + [pltpu.VMEM((4, 384, FC), BF16)] * 3
        + [pltpu.VMEM((2, 2, 192, FC), BF16)] * 3
        + [pltpu.VMEM((2, 192, FC), BF16)] * 3
        + [pltpu.VMEM((2, 2, 48, FC), BF16)] * 3
        + [pltpu.VMEM((2, 48, FC), BF16)] * 3
        + [pltpu.VMEM((4, 384, 256), BF16)]
        + [pltpu.VMEM((2, 2, 192, 256), BF16)] * 3
        + [pltpu.VMEM((2, 192, 256), BF16)] * 3
        + [pltpu.VMEM((3, 96, 256), BF16)] * 3
        + [pltpu.VMEM((2, 2, 2, 4, r, 128), BF16) for r in rows]
        + [pltpu.VMEM((2, 2, 4, r, 128), BF16) for r in rows]
        + [pltpu.VMEM((3, 4, r, 128), BF16) for r in rows]
        + [pltpu.VMEM((3, r, 128), BF16) for r in rows]
        + [pltpu.VMEM((3, 24, FC), F32)] * 3
        + [pltpu.VMEM((3, 24, 256), F32)] * 3
        + [pltpu.VMEM((3, 96, n), BF16) for n in cols]
        + [pltpu.VMEM((96, n), F32) for n in cols]
        + [pltpu.VMEM((3, 24, n), F32) for n in cols]
        + [
            pltpu.VMEM((4, SMALL, 128), F32),
            pltpu.VMEM((12, SMALL, 128), F32),
            pltpu.VMEM((128, 1024), BF16),
            pltpu.VMEM((128, 1536), F32),
            pltpu.VMEM((128, 1536), F32),
            DMA((7 + n_late + 8,)),
            DMA((224,)),
            DMA((224,)),
        ]
    )
    vm, sm, hbm = (pl.BlockSpec(memory_space=m) for m in (pltpu.VMEM, pltpu.SMEM, pl.ANY))
    f32 = lambda *s: jax.ShapeDtypeStruct(s, F32)
    shape = (f32(128, 1536), f32(6, 24, 128), f32(24, 128), f32(24, 128), f32(6, 24, 128), f32(SMALL, 128))
    shape = shape + (f32(24, 4480),) * 3
    return pl.pallas_call(
        body,
        out_shape=shape,
        in_specs=[sm] + [hbm] * (10 + n_late) + [vm] * 11,
        out_specs=(vm,) * 9,
        scratch_shapes=scratch,
        compiler_params=pltpu.CompilerParams(collective_id=2, has_side_effects=True, vmem_limit_bytes=VMEM_BYTES),
        name="backward",
    )(lengths, *xs_in, *gs_in, kv, wq.reshape(6, 4, 384, 128), wk.reshape(4, 384, 128), wv.reshape(4, 384, 128), *late, q, g, lse, delta, branch_t, attn_low, cos, sin, norm_t, gain, d_norm2)


def hand_out(*arrays):
    n = len(arrays)

    def body(*refs):
        ins, outs, held, sem = refs[:n], refs[n : 2 * n], refs[2 * n : 3 * n], refs[3 * n]
        to = [pltpu.make_async_copy(a, b, sem.at[i]) for i, (a, b) in enumerate(zip(ins, held))]
        back = [pltpu.make_async_copy(a, b, sem.at[n + i]) for i, (a, b) in enumerate(zip(held, outs))]
        for copy in to:
            copy.start()
        for i in range(n):
            to[i].wait()
            back[i].start()
        for copy in back:
            copy.wait()

    hbm = pl.BlockSpec(memory_space=pl.ANY)
    return pl.pallas_call(
        body,
        out_shape=tuple(jax.ShapeDtypeStruct(v.shape, v.dtype) for v in arrays),
        in_specs=[hbm] * n,
        out_specs=(hbm,) * n,
        scratch_shapes=[pltpu.VMEM(v.shape, v.dtype) for v in arrays] + [DMA((2 * n,))],
        compiler_params=pltpu.CompilerParams(vmem_limit_bytes=VMEM_BYTES),
        name="hand_out",
    )(*arrays)


def local(
    tokens, cotangent, lengths, norm1_gain, w_query, b_query, w_key, b_key, w_value, b_value, w_out,
    norm2_gain, w_gate, w_up, w_down,
):
    device = lax.axis_index("seq")
    core = lax.axis_index("tensor")
    wq = w_query.transpose(1, 0, 2)
    wk, wv = w_key.reshape(1536, 128), w_value.reshape(1536, 128)
    wo = w_out.reshape(768, 1536)
    gains = jnp.stack([norm1_gain, norm2_gain])

    (output, g_mid, branch_t, g_attn, delta, d_norm2, q, norm_t, cos, sin, attn_low, lse, *shared, kv) = forward(
        tokens, cotangent, lengths, gains, wq, wk, wv, b_query, b_key, b_value, wo, w_gate, w_up, w_down
    )
    grad_tokens, grad_wq, grad_wk, grad_wv, grad_wo, sums, grad_gate, grad_up, grad_down = backward(
        shared[:3], shared[3:], q, g_attn, kv, lse, delta, branch_t, attn_low, lengths,
        cos, sin, norm_t, wq, wk, wv, tokens, gains, g_mid, d_norm2,
    )
    output, grad_tokens, grad_wq, grad_wk, grad_wv, grad_wo, grad_gate, grad_up, grad_down = hand_out(
        output, grad_tokens, grad_wq, grad_wk, grad_wv, grad_wo, grad_gate, grad_up, grad_down
    )
    sums = sums.reshape(-1)
    grad_norm1 = lax.dynamic_slice(sums, (device * 24,), (24,))
    grad_norm2 = lax.dynamic_slice(sums, (1536 + device * 24,), (24,))
    bias = lax.dynamic_slice(sums.reshape(SMALL, 128), (24 + core * 8, device * 2), (8, 2))
    return (
        output,
        grad_tokens,
        grad_norm1,
        grad_wq.transpose(1, 0, 2),
        bias[:6],
        grad_wk.reshape(24, 1, 128),
        bias[6:7],
        grad_wv.reshape(24, 1, 128),
        bias[7:8],
        grad_wo.transpose(0, 2, 1),
        grad_norm2,
        grad_gate,
        grad_up,
        grad_down.T,
    )


def solution(mesh):
    in_specs = (
        P("seq", None), P("seq", None), P(), P(), P(None, "tensor", None), P("tensor", None),
        P(None, "tensor", None), P("tensor", None), P(None, "tensor", None), P("tensor", None),
        P("tensor", None, None), P(), P(None, "tensor"), P(None, "tensor"), P("tensor", None),
    )
    out_specs = (
        P("seq", None), P("seq", None), P("seq"), P("seq", "tensor", None), P("tensor", "seq"),
        P("seq", "tensor", None), P("tensor", "seq"), P("seq", "tensor", None), P("tensor", "seq"),
        P("tensor", None, "seq"), P("seq"), P("seq", "tensor"), P("seq", "tensor"), P("tensor", "seq"),
    )
    return jax.shard_map(local, mesh=mesh, in_specs=in_specs, out_specs=out_specs, check_vma=False)
```

```python
import math

import jax
import jax.numpy as jnp
from jax import lax
from jax.experimental import pallas as pl
from jax.experimental.pallas import tpu as pltpu
from jax.sharding import PartitionSpec as P

MESH = pl.DeviceIdType.MESH
F32 = jnp.float32
BF16 = jnp.bfloat16
VMEM_BYTES = 60 * 1024 * 1024
AXES = ("z", "x", "y")
STRIDE = {"z": 16, "x": 4, "y": 1}


def coords():
    s = lax.axis_index("seq")
    return {"z": s // 16, "x": (s // 4) % 4, "y": s % 4}


def peer(axis, k):
    s = lax.axis_index("seq")
    c = coords()[axis]
    return (s + STRIDE[axis] * ((c + k) % 4 - c), lax.axis_index("tensor"))


def partner():
    return (lax.axis_index("seq"), 1 - lax.axis_index("tensor"))


def barrier(axes=AXES, core=False):
    bar = pltpu.get_barrier_semaphore()
    ids = [peer(a, k) for a in axes for k in (1, 2, 3)]
    if core:
        ids.append(partner())
    for d in ids:
        pl.semaphore_signal(bar, inc=1, device_id=d, device_id_type=MESH)
    pl.semaphore_wait(bar, len(ids))


def remote(src, dst, send, recv, device):
    return pltpu.make_async_remote_copy(
        src_ref=src, dst_ref=dst, send_sem=send, recv_sem=recv, device_id=device, device_id_type=MESH
    )


DMA = pltpu.SemaphoreType.DMA


KV_CHUNK = (
    (0, 48, ("z", "x", "y")),
    (48, 48, ("x", "y", "z")),
    (96, 32, ("y", "z", "x")),
)


def kv_rows(kb, v):
    return pl.ds(pl.multiple_of((kb // 4) * 128 + v * 64 + (kb % 4) * Q_BLK, Q_BLK), Q_BLK)


def kv_index(done, c, r0, rn):
    return tuple(slice(None) if a in done else c[a] for a in AXES) + (pl.ds(r0, rn), slice(None))


def rope_tables(len_ref):
    lane = lax.broadcasted_iota(jnp.int32, (128, 128), 1)
    pos = lax.broadcasted_iota(jnp.int32, (128, 128), 0) * 64 + lax.axis_index("seq")
    rel = (pos - doc_bounds(pos, len_ref)).astype(F32)
    inv_freq = jnp.exp(-(2.0 * (lane % 64).astype(F32) / 128) * math.log(10000.0))
    angle = rel * inv_freq
    sin = jnp.sin(angle)
    return jnp.cos(angle), jnp.where(lane < 64, -sin, sin)


def swap_halves(v):
    return pltpu.roll(v, 64, 1)


Q_BLK = 16
BLK = Q_BLK * 64
SCALE = 1.0 / math.sqrt(128)
SCALE2 = SCALE / math.log(2.0)


def doc_bounds(pos, len_ref):
    start = jnp.zeros_like(pos)
    end = jnp.int32(0)
    for j in range(8):
        end = end + len_ref[j]
        start = jnp.where(pos >= end, end, start)
    return start


FC = 1152


def nt(a, b):
    return lax.dot_general(a, b, (((1,), (1,)), ((), ())), preferred_element_type=F32)


def mm(a, b):
    return jnp.dot(a, b, preferred_element_type=F32)


def col_start(c):
    return pl.multiple_of(jnp.minimum(c * FC, 4480 - FC), 128)


MLP_AXES = (("z", "x", "y"), ("x", "y", "z"), ("y", "z", "x"))


def in_order(v, order):
    place = {}
    rows = []
    for i in range(64):
        for n, a in enumerate(order):
            place[a] = (i // (16, 4, 1)[n]) % 4
        o = place["z"] * 16 + place["x"] * 4 + place["y"]
        rows.append(v[o * 24 : (o + 1) * 24])
    return jnp.concatenate(rows, axis=0)


def forward(tokens, cot, lengths, gains, wq, wk, wv, bq, bk, bv, w_out, w_gate, w_up, w_down):
    def body(len_ref, t_ref, c_ref, g_ref, wk_ref, wv_ref, bq_ref, bk_ref, bv_ref, wq_hbm, wo_hbm, wg_hbm, wu_hbm, wd_hbm,
             out_ref, gmid_ref, bt_ref, ga_ref, delta_ref, dn_ref, q_ref, nt1_ref, cos_out, sin_out, low_ref, lse_ref,
             x0, x1, x2, g0, g1, g2, kv_hbm,
             kv, wq_ref, at_ref, m_ref, l_ref, acc_ref, gh_ref,
             wo_ref, wg, wu, wd, got_br, acc, got, norm_ref, nt_ref, ct_ref, act, w_sem, loc, send, recv):
        xs, gs = (x0, x1, x2), (g0, g1, g2)
        c = coords()
        dev = lax.axis_index("seq")
        turn = c["z"] + c["x"] + c["y"]
        sems = iter(range(128))

        def load(j):
            cols = pl.ds(col_start((turn + j) % 4), FC)
            b = j % 2
            copies = [
                pltpu.make_async_copy(wg_hbm.at[:, cols], wg.at[b], w_sem.at[b, 0]),
                pltpu.make_async_copy(wu_hbm.at[:, cols], wu.at[b], w_sem.at[b, 1]),
                pltpu.make_async_copy(wd_hbm.at[cols, :], wd.at[b], w_sem.at[b, 2]),
            ]
            for copy in copies:
                copy.start()
            return copies

        def load_down(j):
            copy = pltpu.make_async_copy(wd_hbm.at[pl.ds(col_start((turn + j) % 4), FC), :], wd.at[j % 2], w_sem.at[j % 2, 2])
            copy.start()
            return copy

        def push(src, dst, device):
            n = next(sems)
            copy = remote(src, dst, send.at[n], recv.at[n], device)
            copy.start()
            return copy

        def keep(src, dst, n):
            copy = pltpu.make_async_copy(src, dst, loc.at[n])
            copy.start()
            return copy

        wq_load = keep(wq_hbm, wq_ref, 6)
        down = [load_down(0), load_down(1)]
        wo_load = keep(wo_hbm, wo_ref, 7)

        x = t_ref[...].astype(F32)
        inv = lax.rsqrt(jnp.mean(x * x, axis=1, keepdims=True) + 1e-06)
        normed = (x * inv * g_ref[0:1, :]).astype(BF16)
        cos, sin = rope_tables(len_ref)
        cos_out[...], sin_out[...] = cos, sin
        k_pre = mm(normed, wk_ref[...]) + bk_ref[...].astype(F32)
        v_low = (mm(normed, wv_ref[...]) + bv_ref[...].astype(F32)).astype(BF16)
        k_rot = (k_pre * cos + swap_halves(k_pre) * sin).astype(BF16)
        kv[c["z"], c["x"], c["y"]] = jnp.concatenate([k_rot[:64], v_low[:64], k_rot[64:], v_low[64:]], axis=0)
        barrier(core=True)
        kv_pending = [[] for _ in range(6)]

        def kv_wait(chunk):
            for p in range(chunk * 3, chunk * 3 + 3):
                for copy in kv_pending[p]:
                    copy.wait()
                kv_pending[p] = []

        def kv_stage(chunk, stage):
            for i, (r0, rn, order) in enumerate(KV_CHUNK):
                p, r0 = chunk * 3 + i, r0 + chunk * 128
                for copy in kv_pending[p]:
                    copy.wait()
                idx = kv_index(order[:stage], c, r0, rn)
                kv_pending[p] = [push(kv.at[idx], kv.at[idx], peer(order[stage], k)) for k in (1, 2, 3)]

        kv_stage(0, 0)
        kv_stage(1, 0)
        wq_load.wait()
        for h in range(6):
            q = mm(normed, wq_ref[h]) + bq_ref[h : h + 1, :].astype(F32)
            q = (q * cos + swap_halves(q) * sin).astype(BF16)
            q_ref[:, h * Q_BLK : (h + 1) * Q_BLK, :] = q.reshape(8, Q_BLK, 128)

        def g_hidden(j):
            down[j].wait()
            gh_ref[j] = nt(c_ref[...], wd[j % 2])
            if j < 2:
                down.append(load_down(j + 2))
            else:
                loads.append(load(j - 2))

        loads = []
        kv_stage(0, 1)
        kv_stage(1, 1)
        g_hidden(0)
        nt1_ref[...] = normed.T
        g_hidden(1)
        kv_stage(0, 2)
        g_hidden(2)
        g_hidden(3)
        ct_ref[...] = c_ref[...].T.reshape(4, 384, 128)
        own = [keep(ct_ref, x2.at[:, :, pl.ds(0, 128)], 3)]
        kv_wait(0)
        kv_stage(1, 2)
        later = [push(ct_ref, x2.at[:, :, pl.ds(k * 128, 128)], peer("y", k)) for k in (1, 2, 3)]

        row_off = (lax.broadcasted_iota(jnp.int32, (96, 1), 0) % Q_BLK) * 64 + dev
        col = lax.broadcasted_iota(jnp.int32, (96, BLK), 1)
        key_off = (col % Q_BLK) * 64 + col // Q_BLK

        def attend(qb, lo, hi, carry, diagonal):
            q_blk = q_ref[qb]
            pos_q = row_off + qb * BLK
            start_q = doc_bounds(pos_q, len_ref)

            def block(kb, carry, causal):
                m, l, acc = carry
                k_blk = kv[:, :, :, kv_rows(kb, 0), :].reshape(BLK, 128)
                v_blk = kv[:, :, :, kv_rows(kb, 1), :].reshape(BLK, 128)
                pos_k = key_off + kb * BLK
                vis = pos_k >= start_q
                if causal:
                    vis = vis & (pos_k <= pos_q)
                s = jnp.where(vis, nt(q_blk, k_blk) * SCALE2, -1e30)
                m_new = jnp.maximum(m, jnp.max(s, axis=1, keepdims=True))
                p = jnp.exp2(s - m_new)
                a = jnp.exp2(m - m_new)
                return m_new, l * a + jnp.sum(p, axis=1, keepdims=True), acc * a + mm(p.astype(BF16), v_blk)

            carry = lax.fori_loop(lo, hi, lambda kb, carry: block(kb, carry, False), carry)
            return block(qb, carry, True) if diagonal else carry

        def attend_end(qb, carry):
            m, l, acc = carry
            attn = acc / l
            at_ref[qb] = attn
            low = attn.astype(BF16)
            for h in range(6):
                rows = pl.ds(pl.multiple_of(qb * Q_BLK, Q_BLK), Q_BLK)
                low_ref[rows, h * 128 : (h + 1) * 128] = low[h * Q_BLK : (h + 1) * Q_BLK]
            lse_ref[qb] = jnp.broadcast_to(m + jnp.log2(l), (96, 128)).T[0:1]

        init = (jnp.full((96, 1), -1e30, F32), jnp.zeros((96, 1), F32), jnp.zeros((96, 128), F32))

        def upper(qb, _):
            m_ref[qb - 4], l_ref[qb - 4], acc_ref[qb - 4] = attend(qb, 0, 4, init, False)
            return 0

        def whole(qb, _):
            attend_end(qb, attend(qb, 0, qb, init, True))
            return 0

        def rest(qb, _):
            attend_end(qb, attend(qb, 4, qb, (m_ref[qb - 4], l_ref[qb - 4], acc_ref[qb - 4]), True))
            return 0

        out_kv = [keep(kv.at[:, :, :, pl.ds(0, 128), :], kv_hbm.at[:, :, :, pl.ds(0, 128), :], 8)]
        lax.fori_loop(0, 4, whole, 0)
        lax.fori_loop(4, 8, upper, 0)
        kv_wait(1)
        out_kv.append(keep(kv.at[:, :, :, pl.ds(128, 128), :], kv_hbm.at[:, :, :, pl.ds(128, 128), :], 9))
        lax.fori_loop(4, 8, rest, 0)
        wo_load.wait()
        ex = []
        for half in range(2):
            cols = slice(half * 768, (half + 1) * 768)
            acc[half, :, 0:768] = mm(low_ref[...], wo_ref[:, cols])
            ex.append(push(acc.at[half, :, pl.ds(0, 768)], got_br.at[half], partner()))
        for copy in ex:
            copy.wait()
        mid = t_ref[...].astype(F32) + jnp.concatenate([acc[h, :, 0:768] + got_br[h] for h in range(2)], axis=1)
        out_ref[...] = mid
        inv = lax.rsqrt(jnp.mean(mid * mid, axis=1, keepdims=True) + 1e-06)
        normed = (mid * inv * g_ref[1:2, :]).astype(BF16)
        norm_ref[...] = normed
        turned = normed.astype(F32).T
        for m in range(2):
            nt_ref[m] = in_order(turned, MLP_AXES[m][1:] + MLP_AXES[m][:1]).astype(BF16).reshape(4, 384, 128)
        own.append(keep(nt_ref.at[0], x0.at[:, :, pl.ds(0, 128)], 4))
        own.append(keep(nt_ref.at[1], x1.at[:, :, pl.ds(0, 128)], 5))
        for k in (1, 2, 3):
            for m, w in ((0, "z"), (1, "x")):
                later.append(push(nt_ref.at[m], xs[m].at[:, :, pl.ds(k * 128, 128)], peer(w, k)))

        lane = lax.broadcasted_iota(jnp.int32, (128, FC), 1)
        for j in range(4):
            b = j % 2
            d = (turn + j) % 4
            for copy in loads[j]:
                copy.wait()
            n = norm_ref[...]
            gate = mm(n, wg[b])
            up = mm(n, wu[b])
            gh = gh_ref[j]
            sig = 1.0 / (1.0 + jnp.exp(-gate))
            silu = gate * sig
            hidden = (silu * up).astype(BF16)
            g_gate = (gh * up * sig * (1.0 + gate * (1.0 - sig))).astype(BF16)
            g_up = (gh * silu).astype(BF16)
            vals = (g_gate, g_up, hidden)
            for m in range(3):
                act[m, j] = vals[m]
            twice = (lane < 128) & (d == 3)
            zero = jnp.zeros((128, FC), BF16)
            hidden, g_gate, g_up = (jnp.where(twice, zero, v) for v in (hidden, g_gate, g_up))
            add_g = nt(g_gate, wg[b]) + nt(g_up, wu[b])
            acc[1] = add_g if j == 0 else acc[1] + add_g
            if j == 3:
                ex = [push(acc.at[1], got.at[1], partner())]
            add_o = mm(hidden, wd[b])
            acc[0] = add_o if j == 0 else acc[0] + add_o
            if j + 2 < 4:
                loads.append(load(j + 2))
            for m in range(3):
                w = MLP_AXES[m][0]
                k = (d + 4 - c[w]) % 4
                slot = pl.ds(pl.multiple_of(k * 128, 128), 128)

                @pl.when(k == 0)
                def _():
                    pltpu.make_async_copy(act.at[m, j], gs[m].at[pl.ds(0, 128), :], loc.at[m]).start()

                @pl.when(k != 0)
                def _():
                    remote(
                        act.at[m, j], gs[m].at[slot, :], send.at[96 + m * 4 + j], recv.at[96 + m * 4 + k], peer(w, k)
                    ).start()

        ex.append(push(acc.at[0], got.at[0], partner()))
        dn_ref[...] = jnp.sum(acc[1] * out_ref[...] * inv, axis=0, keepdims=True)
        cot_f = c_ref[...].astype(F32)
        ex[0].wait()
        gn = acc[1] + got[1]
        mid = out_ref[...]
        scaled = gn * g_ref[1:2, :]
        g_mid = cot_f + (inv * scaled - mid * (inv * inv * inv) * jnp.mean(scaled * mid, axis=1, keepdims=True))
        gmid_ref[...] = g_mid
        branch_low = g_mid.astype(BF16)
        bt_ref[...] = branch_low.T
        g_attn = nt(branch_low, wo_ref[...]).astype(BF16)
        for h in range(6):
            ga_ref[:, h * Q_BLK : (h + 1) * Q_BLK, :] = g_attn[:, h * 128 : (h + 1) * 128].reshape(8, Q_BLK, 128)
        for qb in range(8):
            delta_ref[qb] = jnp.sum((ga_ref[qb].astype(F32) * at_ref[qb]).T, axis=0, keepdims=True)
        ex[1].wait()
        out_ref[...] += acc[0] + got[0]
        for copy in later + own + out_kv:
            copy.wait()
        for m in range(3):
            w = MLP_AXES[m][0]
            pltpu.make_async_copy(act.at[m, 0], gs[m].at[pl.ds(0, 128), :], loc.at[m]).wait()
            for j in range(4):
                k = ((turn + j) % 4 + 4 - c[w]) % 4

                @pl.when(k != 0)
                def _():
                    slot = pl.ds(pl.multiple_of(k * 128, 128), 128)
                    remote(
                        act.at[m, j], gs[m].at[slot, :], send.at[96 + m * 4 + j], recv.at[96 + m * 4 + k], peer(w, k)
                    ).wait()

    f32 = lambda *s: jax.ShapeDtypeStruct(s, F32)
    b16 = lambda *s: jax.ShapeDtypeStruct(s, BF16)
    vm, sm, hbm = (pl.BlockSpec(memory_space=m) for m in (pltpu.VMEM, pltpu.SMEM, pl.ANY))
    held = [(6, 1536, 128, BF16), (8, 96, 128, F32), (4, 96, 1, F32), (4, 96, 1, F32), (4, 96, 128, F32)]
    held += [(4, 128, FC, F32), (768, 1536, BF16), (2, 1536, FC, BF16), (2, 1536, FC, BF16), (2, FC, 1536, BF16)]
    held += [(2, 128, 768, F32), (2, 128, 1536, F32), (2, 128, 1536, F32), (128, 1536, BF16)]
    held += [(2, 4, 384, 128, BF16), (4, 384, 128, BF16), (3, 4, 128, FC, BF16)]
    return pl.pallas_call(
        body,
        out_shape=(f32(128, 1536), f32(128, 1536), b16(1536, 128), b16(8, 96, 128), f32(8, 1, 96), f32(1, 1536))
        + (b16(8, 96, 128), b16(1536, 128), f32(128, 128), f32(128, 128), b16(128, 768), f32(8, 1, 96))
        + (b16(4, 384, 512),) * 3
        + (b16(512, FC),) * 3
        + (b16(4, 4, 4, 256, 128),),
        in_specs=[sm] + [vm] * 8 + [hbm] * 5,
        out_specs=(vm,) * 12 + (hbm,) * 7,
        scratch_shapes=[pltpu.VMEM((4, 4, 4, 256, 128), BF16)]
        + [pltpu.VMEM(v[:-1], v[-1]) for v in held]
        + [DMA((2, 3)), DMA((10,)), DMA((112,)), DMA((112,))],
        compiler_params=pltpu.CompilerParams(collective_id=4, has_side_effects=True, vmem_limit_bytes=VMEM_BYTES),
        name="forward",
    )(lengths, tokens, cot, gains, wk, wv, bq, bk, bv, wq, w_out, w_gate, w_up, w_down)


OUT_ORDERS = (("z", "x", "y"), ("x", "y", "z"), ("y", "z", "x"))
QKV_PARTS = (
    (0, 256, ("z", "x", "y")),
    (256, 512, ("x", "y", "z")),
    (512, 768, ("y", "z", "x")),
    (768, 896, ("z", "x", "y")),
    (896, 1024, ("x", "y", "z")),
)
SMALL = 40


def slab_products(buf, left, rhs, order):
    def blocks(v, places):
        return jnp.concatenate([v[o * 24 : (o + 1) * 24] for o in places], axis=0)

    if order[0] == "z":
        for z in range(4):
            buf[z] = mm(left[z * 384 : (z + 1) * 384, :], rhs).astype(BF16)
    elif order[0] == "x":
        for x in range(4):
            lhs = jnp.concatenate([left[z * 384 + x * 96 : z * 384 + (x + 1) * 96, :] for z in range(4)], axis=0)
            buf[x] = blocks(mm(lhs, rhs), [z * 4 + y for y in range(4) for z in range(4)]).astype(BF16)
    else:
        for z in range(4):
            v = blocks(mm(left[z * 384 : (z + 1) * 384, :], rhs), [x * 4 + y for y in range(4) for x in range(4)])
            v = v.astype(BF16)
            for y in range(4):
                buf[y, z * 96 : (z + 1) * 96] = v[y * 96 : (y + 1) * 96]


def near(u):
    return u + 1 - 2 * (u % 2)


def far(u):
    return 3 - u


def over(u):
    return (u + 2) % 4


class Halves:
    def __init__(self, push, axis, c, slab, got_first, got_second):
        self.push, self.slab, self.u = push, slab, c[axis]
        self.got_first, self.got_second = got_first, got_second
        self.to = lambda place: peer(axis, place + 4 - c[axis])
        self.one, self.two = {}, []

    def ready(self, which):
        u = self.u
        if which == "over":
            self.one[0, 0] = self.push(self.slab(over(u), 0), self.got_first(0, 0), self.to(near(u)))
            self.one[1, 0] = self.push(self.slab(over(u), 1), self.got_first(1, 0), self.to(far(u)))
        elif which == "near":
            self.one[0, 1] = self.push(self.slab(near(u), 0), self.got_first(0, 1), self.to(near(u)))
        elif which == "far":
            self.one[1, 1] = self.push(self.slab(far(u), 1), self.got_first(1, 1), self.to(far(u)))

    def first(self):
        for which in ("over", "near", "far"):
            self.ready(which)

    def second(self):
        u = self.u
        for h, place in ((0, far(u)), (1, near(u))):
            self.one[h, 0].wait()
            at = self.slab(place, h)
            at[...] = (at[...].astype(F32) + self.got_first(h, 0)[...].astype(F32)).astype(BF16)
            self.two.append(self.push(at, self.got_second(h), self.to(place)))

    def final(self):
        for h in range(2):
            self.one[h, 1].wait()
            self.two[h].wait()
            at = self.slab(self.u, h)
            at[...] = (
                at[...].astype(F32) + self.got_first(h, 1)[...].astype(F32) + self.got_second(h)[...].astype(F32)
            ).astype(BF16)


def sum_first(buf, got, copies, own):
    for copy in copies:
        copy.wait()
    total = buf[own].astype(F32)
    for k in range(3):
        total = total + got[k][...].astype(F32)
    buf[own] = total.astype(BF16)


def backward(xs_in, gs_in, q, g, kv, lse, delta, branch_t, attn_low, lengths,
             cos, sin, norm_t, wq, wk, wv, tokens, gain, g_mid, d_norm2):
    n_late = 2

    def body(*refs):
        r = list(refs)
        take = lambda n: [r.pop(0) for _ in range(n)]
        (len_ref,), xs_hbm, gs_hbm, (kv_hbm, *w_hbm), late = take(1), take(3), take(3), take(4), take(n_late)
        q_ref, g_ref, lse_ref, delta_ref, bt_ref, a_ref, cos_ref, sin_ref, nt_ref, gain_ref, dn2_ref = take(11)
        gt_ref, gq_ref, gk_ref, gv_ref, go_ref, s_out = take(6)
        m_outs = take(3)
        xs, gs, (dkv,), (t_ref,) = take(3), take(3), take(1), take(1)
        held = (t_ref, gt_ref)
        acc2, o_acc2, (dq_ref, own_ref) = take(3), take(3), take(2)
        sendbuf, r1, r2, t1, t2 = take(3), take(3), take(3), take(3), take(3)
        o_buf, o_r1, o_r2, o_got2 = take(1), take(3), take(3), take(3)
        kv1, kv1b, kv2, kv3 = take(6), take(6), take(6), take(6)
        m_got, o_got = take(3), take(3)
        n_parts = len(QKV_PARTS)
        q_got2, q_acc2, q_got3 = (take(n_parts) for _ in range(3))
        o_buf = [xs[2].at[:, :, 0:256], xs[2].at[:, :, 256:512], o_buf[0]]
        room = ((0, 0, 256), (0, 256, 512), (1, 0, 256), (1, 256, 384), (1, 384, 512))
        q_buf = [xs[m].at[:, :, lo:hi] for m, lo, hi in room]
        room = ((0, 0, 256), (1, 0, 256), (2, 0, 256), (0, 768, 128), (1, 768, 128))
        q_got1 = [
            [gs[m].at[192 * (k % 2) : 192 * (k % 2) + 192, lo + k // 2 * n : lo + (k // 2 + 1) * n] for k in range(6)]
            for m, lo, n in room[:3]
        ] + [[gs[m].at[0:384, lo + k * n : lo + (k + 1) * n] for k in range(3)] for m, lo, n in room[3:]]
        s_acc, s_got, gp_ref, part, got_part = take(5)
        loc, send, recv = take(3)
        c = coords()
        loads = [pltpu.make_async_copy(a, b, loc.at[i]) for i, (a, b) in enumerate(
            ((xs_hbm[0], xs[0]), (gs_hbm[0], gs[0]), (xs_hbm[2], xs[2]), (gs_hbm[2], gs[2]),
             (xs_hbm[1], xs[1]), (gs_hbm[1], gs[1]), (kv_hbm, dkv), *zip(late, held)))]
        for copy in loads:
            copy.start()
        barrier(core=True)
        sems = iter(range(256))

        def push(src, dst, device):
            n = next(sems)
            copy = remote(src, dst, send.at[n], recv.at[n], device)
            copy.start()
            return copy

        def mlp_slab(m):
            return lambda u, h: sendbuf[m].at[u, pl.ds(192 * h, 192), :]

        mlp_one = [
            Halves(push, MLP_AXES[m][1], c, mlp_slab(m), lambda h, i, m=m: r1[m].at[h, i], lambda h, m=m: r2[m].at[h])
            for m in range(3)
        ]

        def mlp_rows(m):
            own = sendbuf[m].at[c[MLP_AXES[m][1]]]
            return lambda u, h: own.at[pl.ds(pl.multiple_of(u * 96 + h * 48, 16), 48), :]

        mlp_two = [
            Halves(push, MLP_AXES[m][2], c, mlp_rows(m), lambda h, i, m=m: t1[m].at[h, i], lambda h, m=m: t2[m].at[h])
            for m in range(3)
        ]

        for name, place in (("over", over), ("near", near), ("far", far), ("own", lambda v: v)):
            for i, m in enumerate((0, 2, 1)):
                if name == "over":
                    loads[2 * i].wait()
                    loads[2 * i + 1].wait()
                u = place(c[MLP_AXES[m][1]])
                x = xs[m][u]
                sendbuf[m][u] = mm(x, gs[m][...]).astype(BF16)
                mlp_one[m].ready(name)

        def buf_slab(buf):
            return lambda u, h: buf.at[u, pl.ds(192 * h, 192), :]

        out_one = [
            Halves(push, OUT_ORDERS[p][0], c, buf_slab(o_buf[p]), lambda h, i, p=p: o_r1[p].at[h, i], lambda h, p=p: o_r2[p].at[h])
            for p in range(3)
        ]
        o_second = [[], [], []]

        def out_second(p):
            order = OUT_ORDERS[p]
            out_one[p].final()
            for k in (1, 2, 3):
                rows = pl.ds(pl.multiple_of(((c[order[1]] + k) % 4) * 96, 32), 96)
                o_second[p].append(push(o_buf[p].at[c[order[0]], rows, :], o_got2[p].at[k - 1], peer(order[1], k)))

        def out_sum(p):
            order = OUT_ORDERS[p]
            for copy in o_second[p]:
                copy.wait()
            rows = pl.ds(pl.multiple_of(c[order[1]] * 96, 32), 96)
            total = o_buf[p][c[order[0]], rows, :].astype(F32)
            for k in range(3):
                total = total + o_got2[p][k].astype(F32)
            o_acc2[p][...] = total

        loads[6].wait()
        dev = lax.axis_index("seq")
        row = lax.broadcasted_iota(jnp.int32, (BLK, 96), 0)
        key_off = (row % Q_BLK) * 64 + row // Q_BLK
        q_off = (lax.broadcasted_iota(jnp.int32, (1, 96), 1) % Q_BLK) * 64 + dev
        dq_ref[...] = jnp.zeros_like(dq_ref)

        def k_step(kb, _):
            k_blk = dkv[:, :, :, kv_rows(kb, 0), :].reshape(BLK, 128)
            v_blk = dkv[:, :, :, kv_rows(kb, 1), :].reshape(BLK, 128)
            k_t = k_blk.T
            pos_k = key_off + kb * BLK

            def pair(qb, carry, causal):
                dk, dv = carry
                q_blk, g_blk = q_ref[qb], g_ref[qb]
                pos_q = q_off + qb * BLK
                vis = pos_k >= doc_bounds(pos_q, len_ref)
                if causal:
                    vis = vis & (pos_k <= pos_q)
                s = nt(k_blk, q_blk)
                p = jnp.where(vis, jnp.exp2(s * SCALE2 - lse_ref[qb]), 0.0)
                gp = nt(v_blk, g_blk)
                ds = (p * (gp - delta_ref[qb])).astype(BF16)
                dq_ref[qb] += mm(k_t, ds)
                dk = dk + mm(ds, q_blk)
                dv = dv + mm(p.astype(BF16), g_blk)
                return dk, dv

            zero = jnp.zeros((BLK, 128), F32)
            carry = pair(kb, (zero, zero), True)
            dk, dv = lax.fori_loop(kb + 1, 8, lambda qb, carry: pair(qb, carry, False), carry)
            dkv[:, :, :, kv_rows(kb, 0), :] = (dk * SCALE).astype(BF16).reshape(4, 4, 4, Q_BLK, 128)
            dkv[:, :, :, kv_rows(kb, 1), :] = dv.astype(BF16).reshape(4, 4, 4, Q_BLK, 128)
            return 0

        kv_pending = [[] for _ in range(6)]
        kv_parts = [(r0 + 128 * chunk, rn, order) for chunk in range(2) for r0, rn, order in KV_CHUNK]

        def kv_slab(p):
            r0, rn, order = kv_parts[p]
            rest = [a for a in AXES if a != order[0]]

            def slab(u, h):
                where = {order[0]: u, rest[0]: pl.ds(2 * h, 2), rest[1]: slice(None)}
                return dkv.at[where["z"], where["x"], where["y"], pl.ds(r0, rn), :]

            return slab

        kv_one = [
            Halves(push, kv_parts[p][2][0], c, kv_slab(p), lambda h, i, p=p: kv1[p].at[h, i], lambda h, p=p: kv1b[p].at[h])
            for p in range(6)
        ]

        def kv_halves(chunk, step):
            for p in range(chunk * 3, chunk * 3 + 3):
                getattr(kv_one[p], step)()

        def kv_stage(chunk, stage):
            got = (None, kv2, kv3)
            for p in range(chunk * 3, chunk * 3 + 3):
                r0, rn, order = kv_parts[p]
                if stage == 1:
                    kv_one[p].final()
                else:
                    for copy in kv_pending[p]:
                        copy.wait()
                    kv_pending[p] = []
                    mine = kv_index(order[stage:], c, r0, rn)
                    own = dkv[mine].astype(F32)
                    for k in range(3):
                        own = own + got[stage - 1][p][k].astype(F32)
                    if stage == 3:
                        own_ref[pl.ds(r0, rn), :] = own
                        continue
                    dkv[mine] = own.astype(BF16)
                for k in (1, 2, 3):
                    cc = dict(c)
                    cc[order[stage]] = (c[order[stage]] + k) % 4
                    src = dkv.at[kv_index(order[stage + 1 :], cc, r0, rn)]
                    kv_pending[p].append(push(src, got[stage][p].at[k - 1], peer(order[stage], k)))

        def share(acc, got, axis):
            copies = []
            for k in (1, 2, 3):
                rows = pl.ds(pl.multiple_of(((c[axis] + k) % 4) * 24, 8), 24)
                copies.append(push(acc.at[rows, :], got.at[k - 1], peer(axis, k)))
            return copies

        q_copies = [[] for _ in QKV_PARTS]
        q_one = [
            Halves(push, QKV_PARTS[p][2][0], c, buf_slab(q_buf[p]), lambda h, i, p=p: q_got1[p][2 * h + i], lambda h, p=p: q_got1[p][4 + h])
            for p in range(3)
        ]

        def qkv_first(p):
            lo, hi, order = QKV_PARTS[p]
            slab_products(q_buf[p], nt_ref, gp_ref[:, lo:hi], order)
            if p < 3:
                q_one[p].first()
                return
            for k in (1, 2, 3):
                there = (c[order[0]] + k) % 4
                q_copies[p].append(push(q_buf[p].at[there], q_got1[p][k - 1], peer(order[0], k)))

        def qkv_second(p):
            order = QKV_PARTS[p][2]
            if p < 3:
                q_one[p].final()
            else:
                sum_first(q_buf[p], q_got1[p], q_copies[p], c[order[0]])
            q_copies[p] = []
            for k in (1, 2, 3):
                rows = pl.ds(pl.multiple_of(((c[order[1]] + k) % 4) * 96, 32), 96)
                q_copies[p].append(push(q_buf[p].at[c[order[0]], rows, :], q_got2[p].at[k - 1], peer(order[1], k)))

        def qkv_third(p):
            order = QKV_PARTS[p][2]
            for copy in q_copies[p]:
                copy.wait()
            rows = pl.ds(pl.multiple_of(c[order[1]] * 96, 32), 96)
            total = q_buf[p][c[order[0]], rows, :].astype(F32)
            for k in range(3):
                total = total + q_got2[p][k].astype(F32)
            q_acc2[p][...] = total
            q_copies[p] = share(q_acc2[p], q_got3[p], order[2])

        def qkv_out(p):
            lo, hi, order = QKV_PARTS[p]
            for copy in q_copies[p]:
                copy.wait()
            total = q_acc2[p][pl.ds(pl.multiple_of(c[order[2]] * 24, 8), 24), :]
            for k in range(3):
                total = total + q_got3[p][k]
            for j in range(lo // 128, hi // 128):
                v = total[:, j * 128 - lo : (j + 1) * 128 - lo]
                if j < 6:
                    gq_ref[j] = v
                elif j == 6:
                    gk_ref[...] = v
                else:
                    gv_ref[...] = v

        m_copies = [None] * 3

        def mlp_third(m):
            mlp_two[m].final()
            rows = pl.ds(pl.multiple_of(c[MLP_AXES[m][2]] * 96, 32), 96)
            acc2[m][...] = sendbuf[m][c[MLP_AXES[m][1]], rows, :].astype(F32)
            m_copies[m] = share(acc2[m], m_got[m], MLP_AXES[m][0])

        lax.fori_loop(4, 8, k_step, 0)
        kv_halves(1, "first")
        mlp_one[0].second()
        lax.fori_loop(0, 1, k_step, 0)
        mlp_one[2].second()
        mlp_one[1].second()
        kv_halves(1, "second")
        lax.fori_loop(1, 2, k_step, 0)
        for p, order in enumerate(OUT_ORDERS):
            slab_products(o_buf[p], bt_ref, a_ref[:, p * 256 : (p + 1) * 256], order)
            out_one[p].first()
        mlp_one[0].final()
        mlp_two[0].first()
        kv_stage(1, 1)
        lax.fori_loop(2, 3, k_step, 0)
        for m in (2, 1):
            mlp_one[m].final()
            mlp_two[m].first()
        kv_stage(1, 2)
        lax.fori_loop(3, 4, k_step, 0)
        kv_halves(0, "first")
        mlp_two[0].second()
        kv_stage(1, 3)

        cos_t, sin_t = cos_ref[...], sin_ref[...]
        for qb in range(8):
            dq = dq_ref[qb].T * SCALE
            rows = slice(qb * Q_BLK, (qb + 1) * Q_BLK)
            cs, sn = cos_t[rows], sin_t[rows]
            for h in range(6):
                v = dq[h * Q_BLK : (h + 1) * Q_BLK]
                gp_ref[rows, h * 128 : (h + 1) * 128] = (v * cs - swap_halves(v) * sn).astype(BF16)
        kv_halves(0, "second")
        for p in range(3):
            qkv_first(p)
        kv_stage(0, 1)
        for m in (2, 1):
            mlp_two[m].second()
        for p in range(3):
            out_one[p].second()
        kv_stage(0, 2)
        for m in (0, 2, 1):
            mlp_third(m)
        w_ref = [sendbuf[0].at[:, :, h * 128 : (h + 1) * 128] for h in range(8)]
        w_from = [w_hbm[0].at[h] for h in range(6)] + [w_hbm[1], w_hbm[2]]
        w_loads = [pltpu.make_async_copy(w_from[h], w_ref[h], loc.at[7 + n_late + h]) for h in range(8)]
        for copy in w_loads:
            copy.start()

        def back_through(lo, hi):
            total = nt(gp_ref[:, lo * 128 : (lo + 1) * 128], w_ref[lo][...].reshape(1536, 128))
            for h in range(lo + 1, hi):
                total = total + nt(gp_ref[:, h * 128 : (h + 1) * 128], w_ref[h][...].reshape(1536, 128))
            return total

        kv_stage(0, 3)

        dk = jnp.concatenate([own_ref[0:64, :], own_ref[128:192, :]], axis=0)
        gp_ref[:, 768:896] = (dk * cos_t - swap_halves(dk) * sin_t).astype(BF16)
        gp_ref[:, 896:] = jnp.concatenate([own_ref[64:128, :], own_ref[192:256, :]], axis=0).astype(BF16)
        qkv_first(3)
        qkv_first(4)
        for p in range(3):
            q_one[p].second()
        for p in range(3):
            out_second(p)
        for copy in loads[7:] + w_loads:
            copy.wait()
        part[...] = back_through(0, 8)
        swap = push(part, got_part, partner())

        inputs = t_ref[...].astype(F32)
        inv = lax.rsqrt(jnp.mean(inputs * inputs, axis=1, keepdims=True) + 1e-06)
        d_norm1 = jnp.sum(part[...] * inputs * inv, axis=0, keepdims=True)
        d_bias = jnp.sum(gp_ref[...].astype(F32), axis=0, keepdims=True)
        core = lax.axis_index("tensor")
        for j in range(12):
            s_acc[0, j : j + 1, :] = d_norm1[:, j * 128 : (j + 1) * 128]
            s_acc[0, 12 + j : 13 + j, :] = dn2_ref[:, j * 128 : (j + 1) * 128]
        for j in range(8):
            v = d_bias[:, j * 128 : (j + 1) * 128]
            s_acc[0, 24 + j : 25 + j, :] = jnp.where(core == 0, v, 0.0)
            s_acc[0, 32 + j : 33 + j, :] = jnp.where(core == 1, v, 0.0)
        s_pending = []

        def send_small(stage):
            peers = [partner()] if stage == 0 else [peer(AXES[stage - 1], k) for k in (1, 2, 3)]
            for i, d in enumerate(peers):
                s_pending.append(push(s_acc.at[stage], s_got.at[stage * 3 + i], d))

        def sum_small(stage):
            for copy in s_pending:
                copy.wait()
            s_pending.clear()
            if stage == 0:
                return s_acc[0] + s_got[0]
            axis = AXES[stage - 1]
            parts = [s_acc[stage]] + [s_got[stage * 3 + k] for k in range(3)]
            total = jnp.zeros_like(parts[0])
            for w in range(4):
                term = jnp.zeros_like(total)
                for k in range(4):
                    term = jnp.where((c[axis] + 4 - k) % 4 == w, parts[k], term)
                total = total + term
            return total

        send_small(0)
        qkv_second(3)
        qkv_second(4)
        for p in range(3):
            qkv_second(p)
        s_acc[1] = sum_small(0)
        send_small(1)
        o_copies = [None] * 3
        for p in range(3):
            out_sum(p)
            o_copies[p] = share(o_acc2[p], o_got[p], OUT_ORDERS[p][2])
        swap.wait()
        g_norm = part[...] + got_part[...]
        scaled = g_norm * gain_ref[0:1, :]
        gt_ref[...] += (
            inv * scaled - inputs * (inv * inv * inv) * jnp.mean(scaled * inputs, axis=1, keepdims=True)
        )
        qkv_third(3)
        qkv_third(4)
        s_acc[2] = sum_small(1)
        send_small(2)
        for p in range(3):
            qkv_third(p)
        for p in range(3):
            for copy in o_copies[p]:
                copy.wait()
            rows = pl.ds(pl.multiple_of(c[OUT_ORDERS[p][2]] * 24, 8), 24)
            total = o_acc2[p][rows, :]
            for k in range(3):
                total = total + o_got[p][k]
            for j in range(2):
                go_ref[p * 2 + j] = total[:, j * 128 : (j + 1) * 128]
        for m in range(3):
            for copy in m_copies[m]:
                copy.wait()
            here = c[MLP_AXES[m][0]]
            m_outs[m][:, pl.ds(col_start(here), FC)] = acc2[m][pl.ds(pl.multiple_of(here * 24, 8), 24), :]
            for k in (1, 2, 3):
                m_outs[m][:, pl.ds(col_start((here + 4 - k) % 4), FC)] = m_got[m][k - 1]
        s_acc[3] = sum_small(2)
        send_small(3)
        for p in range(n_parts):
            qkv_out(p)
        s_out[...] = sum_small(3)

    rows = [rn for _, rn, _ in KV_CHUNK] * 2
    cols = [hi - lo for lo, hi, _ in QKV_PARTS]
    late = (tokens, g_mid)
    scratch = (
        [pltpu.VMEM((4, 384, 512), BF16)] * 3
        + [pltpu.VMEM((512, FC), BF16)] * 3
        + [pltpu.VMEM((4, 4, 4, 256, 128), BF16)]
        + [pltpu.VMEM((128, 1536), BF16)]
        + [pltpu.VMEM((96, FC), F32)] * 3
        + [pltpu.VMEM((96, 256), F32)] * 3
        + [pltpu.VMEM((8, 128, 96), F32), pltpu.VMEM((256, 128), F32)]
        + [pltpu.VMEM((4, 384, FC), BF16)] * 3
        + [pltpu.VMEM((2, 2, 192, FC), BF16)] * 3
        + [pltpu.VMEM((2, 192, FC), BF16)] * 3
        + [pltpu.VMEM((2, 2, 48, FC), BF16)] * 3
        + [pltpu.VMEM((2, 48, FC), BF16)] * 3
        + [pltpu.VMEM((4, 384, 256), BF16)]
        + [pltpu.VMEM((2, 2, 192, 256), BF16)] * 3
        + [pltpu.VMEM((2, 192, 256), BF16)] * 3
        + [pltpu.VMEM((3, 96, 256), BF16)] * 3
        + [pltpu.VMEM((2, 2, 2, 4, r, 128), BF16) for r in rows]
        + [pltpu.VMEM((2, 2, 4, r, 128), BF16) for r in rows]
        + [pltpu.VMEM((3, 4, r, 128), BF16) for r in rows]
        + [pltpu.VMEM((3, r, 128), BF16) for r in rows]
        + [pltpu.VMEM((3, 24, FC), F32)] * 3
        + [pltpu.VMEM((3, 24, 256), F32)] * 3
        + [pltpu.VMEM((3, 96, n), BF16) for n in cols]
        + [pltpu.VMEM((96, n), F32) for n in cols]
        + [pltpu.VMEM((3, 24, n), F32) for n in cols]
        + [
            pltpu.VMEM((4, SMALL, 128), F32),
            pltpu.VMEM((12, SMALL, 128), F32),
            pltpu.VMEM((128, 1024), BF16),
            pltpu.VMEM((128, 1536), F32),
            pltpu.VMEM((128, 1536), F32),
            DMA((7 + n_late + 8,)),
            DMA((224,)),
            DMA((224,)),
        ]
    )
    vm, sm, hbm = (pl.BlockSpec(memory_space=m) for m in (pltpu.VMEM, pltpu.SMEM, pl.ANY))
    f32 = lambda *s: jax.ShapeDtypeStruct(s, F32)
    shape = (f32(128, 1536), f32(6, 24, 128), f32(24, 128), f32(24, 128), f32(6, 24, 128), f32(SMALL, 128))
    shape = shape + (f32(24, 4480),) * 3
    return pl.pallas_call(
        body,
        out_shape=shape,
        in_specs=[sm] + [hbm] * (10 + n_late) + [vm] * 11,
        out_specs=(vm,) * 9,
        scratch_shapes=scratch,
        compiler_params=pltpu.CompilerParams(collective_id=2, has_side_effects=True, vmem_limit_bytes=VMEM_BYTES),
        name="backward",
    )(lengths, *xs_in, *gs_in, kv, wq.reshape(6, 4, 384, 128), wk.reshape(4, 384, 128), wv.reshape(4, 384, 128), *late, q, g, lse, delta, branch_t, attn_low, cos, sin, norm_t, gain, d_norm2)


def hand_out(*arrays):
    n = len(arrays)

    def body(*refs):
        ins, outs, held, sem = refs[:n], refs[n : 2 * n], refs[2 * n : 3 * n], refs[3 * n]
        to = [pltpu.make_async_copy(a, b, sem.at[i]) for i, (a, b) in enumerate(zip(ins, held))]
        back = [pltpu.make_async_copy(a, b, sem.at[n + i]) for i, (a, b) in enumerate(zip(held, outs))]
        for copy in to:
            copy.start()
        for i in range(n):
            to[i].wait()
            back[i].start()
        for copy in back:
            copy.wait()

    hbm = pl.BlockSpec(memory_space=pl.ANY)
    return pl.pallas_call(
        body,
        out_shape=tuple(jax.ShapeDtypeStruct(v.shape, v.dtype) for v in arrays),
        in_specs=[hbm] * n,
        out_specs=(hbm,) * n,
        scratch_shapes=[pltpu.VMEM(v.shape, v.dtype) for v in arrays] + [DMA((2 * n,))],
        compiler_params=pltpu.CompilerParams(vmem_limit_bytes=VMEM_BYTES),
        name="hand_out",
    )(*arrays)


def local(
    tokens, cotangent, lengths, norm1_gain, w_query, b_query, w_key, b_key, w_value, b_value, w_out,
    norm2_gain, w_gate, w_up, w_down,
):
    device = lax.axis_index("seq")
    core = lax.axis_index("tensor")
    wq = w_query.transpose(1, 0, 2)
    wk, wv = w_key.reshape(1536, 128), w_value.reshape(1536, 128)
    wo = w_out.reshape(768, 1536)
    gains = jnp.stack([norm1_gain, norm2_gain])

    (output, g_mid, branch_t, g_attn, delta, d_norm2, q, norm_t, cos, sin, attn_low, lse, *shared, kv) = forward(
        tokens, cotangent, lengths, gains, wq, wk, wv, b_query, b_key, b_value, wo, w_gate, w_up, w_down
    )
    grad_tokens, grad_wq, grad_wk, grad_wv, grad_wo, sums, grad_gate, grad_up, grad_down = backward(
        shared[:3], shared[3:], q, g_attn, kv, lse, delta, branch_t, attn_low, lengths,
        cos, sin, norm_t, wq, wk, wv, tokens, gains, g_mid, d_norm2,
    )
    output, grad_tokens, grad_wq, grad_wk, grad_wv, grad_wo, grad_gate, grad_up, grad_down = hand_out(
        output, grad_tokens, grad_wq, grad_wk, grad_wv, grad_wo, grad_gate, grad_up, grad_down
    )
    sums = sums.reshape(-1)
    grad_norm1 = lax.dynamic_slice(sums, (device * 24,), (24,))
    grad_norm2 = lax.dynamic_slice(sums, (1536 + device * 24,), (24,))
    bias = lax.dynamic_slice(sums.reshape(SMALL, 128), (24 + core * 8, device * 2), (8, 2))
    return (
        output,
        grad_tokens,
        grad_norm1,
        grad_wq.transpose(1, 0, 2),
        bias[:6],
        grad_wk.reshape(24, 1, 128),
        bias[6:7],
        grad_wv.reshape(24, 1, 128),
        bias[7:8],
        grad_wo.transpose(0, 2, 1),
        grad_norm2,
        grad_gate,
        grad_up,
        grad_down.T,
    )


def solution(mesh):
    in_specs = (
        P("seq", None), P("seq", None), P(), P(), P(None, "tensor", None), P("tensor", None),
        P(None, "tensor", None), P("tensor", None), P(None, "tensor", None), P("tensor", None),
        P("tensor", None, None), P(), P(None, "tensor"), P(None, "tensor"), P("tensor", None),
    )
    out_specs = (
        P("seq", None), P("seq", None), P("seq"), P("seq", "tensor", None), P("tensor", "seq"),
        P("seq", "tensor", None), P("tensor", "seq"), P("seq", "tensor", None), P("tensor", "seq"),
        P("tensor", None, "seq"), P("seq"), P("seq", "tensor"), P("seq", "tensor"), P("tensor", "seq"),
    )
    return jax.shard_map(local, mesh=mesh, in_specs=in_specs, out_specs=out_specs, check_vma=False)
```

```python
import math

import jax
import jax.numpy as jnp
from jax import lax
from jax.experimental import pallas as pl
from jax.experimental.pallas import tpu as pltpu
from jax.sharding import PartitionSpec as P

MESH = pl.DeviceIdType.MESH
F32 = jnp.float32
BF16 = jnp.bfloat16
VMEM_BYTES = 60 * 1024 * 1024
AXES = ("z", "x", "y")
STRIDE = {"z": 16, "x": 4, "y": 1}


def coords():
    s = lax.axis_index("seq")
    return {"z": s // 16, "x": (s // 4) % 4, "y": s % 4}


def peer(axis, k):
    s = lax.axis_index("seq")
    c = coords()[axis]
    return (s + STRIDE[axis] * ((c + k) % 4 - c), lax.axis_index("tensor"))


def partner():
    return (lax.axis_index("seq"), 1 - lax.axis_index("tensor"))


def barrier(axes=AXES, core=False):
    bar = pltpu.get_barrier_semaphore()
    ids = [peer(a, k) for a in axes for k in (1, 2, 3)]
    if core:
        ids.append(partner())
    for d in ids:
        pl.semaphore_signal(bar, inc=1, device_id=d, device_id_type=MESH)
    pl.semaphore_wait(bar, len(ids))


def remote(src, dst, send, recv, device):
    return pltpu.make_async_remote_copy(
        src_ref=src, dst_ref=dst, send_sem=send, recv_sem=recv, device_id=device, device_id_type=MESH
    )


DMA = pltpu.SemaphoreType.DMA


KV_CHUNK = (
    (0, 48, ("z", "x", "y")),
    (48, 48, ("x", "y", "z")),
    (96, 32, ("y", "z", "x")),
)


def kv_rows(kb, v):
    return pl.ds(pl.multiple_of((kb // 4) * 128 + v * 64 + (kb % 4) * Q_BLK, Q_BLK), Q_BLK)


def kv_index(done, c, r0, rn):
    return tuple(slice(None) if a in done else c[a] for a in AXES) + (pl.ds(r0, rn), slice(None))


def rope_tables(len_ref):
    lane = lax.broadcasted_iota(jnp.int32, (128, 128), 1)
    pos = lax.broadcasted_iota(jnp.int32, (128, 128), 0) * 64 + lax.axis_index("seq")
    rel = (pos - doc_bounds(pos, len_ref)).astype(F32)
    inv_freq = jnp.exp(-(2.0 * (lane % 64).astype(F32) / 128) * math.log(10000.0))
    angle = rel * inv_freq
    sin = jnp.sin(angle)
    return jnp.cos(angle), jnp.where(lane < 64, -sin, sin)


def swap_halves(v):
    return pltpu.roll(v, 64, 1)


Q_BLK = 16
BLK = Q_BLK * 64
SCALE = 1.0 / math.sqrt(128)
SCALE2 = SCALE / math.log(2.0)


def doc_bounds(pos, len_ref):
    start = jnp.zeros_like(pos)
    end = jnp.int32(0)
    for j in range(8):
        end = end + len_ref[j]
        start = jnp.where(pos >= end, end, start)
    return start


FC = 1152


def nt(a, b):
    return lax.dot_general(a, b, (((1,), (1,)), ((), ())), preferred_element_type=F32)


def mm(a, b):
    return jnp.dot(a, b, preferred_element_type=F32)


def col_start(c):
    return pl.multiple_of(jnp.minimum(c * FC, 4480 - FC), 128)


MLP_AXES = (("z", "x", "y"), ("x", "y", "z"), ("y", "z", "x"))


def in_order(v, order):
    place = {}
    rows = []
    for i in range(64):
        for n, a in enumerate(order):
            place[a] = (i // (16, 4, 1)[n]) % 4
        o = place["z"] * 16 + place["x"] * 4 + place["y"]
        rows.append(v[o * 24 : (o + 1) * 24])
    return jnp.concatenate(rows, axis=0)


def forward(tokens, cot, lengths, gains, wq, wk, wv, bq, bk, bv, w_out, w_gate, w_up, w_down):
    def body(len_ref, t_ref, c_ref, g_ref, wk_ref, wv_ref, bq_ref, bk_ref, bv_ref, wq_hbm, wo_hbm, wg_hbm, wu_hbm, wd_hbm,
             out_ref, gmid_ref, bt_ref, ga_ref, delta_ref, dn_ref, q_ref, cos_out, sin_out, low_ref, lse_ref,
             x0, x1, x2, g0, g1, g2, kv_hbm, xq,
             kv, wq_ref, at_ref, m_ref, l_ref, acc_ref, gh_ref,
             wo_ref, wg, wu, wd, got_br, acc, got, norm_ref, nt_ref, ct_ref, n1_ref, xl, act, w_sem, loc, send, recv):
        xs, gs = (x0, x1, x2), (g0, g1, g2)
        c = coords()
        dev = lax.axis_index("seq")
        turn = c["z"] + c["x"] + c["y"]
        sems = iter(range(128))

        def load(j):
            cols = pl.ds(col_start((turn + j) % 4), FC)
            b = j % 2
            copies = [
                pltpu.make_async_copy(wg_hbm.at[:, cols], wg.at[b], w_sem.at[b, 0]),
                pltpu.make_async_copy(wu_hbm.at[:, cols], wu.at[b], w_sem.at[b, 1]),
                pltpu.make_async_copy(wd_hbm.at[cols, :], wd.at[b], w_sem.at[b, 2]),
            ]
            for copy in copies:
                copy.start()
            return copies

        def load_down(j):
            copy = pltpu.make_async_copy(wd_hbm.at[pl.ds(col_start((turn + j) % 4), FC), :], wd.at[j % 2], w_sem.at[j % 2, 2])
            copy.start()
            return copy

        def push(src, dst, device):
            n = next(sems)
            copy = remote(src, dst, send.at[n], recv.at[n], device)
            copy.start()
            return copy

        def keep(src, dst, n):
            copy = pltpu.make_async_copy(src, dst, loc.at[n])
            copy.start()
            return copy

        wq_load = keep(wq_hbm, wq_ref, 6)
        down = [load_down(0), load_down(1)]
        wo_load = keep(wo_hbm, wo_ref, 7)

        x = t_ref[...].astype(F32)
        inv = lax.rsqrt(jnp.mean(x * x, axis=1, keepdims=True) + 1e-06)
        normed = (x * inv * g_ref[0:1, :]).astype(BF16)
        cos, sin = rope_tables(len_ref)
        cos_out[...], sin_out[...] = cos, sin
        k_pre = mm(normed, wk_ref[...]) + bk_ref[...].astype(F32)
        v_low = (mm(normed, wv_ref[...]) + bv_ref[...].astype(F32)).astype(BF16)
        k_rot = (k_pre * cos + swap_halves(k_pre) * sin).astype(BF16)
        kv[c["z"], c["x"], c["y"]] = jnp.concatenate([k_rot[:64], v_low[:64], k_rot[64:], v_low[64:]], axis=0)
        barrier(core=True)
        kv_pending = [[] for _ in range(6)]

        def kv_wait(chunk):
            for p in range(chunk * 3, chunk * 3 + 3):
                for copy in kv_pending[p]:
                    copy.wait()
                kv_pending[p] = []

        def kv_stage(chunk, stage):
            for i, (r0, rn, order) in enumerate(KV_CHUNK):
                p, r0 = chunk * 3 + i, r0 + chunk * 128
                for copy in kv_pending[p]:
                    copy.wait()
                idx = kv_index(order[:stage], c, r0, rn)
                kv_pending[p] = [push(kv.at[idx], kv.at[idx], peer(order[stage], k)) for k in (1, 2, 3)]

        kv_stage(0, 0)
        kv_stage(1, 0)
        wq_load.wait()
        for h in range(6):
            q = mm(normed, wq_ref[h]) + bq_ref[h : h + 1, :].astype(F32)
            q = (q * cos + swap_halves(q) * sin).astype(BF16)
            q_ref[:, h * Q_BLK : (h + 1) * Q_BLK, :] = q.reshape(8, Q_BLK, 128)

        def g_hidden(j):
            down[j].wait()
            gh_ref[j] = nt(c_ref[...], wd[j % 2])
            if j < 2:
                down.append(load_down(j + 2))
            else:
                loads.append(load(j - 2))

        loads = []
        kv_stage(0, 1)
        kv_stage(1, 1)
        g_hidden(0)
        n1_ref[...] = in_order(normed.astype(F32).T, ("x", "y", "z")).astype(BF16).reshape(4, 384, 128)
        own_q = keep(n1_ref, xq.at[:, :, pl.ds(0, 128)], 10)
        g_hidden(1)
        kv_stage(0, 2)
        g_hidden(2)
        g_hidden(3)
        ct_ref[...] = c_ref[...].T.reshape(4, 384, 128)
        own = [keep(ct_ref, x2.at[:, :, pl.ds(0, 128)], 3)]
        kv_wait(0)
        kv_stage(1, 2)
        later = [push(ct_ref, x2.at[:, :, pl.ds(k * 128, 128)], peer("y", k)) for k in (1, 2, 3)]
        later += [push(n1_ref, xq.at[:, :, pl.ds(k * 128, 128)], peer("z", k)) for k in (1, 2, 3)]

        row_off = (lax.broadcasted_iota(jnp.int32, (96, 1), 0) % Q_BLK) * 64 + dev
        col = lax.broadcasted_iota(jnp.int32, (96, BLK), 1)
        key_off = (col % Q_BLK) * 64 + col // Q_BLK

        def attend(qb, lo, hi, carry, diagonal):
            q_blk = q_ref[qb]
            pos_q = row_off + qb * BLK
            start_q = doc_bounds(pos_q, len_ref)

            def block(kb, carry, causal):
                m, l, acc = carry
                k_blk = kv[:, :, :, kv_rows(kb, 0), :].reshape(BLK, 128)
                v_blk = kv[:, :, :, kv_rows(kb, 1), :].reshape(BLK, 128)
                pos_k = key_off + kb * BLK
                vis = pos_k >= start_q
                if causal:
                    vis = vis & (pos_k <= pos_q)
                s = jnp.where(vis, nt(q_blk, k_blk) * SCALE2, -1e30)
                m_new = jnp.maximum(m, jnp.max(s, axis=1, keepdims=True))
                p = jnp.exp2(s - m_new)
                a = jnp.exp2(m - m_new)
                return m_new, l * a + jnp.sum(p, axis=1, keepdims=True), acc * a + mm(p.astype(BF16), v_blk)

            carry = lax.fori_loop(lo, hi, lambda kb, carry: block(kb, carry, False), carry)
            return block(qb, carry, True) if diagonal else carry

        def attend_end(qb, carry):
            m, l, acc = carry
            attn = acc / l
            at_ref[qb] = attn
            low = attn.astype(BF16)
            for h in range(6):
                rows = pl.ds(pl.multiple_of(qb * Q_BLK, Q_BLK), Q_BLK)
                low_ref[rows, h * 128 : (h + 1) * 128] = low[h * Q_BLK : (h + 1) * Q_BLK]
            lse_ref[qb] = jnp.broadcast_to(m + jnp.log2(l), (96, 128)).T[0:1]

        init = (jnp.full((96, 1), -1e30, F32), jnp.zeros((96, 1), F32), jnp.zeros((96, 128), F32))

        def upper(qb, _):
            m_ref[qb - 4], l_ref[qb - 4], acc_ref[qb - 4] = attend(qb, 0, 4, init, False)
            return 0

        def whole(qb, _):
            attend_end(qb, attend(qb, 0, qb, init, True))
            return 0

        def rest(qb, _):
            attend_end(qb, attend(qb, 4, qb, (m_ref[qb - 4], l_ref[qb - 4], acc_ref[qb - 4]), True))
            return 0

        out_kv = [keep(kv.at[:, :, :, pl.ds(0, 128), :], kv_hbm.at[:, :, :, pl.ds(0, 128), :], 8)]
        lax.fori_loop(0, 4, whole, 0)
        lax.fori_loop(4, 8, upper, 0)
        kv_wait(1)
        out_kv.append(keep(kv.at[:, :, :, pl.ds(128, 128), :], kv_hbm.at[:, :, :, pl.ds(128, 128), :], 9))
        lax.fori_loop(4, 8, rest, 0)
        wo_load.wait()
        ex = []
        for half in range(2):
            cols = slice(half * 768, (half + 1) * 768)
            acc[half, :, 0:768] = mm(low_ref[...], wo_ref[:, cols])
            ex.append(push(acc.at[half, :, pl.ds(0, 768)], got_br.at[half], partner()))
        for copy in ex:
            copy.wait()
        mid = t_ref[...].astype(F32) + jnp.concatenate([acc[h, :, 0:768] + got_br[h] for h in range(2)], axis=1)
        out_ref[...] = mid
        inv = lax.rsqrt(jnp.mean(mid * mid, axis=1, keepdims=True) + 1e-06)
        normed = (mid * inv * g_ref[1:2, :]).astype(BF16)
        norm_ref[...] = normed
        turned = normed.astype(F32).T
        for m in range(2):
            nt_ref[m] = in_order(turned, MLP_AXES[m][1:] + MLP_AXES[m][:1]).astype(BF16).reshape(4, 384, 128)
        own.append(keep(nt_ref.at[0], x0.at[:, :, pl.ds(0, 128)], 4))
        own.append(keep(nt_ref.at[1], x1.at[:, :, pl.ds(0, 128)], 5))
        half = pl.ds(2 * lax.axis_index("tensor"), 2)
        halves = {}
        for k in (1, 2, 3):
            for m, w in ((0, "z"), (1, "x")):
                halves[m, k] = push(nt_ref.at[m, half], xl.at[m, k - 1], peer(w, k))

        def pass_on():
            n = 11
            for (m, k), copy in halves.items():
                copy.wait()
                there = xs[m].at[half, :, pl.ds(k * 128, 128)]
                later.append(push(xl.at[m, k - 1], there, partner()))
                later.append(keep(xl.at[m, k - 1], there, n))
                n += 1

        lane = lax.broadcasted_iota(jnp.int32, (128, FC), 1)
        for j in range(4):
            b = j % 2
            d = (turn + j) % 4
            for copy in loads[j]:
                copy.wait()
            n = norm_ref[...]
            gate = mm(n, wg[b])
            up = mm(n, wu[b])
            gh = gh_ref[j]
            sig = 1.0 / (1.0 + jnp.exp(-gate))
            silu = gate * sig
            hidden = (silu * up).astype(BF16)
            g_gate = (gh * up * sig * (1.0 + gate * (1.0 - sig))).astype(BF16)
            g_up = (gh * silu).astype(BF16)
            vals = (g_gate, g_up, hidden)
            for m in range(3):
                act[m, j] = vals[m]
            twice = (lane < 128) & (d == 3)
            zero = jnp.zeros((128, FC), BF16)
            hidden, g_gate, g_up = (jnp.where(twice, zero, v) for v in (hidden, g_gate, g_up))
            add_g = nt(g_gate, wg[b]) + nt(g_up, wu[b])
            acc[1] = add_g if j == 0 else acc[1] + add_g
            if j == 3:
                ex = [push(acc.at[1], got.at[1], partner())]
            add_o = mm(hidden, wd[b])
            acc[0] = add_o if j == 0 else acc[0] + add_o
            if j + 2 < 4:
                loads.append(load(j + 2))
            if j == 2:
                pass_on()
            for m in range(3):
                w = MLP_AXES[m][0]
                k = (d + 4 - c[w]) % 4
                slot = pl.ds(pl.multiple_of(k * 128, 128), 128)

                @pl.when(k == 0)
                def _():
                    pltpu.make_async_copy(act.at[m, j], gs[m].at[pl.ds(0, 128), :], loc.at[m]).start()

                @pl.when(k != 0)
                def _():
                    remote(
                        act.at[m, j], gs[m].at[slot, :], send.at[96 + m * 4 + j], recv.at[96 + m * 4 + k], peer(w, k)
                    ).start()

        ex.append(push(acc.at[0], got.at[0], partner()))
        dn_ref[...] = jnp.sum(acc[1] * out_ref[...] * inv, axis=0, keepdims=True)
        cot_f = c_ref[...].astype(F32)
        ex[0].wait()
        gn = acc[1] + got[1]
        mid = out_ref[...]
        scaled = gn * g_ref[1:2, :]
        g_mid = cot_f + (inv * scaled - mid * (inv * inv * inv) * jnp.mean(scaled * mid, axis=1, keepdims=True))
        gmid_ref[...] = g_mid
        branch_low = g_mid.astype(BF16)
        bt_ref[...] = branch_low.T
        g_attn = nt(branch_low, wo_ref[...]).astype(BF16)
        for h in range(6):
            ga_ref[:, h * Q_BLK : (h + 1) * Q_BLK, :] = g_attn[:, h * 128 : (h + 1) * 128].reshape(8, Q_BLK, 128)
        for qb in range(8):
            delta_ref[qb] = jnp.sum((ga_ref[qb].astype(F32) * at_ref[qb]).T, axis=0, keepdims=True)
        ex[1].wait()
        out_ref[...] += acc[0] + got[0]
        for copy in later + own + out_kv + [own_q]:
            copy.wait()
        for m in range(3):
            w = MLP_AXES[m][0]
            pltpu.make_async_copy(act.at[m, 0], gs[m].at[pl.ds(0, 128), :], loc.at[m]).wait()
            for j in range(4):
                k = ((turn + j) % 4 + 4 - c[w]) % 4

                @pl.when(k != 0)
                def _():
                    slot = pl.ds(pl.multiple_of(k * 128, 128), 128)
                    remote(
                        act.at[m, j], gs[m].at[slot, :], send.at[96 + m * 4 + j], recv.at[96 + m * 4 + k], peer(w, k)
                    ).wait()

    f32 = lambda *s: jax.ShapeDtypeStruct(s, F32)
    b16 = lambda *s: jax.ShapeDtypeStruct(s, BF16)
    vm, sm, hbm = (pl.BlockSpec(memory_space=m) for m in (pltpu.VMEM, pltpu.SMEM, pl.ANY))
    held = [(6, 1536, 128, BF16), (8, 96, 128, F32), (4, 96, 1, F32), (4, 96, 1, F32), (4, 96, 128, F32)]
    held += [(4, 128, FC, F32), (768, 1536, BF16), (2, 1536, FC, BF16), (2, 1536, FC, BF16), (2, FC, 1536, BF16)]
    held += [(2, 128, 768, F32), (2, 128, 1536, F32), (2, 128, 1536, F32), (128, 1536, BF16)]
    held += [(2, 4, 384, 128, BF16), (4, 384, 128, BF16), (4, 384, 128, BF16), (2, 3, 2, 384, 128, BF16), (3, 4, 128, FC, BF16)]
    return pl.pallas_call(
        body,
        out_shape=(f32(128, 1536), f32(128, 1536), b16(1536, 128), b16(8, 96, 128), f32(8, 1, 96), f32(1, 1536))
        + (b16(8, 96, 128), f32(128, 128), f32(128, 128), b16(128, 768), f32(8, 1, 96))
        + (b16(4, 384, 512),) * 3
        + (b16(512, FC),) * 3
        + (b16(4, 4, 4, 256, 128), b16(4, 384, 512)),
        in_specs=[sm] + [vm] * 8 + [hbm] * 5,
        out_specs=(vm,) * 11 + (hbm,) * 8,
        scratch_shapes=[pltpu.VMEM((4, 4, 4, 256, 128), BF16)]
        + [pltpu.VMEM(v[:-1], v[-1]) for v in held]
        + [DMA((2, 3)), DMA((17,)), DMA((112,)), DMA((112,))],
        compiler_params=pltpu.CompilerParams(collective_id=4, has_side_effects=True, vmem_limit_bytes=VMEM_BYTES),
        name="forward",
    )(lengths, tokens, cot, gains, wk, wv, bq, bk, bv, wq, w_out, w_gate, w_up, w_down)


OUT_ORDERS = (("z", "x", "y"), ("x", "y", "z"), ("y", "z", "x"))
QKV_ORDERS = (("x", "y"), ("y", "x"))
SMALL = 40


def slab_products(buf, left, rhs, order):
    def blocks(v, places):
        return jnp.concatenate([v[o * 24 : (o + 1) * 24] for o in places], axis=0)

    if order[0] == "z":
        for z in range(4):
            buf[z] = mm(left[z * 384 : (z + 1) * 384, :], rhs).astype(BF16)
    elif order[0] == "x":
        for x in range(4):
            lhs = jnp.concatenate([left[z * 384 + x * 96 : z * 384 + (x + 1) * 96, :] for z in range(4)], axis=0)
            buf[x] = blocks(mm(lhs, rhs), [z * 4 + y for y in range(4) for z in range(4)]).astype(BF16)
    else:
        for z in range(4):
            v = blocks(mm(left[z * 384 : (z + 1) * 384, :], rhs), [x * 4 + y for y in range(4) for x in range(4)])
            v = v.astype(BF16)
            for y in range(4):
                buf[y, z * 96 : (z + 1) * 96] = v[y * 96 : (y + 1) * 96]


def near(u):
    return u + 1 - 2 * (u % 2)


def far(u):
    return 3 - u


def over(u):
    return (u + 2) % 4


class Halves:
    def __init__(self, push, axis, c, slab, got_first, got_second):
        self.push, self.slab, self.u = push, slab, c[axis]
        self.got_first, self.got_second = got_first, got_second
        self.to = lambda place: peer(axis, place + 4 - c[axis])
        self.one, self.two = {}, []

    def ready(self, which):
        u = self.u
        if which == "over":
            self.one[0, 0] = self.push(self.slab(over(u), 0), self.got_first(0, 0), self.to(near(u)))
            self.one[1, 0] = self.push(self.slab(over(u), 1), self.got_first(1, 0), self.to(far(u)))
        elif which == "near":
            self.one[0, 1] = self.push(self.slab(near(u), 0), self.got_first(0, 1), self.to(near(u)))
        elif which == "far":
            self.one[1, 1] = self.push(self.slab(far(u), 1), self.got_first(1, 1), self.to(far(u)))

    def first(self):
        for which in ("over", "near", "far"):
            self.ready(which)

    def second(self):
        u = self.u
        for h, place in ((0, far(u)), (1, near(u))):
            self.one[h, 0].wait()
            at = self.slab(place, h)
            at[...] = (at[...].astype(F32) + self.got_first(h, 0)[...].astype(F32)).astype(BF16)
            self.two.append(self.push(at, self.got_second(h), self.to(place)))

    def final(self):
        for h in range(2):
            self.one[h, 1].wait()
            self.two[h].wait()
            at = self.slab(self.u, h)
            at[...] = (
                at[...].astype(F32) + self.got_first(h, 1)[...].astype(F32) + self.got_second(h)[...].astype(F32)
            ).astype(BF16)


def sum_first(buf, got, copies, own):
    for copy in copies:
        copy.wait()
    total = buf[own].astype(F32)
    for k in range(3):
        total = total + got[k][...].astype(F32)
    buf[own] = total.astype(BF16)


def backward(xs_in, gs_in, q, g, kv, lse, delta, branch_t, attn_low, lengths,
             cos, sin, norm_shared, wq, wk, wv, tokens, gain, g_mid, d_norm2):
    n_late = 2

    def body(*refs):
        r = list(refs)
        take = lambda n: [r.pop(0) for _ in range(n)]
        (len_ref,), xs_hbm, gs_hbm, (kv_hbm, *w_hbm, xq_hbm), late = take(1), take(3), take(3), take(5), take(n_late)
        q_ref, g_ref, lse_ref, delta_ref, bt_ref, a_ref, cos_ref, sin_ref, gain_ref, dn2_ref = take(10)
        gt_ref, gqkv_ref, go_ref, s_out = take(4)
        m_outs = take(3)
        xs, gs, (dkv,), (t_ref,) = take(3), take(3), take(1), take(1)
        held = (t_ref, gt_ref)
        acc2, o_acc2, (dq_ref, own_ref) = take(3), take(3), take(2)
        sendbuf, r1, r2, t1, t2 = take(3), take(3), take(3), take(3), take(3)
        o_buf, o_r1, o_r2, o_got2 = take(1), take(3), take(3), take(3)
        kv1, kv1b, kv2, kv3 = take(6), take(6), take(6), take(6)
        m_got, o_got = take(3), take(3)
        q_got2, (q_acc2, q_got3) = take(2), take(2)
        o_buf = [xs[2].at[:, :, 0:256], xs[2].at[:, :, 256:512], o_buf[0]]
        q_left, q_right = xs[0], gs[0].at[:, 0:256]
        q_buf = [xs[1].at[:, :, 0:128], xs[1].at[:, :, 128:256]]
        q_got1 = [
            [gs[0].at[192 * (i % 2) : 192 * (i % 2) + 192, lo + i // 2 * 128 : lo + (i // 2 + 1) * 128] for i in range(6)]
            for lo in (256, 640)
        ]
        s_acc, s_got, gp_ref, part, got_part = take(5)
        loc, send, recv = take(3)
        c = coords()
        loads = [pltpu.make_async_copy(a, b, loc.at[i]) for i, (a, b) in enumerate(
            ((xs_hbm[0], xs[0]), (gs_hbm[0], gs[0]), (xs_hbm[2], xs[2]), (gs_hbm[2], gs[2]),
             (xs_hbm[1], xs[1]), (gs_hbm[1], gs[1]), (kv_hbm, dkv), *zip(late, held)))]
        for copy in loads:
            copy.start()
        barrier(core=True)
        sems = iter(range(256))

        def push(src, dst, device):
            n = next(sems)
            copy = remote(src, dst, send.at[n], recv.at[n], device)
            copy.start()
            return copy

        def mlp_slab(m):
            return lambda u, h: sendbuf[m].at[u, pl.ds(192 * h, 192), :]

        mlp_one = [
            Halves(push, MLP_AXES[m][1], c, mlp_slab(m), lambda h, i, m=m: r1[m].at[h, i], lambda h, m=m: r2[m].at[h])
            for m in range(3)
        ]

        def mlp_rows(m):
            own = sendbuf[m].at[c[MLP_AXES[m][1]]]
            return lambda u, h: own.at[pl.ds(pl.multiple_of(u * 96 + h * 48, 16), 48), :]

        mlp_two = [
            Halves(push, MLP_AXES[m][2], c, mlp_rows(m), lambda h, i, m=m: t1[m].at[h, i], lambda h, m=m: t2[m].at[h])
            for m in range(3)
        ]

        for name, place in (("over", over), ("near", near), ("far", far), ("own", lambda v: v)):
            for i, m in enumerate((0, 2, 1)):
                if name == "over":
                    loads[2 * i].wait()
                    loads[2 * i + 1].wait()
                u = place(c[MLP_AXES[m][1]])
                x = xs[m][u]
                sendbuf[m][u] = mm(x, gs[m][...]).astype(BF16)
                mlp_one[m].ready(name)

        def buf_slab(buf):
            return lambda u, h: buf.at[u, pl.ds(192 * h, 192), :]

        out_one = [
            Halves(push, OUT_ORDERS[p][0], c, buf_slab(o_buf[p]), lambda h, i, p=p: o_r1[p].at[h, i], lambda h, p=p: o_r2[p].at[h])
            for p in range(3)
        ]
        o_second = [[], [], []]

        def out_second(p):
            order = OUT_ORDERS[p]
            out_one[p].final()
            for k in (1, 2, 3):
                rows = pl.ds(pl.multiple_of(((c[order[1]] + k) % 4) * 96, 32), 96)
                o_second[p].append(push(o_buf[p].at[c[order[0]], rows, :], o_got2[p].at[k - 1], peer(order[1], k)))

        def out_sum(p):
            order = OUT_ORDERS[p]
            for copy in o_second[p]:
                copy.wait()
            rows = pl.ds(pl.multiple_of(c[order[1]] * 96, 32), 96)
            total = o_buf[p][c[order[0]], rows, :].astype(F32)
            for k in range(3):
                total = total + o_got2[p][k].astype(F32)
            o_acc2[p][...] = total

        loads[6].wait()
        dev = lax.axis_index("seq")
        row = lax.broadcasted_iota(jnp.int32, (BLK, 96), 0)
        key_off = (row % Q_BLK) * 64 + row // Q_BLK
        q_off = (lax.broadcasted_iota(jnp.int32, (1, 96), 1) % Q_BLK) * 64 + dev
        dq_ref[...] = jnp.zeros_like(dq_ref)

        def k_step(kb, _):
            k_blk = dkv[:, :, :, kv_rows(kb, 0), :].reshape(BLK, 128)
            v_blk = dkv[:, :, :, kv_rows(kb, 1), :].reshape(BLK, 128)
            k_t = k_blk.T
            pos_k = key_off + kb * BLK

            def pair(qb, carry, causal):
                dk, dv = carry
                q_blk, g_blk = q_ref[qb], g_ref[qb]
                pos_q = q_off + qb * BLK
                vis = pos_k >= doc_bounds(pos_q, len_ref)
                if causal:
                    vis = vis & (pos_k <= pos_q)
                s = nt(k_blk, q_blk)
                p = jnp.where(vis, jnp.exp2(s * SCALE2 - lse_ref[qb]), 0.0)
                gp = nt(v_blk, g_blk)
                ds = (p * (gp - delta_ref[qb])).astype(BF16)
                dq_ref[qb] += mm(k_t, ds)
                dk = dk + mm(ds, q_blk)
                dv = dv + mm(p.astype(BF16), g_blk)
                return dk, dv

            zero = jnp.zeros((BLK, 128), F32)
            carry = pair(kb, (zero, zero), True)
            dk, dv = lax.fori_loop(kb + 1, 8, lambda qb, carry: pair(qb, carry, False), carry)
            dkv[:, :, :, kv_rows(kb, 0), :] = (dk * SCALE).astype(BF16).reshape(4, 4, 4, Q_BLK, 128)
            dkv[:, :, :, kv_rows(kb, 1), :] = dv.astype(BF16).reshape(4, 4, 4, Q_BLK, 128)
            return 0

        kv_pending = [[] for _ in range(6)]
        kv_parts = [(r0 + 128 * chunk, rn, order) for chunk in range(2) for r0, rn, order in KV_CHUNK]

        def kv_slab(p):
            r0, rn, order = kv_parts[p]
            rest = [a for a in AXES if a != order[0]]

            def slab(u, h):
                where = {order[0]: u, rest[0]: pl.ds(2 * h, 2), rest[1]: slice(None)}
                return dkv.at[where["z"], where["x"], where["y"], pl.ds(r0, rn), :]

            return slab

        kv_one = [
            Halves(push, kv_parts[p][2][0], c, kv_slab(p), lambda h, i, p=p: kv1[p].at[h, i], lambda h, p=p: kv1b[p].at[h])
            for p in range(6)
        ]

        def kv_halves(chunk, step):
            for p in range(chunk * 3, chunk * 3 + 3):
                getattr(kv_one[p], step)()

        def kv_stage(chunk, stage):
            got = (None, kv2, kv3)
            for p in range(chunk * 3, chunk * 3 + 3):
                r0, rn, order = kv_parts[p]
                if stage == 1:
                    kv_one[p].final()
                else:
                    for copy in kv_pending[p]:
                        copy.wait()
                    kv_pending[p] = []
                    mine = kv_index(order[stage:], c, r0, rn)
                    own = dkv[mine].astype(F32)
                    for k in range(3):
                        own = own + got[stage - 1][p][k].astype(F32)
                    if stage == 3:
                        own_ref[pl.ds(r0, rn), :] = own
                        continue
                    dkv[mine] = own.astype(BF16)
                for k in (1, 2, 3):
                    cc = dict(c)
                    cc[order[stage]] = (c[order[stage]] + k) % 4
                    src = dkv.at[kv_index(order[stage + 1 :], cc, r0, rn)]
                    kv_pending[p].append(push(src, got[stage][p].at[k - 1], peer(order[stage], k)))

        def share(acc, got, axis):
            copies = []
            for k in (1, 2, 3):
                rows = pl.ds(pl.multiple_of(((c[axis] + k) % 4) * 24, 8), 24)
                copies.append(push(acc.at[rows, :], got.at[k - 1], peer(axis, k)))
            return copies

        q_one = [
            Halves(push, QKV_ORDERS[p][0], c, buf_slab(q_buf[p]), lambda h, i, p=p: q_got1[p][2 * h + i], lambda h, p=p: q_got1[p][4 + h])
            for p in range(2)
        ]
        q_copies = [[], []]

        def qkv_share():
            mine = pl.ds(pl.multiple_of(c["z"] * 256, 256), 256)
            copies = []
            for k in (1, 2, 3):
                cols = pl.ds(pl.multiple_of((c["z"] + k) % 4 * 256, 256), 256)
                copies.append(push(gp_ref.at[:, cols], q_right.at[k * 128 : (k + 1) * 128, :], peer("z", k)))
            q_right[0:128, :] = gp_ref[:, mine]
            return copies

        def qkv_first():
            for name, place in (("over", over), ("near", near), ("far", far), ("own", lambda v: v)):
                for p in range(2):
                    u = place(c[QKV_ORDERS[p][0]])
                    if p == 0:
                        left = q_left[u]
                    else:
                        rows = pl.ds(pl.multiple_of(u * 96, 32), 96)
                        left = jnp.concatenate([q_left[x, rows, :] for x in range(4)], axis=0)
                    q_buf[p][u] = mm(left, q_right[:, p * 128 : (p + 1) * 128]).astype(BF16)
                    q_one[p].ready(name)

        def qkv_second():
            for p in range(2):
                one, two = QKV_ORDERS[p]
                q_one[p].final()
                for k in (1, 2, 3):
                    rows = pl.ds(pl.multiple_of(((c[two] + k) % 4) * 96, 32), 96)
                    q_copies[p].append(push(q_buf[p].at[c[one], rows, :], q_got2[p].at[k - 1], peer(two, k)))

        def qkv_third():
            for p in range(2):
                one, two = QKV_ORDERS[p]
                for copy in q_copies[p]:
                    copy.wait()
                rows = pl.ds(pl.multiple_of(c[two] * 96, 32), 96)
                total = q_buf[p][c[one], rows, :].astype(F32)
                for k in range(3):
                    total = total + q_got2[p][k].astype(F32)
                q_acc2[:, p * 128 : (p + 1) * 128] = total
            return share(q_acc2, q_got3, "z")

        def qkv_out(copies):
            for copy in copies:
                copy.wait()
            for k in range(4):
                v = q_acc2[pl.ds(pl.multiple_of(c["z"] * 24, 8), 24), :] if k == 0 else q_got3[k - 1]
                block = (c["z"] + 4 - k) % 4
                gqkv_ref[2 * block] = v[:, :128]
                gqkv_ref[2 * block + 1] = v[:, 128:]

        m_copies = [None] * 3

        def mlp_third(m):
            mlp_two[m].final()
            rows = pl.ds(pl.multiple_of(c[MLP_AXES[m][2]] * 96, 32), 96)
            acc2[m][...] = sendbuf[m][c[MLP_AXES[m][1]], rows, :].astype(F32)
            m_copies[m] = share(acc2[m], m_got[m], MLP_AXES[m][0])

        lax.fori_loop(4, 8, k_step, 0)
        kv_halves(1, "first")
        mlp_one[0].second()
        lax.fori_loop(0, 1, k_step, 0)
        mlp_one[2].second()
        mlp_one[1].second()
        kv_halves(1, "second")
        lax.fori_loop(1, 2, k_step, 0)
        for p, order in enumerate(OUT_ORDERS):
            slab_products(o_buf[p], bt_ref, a_ref[:, p * 256 : (p + 1) * 256], order)
            out_one[p].first()
        mlp_one[0].final()
        mlp_two[0].first()
        lax.fori_loop(2, 3, k_step, 0)
        kv_stage(1, 1)
        for m in (2, 1):
            mlp_one[m].final()
            mlp_two[m].first()
        lax.fori_loop(3, 4, k_step, 0)
        kv_halves(0, "first")

        cos_t, sin_t = cos_ref[...], sin_ref[...]
        for qb in range(8):
            dq = dq_ref[qb].T * SCALE
            rows = slice(qb * Q_BLK, (qb + 1) * Q_BLK)
            cs, sn = cos_t[rows], sin_t[rows]
            for h in range(6):
                v = dq[h * Q_BLK : (h + 1) * Q_BLK]
                gp_ref[rows, h * 128 : (h + 1) * 128] = (v * cs - swap_halves(v) * sn).astype(BF16)
        mlp_two[0].second()
        kv_halves(0, "second")
        for p in range(3):
            out_one[p].second()
        for m in (2, 1):
            mlp_two[m].second()
        q_load = pltpu.make_async_copy(xq_hbm, q_left, loc.at[7 + n_late + 8])
        q_load.start()
        kv_stage(1, 2)
        kv_stage(0, 1)
        for m in (0, 2, 1):
            mlp_third(m)
        w_ref = [sendbuf[0].at[:, :, h * 128 : (h + 1) * 128] for h in range(8)]
        w_from = [w_hbm[0].at[h] for h in range(6)] + [w_hbm[1], w_hbm[2]]
        w_loads = [pltpu.make_async_copy(w_from[h], w_ref[h], loc.at[7 + n_late + h]) for h in range(8)]
        for copy in w_loads:
            copy.start()

        def back_through(lo, hi):
            total = nt(gp_ref[:, lo * 128 : (lo + 1) * 128], w_ref[lo][...].reshape(1536, 128))
            for h in range(lo + 1, hi):
                total = total + nt(gp_ref[:, h * 128 : (h + 1) * 128], w_ref[h][...].reshape(1536, 128))
            return total

        kv_stage(0, 2)
        for p in range(3):
            out_second(p)
        kv_stage(1, 3)
        kv_stage(0, 3)

        dk = jnp.concatenate([own_ref[0:64, :], own_ref[128:192, :]], axis=0)
        gp_ref[:, 768:896] = (dk * cos_t - swap_halves(dk) * sin_t).astype(BF16)
        gp_ref[:, 896:] = jnp.concatenate([own_ref[64:128, :], own_ref[192:256, :]], axis=0).astype(BF16)
        shared = qkv_share()
        for copy in loads[7:] + w_loads:
            copy.wait()
        part[...] = back_through(0, 8)
        swap = push(part, got_part, partner())
        q_load.wait()
        for copy in shared:
            copy.wait()
        qkv_first()

        inputs = t_ref[...].astype(F32)
        inv = lax.rsqrt(jnp.mean(inputs * inputs, axis=1, keepdims=True) + 1e-06)
        d_norm1 = jnp.sum(part[...] * inputs * inv, axis=0, keepdims=True)
        d_bias = jnp.sum(gp_ref[...].astype(F32), axis=0, keepdims=True)
        core = lax.axis_index("tensor")
        for j in range(12):
            s_acc[0, j : j + 1, :] = d_norm1[:, j * 128 : (j + 1) * 128]
            s_acc[0, 12 + j : 13 + j, :] = dn2_ref[:, j * 128 : (j + 1) * 128]
        for j in range(8):
            v = d_bias[:, j * 128 : (j + 1) * 128]
            s_acc[0, 24 + j : 25 + j, :] = jnp.where(core == 0, v, 0.0)
            s_acc[0, 32 + j : 33 + j, :] = jnp.where(core == 1, v, 0.0)
        s_pending = []

        def send_small(stage):
            peers = [partner()] if stage == 0 else [peer(AXES[stage - 1], k) for k in (1, 2, 3)]
            for i, d in enumerate(peers):
                s_pending.append(push(s_acc.at[stage], s_got.at[stage * 3 + i], d))

        def sum_small(stage):
            for copy in s_pending:
                copy.wait()
            s_pending.clear()
            if stage == 0:
                return s_acc[0] + s_got[0]
            axis = AXES[stage - 1]
            parts = [s_acc[stage]] + [s_got[stage * 3 + k] for k in range(3)]
            total = jnp.zeros_like(parts[0])
            for w in range(4):
                term = jnp.zeros_like(total)
                for k in range(4):
                    term = jnp.where((c[axis] + 4 - k) % 4 == w, parts[k], term)
                total = total + term
            return total

        send_small(0)
        for p in range(2):
            q_one[p].second()
        o_copies = [None] * 3
        for p in range(3):
            out_sum(p)
            o_copies[p] = share(o_acc2[p], o_got[p], OUT_ORDERS[p][2])
        s_acc[1] = sum_small(0)
        send_small(1)
        qkv_second()
        swap.wait()
        g_norm = part[...] + got_part[...]
        scaled = g_norm * gain_ref[0:1, :]
        gt_ref[...] += (
            inv * scaled - inputs * (inv * inv * inv) * jnp.mean(scaled * inputs, axis=1, keepdims=True)
        )
        s_acc[2] = sum_small(1)
        send_small(2)
        q_out = qkv_third()
        for p in range(3):
            for copy in o_copies[p]:
                copy.wait()
            rows = pl.ds(pl.multiple_of(c[OUT_ORDERS[p][2]] * 24, 8), 24)
            total = o_acc2[p][rows, :]
            for k in range(3):
                total = total + o_got[p][k]
            for j in range(2):
                go_ref[p * 2 + j] = total[:, j * 128 : (j + 1) * 128]
        for m in range(3):
            for copy in m_copies[m]:
                copy.wait()
            here = c[MLP_AXES[m][0]]
            m_outs[m][:, pl.ds(col_start(here), FC)] = acc2[m][pl.ds(pl.multiple_of(here * 24, 8), 24), :]
            for k in (1, 2, 3):
                m_outs[m][:, pl.ds(col_start((here + 4 - k) % 4), FC)] = m_got[m][k - 1]
        s_acc[3] = sum_small(2)
        send_small(3)
        qkv_out(q_out)
        s_out[...] = sum_small(3)

    rows = [rn for _, rn, _ in KV_CHUNK] * 2
    late = (tokens, g_mid)
    scratch = (
        [pltpu.VMEM((4, 384, 512), BF16)] * 3
        + [pltpu.VMEM((512, FC), BF16)] * 3
        + [pltpu.VMEM((4, 4, 4, 256, 128), BF16)]
        + [pltpu.VMEM((128, 1536), BF16)]
        + [pltpu.VMEM((96, FC), F32)] * 3
        + [pltpu.VMEM((96, 256), F32)] * 3
        + [pltpu.VMEM((8, 128, 96), F32), pltpu.VMEM((256, 128), F32)]
        + [pltpu.VMEM((4, 384, FC), BF16)] * 3
        + [pltpu.VMEM((2, 2, 192, FC), BF16)] * 3
        + [pltpu.VMEM((2, 192, FC), BF16)] * 3
        + [pltpu.VMEM((2, 2, 48, FC), BF16)] * 3
        + [pltpu.VMEM((2, 48, FC), BF16)] * 3
        + [pltpu.VMEM((4, 384, 256), BF16)]
        + [pltpu.VMEM((2, 2, 192, 256), BF16)] * 3
        + [pltpu.VMEM((2, 192, 256), BF16)] * 3
        + [pltpu.VMEM((3, 96, 256), BF16)] * 3
        + [pltpu.VMEM((2, 2, 2, 4, r, 128), BF16) for r in rows]
        + [pltpu.VMEM((2, 2, 4, r, 128), BF16) for r in rows]
        + [pltpu.VMEM((3, 4, r, 128), BF16) for r in rows]
        + [pltpu.VMEM((3, r, 128), BF16) for r in rows]
        + [pltpu.VMEM((3, 24, FC), F32)] * 3
        + [pltpu.VMEM((3, 24, 256), F32)] * 3
        + [pltpu.VMEM((3, 96, 128), BF16)] * 2
        + [pltpu.VMEM((96, 256), F32), pltpu.VMEM((3, 24, 256), F32)]
        + [
            pltpu.VMEM((4, SMALL, 128), F32),
            pltpu.VMEM((12, SMALL, 128), F32),
            pltpu.VMEM((128, 1024), BF16),
            pltpu.VMEM((128, 1536), F32),
            pltpu.VMEM((128, 1536), F32),
            DMA((7 + n_late + 9,)),
            DMA((224,)),
            DMA((224,)),
        ]
    )
    vm, sm, hbm = (pl.BlockSpec(memory_space=m) for m in (pltpu.VMEM, pltpu.SMEM, pl.ANY))
    f32 = lambda *s: jax.ShapeDtypeStruct(s, F32)
    shape = (f32(128, 1536), f32(8, 24, 128), f32(6, 24, 128), f32(SMALL, 128))
    shape = shape + (f32(24, 4480),) * 3
    return pl.pallas_call(
        body,
        out_shape=shape,
        in_specs=[sm] + [hbm] * (11 + n_late) + [vm] * 10,
        out_specs=(vm,) * 7,
        scratch_shapes=scratch,
        compiler_params=pltpu.CompilerParams(collective_id=2, has_side_effects=True, vmem_limit_bytes=VMEM_BYTES),
        name="backward",
    )(lengths, *xs_in, *gs_in, kv, wq.reshape(6, 4, 384, 128), wk.reshape(4, 384, 128), wv.reshape(4, 384, 128), norm_shared, *late, q, g, lse, delta, branch_t, attn_low, cos, sin, gain, d_norm2)


def hand_out(qkv, *arrays):
    n = len(arrays)

    def body(*refs):
        ins, outs, held, sem = refs[: n + 1], refs[n + 1 : 2 * n + 4], refs[2 * n + 4 : 3 * n + 5], refs[3 * n + 5]
        to = [pltpu.make_async_copy(a, b, sem.at[i]) for i, (a, b) in enumerate(zip(ins, held))]
        pieces = [[(held[0].at[pl.ds(0, 6)], outs[0]), (held[0].at[6], outs[1]), (held[0].at[7], outs[2])]]
        pieces += [[(held[i], outs[i + 2])] for i in range(1, n + 1)]
        for copy in to:
            copy.start()
        back = []
        for i in range(n + 1):
            to[i].wait()
            for a, b in pieces[i]:
                copy = pltpu.make_async_copy(a, b, sem.at[n + 1 + len(back)])
                copy.start()
                back.append(copy)
        for copy in back:
            copy.wait()

    hbm = pl.BlockSpec(memory_space=pl.ANY)
    f32 = lambda *s: jax.ShapeDtypeStruct(s, F32)
    return pl.pallas_call(
        body,
        out_shape=(f32(6, 24, 128), f32(24, 128), f32(24, 128)) + tuple(f32(*v.shape) for v in arrays),
        in_specs=[hbm] * (n + 1),
        out_specs=(hbm,) * (n + 3),
        scratch_shapes=[pltpu.VMEM(v.shape, v.dtype) for v in (qkv, *arrays)] + [DMA((2 * n + 4,))],
        compiler_params=pltpu.CompilerParams(vmem_limit_bytes=VMEM_BYTES),
        name="hand_out",
    )(qkv, *arrays)


def local(
    tokens, cotangent, lengths, norm1_gain, w_query, b_query, w_key, b_key, w_value, b_value, w_out,
    norm2_gain, w_gate, w_up, w_down,
):
    device = lax.axis_index("seq")
    core = lax.axis_index("tensor")
    wq = w_query.transpose(1, 0, 2)
    wk, wv = w_key.reshape(1536, 128), w_value.reshape(1536, 128)
    wo = w_out.reshape(768, 1536)
    gains = jnp.stack([norm1_gain, norm2_gain])

    (output, g_mid, branch_t, g_attn, delta, d_norm2, q, cos, sin, attn_low, lse, *shared, kv, norm_shared) = forward(
        tokens, cotangent, lengths, gains, wq, wk, wv, b_query, b_key, b_value, wo, w_gate, w_up, w_down
    )
    grad_tokens, grad_qkv, grad_wo, sums, grad_gate, grad_up, grad_down = backward(
        shared[:3], shared[3:], q, g_attn, kv, lse, delta, branch_t, attn_low, lengths,
        cos, sin, norm_shared, wq, wk, wv, tokens, gains, g_mid, d_norm2,
    )
    grad_wq, grad_wk, grad_wv, output, grad_tokens, grad_wo, grad_gate, grad_up, grad_down = hand_out(
        grad_qkv, output, grad_tokens, grad_wo, grad_gate, grad_up, grad_down
    )
    sums = sums.reshape(-1)
    grad_norm1 = lax.dynamic_slice(sums, (device * 24,), (24,))
    grad_norm2 = lax.dynamic_slice(sums, (1536 + device * 24,), (24,))
    bias = lax.dynamic_slice(sums.reshape(SMALL, 128), (24 + core * 8, device * 2), (8, 2))
    return (
        output,
        grad_tokens,
        grad_norm1,
        grad_wq.transpose(1, 0, 2),
        bias[:6],
        grad_wk.reshape(24, 1, 128),
        bias[6:7],
        grad_wv.reshape(24, 1, 128),
        bias[7:8],
        grad_wo.transpose(0, 2, 1),
        grad_norm2,
        grad_gate,
        grad_up,
        grad_down.T,
    )


def solution(mesh):
    in_specs = (
        P("seq", None), P("seq", None), P(), P(), P(None, "tensor", None), P("tensor", None),
        P(None, "tensor", None), P("tensor", None), P(None, "tensor", None), P("tensor", None),
        P("tensor", None, None), P(), P(None, "tensor"), P(None, "tensor"), P("tensor", None),
    )
    out_specs = (
        P("seq", None), P("seq", None), P("seq"), P("seq", "tensor", None), P("tensor", "seq"),
        P("seq", "tensor", None), P("tensor", "seq"), P("seq", "tensor", None), P("tensor", "seq"),
        P("tensor", None, "seq"), P("seq"), P("seq", "tensor"), P("seq", "tensor"), P("tensor", "seq"),
    )
    return jax.shard_map(local, mesh=mesh, in_specs=in_specs, out_specs=out_specs, check_vma=False)
```

```python
import math

import jax
import jax.numpy as jnp
from jax import lax
from jax.experimental import pallas as pl
from jax.experimental.pallas import tpu as pltpu
from jax.sharding import PartitionSpec as P

MESH = pl.DeviceIdType.MESH
F32 = jnp.float32
BF16 = jnp.bfloat16
VMEM_BYTES = 60 * 1024 * 1024
AXES = ("z", "x", "y")
STRIDE = {"z": 16, "x": 4, "y": 1}


def coords():
    s = lax.axis_index("seq")
    return {"z": s // 16, "x": (s // 4) % 4, "y": s % 4}


def peer(axis, k):
    s = lax.axis_index("seq")
    c = coords()[axis]
    return (s + STRIDE[axis] * ((c + k) % 4 - c), lax.axis_index("tensor"))


def partner():
    return (lax.axis_index("seq"), 1 - lax.axis_index("tensor"))


def barrier(axes=AXES, core=False):
    bar = pltpu.get_barrier_semaphore()
    ids = [peer(a, k) for a in axes for k in (1, 2, 3)]
    if core:
        ids.append(partner())
    for d in ids:
        pl.semaphore_signal(bar, inc=1, device_id=d, device_id_type=MESH)
    pl.semaphore_wait(bar, len(ids))


def remote(src, dst, send, recv, device):
    return pltpu.make_async_remote_copy(
        src_ref=src, dst_ref=dst, send_sem=send, recv_sem=recv, device_id=device, device_id_type=MESH
    )


DMA = pltpu.SemaphoreType.DMA


KV_CHUNK = (
    (0, 48, ("z", "x", "y")),
    (48, 48, ("x", "y", "z")),
    (96, 32, ("y", "z", "x")),
)


def kv_rows(kb, v):
    return pl.ds(pl.multiple_of((kb // 4) * 128 + v * 64 + (kb % 4) * Q_BLK, Q_BLK), Q_BLK)


def kv_index(done, c, r0, rn):
    return tuple(slice(None) if a in done else c[a] for a in AXES) + (pl.ds(r0, rn), slice(None))


def rope_tables(len_ref):
    lane = lax.broadcasted_iota(jnp.int32, (128, 128), 1)
    pos = lax.broadcasted_iota(jnp.int32, (128, 128), 0) * 64 + lax.axis_index("seq")
    rel = (pos - doc_bounds(pos, len_ref)).astype(F32)
    inv_freq = jnp.exp(-(2.0 * (lane % 64).astype(F32) / 128) * math.log(10000.0))
    angle = rel * inv_freq
    sin = jnp.sin(angle)
    return jnp.cos(angle), jnp.where(lane < 64, -sin, sin)


def swap_halves(v):
    return pltpu.roll(v, 64, 1)


Q_BLK = 16
BLK = Q_BLK * 64
SCALE = 1.0 / math.sqrt(128)
SCALE2 = SCALE / math.log(2.0)


def doc_bounds(pos, len_ref):
    start = jnp.zeros_like(pos)
    end = jnp.int32(0)
    for j in range(8):
        end = end + len_ref[j]
        start = jnp.where(pos >= end, end, start)
    return start


FC = 1152


def nt(a, b):
    return lax.dot_general(a, b, (((1,), (1,)), ((), ())), preferred_element_type=F32)


def mm(a, b):
    return jnp.dot(a, b, preferred_element_type=F32)


def col_start(c):
    return pl.multiple_of(jnp.minimum(c * FC, 4480 - FC), 128)


MLP_AXES = (("z", "x", "y"), ("x", "y", "z"), ("y", "z", "x"))


def in_order(v, order):
    place = {}
    rows = []
    for i in range(64):
        for n, a in enumerate(order):
            place[a] = (i // (16, 4, 1)[n]) % 4
        o = place["z"] * 16 + place["x"] * 4 + place["y"]
        rows.append(v[o * 24 : (o + 1) * 24])
    return jnp.concatenate(rows, axis=0)


def forward(tokens, cot, lengths, gains, wq, wk, wv, bq, bk, bv, w_out, w_gate, w_up, w_down):
    def body(len_ref, t_ref, c_ref, g_ref, wk_ref, wv_ref, bq_ref, bk_ref, bv_ref, wq_hbm, wo_hbm, wg_hbm, wu_hbm, wd_hbm,
             out_ref, gmid_ref, bt_ref, ga_ref, delta_ref, dn_ref, q_ref, cos_out, sin_out, low_ref, lse_ref,
             x0, x1, x2, g0, g1, g2, kv_hbm, xq,
             kv, wq_ref, at_ref, m_ref, l_ref, acc_ref, gh_ref,
             wo_ref, wg, wu, wd, got_br, acc, got, norm_ref, nt_ref, ct_ref, n1_ref, xl, act, w_sem, loc, send, recv):
        xs, gs = (x0, x1, x2), (g0, g1, g2)
        c = coords()
        dev = lax.axis_index("seq")
        turn = c["z"] + c["x"] + c["y"]
        sems = iter(range(128))

        def load(j):
            cols = pl.ds(col_start((turn + j) % 4), FC)
            b = j % 2
            copies = [
                pltpu.make_async_copy(wg_hbm.at[:, cols], wg.at[b], w_sem.at[b, 0]),
                pltpu.make_async_copy(wu_hbm.at[:, cols], wu.at[b], w_sem.at[b, 1]),
                pltpu.make_async_copy(wd_hbm.at[cols, :], wd.at[b], w_sem.at[b, 2]),
            ]
            for copy in copies:
                copy.start()
            return copies

        def load_down(j):
            copy = pltpu.make_async_copy(wd_hbm.at[pl.ds(col_start((turn + j) % 4), FC), :], wd.at[j % 2], w_sem.at[j % 2, 2])
            copy.start()
            return copy

        def push(src, dst, device):
            n = next(sems)
            copy = remote(src, dst, send.at[n], recv.at[n], device)
            copy.start()
            return copy

        def keep(src, dst, n):
            copy = pltpu.make_async_copy(src, dst, loc.at[n])
            copy.start()
            return copy

        wq_load = keep(wq_hbm, wq_ref, 6)
        down = [load_down(0), load_down(1)]
        wo_load = keep(wo_hbm, wo_ref, 7)

        x = t_ref[...].astype(F32)
        inv = lax.rsqrt(jnp.mean(x * x, axis=1, keepdims=True) + 1e-06)
        normed = (x * inv * g_ref[0:1, :]).astype(BF16)
        cos, sin = rope_tables(len_ref)
        cos_out[...], sin_out[...] = cos, sin
        k_pre = mm(normed, wk_ref[...]) + bk_ref[...].astype(F32)
        v_low = (mm(normed, wv_ref[...]) + bv_ref[...].astype(F32)).astype(BF16)
        k_rot = (k_pre * cos + swap_halves(k_pre) * sin).astype(BF16)
        kv[c["z"], c["x"], c["y"]] = jnp.concatenate([k_rot[:64], v_low[:64], k_rot[64:], v_low[64:]], axis=0)
        barrier(core=True)
        kv_pending = [[] for _ in range(6)]

        def kv_wait(chunk):
            for p in range(chunk * 3, chunk * 3 + 3):
                for copy in kv_pending[p]:
                    copy.wait()
                kv_pending[p] = []

        def kv_stage(chunk, stage):
            for i, (r0, rn, order) in enumerate(KV_CHUNK):
                p, r0 = chunk * 3 + i, r0 + chunk * 128
                for copy in kv_pending[p]:
                    copy.wait()
                idx = kv_index(order[:stage], c, r0, rn)
                kv_pending[p] = [push(kv.at[idx], kv.at[idx], peer(order[stage], k)) for k in (1, 2, 3)]

        kv_stage(0, 0)
        kv_stage(1, 0)
        wq_load.wait()
        for h in range(6):
            q = mm(normed, wq_ref[h]) + bq_ref[h : h + 1, :].astype(F32)
            q = (q * cos + swap_halves(q) * sin).astype(BF16)
            q_ref[:, h * Q_BLK : (h + 1) * Q_BLK, :] = q.reshape(8, Q_BLK, 128)

        def g_hidden(j):
            down[j].wait()
            gh_ref[j] = nt(c_ref[...], wd[j % 2])
            if j < 2:
                down.append(load_down(j + 2))
            else:
                loads.append(load(j - 2))

        loads = []
        kv_stage(0, 1)
        kv_stage(1, 1)
        g_hidden(0)
        n1_ref[...] = in_order(normed.astype(F32).T, ("x", "y", "z")).astype(BF16).reshape(4, 384, 128)
        own_q = keep(n1_ref, xq.at[:, :, pl.ds(0, 128)], 10)
        g_hidden(1)
        kv_stage(0, 2)
        g_hidden(2)
        g_hidden(3)
        ct_ref[...] = c_ref[...].T.reshape(4, 384, 128)
        own = [keep(ct_ref, x2.at[:, :, pl.ds(0, 128)], 3)]
        kv_wait(0)
        kv_stage(1, 2)
        later = [push(ct_ref, x2.at[:, :, pl.ds(k * 128, 128)], peer("y", k)) for k in (1, 2, 3)]
        later += [push(n1_ref, xq.at[:, :, pl.ds(k * 128, 128)], peer("z", k)) for k in (1, 2, 3)]

        row_off = (lax.broadcasted_iota(jnp.int32, (96, 1), 0) % Q_BLK) * 64 + dev
        col = lax.broadcasted_iota(jnp.int32, (96, BLK), 1)
        key_off = (col % Q_BLK) * 64 + col // Q_BLK

        def attend(qb, lo, hi, carry, diagonal):
            q_blk = q_ref[qb]
            pos_q = row_off + qb * BLK
            start_q = doc_bounds(pos_q, len_ref)

            def block(kb, carry, causal):
                m, l, acc = carry
                k_blk = kv[:, :, :, kv_rows(kb, 0), :].reshape(BLK, 128)
                v_blk = kv[:, :, :, kv_rows(kb, 1), :].reshape(BLK, 128)
                pos_k = key_off + kb * BLK
                vis = pos_k >= start_q
                if causal:
                    vis = vis & (pos_k <= pos_q)
                s = jnp.where(vis, nt(q_blk, k_blk) * SCALE2, -1e30)
                m_new = jnp.maximum(m, jnp.max(s, axis=1, keepdims=True))
                p = jnp.exp2(s - m_new)
                a = jnp.exp2(m - m_new)
                return m_new, l * a + jnp.sum(p, axis=1, keepdims=True), acc * a + mm(p.astype(BF16), v_blk)

            carry = lax.fori_loop(lo, hi, lambda kb, carry: block(kb, carry, False), carry)
            return block(qb, carry, True) if diagonal else carry

        def attend_end(qb, carry):
            m, l, acc = carry
            attn = acc / l
            at_ref[qb] = attn
            low = attn.astype(BF16)
            for h in range(6):
                rows = pl.ds(pl.multiple_of(qb * Q_BLK, Q_BLK), Q_BLK)
                low_ref[rows, h * 128 : (h + 1) * 128] = low[h * Q_BLK : (h + 1) * Q_BLK]
            lse_ref[qb] = jnp.broadcast_to(m + jnp.log2(l), (96, 128)).T[0:1]

        init = (jnp.full((96, 1), -1e30, F32), jnp.zeros((96, 1), F32), jnp.zeros((96, 128), F32))

        def upper(qb, _):
            m_ref[qb - 4], l_ref[qb - 4], acc_ref[qb - 4] = attend(qb, 0, 4, init, False)
            return 0

        def whole(qb, _):
            attend_end(qb, attend(qb, 0, qb, init, True))
            return 0

        def rest(qb, _):
            attend_end(qb, attend(qb, 4, qb, (m_ref[qb - 4], l_ref[qb - 4], acc_ref[qb - 4]), True))
            return 0

        out_kv = [keep(kv.at[:, :, :, pl.ds(0, 128), :], kv_hbm.at[:, :, :, pl.ds(0, 128), :], 8)]
        lax.fori_loop(0, 4, whole, 0)
        lax.fori_loop(4, 8, upper, 0)
        kv_wait(1)
        out_kv.append(keep(kv.at[:, :, :, pl.ds(128, 128), :], kv_hbm.at[:, :, :, pl.ds(128, 128), :], 9))
        lax.fori_loop(4, 8, rest, 0)
        wo_load.wait()
        ex = []
        for half in range(2):
            cols = slice(half * 768, (half + 1) * 768)
            acc[half, :, 0:768] = mm(low_ref[...], wo_ref[:, cols])
            ex.append(push(acc.at[half, :, pl.ds(0, 768)], got_br.at[half], partner()))
        for copy in ex:
            copy.wait()
        mid = t_ref[...].astype(F32) + jnp.concatenate([acc[h, :, 0:768] + got_br[h] for h in range(2)], axis=1)
        out_ref[...] = mid
        inv = lax.rsqrt(jnp.mean(mid * mid, axis=1, keepdims=True) + 1e-06)
        normed = (mid * inv * g_ref[1:2, :]).astype(BF16)
        norm_ref[...] = normed
        turned = normed.astype(F32).T
        for m in range(2):
            nt_ref[m] = in_order(turned, MLP_AXES[m][1:] + MLP_AXES[m][:1]).astype(BF16).reshape(4, 384, 128)
        own.append(keep(nt_ref.at[0], x0.at[:, :, pl.ds(0, 128)], 4))
        own.append(keep(nt_ref.at[1], x1.at[:, :, pl.ds(0, 128)], 5))
        half = pl.ds(2 * lax.axis_index("tensor"), 2)
        halves = {}
        for k in (1, 2, 3):
            for m, w in ((0, "z"), (1, "x")):
                halves[m, k] = push(nt_ref.at[m, half], xl.at[m, k - 1], peer(w, k))

        def pass_on():
            n = 11
            for (m, k), copy in halves.items():
                copy.wait()
                there = xs[m].at[half, :, pl.ds(k * 128, 128)]
                later.append(push(xl.at[m, k - 1], there, partner()))
                later.append(keep(xl.at[m, k - 1], there, n))
                n += 1

        lane = lax.broadcasted_iota(jnp.int32, (128, FC), 1)
        for j in range(4):
            b = j % 2
            d = (turn + j) % 4
            for copy in loads[j]:
                copy.wait()
            n = norm_ref[...]
            gate = mm(n, wg[b])
            up = mm(n, wu[b])
            gh = gh_ref[j]
            sig = 1.0 / (1.0 + jnp.exp(-gate))
            silu = gate * sig
            hidden = (silu * up).astype(BF16)
            g_gate = (gh * up * sig * (1.0 + gate * (1.0 - sig))).astype(BF16)
            g_up = (gh * silu).astype(BF16)
            vals = (g_gate, g_up, hidden)
            for m in range(3):
                act[m, j] = vals[m]
            twice = (lane < 128) & (d == 3)
            zero = jnp.zeros((128, FC), BF16)
            hidden, g_gate, g_up = (jnp.where(twice, zero, v) for v in (hidden, g_gate, g_up))
            add_g = nt(g_gate, wg[b]) + nt(g_up, wu[b])
            acc[1] = add_g if j == 0 else acc[1] + add_g
            if j == 3:
                ex = [push(acc.at[1], got.at[1], partner())]
            add_o = mm(hidden, wd[b])
            acc[0] = add_o if j == 0 else acc[0] + add_o
            if j + 2 < 4:
                loads.append(load(j + 2))
            if j == 2:
                pass_on()
            for m in range(3):
                w = MLP_AXES[m][0]
                k = (d + 4 - c[w]) % 4
                slot = pl.ds(pl.multiple_of(k * 128, 128), 128)

                @pl.when(k == 0)
                def _():
                    pltpu.make_async_copy(act.at[m, j], gs[m].at[pl.ds(0, 128), :], loc.at[m]).start()

                @pl.when(k != 0)
                def _():
                    remote(
                        act.at[m, j], gs[m].at[slot, :], send.at[96 + m * 4 + j], recv.at[96 + m * 4 + k], peer(w, k)
                    ).start()

        ex.append(push(acc.at[0], got.at[0], partner()))
        dn_ref[...] = jnp.sum(acc[1] * out_ref[...] * inv, axis=0, keepdims=True)
        cot_f = c_ref[...].astype(F32)
        ex[0].wait()
        gn = acc[1] + got[1]
        mid = out_ref[...]
        scaled = gn * g_ref[1:2, :]
        g_mid = cot_f + (inv * scaled - mid * (inv * inv * inv) * jnp.mean(scaled * mid, axis=1, keepdims=True))
        gmid_ref[...] = g_mid
        branch_low = g_mid.astype(BF16)
        bt_ref[...] = branch_low.T
        g_attn = nt(branch_low, wo_ref[...]).astype(BF16)
        for h in range(6):
            ga_ref[:, h * Q_BLK : (h + 1) * Q_BLK, :] = g_attn[:, h * 128 : (h + 1) * 128].reshape(8, Q_BLK, 128)
        for qb in range(8):
            delta_ref[qb] = jnp.sum((ga_ref[qb].astype(F32) * at_ref[qb]).T, axis=0, keepdims=True)
        ex[1].wait()
        out_ref[...] += acc[0] + got[0]
        for copy in later + own + out_kv + [own_q]:
            copy.wait()
        for m in range(3):
            w = MLP_AXES[m][0]
            pltpu.make_async_copy(act.at[m, 0], gs[m].at[pl.ds(0, 128), :], loc.at[m]).wait()
            for j in range(4):
                k = ((turn + j) % 4 + 4 - c[w]) % 4

                @pl.when(k != 0)
                def _():
                    slot = pl.ds(pl.multiple_of(k * 128, 128), 128)
                    remote(
                        act.at[m, j], gs[m].at[slot, :], send.at[96 + m * 4 + j], recv.at[96 + m * 4 + k], peer(w, k)
                    ).wait()

    f32 = lambda *s: jax.ShapeDtypeStruct(s, F32)
    b16 = lambda *s: jax.ShapeDtypeStruct(s, BF16)
    vm, sm, hbm = (pl.BlockSpec(memory_space=m) for m in (pltpu.VMEM, pltpu.SMEM, pl.ANY))
    held = [(6, 1536, 128, BF16), (8, 96, 128, F32), (4, 96, 1, F32), (4, 96, 1, F32), (4, 96, 128, F32)]
    held += [(4, 128, FC, F32), (768, 1536, BF16), (2, 1536, FC, BF16), (2, 1536, FC, BF16), (2, FC, 1536, BF16)]
    held += [(2, 128, 768, F32), (2, 128, 1536, F32), (2, 128, 1536, F32), (128, 1536, BF16)]
    held += [(2, 4, 384, 128, BF16), (4, 384, 128, BF16), (4, 384, 128, BF16), (2, 3, 2, 384, 128, BF16), (3, 4, 128, FC, BF16)]
    return pl.pallas_call(
        body,
        out_shape=(f32(128, 1536), f32(128, 1536), b16(1536, 128), b16(8, 96, 128), f32(8, 1, 96), f32(1, 1536))
        + (b16(8, 96, 128), f32(128, 128), f32(128, 128), b16(128, 768), f32(8, 1, 96))
        + (b16(4, 384, 512),) * 3
        + (b16(512, FC),) * 3
        + (b16(4, 4, 4, 256, 128), b16(4, 384, 512)),
        in_specs=[sm] + [vm] * 8 + [hbm] * 5,
        out_specs=(vm,) * 11 + (hbm,) * 8,
        scratch_shapes=[pltpu.VMEM((4, 4, 4, 256, 128), BF16)]
        + [pltpu.VMEM(v[:-1], v[-1]) for v in held]
        + [DMA((2, 3)), DMA((17,)), DMA((112,)), DMA((112,))],
        compiler_params=pltpu.CompilerParams(collective_id=4, has_side_effects=True, vmem_limit_bytes=VMEM_BYTES),
        name="forward",
    )(lengths, tokens, cot, gains, wk, wv, bq, bk, bv, wq, w_out, w_gate, w_up, w_down)


OUT_ORDERS = (("z", "x", "y"), ("x", "y", "z"), ("y", "z", "x"))
QKV_ORDERS = (("x", "y"), ("y", "x"))
SMALL = 40


def slab_products(buf, left, rhs, order):
    def blocks(v, places):
        return jnp.concatenate([v[o * 24 : (o + 1) * 24] for o in places], axis=0)

    if order[0] == "z":
        for z in range(4):
            buf[z] = mm(left[z * 384 : (z + 1) * 384, :], rhs).astype(BF16)
    elif order[0] == "x":
        for x in range(4):
            lhs = jnp.concatenate([left[z * 384 + x * 96 : z * 384 + (x + 1) * 96, :] for z in range(4)], axis=0)
            buf[x] = blocks(mm(lhs, rhs), [z * 4 + y for y in range(4) for z in range(4)]).astype(BF16)
    else:
        for z in range(4):
            v = blocks(mm(left[z * 384 : (z + 1) * 384, :], rhs), [x * 4 + y for y in range(4) for x in range(4)])
            v = v.astype(BF16)
            for y in range(4):
                buf[y, z * 96 : (z + 1) * 96] = v[y * 96 : (y + 1) * 96]


def near(u):
    return u + 1 - 2 * (u % 2)


def far(u):
    return 3 - u


def over(u):
    return (u + 2) % 4


class Halves:
    def __init__(self, push, axis, c, slab, got_first, got_second):
        self.push, self.slab, self.u = push, slab, c[axis]
        self.got_first, self.got_second = got_first, got_second
        self.to = lambda place: peer(axis, place + 4 - c[axis])
        self.one, self.two = {}, []

    def ready(self, which):
        u = self.u
        if which == "over":
            self.one[0, 0] = self.push(self.slab(over(u), 0), self.got_first(0, 0), self.to(near(u)))
            self.one[1, 0] = self.push(self.slab(over(u), 1), self.got_first(1, 0), self.to(far(u)))
        elif which == "near":
            self.one[0, 1] = self.push(self.slab(near(u), 0), self.got_first(0, 1), self.to(near(u)))
        elif which == "far":
            self.one[1, 1] = self.push(self.slab(far(u), 1), self.got_first(1, 1), self.to(far(u)))

    def first(self):
        for which in ("over", "near", "far"):
            self.ready(which)

    def second(self):
        u = self.u
        for h, place in ((0, far(u)), (1, near(u))):
            self.one[h, 0].wait()
            at = self.slab(place, h)
            at[...] = (at[...].astype(F32) + self.got_first(h, 0)[...].astype(F32)).astype(BF16)
            self.two.append(self.push(at, self.got_second(h), self.to(place)))

    def final(self):
        for h in range(2):
            self.one[h, 1].wait()
            self.two[h].wait()
            at = self.slab(self.u, h)
            at[...] = (
                at[...].astype(F32) + self.got_first(h, 1)[...].astype(F32) + self.got_second(h)[...].astype(F32)
            ).astype(BF16)


def sum_first(buf, got, copies, own):
    for copy in copies:
        copy.wait()
    total = buf[own].astype(F32)
    for k in range(3):
        total = total + got[k][...].astype(F32)
    buf[own] = total.astype(BF16)


def backward(xs_in, gs_in, q, g, kv, lse, delta, branch_t, attn_low, lengths,
             cos, sin, norm_shared, wq, wk, wv, tokens, gain, g_mid, d_norm2):
    n_late = 2

    def body(*refs):
        r = list(refs)
        take = lambda n: [r.pop(0) for _ in range(n)]
        (len_ref,), xs_hbm, gs_hbm, (kv_hbm, *w_hbm, xq_hbm), late = take(1), take(3), take(3), take(5), take(n_late)
        q_ref, g_ref, lse_ref, delta_ref, bt_ref, a_ref, cos_ref, sin_ref, gain_ref, dn2_ref = take(10)
        gt_ref, gqkv_ref, go_ref, s_out = take(4)
        m_outs = take(3)
        xs, gs, (dkv,), (t_ref,) = take(3), take(3), take(1), take(1)
        held = (t_ref, gt_ref)
        acc2, o_acc2, (dq_ref, own_ref) = take(3), take(3), take(2)
        sendbuf, r1, r2, t1, t2 = take(3), take(3), take(3), take(3), take(3)
        o_buf, o_r1, o_r2, o_got2 = take(1), take(3), take(3), take(3)
        kv1, kv1b, kv2, kv3 = take(6), take(3), take(6), take(6)
        m_got, o_got = take(3), take(3)
        q_got2, (q_acc2, q_got3) = take(2), take(2)
        o_buf = [xs[2].at[:, :, 0:256], xs[2].at[:, :, 256:512], o_buf[0]]
        q_left, q_right = xs[0], gs[0].at[:, 0:256]
        q_buf = [xs[1].at[:, :, 0:128], xs[1].at[:, :, 128:256]]
        q_got1 = [
            [gs[0].at[0:384, lo + k * 128 : lo + (k + 1) * 128] for k in range(3)] for lo in (256, 640)
        ]
        s_acc, s_got, gp_ref, part, got_part = take(5)
        loc, send, recv = take(3)
        c = coords()
        loads = [pltpu.make_async_copy(a, b, loc.at[i]) for i, (a, b) in enumerate(
            ((xs_hbm[0], xs[0]), (gs_hbm[0], gs[0]), (xs_hbm[2], xs[2]), (gs_hbm[2], gs[2]),
             (xs_hbm[1], xs[1]), (gs_hbm[1], gs[1]), (kv_hbm, dkv), *zip(late, held)))]
        for copy in loads:
            copy.start()
        barrier(core=True)
        sems = iter(range(256))

        def push(src, dst, device):
            n = next(sems)
            copy = remote(src, dst, send.at[n], recv.at[n], device)
            copy.start()
            return copy

        def mlp_slab(m):
            return lambda u, h: sendbuf[m].at[u, pl.ds(192 * h, 192), :]

        mlp_one = [
            Halves(push, MLP_AXES[m][1], c, mlp_slab(m), lambda h, i, m=m: r1[m].at[h, i], lambda h, m=m: r2[m].at[h])
            for m in range(3)
        ]

        def mlp_rows(m):
            own = sendbuf[m].at[c[MLP_AXES[m][1]]]
            return lambda u, h: own.at[pl.ds(pl.multiple_of(u * 96 + h * 48, 16), 48), :]

        mlp_two = [
            Halves(push, MLP_AXES[m][2], c, mlp_rows(m), lambda h, i, m=m: t1[m].at[h, i], lambda h, m=m: t2[m].at[h])
            for m in range(3)
        ]

        def products(*weights):
            for name, place in (("over", over), ("near", near), ("far", far), ("own", lambda v: v)):
                for m in weights:
                    if name == "over":
                        loads[2 * (0, 2, 1).index(m)].wait()
                        loads[2 * (0, 2, 1).index(m) + 1].wait()
                    u = place(c[MLP_AXES[m][1]])
                    sendbuf[m][u] = mm(xs[m][u], gs[m][...]).astype(BF16)
                    mlp_one[m].ready(name)

        products(0, 2)

        def buf_slab(buf):
            return lambda u, h: buf.at[u, pl.ds(192 * h, 192), :]

        out_one = [
            Halves(push, OUT_ORDERS[p][0], c, buf_slab(o_buf[p]), lambda h, i, p=p: o_r1[p].at[h, i], lambda h, p=p: o_r2[p].at[h])
            for p in range(3)
        ]
        o_second = [[], [], []]

        def out_second(p):
            order = OUT_ORDERS[p]
            out_one[p].final()
            for k in (1, 2, 3):
                rows = pl.ds(pl.multiple_of(((c[order[1]] + k) % 4) * 96, 32), 96)
                o_second[p].append(push(o_buf[p].at[c[order[0]], rows, :], o_got2[p].at[k - 1], peer(order[1], k)))

        def out_sum(p):
            order = OUT_ORDERS[p]
            for copy in o_second[p]:
                copy.wait()
            rows = pl.ds(pl.multiple_of(c[order[1]] * 96, 32), 96)
            total = o_buf[p][c[order[0]], rows, :].astype(F32)
            for k in range(3):
                total = total + o_got2[p][k].astype(F32)
            o_acc2[p][...] = total

        loads[6].wait()
        dev = lax.axis_index("seq")
        row = lax.broadcasted_iota(jnp.int32, (BLK, 96), 0)
        key_off = (row % Q_BLK) * 64 + row // Q_BLK
        q_off = (lax.broadcasted_iota(jnp.int32, (1, 96), 1) % Q_BLK) * 64 + dev
        dq_ref[...] = jnp.zeros_like(dq_ref)

        def k_step(kb, _):
            k_blk = dkv[:, :, :, kv_rows(kb, 0), :].reshape(BLK, 128)
            v_blk = dkv[:, :, :, kv_rows(kb, 1), :].reshape(BLK, 128)
            k_t = k_blk.T
            pos_k = key_off + kb * BLK

            def pair(qb, carry, causal):
                dk, dv = carry
                q_blk, g_blk = q_ref[qb], g_ref[qb]
                pos_q = q_off + qb * BLK
                vis = pos_k >= doc_bounds(pos_q, len_ref)
                if causal:
                    vis = vis & (pos_k <= pos_q)
                s = nt(k_blk, q_blk)
                p = jnp.where(vis, jnp.exp2(s * SCALE2 - lse_ref[qb]), 0.0)
                gp = nt(v_blk, g_blk)
                ds = (p * (gp - delta_ref[qb])).astype(BF16)
                dq_ref[qb] += mm(k_t, ds)
                dk = dk + mm(ds, q_blk)
                dv = dv + mm(p.astype(BF16), g_blk)
                return dk, dv

            zero = jnp.zeros((BLK, 128), F32)
            carry = pair(kb, (zero, zero), True)
            dk, dv = lax.fori_loop(kb + 1, 8, lambda qb, carry: pair(qb, carry, False), carry)
            dkv[:, :, :, kv_rows(kb, 0), :] = (dk * SCALE).astype(BF16).reshape(4, 4, 4, Q_BLK, 128)
            dkv[:, :, :, kv_rows(kb, 1), :] = dv.astype(BF16).reshape(4, 4, 4, Q_BLK, 128)
            return 0

        kv_pending = [[] for _ in range(6)]
        kv_parts = [(r0 + 128 * chunk, rn, order) for chunk in range(2) for r0, rn, order in KV_CHUNK]

        def kv_slab(p):
            r0, rn, order = kv_parts[p]
            rest = [a for a in AXES if a != order[0]]

            def slab(u, h):
                where = {order[0]: u, rest[0]: pl.ds(2 * h, 2), rest[1]: slice(None)}
                return dkv.at[where["z"], where["x"], where["y"], pl.ds(r0, rn), :]

            return slab

        kv_one = {
            p: Halves(
                push, kv_parts[p][2][0], c, kv_slab(p), lambda h, i, p=p: kv1[p].at[h, i], lambda h, p=p: kv1b[p - 3].at[h]
            )
            for p in range(3, 6)
        }

        def kv_push(p, stage):
            r0, rn, order = kv_parts[p]
            for k in (1, 2, 3):
                cc = dict(c)
                cc[order[stage]] = (c[order[stage]] + k) % 4
                src = dkv.at[kv_index(order[stage + 1 :], cc, r0, rn)]
                kv_pending[p].append(push(src, (kv1, kv2, kv3)[stage][p].at[k - 1], peer(order[stage], k)))

        def kv_stage(chunk, stage):
            got = (kv1, kv2, kv3)
            for p in range(chunk * 3, chunk * 3 + 3):
                r0, rn, order = kv_parts[p]
                if stage == 1 and chunk == 1:
                    kv_one[p].final()
                else:
                    for copy in kv_pending[p]:
                        copy.wait()
                    kv_pending[p] = []
                    mine = kv_index(order[stage:], c, r0, rn)
                    own = dkv[mine].astype(F32)
                    for k in range(3):
                        own = own + got[stage - 1][p][k].astype(F32)
                    if stage == 3:
                        own_ref[pl.ds(r0, rn), :] = own
                        continue
                    dkv[mine] = own.astype(BF16)
                kv_push(p, stage)

        def share(acc, got, axis):
            copies = []
            for k in (1, 2, 3):
                rows = pl.ds(pl.multiple_of(((c[axis] + k) % 4) * 24, 8), 24)
                copies.append(push(acc.at[rows, :], got.at[k - 1], peer(axis, k)))
            return copies

        q_copies = [[], []]

        def qkv_share():
            mine = pl.ds(pl.multiple_of(c["z"] * 256, 256), 256)
            copies = []
            for k in (1, 2, 3):
                cols = pl.ds(pl.multiple_of((c["z"] + k) % 4 * 256, 256), 256)
                copies.append(push(gp_ref.at[:, cols], q_right.at[k * 128 : (k + 1) * 128, :], peer("z", k)))
            q_right[0:128, :] = gp_ref[:, mine]
            return copies

        def qkv_first():
            for k in (2, 1, 3, 0):
                for p, (one, _) in enumerate(QKV_ORDERS):
                    u = (c[one] + k) % 4
                    if p == 0:
                        left = q_left[u]
                    else:
                        rows = pl.ds(pl.multiple_of(u * 96, 32), 96)
                        left = jnp.concatenate([q_left[x, rows, :] for x in range(4)], axis=0)
                    q_buf[p][u] = mm(left, q_right[:, p * 128 : (p + 1) * 128]).astype(BF16)
                    if k:
                        q_copies[p].append(push(q_buf[p].at[u], q_got1[p][k - 1], peer(one, k)))

        def qkv_second():
            for p, (one, two) in enumerate(QKV_ORDERS):
                sum_first(q_buf[p], q_got1[p], q_copies[p], c[one])
                q_copies[p] = []
                for k in (1, 2, 3):
                    rows = pl.ds(pl.multiple_of(((c[two] + k) % 4) * 96, 32), 96)
                    q_copies[p].append(push(q_buf[p].at[c[one], rows, :], q_got2[p].at[k - 1], peer(two, k)))

        def qkv_third():
            for p in range(2):
                one, two = QKV_ORDERS[p]
                for copy in q_copies[p]:
                    copy.wait()
                rows = pl.ds(pl.multiple_of(c[two] * 96, 32), 96)
                total = q_buf[p][c[one], rows, :].astype(F32)
                for k in range(3):
                    total = total + q_got2[p][k].astype(F32)
                q_acc2[:, p * 128 : (p + 1) * 128] = total
            return share(q_acc2, q_got3, "z")

        def qkv_out(copies):
            for copy in copies:
                copy.wait()
            for k in range(4):
                v = q_acc2[pl.ds(pl.multiple_of(c["z"] * 24, 8), 24), :] if k == 0 else q_got3[k - 1]
                block = (c["z"] + 4 - k) % 4
                gqkv_ref[2 * block] = v[:, :128]
                gqkv_ref[2 * block + 1] = v[:, 128:]

        m_copies = [None] * 3

        def mlp_third(m):
            mlp_two[m].final()
            rows = pl.ds(pl.multiple_of(c[MLP_AXES[m][2]] * 96, 32), 96)
            acc2[m][...] = sendbuf[m][c[MLP_AXES[m][1]], rows, :].astype(F32)
            m_copies[m] = share(acc2[m], m_got[m], MLP_AXES[m][0])

        lax.fori_loop(4, 8, k_step, 0)
        for p in range(3, 6):
            kv_one[p].first()
        mlp_one[0].second()
        lax.fori_loop(0, 1, k_step, 0)
        mlp_one[2].second()
        for p in range(3, 6):
            kv_one[p].second()
        lax.fori_loop(1, 2, k_step, 0)
        for p, order in enumerate(OUT_ORDERS):
            slab_products(o_buf[p], bt_ref, a_ref[:, p * 256 : (p + 1) * 256], order)
            out_one[p].first()
        mlp_one[0].final()
        mlp_two[0].first()
        lax.fori_loop(2, 3, k_step, 0)
        kv_stage(1, 1)
        mlp_one[2].final()
        mlp_two[2].first()
        lax.fori_loop(3, 4, k_step, 0)
        for p in range(3):
            kv_push(p, 0)
        products(1)

        cos_t, sin_t = cos_ref[...], sin_ref[...]
        for qb in range(8):
            dq = dq_ref[qb].T * SCALE
            rows = slice(qb * Q_BLK, (qb + 1) * Q_BLK)
            cs, sn = cos_t[rows], sin_t[rows]
            for h in range(6):
                v = dq[h * Q_BLK : (h + 1) * Q_BLK]
                gp_ref[rows, h * 128 : (h + 1) * 128] = (v * cs - swap_halves(v) * sn).astype(BF16)
        kv_stage(0, 1)
        mlp_two[0].second()
        mlp_two[2].second()
        q_load = pltpu.make_async_copy(xq_hbm, q_left, loc.at[7 + n_late + 8])
        q_load.start()
        kv_stage(1, 2)
        for p in range(3):
            out_one[p].second()
        kv_stage(0, 2)
        mlp_one[1].second()
        mlp_third(0)
        mlp_third(2)
        w_ref = [sendbuf[0].at[:, :, h * 128 : (h + 1) * 128] for h in range(8)]
        w_from = [w_hbm[0].at[h] for h in range(6)] + [w_hbm[1], w_hbm[2]]
        w_loads = [pltpu.make_async_copy(w_from[h], w_ref[h], loc.at[7 + n_late + h]) for h in range(8)]
        for copy in w_loads:
            copy.start()

        def back_through(lo, hi):
            total = nt(gp_ref[:, lo * 128 : (lo + 1) * 128], w_ref[lo][...].reshape(1536, 128))
            for h in range(lo + 1, hi):
                total = total + nt(gp_ref[:, h * 128 : (h + 1) * 128], w_ref[h][...].reshape(1536, 128))
            return total

        kv_stage(1, 3)
        kv_stage(0, 3)

        dk = jnp.concatenate([own_ref[0:64, :], own_ref[128:192, :]], axis=0)
        gp_ref[:, 768:896] = (dk * cos_t - swap_halves(dk) * sin_t).astype(BF16)
        gp_ref[:, 896:] = jnp.concatenate([own_ref[64:128, :], own_ref[192:256, :]], axis=0).astype(BF16)
        shared = qkv_share()
        for p in range(3):
            out_second(p)
        for copy in loads[7:] + w_loads:
            copy.wait()
        part[...] = back_through(0, 8)
        swap = push(part, got_part, partner())
        mlp_one[1].final()
        mlp_two[1].first()
        q_load.wait()
        for copy in shared:
            copy.wait()
        qkv_first()

        inputs = t_ref[...].astype(F32)
        inv = lax.rsqrt(jnp.mean(inputs * inputs, axis=1, keepdims=True) + 1e-06)
        d_norm1 = jnp.sum(part[...] * inputs * inv, axis=0, keepdims=True)
        d_bias = jnp.sum(gp_ref[...].astype(F32), axis=0, keepdims=True)
        core = lax.axis_index("tensor")
        for j in range(12):
            s_acc[0, j : j + 1, :] = d_norm1[:, j * 128 : (j + 1) * 128]
            s_acc[0, 12 + j : 13 + j, :] = dn2_ref[:, j * 128 : (j + 1) * 128]
        for j in range(8):
            v = d_bias[:, j * 128 : (j + 1) * 128]
            s_acc[0, 24 + j : 25 + j, :] = jnp.where(core == 0, v, 0.0)
            s_acc[0, 32 + j : 33 + j, :] = jnp.where(core == 1, v, 0.0)
        s_pending = []

        def send_small(stage):
            peers = [partner()] if stage == 0 else [peer(AXES[stage - 1], k) for k in (1, 2, 3)]
            for i, d in enumerate(peers):
                s_pending.append(push(s_acc.at[stage], s_got.at[stage * 3 + i], d))

        def sum_small(stage):
            for copy in s_pending:
                copy.wait()
            s_pending.clear()
            if stage == 0:
                return s_acc[0] + s_got[0]
            axis = AXES[stage - 1]
            parts = [s_acc[stage]] + [s_got[stage * 3 + k] for k in range(3)]
            total = jnp.zeros_like(parts[0])
            for w in range(4):
                term = jnp.zeros_like(total)
                for k in range(4):
                    term = jnp.where((c[axis] + 4 - k) % 4 == w, parts[k], term)
                total = total + term
            return total

        send_small(0)
        o_copies = [None] * 3
        for p in range(3):
            out_sum(p)
            o_copies[p] = share(o_acc2[p], o_got[p], OUT_ORDERS[p][2])
        s_acc[1] = sum_small(0)
        send_small(1)
        qkv_second()
        mlp_two[1].second()
        swap.wait()
        g_norm = part[...] + got_part[...]
        scaled = g_norm * gain_ref[0:1, :]
        gt_ref[...] += (
            inv * scaled - inputs * (inv * inv * inv) * jnp.mean(scaled * inputs, axis=1, keepdims=True)
        )
        s_acc[2] = sum_small(1)
        send_small(2)
        q_out = qkv_third()
        mlp_third(1)
        for p in range(3):
            for copy in o_copies[p]:
                copy.wait()
            rows = pl.ds(pl.multiple_of(c[OUT_ORDERS[p][2]] * 24, 8), 24)
            total = o_acc2[p][rows, :]
            for k in range(3):
                total = total + o_got[p][k]
            for j in range(2):
                go_ref[p * 2 + j] = total[:, j * 128 : (j + 1) * 128]
        for m in range(3):
            for copy in m_copies[m]:
                copy.wait()
            here = c[MLP_AXES[m][0]]
            m_outs[m][:, pl.ds(col_start(here), FC)] = acc2[m][pl.ds(pl.multiple_of(here * 24, 8), 24), :]
            for k in (1, 2, 3):
                m_outs[m][:, pl.ds(col_start((here + 4 - k) % 4), FC)] = m_got[m][k - 1]
        s_acc[3] = sum_small(2)
        send_small(3)
        qkv_out(q_out)
        s_out[...] = sum_small(3)

    rows = [rn for _, rn, _ in KV_CHUNK] * 2
    late = (tokens, g_mid)
    scratch = (
        [pltpu.VMEM((4, 384, 512), BF16)] * 3
        + [pltpu.VMEM((512, FC), BF16)] * 3
        + [pltpu.VMEM((4, 4, 4, 256, 128), BF16)]
        + [pltpu.VMEM((128, 1536), BF16)]
        + [pltpu.VMEM((96, FC), F32)] * 3
        + [pltpu.VMEM((96, 256), F32)] * 3
        + [pltpu.VMEM((8, 128, 96), F32), pltpu.VMEM((256, 128), F32)]
        + [pltpu.VMEM((4, 384, FC), BF16)] * 3
        + [pltpu.VMEM((2, 2, 192, FC), BF16)] * 3
        + [pltpu.VMEM((2, 192, FC), BF16)] * 3
        + [pltpu.VMEM((2, 2, 48, FC), BF16)] * 3
        + [pltpu.VMEM((2, 48, FC), BF16)] * 3
        + [pltpu.VMEM((4, 384, 256), BF16)]
        + [pltpu.VMEM((2, 2, 192, 256), BF16)] * 3
        + [pltpu.VMEM((2, 192, 256), BF16)] * 3
        + [pltpu.VMEM((3, 96, 256), BF16)] * 3
        + [pltpu.VMEM((3, 4, 4, r, 128), BF16) for r in rows[:3]]
        + [pltpu.VMEM((2, 2, 2, 4, r, 128), BF16) for r in rows[3:]]
        + [pltpu.VMEM((2, 2, 4, r, 128), BF16) for r in rows[3:]]
        + [pltpu.VMEM((3, 4, r, 128), BF16) for r in rows]
        + [pltpu.VMEM((3, r, 128), BF16) for r in rows]
        + [pltpu.VMEM((3, 24, FC), F32)] * 3
        + [pltpu.VMEM((3, 24, 256), F32)] * 3
        + [pltpu.VMEM((3, 96, 128), BF16)] * 2
        + [pltpu.VMEM((96, 256), F32), pltpu.VMEM((3, 24, 256), F32)]
        + [
            pltpu.VMEM((4, SMALL, 128), F32),
            pltpu.VMEM((12, SMALL, 128), F32),
            pltpu.VMEM((128, 1024), BF16),
            pltpu.VMEM((128, 1536), F32),
            pltpu.VMEM((128, 1536), F32),
            DMA((7 + n_late + 9,)),
            DMA((224,)),
            DMA((224,)),
        ]
    )
    vm, sm, hbm = (pl.BlockSpec(memory_space=m) for m in (pltpu.VMEM, pltpu.SMEM, pl.ANY))
    f32 = lambda *s: jax.ShapeDtypeStruct(s, F32)
    shape = (f32(128, 1536), f32(8, 24, 128), f32(6, 24, 128), f32(SMALL, 128))
    shape = shape + (f32(24, 4480),) * 3
    return pl.pallas_call(
        body,
        out_shape=shape,
        in_specs=[sm] + [hbm] * (11 + n_late) + [vm] * 10,
        out_specs=(vm,) * 7,
        scratch_shapes=scratch,
        compiler_params=pltpu.CompilerParams(collective_id=2, has_side_effects=True, vmem_limit_bytes=VMEM_BYTES),
        name="backward",
    )(lengths, *xs_in, *gs_in, kv, wq.reshape(6, 4, 384, 128), wk.reshape(4, 384, 128), wv.reshape(4, 384, 128), norm_shared, *late, q, g, lse, delta, branch_t, attn_low, cos, sin, gain, d_norm2)


def hand_out(qkv, *arrays):
    n = len(arrays)

    def body(*refs):
        ins, outs, held, sem = refs[: n + 1], refs[n + 1 : 2 * n + 4], refs[2 * n + 4 : 3 * n + 5], refs[3 * n + 5]
        to = [pltpu.make_async_copy(a, b, sem.at[i]) for i, (a, b) in enumerate(zip(ins, held))]
        pieces = [[(held[0].at[pl.ds(0, 6)], outs[0]), (held[0].at[6], outs[1]), (held[0].at[7], outs[2])]]
        pieces += [[(held[i], outs[i + 2])] for i in range(1, n + 1)]
        for copy in to:
            copy.start()
        back = []
        for i in range(n + 1):
            to[i].wait()
            for a, b in pieces[i]:
                copy = pltpu.make_async_copy(a, b, sem.at[n + 1 + len(back)])
                copy.start()
                back.append(copy)
        for copy in back:
            copy.wait()

    hbm = pl.BlockSpec(memory_space=pl.ANY)
    f32 = lambda *s: jax.ShapeDtypeStruct(s, F32)
    return pl.pallas_call(
        body,
        out_shape=(f32(6, 24, 128), f32(24, 128), f32(24, 128)) + tuple(f32(*v.shape) for v in arrays),
        in_specs=[hbm] * (n + 1),
        out_specs=(hbm,) * (n + 3),
        scratch_shapes=[pltpu.VMEM(v.shape, v.dtype) for v in (qkv, *arrays)] + [DMA((2 * n + 4,))],
        compiler_params=pltpu.CompilerParams(vmem_limit_bytes=VMEM_BYTES),
        name="hand_out",
    )(qkv, *arrays)


def local(
    tokens, cotangent, lengths, norm1_gain, w_query, b_query, w_key, b_key, w_value, b_value, w_out,
    norm2_gain, w_gate, w_up, w_down,
):
    device = lax.axis_index("seq")
    core = lax.axis_index("tensor")
    wq = w_query.transpose(1, 0, 2)
    wk, wv = w_key.reshape(1536, 128), w_value.reshape(1536, 128)
    wo = w_out.reshape(768, 1536)
    gains = jnp.stack([norm1_gain, norm2_gain])

    (output, g_mid, branch_t, g_attn, delta, d_norm2, q, cos, sin, attn_low, lse, *shared, kv, norm_shared) = forward(
        tokens, cotangent, lengths, gains, wq, wk, wv, b_query, b_key, b_value, wo, w_gate, w_up, w_down
    )
    grad_tokens, grad_qkv, grad_wo, sums, grad_gate, grad_up, grad_down = backward(
        shared[:3], shared[3:], q, g_attn, kv, lse, delta, branch_t, attn_low, lengths,
        cos, sin, norm_shared, wq, wk, wv, tokens, gains, g_mid, d_norm2,
    )
    grad_wq, grad_wk, grad_wv, output, grad_tokens, grad_wo, grad_gate, grad_up, grad_down = hand_out(
        grad_qkv, output, grad_tokens, grad_wo, grad_gate, grad_up, grad_down
    )
    sums = sums.reshape(-1)
    grad_norm1 = lax.dynamic_slice(sums, (device * 24,), (24,))
    grad_norm2 = lax.dynamic_slice(sums, (1536 + device * 24,), (24,))
    bias = lax.dynamic_slice(sums.reshape(SMALL, 128), (24 + core * 8, device * 2), (8, 2))
    return (
        output,
        grad_tokens,
        grad_norm1,
        grad_wq.transpose(1, 0, 2),
        bias[:6],
        grad_wk.reshape(24, 1, 128),
        bias[6:7],
        grad_wv.reshape(24, 1, 128),
        bias[7:8],
        grad_wo.transpose(0, 2, 1),
        grad_norm2,
        grad_gate,
        grad_up,
        grad_down.T,
    )


def solution(mesh):
    in_specs = (
        P("seq", None), P("seq", None), P(), P(), P(None, "tensor", None), P("tensor", None),
        P(None, "tensor", None), P("tensor", None), P(None, "tensor", None), P("tensor", None),
        P("tensor", None, None), P(), P(None, "tensor"), P(None, "tensor"), P("tensor", None),
    )
    out_specs = (
        P("seq", None), P("seq", None), P("seq"), P("seq", "tensor", None), P("tensor", "seq"),
        P("seq", "tensor", None), P("tensor", "seq"), P("seq", "tensor", None), P("tensor", "seq"),
        P("tensor", None, "seq"), P("seq"), P("seq", "tensor"), P("seq", "tensor"), P("tensor", "seq"),
    )
    return jax.shard_map(local, mesh=mesh, in_specs=in_specs, out_specs=out_specs, check_vma=False)
```

```python
import math

import jax
import jax.numpy as jnp
from jax import lax
from jax.experimental import pallas as pl
from jax.experimental.pallas import tpu as pltpu
from jax.sharding import PartitionSpec as P

MESH = pl.DeviceIdType.MESH
F32 = jnp.float32
BF16 = jnp.bfloat16
VMEM_BYTES = 60 * 1024 * 1024
AXES = ("z", "x", "y")
STRIDE = {"z": 16, "x": 4, "y": 1}


def coords():
    s = lax.axis_index("seq")
    return {"z": s // 16, "x": (s // 4) % 4, "y": s % 4}


def peer(axis, k):
    s = lax.axis_index("seq")
    c = coords()[axis]
    return (s + STRIDE[axis] * ((c + k) % 4 - c), lax.axis_index("tensor"))


def partner():
    return (lax.axis_index("seq"), 1 - lax.axis_index("tensor"))


def barrier(axes=AXES, core=False):
    bar = pltpu.get_barrier_semaphore()
    ids = [peer(a, k) for a in axes for k in (1, 2, 3)]
    if core:
        ids.append(partner())
    for d in ids:
        pl.semaphore_signal(bar, inc=1, device_id=d, device_id_type=MESH)
    pl.semaphore_wait(bar, len(ids))


def remote(src, dst, send, recv, device):
    return pltpu.make_async_remote_copy(
        src_ref=src, dst_ref=dst, send_sem=send, recv_sem=recv, device_id=device, device_id_type=MESH
    )


DMA = pltpu.SemaphoreType.DMA


KV_CHUNK = (
    (0, 48, ("z", "x", "y")),
    (48, 48, ("x", "y", "z")),
    (96, 32, ("y", "z", "x")),
)


def kv_rows(kb, v):
    return pl.ds(pl.multiple_of((kb // 4) * 128 + v * 64 + (kb % 4) * Q_BLK, Q_BLK), Q_BLK)


def kv_index(done, c, r0, rn):
    return tuple(slice(None) if a in done else c[a] for a in AXES) + (pl.ds(r0, rn), slice(None))


def rope_tables(len_ref):
    lane = lax.broadcasted_iota(jnp.int32, (128, 128), 1)
    pos = lax.broadcasted_iota(jnp.int32, (128, 128), 0) * 64 + lax.axis_index("seq")
    rel = (pos - doc_bounds(pos, len_ref)).astype(F32)
    inv_freq = jnp.exp(-(2.0 * (lane % 64).astype(F32) / 128) * math.log(10000.0))
    angle = rel * inv_freq
    sin = jnp.sin(angle)
    return jnp.cos(angle), jnp.where(lane < 64, -sin, sin)


def swap_halves(v):
    return pltpu.roll(v, 64, 1)


Q_BLK = 16
BLK = Q_BLK * 64
SCALE = 1.0 / math.sqrt(128)
SCALE2 = SCALE / math.log(2.0)


def doc_bounds(pos, len_ref):
    start = jnp.zeros_like(pos)
    end = jnp.int32(0)
    for j in range(8):
        end = end + len_ref[j]
        start = jnp.where(pos >= end, end, start)
    return start


FC = 1152


def nt(a, b):
    return lax.dot_general(a, b, (((1,), (1,)), ((), ())), preferred_element_type=F32)


def mm(a, b):
    return jnp.dot(a, b, preferred_element_type=F32)


def col_start(c):
    return pl.multiple_of(jnp.minimum(c * FC, 4480 - FC), 128)


MLP_AXES = (("z", "x", "y"), ("x", "y", "z"), ("y", "z", "x"))


def in_order(v, order):
    place = {}
    rows = []
    for i in range(64):
        for n, a in enumerate(order):
            place[a] = (i // (16, 4, 1)[n]) % 4
        o = place["z"] * 16 + place["x"] * 4 + place["y"]
        rows.append(v[o * 24 : (o + 1) * 24])
    return jnp.concatenate(rows, axis=0)


def forward(tokens, cot, lengths, gains, wq, wk, wv, bq, bk, bv, w_out, w_gate, w_up, w_down):
    def body(len_ref, t_ref, c_ref, g_ref, wk_ref, wv_ref, bq_ref, bk_ref, bv_ref, wq_hbm, wo_hbm, wg_hbm, wu_hbm, wd_hbm,
             out_ref, gmid_ref, bt_ref, ga_ref, delta_ref, dn_ref, q_ref, cos_out, sin_out, low_ref, lse_ref,
             x0, x1, x2, g0, g1, g2, kv_hbm, xq,
             kv, wq_ref, at_ref, m_ref, l_ref, acc_ref, gh_ref,
             wo_ref, wg, wu, wd, got_br, acc, got, norm_ref, nt_ref, ct_ref, n1_ref, xl, act, w_sem, loc, send, recv):
        xs, gs = (x0, x1, x2), (g0, g1, g2)
        c = coords()
        dev = lax.axis_index("seq")
        turn = c["z"] + c["x"] + c["y"]
        sems = iter(range(128))

        def load(j):
            cols = pl.ds(col_start((turn + j) % 4), FC)
            b = j % 2
            copies = [
                pltpu.make_async_copy(wg_hbm.at[:, cols], wg.at[b], w_sem.at[b, 0]),
                pltpu.make_async_copy(wu_hbm.at[:, cols], wu.at[b], w_sem.at[b, 1]),
                pltpu.make_async_copy(wd_hbm.at[cols, :], wd.at[b], w_sem.at[b, 2]),
            ]
            for copy in copies:
                copy.start()
            return copies

        def load_down(j):
            copy = pltpu.make_async_copy(wd_hbm.at[pl.ds(col_start((turn + j) % 4), FC), :], wd.at[j % 2], w_sem.at[j % 2, 2])
            copy.start()
            return copy

        def push(src, dst, device):
            n = next(sems)
            copy = remote(src, dst, send.at[n], recv.at[n], device)
            copy.start()
            return copy

        def keep(src, dst, n):
            copy = pltpu.make_async_copy(src, dst, loc.at[n])
            copy.start()
            return copy

        wq_load = keep(wq_hbm, wq_ref, 6)
        down = [load_down(0), load_down(1)]
        wo_load = keep(wo_hbm, wo_ref, 7)

        x = t_ref[...].astype(F32)
        inv = lax.rsqrt(jnp.mean(x * x, axis=1, keepdims=True) + 1e-06)
        normed = (x * inv * g_ref[0:1, :]).astype(BF16)
        cos, sin = rope_tables(len_ref)
        cos_out[...], sin_out[...] = cos, sin
        k_pre = mm(normed, wk_ref[...]) + bk_ref[...].astype(F32)
        v_low = (mm(normed, wv_ref[...]) + bv_ref[...].astype(F32)).astype(BF16)
        k_rot = (k_pre * cos + swap_halves(k_pre) * sin).astype(BF16)
        kv[c["z"], c["x"], c["y"]] = jnp.concatenate([k_rot[:64], v_low[:64], k_rot[64:], v_low[64:]], axis=0)
        barrier(core=True)
        kv_pending = [[] for _ in range(6)]

        def kv_wait(chunk):
            for p in range(chunk * 3, chunk * 3 + 3):
                for copy in kv_pending[p]:
                    copy.wait()
                kv_pending[p] = []

        def kv_stage(chunk, stage):
            for i, (r0, rn, order) in enumerate(KV_CHUNK):
                p, r0 = chunk * 3 + i, r0 + chunk * 128
                for copy in kv_pending[p]:
                    copy.wait()
                idx = kv_index(order[:stage], c, r0, rn)
                kv_pending[p] = [push(kv.at[idx], kv.at[idx], peer(order[stage], k)) for k in (1, 2, 3)]

        kv_stage(0, 0)
        kv_stage(1, 0)
        wq_load.wait()
        for h in range(6):
            q = mm(normed, wq_ref[h]) + bq_ref[h : h + 1, :].astype(F32)
            q = (q * cos + swap_halves(q) * sin).astype(BF16)
            q_ref[:, h * Q_BLK : (h + 1) * Q_BLK, :] = q.reshape(8, Q_BLK, 128)

        def g_hidden(j):
            down[j].wait()
            gh_ref[j] = nt(c_ref[...], wd[j % 2])
            if j < 2:
                down.append(load_down(j + 2))
            else:
                loads.append(load(j - 2))

        loads = []
        kv_stage(0, 1)
        kv_stage(1, 1)
        g_hidden(0)
        n1_ref[...] = in_order(normed.astype(F32).T, ("x", "y", "z")).astype(BF16).reshape(4, 384, 128)
        own_q = keep(n1_ref, xq.at[:, :, pl.ds(0, 128)], 10)
        g_hidden(1)
        kv_stage(0, 2)
        g_hidden(2)
        g_hidden(3)
        ct_ref[...] = c_ref[...].T.reshape(4, 384, 128)
        own = [keep(ct_ref, x2.at[:, :, pl.ds(0, 128)], 3)]
        kv_wait(0)
        kv_stage(1, 2)
        later = [push(ct_ref, x2.at[:, :, pl.ds(k * 128, 128)], peer("y", k)) for k in (1, 2, 3)]
        later += [push(n1_ref, xq.at[:, :, pl.ds(k * 128, 128)], peer("z", k)) for k in (1, 2, 3)]

        row_off = (lax.broadcasted_iota(jnp.int32, (96, 1), 0) % Q_BLK) * 64 + dev
        col = lax.broadcasted_iota(jnp.int32, (96, BLK), 1)
        key_off = (col % Q_BLK) * 64 + col // Q_BLK

        def attend(qb, lo, hi, carry, diagonal):
            q_blk = q_ref[qb]
            pos_q = row_off + qb * BLK
            start_q = doc_bounds(pos_q, len_ref)

            def block(kb, carry, causal):
                m, l, acc = carry
                k_blk = kv[:, :, :, kv_rows(kb, 0), :].reshape(BLK, 128)
                v_blk = kv[:, :, :, kv_rows(kb, 1), :].reshape(BLK, 128)
                pos_k = key_off + kb * BLK
                vis = pos_k >= start_q
                if causal:
                    vis = vis & (pos_k <= pos_q)
                s = jnp.where(vis, nt(q_blk, k_blk) * SCALE2, -1e30)
                m_new = jnp.maximum(m, jnp.max(s, axis=1, keepdims=True))
                p = jnp.exp2(s - m_new)
                a = jnp.exp2(m - m_new)
                return m_new, l * a + jnp.sum(p, axis=1, keepdims=True), acc * a + mm(p.astype(BF16), v_blk)

            carry = lax.fori_loop(lo, hi, lambda kb, carry: block(kb, carry, False), carry)
            return block(qb, carry, True) if diagonal else carry

        def attend_end(qb, carry):
            m, l, acc = carry
            attn = acc / l
            at_ref[qb] = attn
            low = attn.astype(BF16)
            for h in range(6):
                rows = pl.ds(pl.multiple_of(qb * Q_BLK, Q_BLK), Q_BLK)
                low_ref[rows, h * 128 : (h + 1) * 128] = low[h * Q_BLK : (h + 1) * Q_BLK]
            lse_ref[qb] = jnp.broadcast_to(m + jnp.log2(l), (96, 128)).T[0:1]

        init = (jnp.full((96, 1), -1e30, F32), jnp.zeros((96, 1), F32), jnp.zeros((96, 128), F32))

        def upper(qb, _):
            m_ref[qb - 4], l_ref[qb - 4], acc_ref[qb - 4] = attend(qb, 0, 4, init, False)
            return 0

        def whole(qb, _):
            attend_end(qb, attend(qb, 0, qb, init, True))
            return 0

        def rest(qb, _):
            attend_end(qb, attend(qb, 4, qb, (m_ref[qb - 4], l_ref[qb - 4], acc_ref[qb - 4]), True))
            return 0

        out_kv = [keep(kv.at[:, :, :, pl.ds(0, 128), :], kv_hbm.at[:, :, :, pl.ds(0, 128), :], 8)]
        lax.fori_loop(0, 4, whole, 0)
        lax.fori_loop(4, 8, upper, 0)
        kv_wait(1)
        out_kv.append(keep(kv.at[:, :, :, pl.ds(128, 128), :], kv_hbm.at[:, :, :, pl.ds(128, 128), :], 9))
        lax.fori_loop(4, 8, rest, 0)
        wo_load.wait()
        ex = []
        for half in range(2):
            cols = slice(half * 768, (half + 1) * 768)
            acc[half, :, 0:768] = mm(low_ref[...], wo_ref[:, cols])
            ex.append(push(acc.at[half, :, pl.ds(0, 768)], got_br.at[half], partner()))
        for copy in ex:
            copy.wait()
        mid = t_ref[...].astype(F32) + jnp.concatenate([acc[h, :, 0:768] + got_br[h] for h in range(2)], axis=1)
        out_ref[...] = mid
        inv = lax.rsqrt(jnp.mean(mid * mid, axis=1, keepdims=True) + 1e-06)
        normed = (mid * inv * g_ref[1:2, :]).astype(BF16)
        norm_ref[...] = normed
        turned = normed.astype(F32).T
        for m in range(2):
            nt_ref[m] = in_order(turned, MLP_AXES[m][1:] + MLP_AXES[m][:1]).astype(BF16).reshape(4, 384, 128)
        own.append(keep(nt_ref.at[0], x0.at[:, :, pl.ds(0, 128)], 4))
        own.append(keep(nt_ref.at[1], x1.at[:, :, pl.ds(0, 128)], 5))
        half = pl.ds(2 * lax.axis_index("tensor"), 2)
        halves = {}
        for k in (1, 2, 3):
            for m, w in ((0, "z"), (1, "x")):
                halves[m, k] = push(nt_ref.at[m, half], xl.at[m, k - 1], peer(w, k))

        def pass_on():
            n = 11
            for (m, k), copy in halves.items():
                copy.wait()
                there = xs[m].at[half, :, pl.ds(k * 128, 128)]
                later.append(push(xl.at[m, k - 1], there, partner()))
                later.append(keep(xl.at[m, k - 1], there, n))
                n += 1

        lane = lax.broadcasted_iota(jnp.int32, (128, FC), 1)
        for j in range(4):
            b = j % 2
            d = (turn + j) % 4
            for copy in loads[j]:
                copy.wait()
            n = norm_ref[...]
            gate = mm(n, wg[b])
            up = mm(n, wu[b])
            gh = gh_ref[j]
            sig = 1.0 / (1.0 + jnp.exp(-gate))
            silu = gate * sig
            hidden = (silu * up).astype(BF16)
            g_gate = (gh * up * sig * (1.0 + gate * (1.0 - sig))).astype(BF16)
            g_up = (gh * silu).astype(BF16)
            vals = (g_gate, g_up, hidden)
            for m in range(3):
                act[m, j] = vals[m]
            twice = (lane < 128) & (d == 3)
            zero = jnp.zeros((128, FC), BF16)
            hidden, g_gate, g_up = (jnp.where(twice, zero, v) for v in (hidden, g_gate, g_up))
            add_g = nt(g_gate, wg[b]) + nt(g_up, wu[b])
            acc[1] = add_g if j == 0 else acc[1] + add_g
            if j == 3:
                ex = [push(acc.at[1], got.at[1], partner())]
            add_o = mm(hidden, wd[b])
            acc[0] = add_o if j == 0 else acc[0] + add_o
            if j + 2 < 4:
                loads.append(load(j + 2))
            if j == 2:
                pass_on()
            for m in range(3):
                w = MLP_AXES[m][0]
                k = (d + 4 - c[w]) % 4
                slot = pl.ds(pl.multiple_of(k * 128, 128), 128)

                @pl.when(k == 0)
                def _():
                    pltpu.make_async_copy(act.at[m, j], gs[m].at[pl.ds(0, 128), :], loc.at[m]).start()

                @pl.when(k != 0)
                def _():
                    remote(
                        act.at[m, j], gs[m].at[slot, :], send.at[96 + m * 4 + j], recv.at[96 + m * 4 + k], peer(w, k)
                    ).start()

        ex.append(push(acc.at[0], got.at[0], partner()))
        dn_ref[...] = jnp.sum(acc[1] * out_ref[...] * inv, axis=0, keepdims=True)
        cot_f = c_ref[...].astype(F32)
        ex[0].wait()
        gn = acc[1] + got[1]
        mid = out_ref[...]
        scaled = gn * g_ref[1:2, :]
        g_mid = cot_f + (inv * scaled - mid * (inv * inv * inv) * jnp.mean(scaled * mid, axis=1, keepdims=True))
        gmid_ref[...] = g_mid
        branch_low = g_mid.astype(BF16)
        bt_ref[...] = branch_low.T
        g_attn = nt(branch_low, wo_ref[...]).astype(BF16)
        for h in range(6):
            ga_ref[:, h * Q_BLK : (h + 1) * Q_BLK, :] = g_attn[:, h * 128 : (h + 1) * 128].reshape(8, Q_BLK, 128)
        for qb in range(8):
            delta_ref[qb] = jnp.sum((ga_ref[qb].astype(F32) * at_ref[qb]).T, axis=0, keepdims=True)
        ex[1].wait()
        out_ref[...] += acc[0] + got[0]
        for copy in later + own + out_kv + [own_q]:
            copy.wait()
        for m in range(3):
            w = MLP_AXES[m][0]
            pltpu.make_async_copy(act.at[m, 0], gs[m].at[pl.ds(0, 128), :], loc.at[m]).wait()
            for j in range(4):
                k = ((turn + j) % 4 + 4 - c[w]) % 4

                @pl.when(k != 0)
                def _():
                    slot = pl.ds(pl.multiple_of(k * 128, 128), 128)
                    remote(
                        act.at[m, j], gs[m].at[slot, :], send.at[96 + m * 4 + j], recv.at[96 + m * 4 + k], peer(w, k)
                    ).wait()

    f32 = lambda *s: jax.ShapeDtypeStruct(s, F32)
    b16 = lambda *s: jax.ShapeDtypeStruct(s, BF16)
    vm, sm, hbm = (pl.BlockSpec(memory_space=m) for m in (pltpu.VMEM, pltpu.SMEM, pl.ANY))
    held = [(6, 1536, 128, BF16), (8, 96, 128, F32), (4, 96, 1, F32), (4, 96, 1, F32), (4, 96, 128, F32)]
    held += [(4, 128, FC, F32), (768, 1536, BF16), (2, 1536, FC, BF16), (2, 1536, FC, BF16), (2, FC, 1536, BF16)]
    held += [(2, 128, 768, F32), (2, 128, 1536, F32), (2, 128, 1536, F32), (128, 1536, BF16)]
    held += [(2, 4, 384, 128, BF16), (4, 384, 128, BF16), (4, 384, 128, BF16), (2, 3, 2, 384, 128, BF16), (3, 4, 128, FC, BF16)]
    return pl.pallas_call(
        body,
        out_shape=(f32(128, 1536), f32(128, 1536), b16(1536, 128), b16(8, 96, 128), f32(8, 1, 96), f32(1, 1536))
        + (b16(8, 96, 128), f32(128, 128), f32(128, 128), b16(128, 768), f32(8, 1, 96))
        + (b16(4, 384, 512),) * 3
        + (b16(512, FC),) * 3
        + (b16(4, 4, 4, 256, 128), b16(4, 384, 512)),
        in_specs=[sm] + [vm] * 8 + [hbm] * 5,
        out_specs=(vm,) * 11 + (hbm,) * 8,
        scratch_shapes=[pltpu.VMEM((4, 4, 4, 256, 128), BF16)]
        + [pltpu.VMEM(v[:-1], v[-1]) for v in held]
        + [DMA((2, 3)), DMA((17,)), DMA((112,)), DMA((112,))],
        compiler_params=pltpu.CompilerParams(collective_id=4, has_side_effects=True, vmem_limit_bytes=VMEM_BYTES),
        name="forward",
    )(lengths, tokens, cot, gains, wk, wv, bq, bk, bv, wq, w_out, w_gate, w_up, w_down)


OUT_ORDERS = (("z", "x", "y"), ("x", "y", "z"), ("y", "z", "x"))
QKV_ORDERS = (("x", "y"), ("y", "x"))
SMALL = 40


def slab_products(buf, left, rhs, order):
    def blocks(v, places):
        return jnp.concatenate([v[o * 24 : (o + 1) * 24] for o in places], axis=0)

    if order[0] == "z":
        for z in range(4):
            buf[z] = mm(left[z * 384 : (z + 1) * 384, :], rhs).astype(BF16)
    elif order[0] == "x":
        for x in range(4):
            lhs = jnp.concatenate([left[z * 384 + x * 96 : z * 384 + (x + 1) * 96, :] for z in range(4)], axis=0)
            buf[x] = blocks(mm(lhs, rhs), [z * 4 + y for y in range(4) for z in range(4)]).astype(BF16)
    else:
        for z in range(4):
            v = blocks(mm(left[z * 384 : (z + 1) * 384, :], rhs), [x * 4 + y for y in range(4) for x in range(4)])
            v = v.astype(BF16)
            for y in range(4):
                buf[y, z * 96 : (z + 1) * 96] = v[y * 96 : (y + 1) * 96]


def near(u):
    return u + 1 - 2 * (u % 2)


def far(u):
    return 3 - u


def over(u):
    return (u + 2) % 4


class Halves:
    def __init__(self, push, axis, c, slab, got_first, got_second):
        self.push, self.slab, self.u = push, slab, c[axis]
        self.got_first, self.got_second = got_first, got_second
        self.to = lambda place: peer(axis, place + 4 - c[axis])
        self.one, self.two = {}, []

    def ready(self, which):
        u = self.u
        if which == "over":
            self.one[0, 0] = self.push(self.slab(over(u), 0), self.got_first(0, 0), self.to(near(u)))
            self.one[1, 0] = self.push(self.slab(over(u), 1), self.got_first(1, 0), self.to(far(u)))
        elif which == "near":
            self.one[0, 1] = self.push(self.slab(near(u), 0), self.got_first(0, 1), self.to(near(u)))
        elif which == "far":
            self.one[1, 1] = self.push(self.slab(far(u), 1), self.got_first(1, 1), self.to(far(u)))

    def first(self):
        for which in ("over", "near", "far"):
            self.ready(which)

    def second(self):
        u = self.u
        for h, place in ((0, far(u)), (1, near(u))):
            self.one[h, 0].wait()
            at = self.slab(place, h)
            at[...] = (at[...].astype(F32) + self.got_first(h, 0)[...].astype(F32)).astype(BF16)
            self.two.append(self.push(at, self.got_second(h), self.to(place)))

    def final(self):
        for h in range(2):
            self.one[h, 1].wait()
            self.two[h].wait()
            at = self.slab(self.u, h)
            at[...] = (
                at[...].astype(F32) + self.got_first(h, 1)[...].astype(F32) + self.got_second(h)[...].astype(F32)
            ).astype(BF16)


def sum_first(buf, got, copies, own):
    for copy in copies:
        copy.wait()
    total = buf[own].astype(F32)
    for k in range(3):
        total = total + got[k][...].astype(F32)
    buf[own] = total.astype(BF16)


def backward(xs_in, gs_in, q, g, kv, lse, delta, branch_t, attn_low, lengths,
             cos, sin, norm_shared, wq, wk, wv, tokens, gain, g_mid, d_norm2):
    n_late = 2

    def body(*refs):
        r = list(refs)
        take = lambda n: [r.pop(0) for _ in range(n)]
        (len_ref,), xs_hbm, gs_hbm, (kv_hbm, *w_hbm, xq_hbm), late = take(1), take(3), take(3), take(5), take(n_late)
        q_ref, g_ref, lse_ref, delta_ref, bt_ref, a_ref, cos_ref, sin_ref, gain_ref, dn2_ref = take(10)
        gt_ref, gqkv_ref, go_ref, s_out = take(4)
        m_outs = take(3)
        xs, gs, (dkv,), (t_ref,) = take(3), take(3), take(1), take(1)
        held = (t_ref, gt_ref)
        acc2, o_acc2, (dq_ref, own_ref) = take(3), take(3), take(2)
        sendbuf, r1, r2, t1, t2 = take(3), take(3), take(3), take(3), take(3)
        o_buf, o_r1, o_r2, o_got2 = take(1), take(3), take(3), take(3)
        kv1, kv1b, kv2, kv3 = take(6), take(6), take(6), take(6)
        m_got, o_got = take(3), take(3)
        q_got2, (q_acc2, q_got3) = take(2), take(2)
        o_buf = [xs[2].at[:, :, 0:256], xs[2].at[:, :, 256:512], o_buf[0]]
        q_left, q_right = xs[0], gs[0].at[:, 0:256]
        q_buf = [xs[1].at[:, :, 0:128], xs[1].at[:, :, 128:256]]
        q_got1 = [
            [gs[0].at[0:384, lo + k * 128 : lo + (k + 1) * 128] for k in range(3)] for lo in (256, 640)
        ]
        s_acc, s_got, gp_ref, part, got_part = take(5)
        loc, send, recv = take(3)
        c = coords()
        loads = [pltpu.make_async_copy(a, b, loc.at[i]) for i, (a, b) in enumerate(
            ((xs_hbm[0], xs[0]), (gs_hbm[0], gs[0]), (xs_hbm[2], xs[2]), (gs_hbm[2], gs[2]),
             (xs_hbm[1], xs[1]), (gs_hbm[1], gs[1]), (kv_hbm, dkv), *zip(late, held)))]
        for copy in loads:
            copy.start()
        barrier(core=True)
        sems = iter(range(256))

        def push(src, dst, device):
            n = next(sems)
            copy = remote(src, dst, send.at[n], recv.at[n], device)
            copy.start()
            return copy

        def mlp_slab(m):
            return lambda u, h: sendbuf[m].at[u, pl.ds(192 * h, 192), :]

        mlp_one = [
            Halves(push, MLP_AXES[m][1], c, mlp_slab(m), lambda h, i, m=m: r1[m].at[h, i], lambda h, m=m: r2[m].at[h])
            for m in range(3)
        ]

        def mlp_rows(m):
            own = sendbuf[m].at[c[MLP_AXES[m][1]]]
            return lambda u, h: own.at[pl.ds(pl.multiple_of(u * 96 + h * 48, 16), 48), :]

        mlp_two = [
            Halves(push, MLP_AXES[m][2], c, mlp_rows(m), lambda h, i, m=m: t1[m].at[h, i], lambda h, m=m: t2[m].at[h])
            for m in range(3)
        ]

        for name, place in (("over", over), ("near", near), ("far", far), ("own", lambda v: v)):
            for i, m in enumerate((0, 2, 1)):
                if name == "over":
                    loads[2 * i].wait()
                    loads[2 * i + 1].wait()
                u = place(c[MLP_AXES[m][1]])
                x = xs[m][u]
                sendbuf[m][u] = mm(x, gs[m][...]).astype(BF16)
                mlp_one[m].ready(name)

        def buf_slab(buf):
            return lambda u, h: buf.at[u, pl.ds(192 * h, 192), :]

        out_one = [
            Halves(push, OUT_ORDERS[p][0], c, buf_slab(o_buf[p]), lambda h, i, p=p: o_r1[p].at[h, i], lambda h, p=p: o_r2[p].at[h])
            for p in range(3)
        ]
        o_second = [[], [], []]

        def out_second(p):
            order = OUT_ORDERS[p]
            out_one[p].final()
            for k in (1, 2, 3):
                rows = pl.ds(pl.multiple_of(((c[order[1]] + k) % 4) * 96, 32), 96)
                o_second[p].append(push(o_buf[p].at[c[order[0]], rows, :], o_got2[p].at[k - 1], peer(order[1], k)))

        def out_sum(p):
            order = OUT_ORDERS[p]
            for copy in o_second[p]:
                copy.wait()
            rows = pl.ds(pl.multiple_of(c[order[1]] * 96, 32), 96)
            total = o_buf[p][c[order[0]], rows, :].astype(F32)
            for k in range(3):
                total = total + o_got2[p][k].astype(F32)
            o_acc2[p][...] = total

        loads[6].wait()
        dev = lax.axis_index("seq")
        row = lax.broadcasted_iota(jnp.int32, (BLK, 96), 0)
        key_off = (row % Q_BLK) * 64 + row // Q_BLK
        q_off = (lax.broadcasted_iota(jnp.int32, (1, 96), 1) % Q_BLK) * 64 + dev
        dq_ref[...] = jnp.zeros_like(dq_ref)

        def k_step(kb, _):
            k_blk = dkv[:, :, :, kv_rows(kb, 0), :].reshape(BLK, 128)
            v_blk = dkv[:, :, :, kv_rows(kb, 1), :].reshape(BLK, 128)
            k_t = k_blk.T
            pos_k = key_off + kb * BLK

            def pair(qb, carry, causal):
                dk, dv = carry
                q_blk, g_blk = q_ref[qb], g_ref[qb]
                pos_q = q_off + qb * BLK
                vis = pos_k >= doc_bounds(pos_q, len_ref)
                if causal:
                    vis = vis & (pos_k <= pos_q)
                s = nt(k_blk, q_blk)
                p = jnp.where(vis, jnp.exp2(s * SCALE2 - lse_ref[qb]), 0.0)
                gp = nt(v_blk, g_blk)
                ds = (p * (gp - delta_ref[qb])).astype(BF16)
                dq_ref[qb] += mm(k_t, ds)
                dk = dk + mm(ds, q_blk)
                dv = dv + mm(p.astype(BF16), g_blk)
                return dk, dv

            zero = jnp.zeros((BLK, 128), F32)
            carry = pair(kb, (zero, zero), True)
            dk, dv = lax.fori_loop(kb + 1, 8, lambda qb, carry: pair(qb, carry, False), carry)
            dkv[:, :, :, kv_rows(kb, 0), :] = (dk * SCALE).astype(BF16).reshape(4, 4, 4, Q_BLK, 128)
            dkv[:, :, :, kv_rows(kb, 1), :] = dv.astype(BF16).reshape(4, 4, 4, Q_BLK, 128)
            return 0

        kv_pending = [[] for _ in range(6)]
        kv_parts = [(r0 + 128 * chunk, rn, order) for chunk in range(2) for r0, rn, order in KV_CHUNK]

        def kv_slab(p):
            r0, rn, order = kv_parts[p]
            rest = [a for a in AXES if a != order[0]]

            def slab(u, h):
                where = {order[0]: u, rest[0]: pl.ds(2 * h, 2), rest[1]: slice(None)}
                return dkv.at[where["z"], where["x"], where["y"], pl.ds(r0, rn), :]

            return slab

        kv_one = [
            Halves(push, kv_parts[p][2][0], c, kv_slab(p), lambda h, i, p=p: kv1[p].at[h, i], lambda h, p=p: kv1b[p].at[h])
            for p in range(6)
        ]

        def kv_halves(chunk, step):
            for p in range(chunk * 3, chunk * 3 + 3):
                getattr(kv_one[p], step)()

        def kv_stage(chunk, stage):
            got = (None, kv2, kv3)
            for p in range(chunk * 3, chunk * 3 + 3):
                r0, rn, order = kv_parts[p]
                if stage == 1:
                    kv_one[p].final()
                else:
                    for copy in kv_pending[p]:
                        copy.wait()
                    kv_pending[p] = []
                    mine = kv_index(order[stage:], c, r0, rn)
                    own = dkv[mine].astype(F32)
                    for k in range(3):
                        own = own + got[stage - 1][p][k].astype(F32)
                    if stage == 3:
                        own_ref[pl.ds(r0, rn), :] = own
                        continue
                    dkv[mine] = own.astype(BF16)
                for k in (1, 2, 3):
                    cc = dict(c)
                    cc[order[stage]] = (c[order[stage]] + k) % 4
                    src = dkv.at[kv_index(order[stage + 1 :], cc, r0, rn)]
                    kv_pending[p].append(push(src, got[stage][p].at[k - 1], peer(order[stage], k)))

        def share(acc, got, axis):
            copies = []
            for k in (1, 2, 3):
                rows = pl.ds(pl.multiple_of(((c[axis] + k) % 4) * 24, 8), 24)
                copies.append(push(acc.at[rows, :], got.at[k - 1], peer(axis, k)))
            return copies

        q_copies = [[], []]

        def qkv_share():
            mine = pl.ds(pl.multiple_of(c["z"] * 256, 256), 256)
            copies = []
            for k in (1, 2, 3):
                cols = pl.ds(pl.multiple_of((c["z"] + k) % 4 * 256, 256), 256)
                copies.append(push(gp_ref.at[:, cols], q_right.at[k * 128 : (k + 1) * 128, :], peer("z", k)))
            q_right[0:128, :] = gp_ref[:, mine]
            return copies

        def qkv_first():
            for k in (2, 1, 3, 0):
                for p, (one, _) in enumerate(QKV_ORDERS):
                    u = (c[one] + k) % 4
                    if p == 0:
                        left = q_left[u]
                    else:
                        rows = pl.ds(pl.multiple_of(u * 96, 32), 96)
                        left = jnp.concatenate([q_left[x, rows, :] for x in range(4)], axis=0)
                    q_buf[p][u] = mm(left, q_right[:, p * 128 : (p + 1) * 128]).astype(BF16)
                    if k:
                        q_copies[p].append(push(q_buf[p].at[u], q_got1[p][k - 1], peer(one, k)))

        def qkv_second():
            for p, (one, two) in enumerate(QKV_ORDERS):
                sum_first(q_buf[p], q_got1[p], q_copies[p], c[one])
                q_copies[p] = []
                for k in (1, 2, 3):
                    rows = pl.ds(pl.multiple_of(((c[two] + k) % 4) * 96, 32), 96)
                    q_copies[p].append(push(q_buf[p].at[c[one], rows, :], q_got2[p].at[k - 1], peer(two, k)))

        def qkv_third():
            for p in range(2):
                one, two = QKV_ORDERS[p]
                for copy in q_copies[p]:
                    copy.wait()
                rows = pl.ds(pl.multiple_of(c[two] * 96, 32), 96)
                total = q_buf[p][c[one], rows, :].astype(F32)
                for k in range(3):
                    total = total + q_got2[p][k].astype(F32)
                q_acc2[:, p * 128 : (p + 1) * 128] = total
            return share(q_acc2, q_got3, "z")

        def qkv_out(copies):
            for copy in copies:
                copy.wait()
            for k in range(4):
                v = q_acc2[pl.ds(pl.multiple_of(c["z"] * 24, 8), 24), :] if k == 0 else q_got3[k - 1]
                block = (c["z"] + 4 - k) % 4
                gqkv_ref[2 * block] = v[:, :128]
                gqkv_ref[2 * block + 1] = v[:, 128:]

        m_copies = [None] * 3

        def mlp_third(m):
            mlp_two[m].final()
            rows = pl.ds(pl.multiple_of(c[MLP_AXES[m][2]] * 96, 32), 96)
            acc2[m][...] = sendbuf[m][c[MLP_AXES[m][1]], rows, :].astype(F32)
            m_copies[m] = share(acc2[m], m_got[m], MLP_AXES[m][0])

        lax.fori_loop(4, 8, k_step, 0)
        kv_halves(1, "first")
        mlp_one[0].second()
        lax.fori_loop(0, 1, k_step, 0)
        mlp_one[2].second()
        mlp_one[1].second()
        kv_halves(1, "second")
        lax.fori_loop(1, 2, k_step, 0)
        for p, order in enumerate(OUT_ORDERS):
            slab_products(o_buf[p], bt_ref, a_ref[:, p * 256 : (p + 1) * 256], order)
            out_one[p].first()
        mlp_one[0].final()
        mlp_two[0].first()
        lax.fori_loop(2, 3, k_step, 0)
        kv_stage(1, 1)
        for m in (2, 1):
            mlp_one[m].final()
            mlp_two[m].first()
        lax.fori_loop(3, 4, k_step, 0)
        kv_halves(0, "first")

        cos_t, sin_t = cos_ref[...], sin_ref[...]
        for qb in range(8):
            dq = dq_ref[qb].T * SCALE
            rows = slice(qb * Q_BLK, (qb + 1) * Q_BLK)
            cs, sn = cos_t[rows], sin_t[rows]
            for h in range(6):
                v = dq[h * Q_BLK : (h + 1) * Q_BLK]
                gp_ref[rows, h * 128 : (h + 1) * 128] = (v * cs - swap_halves(v) * sn).astype(BF16)
        mlp_two[0].second()
        kv_halves(0, "second")
        for p in range(3):
            out_one[p].second()
        for m in (2, 1):
            mlp_two[m].second()
        q_load = pltpu.make_async_copy(xq_hbm, q_left, loc.at[7 + n_late + 8])
        q_load.start()
        kv_stage(1, 2)
        kv_stage(0, 1)
        kv_stage(0, 2)
        for m in (0, 2, 1):
            mlp_third(m)
        w_ref = [sendbuf[0].at[:, :, h * 128 : (h + 1) * 128] for h in range(8)]
        w_from = [w_hbm[0].at[h] for h in range(6)] + [w_hbm[1], w_hbm[2]]
        w_loads = [pltpu.make_async_copy(w_from[h], w_ref[h], loc.at[7 + n_late + h]) for h in range(8)]
        for copy in w_loads:
            copy.start()

        def back_through(lo, hi):
            total = nt(gp_ref[:, lo * 128 : (lo + 1) * 128], w_ref[lo][...].reshape(1536, 128))
            for h in range(lo + 1, hi):
                total = total + nt(gp_ref[:, h * 128 : (h + 1) * 128], w_ref[h][...].reshape(1536, 128))
            return total

        kv_stage(1, 3)
        kv_stage(0, 3)

        dk = jnp.concatenate([own_ref[0:64, :], own_ref[128:192, :]], axis=0)
        gp_ref[:, 768:896] = (dk * cos_t - swap_halves(dk) * sin_t).astype(BF16)
        gp_ref[:, 896:] = jnp.concatenate([own_ref[64:128, :], own_ref[192:256, :]], axis=0).astype(BF16)
        shared = qkv_share()
        for p in range(3):
            out_second(p)
        for copy in loads[7:] + w_loads:
            copy.wait()
        part[...] = back_through(0, 8)
        swap = push(part, got_part, partner())
        q_load.wait()
        for copy in shared:
            copy.wait()
        qkv_first()

        inputs = t_ref[...].astype(F32)
        inv = lax.rsqrt(jnp.mean(inputs * inputs, axis=1, keepdims=True) + 1e-06)
        d_norm1 = jnp.sum(part[...] * inputs * inv, axis=0, keepdims=True)
        d_bias = jnp.sum(gp_ref[...].astype(F32), axis=0, keepdims=True)
        core = lax.axis_index("tensor")
        for j in range(12):
            s_acc[0, j : j + 1, :] = d_norm1[:, j * 128 : (j + 1) * 128]
            s_acc[0, 12 + j : 13 + j, :] = dn2_ref[:, j * 128 : (j + 1) * 128]
        for j in range(8):
            v = d_bias[:, j * 128 : (j + 1) * 128]
            s_acc[0, 24 + j : 25 + j, :] = jnp.where(core == 0, v, 0.0)
            s_acc[0, 32 + j : 33 + j, :] = jnp.where(core == 1, v, 0.0)
        s_pending = []

        def send_small(stage):
            peers = [partner()] if stage == 0 else [peer(AXES[stage - 1], k) for k in (1, 2, 3)]
            for i, d in enumerate(peers):
                s_pending.append(push(s_acc.at[stage], s_got.at[stage * 3 + i], d))

        def sum_small(stage):
            for copy in s_pending:
                copy.wait()
            s_pending.clear()
            if stage == 0:
                return s_acc[0] + s_got[0]
            axis = AXES[stage - 1]
            parts = [s_acc[stage]] + [s_got[stage * 3 + k] for k in range(3)]
            total = jnp.zeros_like(parts[0])
            for w in range(4):
                term = jnp.zeros_like(total)
                for k in range(4):
                    term = jnp.where((c[axis] + 4 - k) % 4 == w, parts[k], term)
                total = total + term
            return total

        send_small(0)
        qkv_second()
        o_copies = [None] * 3
        for p in range(3):
            out_sum(p)
            o_copies[p] = share(o_acc2[p], o_got[p], OUT_ORDERS[p][2])
        s_acc[1] = sum_small(0)
        send_small(1)
        swap.wait()
        g_norm = part[...] + got_part[...]
        scaled = g_norm * gain_ref[0:1, :]
        gt_ref[...] += (
            inv * scaled - inputs * (inv * inv * inv) * jnp.mean(scaled * inputs, axis=1, keepdims=True)
        )
        s_acc[2] = sum_small(1)
        send_small(2)
        q_out = qkv_third()
        for p in range(3):
            for copy in o_copies[p]:
                copy.wait()
            rows = pl.ds(pl.multiple_of(c[OUT_ORDERS[p][2]] * 24, 8), 24)
            total = o_acc2[p][rows, :]
            for k in range(3):
                total = total + o_got[p][k]
            for j in range(2):
                go_ref[p * 2 + j] = total[:, j * 128 : (j + 1) * 128]
        for m in range(3):
            for copy in m_copies[m]:
                copy.wait()
            here = c[MLP_AXES[m][0]]
            m_outs[m][:, pl.ds(col_start(here), FC)] = acc2[m][pl.ds(pl.multiple_of(here * 24, 8), 24), :]
            for k in (1, 2, 3):
                m_outs[m][:, pl.ds(col_start((here + 4 - k) % 4), FC)] = m_got[m][k - 1]
        s_acc[3] = sum_small(2)
        send_small(3)
        qkv_out(q_out)
        s_out[...] = sum_small(3)

    rows = [rn for _, rn, _ in KV_CHUNK] * 2
    late = (tokens, g_mid)
    scratch = (
        [pltpu.VMEM((4, 384, 512), BF16)] * 3
        + [pltpu.VMEM((512, FC), BF16)] * 3
        + [pltpu.VMEM((4, 4, 4, 256, 128), BF16)]
        + [pltpu.VMEM((128, 1536), BF16)]
        + [pltpu.VMEM((96, FC), F32)] * 3
        + [pltpu.VMEM((96, 256), F32)] * 3
        + [pltpu.VMEM((8, 128, 96), F32), pltpu.VMEM((256, 128), F32)]
        + [pltpu.VMEM((4, 384, FC), BF16)] * 3
        + [pltpu.VMEM((2, 2, 192, FC), BF16)] * 3
        + [pltpu.VMEM((2, 192, FC), BF16)] * 3
        + [pltpu.VMEM((2, 2, 48, FC), BF16)] * 3
        + [pltpu.VMEM((2, 48, FC), BF16)] * 3
        + [pltpu.VMEM((4, 384, 256), BF16)]
        + [pltpu.VMEM((2, 2, 192, 256), BF16)] * 3
        + [pltpu.VMEM((2, 192, 256), BF16)] * 3
        + [pltpu.VMEM((3, 96, 256), BF16)] * 3
        + [pltpu.VMEM((2, 2, 2, 4, r, 128), BF16) for r in rows]
        + [pltpu.VMEM((2, 2, 4, r, 128), BF16) for r in rows]
        + [pltpu.VMEM((3, 4, r, 128), BF16) for r in rows]
        + [pltpu.VMEM((3, r, 128), BF16) for r in rows]
        + [pltpu.VMEM((3, 24, FC), F32)] * 3
        + [pltpu.VMEM((3, 24, 256), F32)] * 3
        + [pltpu.VMEM((3, 96, 128), BF16)] * 2
        + [pltpu.VMEM((96, 256), F32), pltpu.VMEM((3, 24, 256), F32)]
        + [
            pltpu.VMEM((4, SMALL, 128), F32),
            pltpu.VMEM((12, SMALL, 128), F32),
            pltpu.VMEM((128, 1024), BF16),
            pltpu.VMEM((128, 1536), F32),
            pltpu.VMEM((128, 1536), F32),
            DMA((7 + n_late + 9,)),
            DMA((224,)),
            DMA((224,)),
        ]
    )
    vm, sm, hbm = (pl.BlockSpec(memory_space=m) for m in (pltpu.VMEM, pltpu.SMEM, pl.ANY))
    f32 = lambda *s: jax.ShapeDtypeStruct(s, F32)
    shape = (f32(128, 1536), f32(8, 24, 128), f32(6, 24, 128), f32(SMALL, 128))
    shape = shape + (f32(24, 4480),) * 3
    return pl.pallas_call(
        body,
        out_shape=shape,
        in_specs=[sm] + [hbm] * (11 + n_late) + [vm] * 10,
        out_specs=(vm,) * 7,
        scratch_shapes=scratch,
        compiler_params=pltpu.CompilerParams(collective_id=2, has_side_effects=True, vmem_limit_bytes=VMEM_BYTES),
        name="backward",
    )(lengths, *xs_in, *gs_in, kv, wq.reshape(6, 4, 384, 128), wk.reshape(4, 384, 128), wv.reshape(4, 384, 128), norm_shared, *late, q, g, lse, delta, branch_t, attn_low, cos, sin, gain, d_norm2)


def hand_out(qkv, *arrays):
    n = len(arrays)

    def body(*refs):
        ins, outs, held, sem = refs[: n + 1], refs[n + 1 : 2 * n + 4], refs[2 * n + 4 : 3 * n + 5], refs[3 * n + 5]
        to = [pltpu.make_async_copy(a, b, sem.at[i]) for i, (a, b) in enumerate(zip(ins, held))]
        pieces = [[(held[0].at[pl.ds(0, 6)], outs[0]), (held[0].at[6], outs[1]), (held[0].at[7], outs[2])]]
        pieces += [[(held[i], outs[i + 2])] for i in range(1, n + 1)]
        for copy in to:
            copy.start()
        back = []
        for i in range(n + 1):
            to[i].wait()
            for a, b in pieces[i]:
                copy = pltpu.make_async_copy(a, b, sem.at[n + 1 + len(back)])
                copy.start()
                back.append(copy)
        for copy in back:
            copy.wait()

    hbm = pl.BlockSpec(memory_space=pl.ANY)
    f32 = lambda *s: jax.ShapeDtypeStruct(s, F32)
    return pl.pallas_call(
        body,
        out_shape=(f32(6, 24, 128), f32(24, 128), f32(24, 128)) + tuple(f32(*v.shape) for v in arrays),
        in_specs=[hbm] * (n + 1),
        out_specs=(hbm,) * (n + 3),
        scratch_shapes=[pltpu.VMEM(v.shape, v.dtype) for v in (qkv, *arrays)] + [DMA((2 * n + 4,))],
        compiler_params=pltpu.CompilerParams(vmem_limit_bytes=VMEM_BYTES),
        name="hand_out",
    )(qkv, *arrays)


def local(
    tokens, cotangent, lengths, norm1_gain, w_query, b_query, w_key, b_key, w_value, b_value, w_out,
    norm2_gain, w_gate, w_up, w_down,
):
    device = lax.axis_index("seq")
    core = lax.axis_index("tensor")
    wq = w_query.transpose(1, 0, 2)
    wk, wv = w_key.reshape(1536, 128), w_value.reshape(1536, 128)
    wo = w_out.reshape(768, 1536)
    gains = jnp.stack([norm1_gain, norm2_gain])

    (output, g_mid, branch_t, g_attn, delta, d_norm2, q, cos, sin, attn_low, lse, *shared, kv, norm_shared) = forward(
        tokens, cotangent, lengths, gains, wq, wk, wv, b_query, b_key, b_value, wo, w_gate, w_up, w_down
    )
    grad_tokens, grad_qkv, grad_wo, sums, grad_gate, grad_up, grad_down = backward(
        shared[:3], shared[3:], q, g_attn, kv, lse, delta, branch_t, attn_low, lengths,
        cos, sin, norm_shared, wq, wk, wv, tokens, gains, g_mid, d_norm2,
    )
    grad_wq, grad_wk, grad_wv, output, grad_tokens, grad_wo, grad_gate, grad_up, grad_down = hand_out(
        grad_qkv, output, grad_tokens, grad_wo, grad_gate, grad_up, grad_down
    )
    sums = sums.reshape(-1)
    grad_norm1 = lax.dynamic_slice(sums, (device * 24,), (24,))
    grad_norm2 = lax.dynamic_slice(sums, (1536 + device * 24,), (24,))
    bias = lax.dynamic_slice(sums.reshape(SMALL, 128), (24 + core * 8, device * 2), (8, 2))
    return (
        output,
        grad_tokens,
        grad_norm1,
        grad_wq.transpose(1, 0, 2),
        bias[:6],
        grad_wk.reshape(24, 1, 128),
        bias[6:7],
        grad_wv.reshape(24, 1, 128),
        bias[7:8],
        grad_wo.transpose(0, 2, 1),
        grad_norm2,
        grad_gate,
        grad_up,
        grad_down.T,
    )


def solution(mesh):
    in_specs = (
        P("seq", None), P("seq", None), P(), P(), P(None, "tensor", None), P("tensor", None),
        P(None, "tensor", None), P("tensor", None), P(None, "tensor", None), P("tensor", None),
        P("tensor", None, None), P(), P(None, "tensor"), P(None, "tensor"), P("tensor", None),
    )
    out_specs = (
        P("seq", None), P("seq", None), P("seq"), P("seq", "tensor", None), P("tensor", "seq"),
        P("seq", "tensor", None), P("tensor", "seq"), P("seq", "tensor", None), P("tensor", "seq"),
        P("tensor", None, "seq"), P("seq"), P("seq", "tensor"), P("seq", "tensor"), P("tensor", "seq"),
    )
    return jax.shard_map(local, mesh=mesh, in_specs=in_specs, out_specs=out_specs, check_vma=False)
```

```python
import math

import jax
import jax.numpy as jnp
from jax import lax
from jax.experimental import pallas as pl
from jax.experimental.pallas import tpu as pltpu
from jax.sharding import PartitionSpec as P

MESH = pl.DeviceIdType.MESH
F32 = jnp.float32
BF16 = jnp.bfloat16
VMEM_BYTES = 60 * 1024 * 1024
AXES = ("z", "x", "y")
STRIDE = {"z": 16, "x": 4, "y": 1}


def coords():
    s = lax.axis_index("seq")
    return {"z": s // 16, "x": (s // 4) % 4, "y": s % 4}


def peer(axis, k):
    s = lax.axis_index("seq")
    c = coords()[axis]
    return (s + STRIDE[axis] * ((c + k) % 4 - c), lax.axis_index("tensor"))


def partner():
    return (lax.axis_index("seq"), 1 - lax.axis_index("tensor"))


def barrier(axes=AXES, core=False):
    bar = pltpu.get_barrier_semaphore()
    ids = [peer(a, k) for a in axes for k in (1, 2, 3)]
    if core:
        ids.append(partner())
    for d in ids:
        pl.semaphore_signal(bar, inc=1, device_id=d, device_id_type=MESH)
    pl.semaphore_wait(bar, len(ids))


def remote(src, dst, send, recv, device):
    return pltpu.make_async_remote_copy(
        src_ref=src, dst_ref=dst, send_sem=send, recv_sem=recv, device_id=device, device_id_type=MESH
    )


DMA = pltpu.SemaphoreType.DMA


KV_CHUNK = (
    (0, 48, ("z", "x", "y")),
    (48, 48, ("x", "y", "z")),
    (96, 32, ("y", "z", "x")),
)


def kv_rows(kb, v):
    return pl.ds(pl.multiple_of((kb // 4) * 128 + v * 64 + (kb % 4) * Q_BLK, Q_BLK), Q_BLK)


def kv_index(done, c, r0, rn):
    return tuple(slice(None) if a in done else c[a] for a in AXES) + (pl.ds(r0, rn), slice(None))


def rope_tables(len_ref):
    lane = lax.broadcasted_iota(jnp.int32, (128, 128), 1)
    pos = lax.broadcasted_iota(jnp.int32, (128, 128), 0) * 64 + lax.axis_index("seq")
    rel = (pos - doc_bounds(pos, len_ref)).astype(F32)
    inv_freq = jnp.exp(-(2.0 * (lane % 64).astype(F32) / 128) * math.log(10000.0))
    angle = rel * inv_freq
    sin = jnp.sin(angle)
    return jnp.cos(angle), jnp.where(lane < 64, -sin, sin)


def swap_halves(v):
    return pltpu.roll(v, 64, 1)


Q_BLK = 16
BLK = Q_BLK * 64
SCALE = 1.0 / math.sqrt(128)
SCALE2 = SCALE / math.log(2.0)


def doc_bounds(pos, len_ref):
    start = jnp.zeros_like(pos)
    end = jnp.int32(0)
    for j in range(8):
        end = end + len_ref[j]
        start = jnp.where(pos >= end, end, start)
    return start


FC = 1152


def nt(a, b):
    return lax.dot_general(a, b, (((1,), (1,)), ((), ())), preferred_element_type=F32)


def mm(a, b):
    return jnp.dot(a, b, preferred_element_type=F32)


def col_start(c):
    return pl.multiple_of(jnp.minimum(c * FC, 4480 - FC), 128)


MLP_AXES = (("z", "x", "y"), ("x", "y", "z"), ("y", "z", "x"))


def in_order(v, order):
    place = {}
    rows = []
    for i in range(64):
        for n, a in enumerate(order):
            place[a] = (i // (16, 4, 1)[n]) % 4
        o = place["z"] * 16 + place["x"] * 4 + place["y"]
        rows.append(v[o * 24 : (o + 1) * 24])
    return jnp.concatenate(rows, axis=0)


def forward(tokens, cot, lengths, gains, wq, wk, wv, bq, bk, bv, w_out, w_gate, w_up, w_down):
    def body(len_ref, t_ref, c_ref, g_ref, wk_ref, wv_ref, bq_ref, bk_ref, bv_ref, wq_hbm, wo_hbm, wg_hbm, wu_hbm, wd_hbm,
             out_ref, gmid_ref, bt_ref, ga_ref, delta_ref, dn_ref, q_ref, cos_out, sin_out, low_ref, lse_ref,
             x0, x1, x2, g0, g1, g2, kv_hbm, xq,
             kv, wq_ref, at_ref, m_ref, l_ref, acc_ref, gh_ref,
             wo_ref, wg, wu, wd, got_br, acc, got, norm_ref, nt_ref, ct_ref, n1_ref, xl, act, w_sem, loc, send, recv):
        xs, gs = (x0, x1, x2), (g0, g1, g2)
        c = coords()
        dev = lax.axis_index("seq")
        turn = c["z"] + c["x"] + c["y"]
        sems = iter(range(128))

        def load(j):
            cols = pl.ds(col_start((turn + j) % 4), FC)
            b = j % 2
            copies = [
                pltpu.make_async_copy(wg_hbm.at[:, cols], wg.at[b], w_sem.at[b, 0]),
                pltpu.make_async_copy(wu_hbm.at[:, cols], wu.at[b], w_sem.at[b, 1]),
                pltpu.make_async_copy(wd_hbm.at[cols, :], wd.at[b], w_sem.at[b, 2]),
            ]
            for copy in copies:
                copy.start()
            return copies

        def load_down(j):
            copy = pltpu.make_async_copy(wd_hbm.at[pl.ds(col_start((turn + j) % 4), FC), :], wd.at[j % 2], w_sem.at[j % 2, 2])
            copy.start()
            return copy

        def push(src, dst, device):
            n = next(sems)
            copy = remote(src, dst, send.at[n], recv.at[n], device)
            copy.start()
            return copy

        def keep(src, dst, n):
            copy = pltpu.make_async_copy(src, dst, loc.at[n])
            copy.start()
            return copy

        wq_load = keep(wq_hbm, wq_ref, 6)
        down = [load_down(0), load_down(1)]
        wo_load = keep(wo_hbm, wo_ref, 7)

        x = t_ref[...].astype(F32)
        inv = lax.rsqrt(jnp.mean(x * x, axis=1, keepdims=True) + 1e-06)
        normed = (x * inv * g_ref[0:1, :]).astype(BF16)
        cos, sin = rope_tables(len_ref)
        cos_out[...], sin_out[...] = cos, sin
        k_pre = mm(normed, wk_ref[...]) + bk_ref[...].astype(F32)
        v_low = (mm(normed, wv_ref[...]) + bv_ref[...].astype(F32)).astype(BF16)
        k_rot = (k_pre * cos + swap_halves(k_pre) * sin).astype(BF16)
        kv[c["z"], c["x"], c["y"]] = jnp.concatenate([k_rot[:64], v_low[:64], k_rot[64:], v_low[64:]], axis=0)
        barrier(core=True)
        kv_pending = [[] for _ in range(6)]

        def kv_wait(chunk):
            for p in range(chunk * 3, chunk * 3 + 3):
                for copy in kv_pending[p]:
                    copy.wait()
                kv_pending[p] = []

        def kv_stage(chunk, stage):
            for i, (r0, rn, order) in enumerate(KV_CHUNK):
                p, r0 = chunk * 3 + i, r0 + chunk * 128
                for copy in kv_pending[p]:
                    copy.wait()
                idx = kv_index(order[:stage], c, r0, rn)
                kv_pending[p] = [push(kv.at[idx], kv.at[idx], peer(order[stage], k)) for k in (1, 2, 3)]

        kv_stage(0, 0)
        kv_stage(1, 0)
        wq_load.wait()
        for h in range(6):
            q = mm(normed, wq_ref[h]) + bq_ref[h : h + 1, :].astype(F32)
            q = (q * cos + swap_halves(q) * sin).astype(BF16)
            q_ref[:, h * Q_BLK : (h + 1) * Q_BLK, :] = q.reshape(8, Q_BLK, 128)

        def g_hidden(j):
            down[j].wait()
            gh_ref[j] = nt(c_ref[...], wd[j % 2])
            if j < 2:
                down.append(load_down(j + 2))
            else:
                loads.append(load(j - 2))

        loads = []
        kv_stage(0, 1)
        kv_stage(1, 1)
        g_hidden(0)
        n1_ref[...] = in_order(normed.astype(F32).T, ("x", "y", "z")).astype(BF16).reshape(4, 384, 128)
        own_q = keep(n1_ref, xq.at[:, :, pl.ds(0, 128)], 10)
        g_hidden(1)
        kv_stage(0, 2)
        g_hidden(2)
        g_hidden(3)
        ct_ref[...] = c_ref[...].T.reshape(4, 384, 128)
        own = [keep(ct_ref, x2.at[:, :, pl.ds(0, 128)], 3)]
        kv_wait(0)
        kv_stage(1, 2)
        later = [push(ct_ref, x2.at[:, :, pl.ds(k * 128, 128)], peer("y", k)) for k in (1, 2, 3)]
        later += [push(n1_ref, xq.at[:, :, pl.ds(k * 128, 128)], peer("z", k)) for k in (1, 2, 3)]

        row_off = (lax.broadcasted_iota(jnp.int32, (96, 1), 0) % Q_BLK) * 64 + dev
        col = lax.broadcasted_iota(jnp.int32, (96, BLK), 1)
        key_off = (col % Q_BLK) * 64 + col // Q_BLK

        def attend(qb, lo, hi, carry, diagonal):
            q_blk = q_ref[qb]
            pos_q = row_off + qb * BLK
            start_q = doc_bounds(pos_q, len_ref)

            def block(kb, carry, causal):
                m, l, acc = carry
                k_blk = kv[:, :, :, kv_rows(kb, 0), :].reshape(BLK, 128)
                v_blk = kv[:, :, :, kv_rows(kb, 1), :].reshape(BLK, 128)
                pos_k = key_off + kb * BLK
                vis = pos_k >= start_q
                if causal:
                    vis = vis & (pos_k <= pos_q)
                s = jnp.where(vis, nt(q_blk, k_blk) * SCALE2, -1e30)
                m_new = jnp.maximum(m, jnp.max(s, axis=1, keepdims=True))
                p = jnp.exp2(s - m_new)
                a = jnp.exp2(m - m_new)
                return m_new, l * a + jnp.sum(p, axis=1, keepdims=True), acc * a + mm(p.astype(BF16), v_blk)

            carry = lax.fori_loop(lo, hi, lambda kb, carry: block(kb, carry, False), carry)
            return block(qb, carry, True) if diagonal else carry

        def attend_end(qb, carry):
            m, l, acc = carry
            attn = acc / l
            at_ref[qb] = attn
            low = attn.astype(BF16)
            for h in range(6):
                rows = pl.ds(pl.multiple_of(qb * Q_BLK, Q_BLK), Q_BLK)
                low_ref[rows, h * 128 : (h + 1) * 128] = low[h * Q_BLK : (h + 1) * Q_BLK]
            lse_ref[qb] = jnp.broadcast_to(m + jnp.log2(l), (96, 128)).T[0:1]

        init = (jnp.full((96, 1), -1e30, F32), jnp.zeros((96, 1), F32), jnp.zeros((96, 128), F32))

        def upper(qb, _):
            m_ref[qb - 4], l_ref[qb - 4], acc_ref[qb - 4] = attend(qb, 0, 4, init, False)
            return 0

        def whole(qb, _):
            attend_end(qb, attend(qb, 0, qb, init, True))
            return 0

        def rest(qb, _):
            attend_end(qb, attend(qb, 4, qb, (m_ref[qb - 4], l_ref[qb - 4], acc_ref[qb - 4]), True))
            return 0

        out_kv = [keep(kv.at[:, :, :, pl.ds(0, 128), :], kv_hbm.at[:, :, :, pl.ds(0, 128), :], 8)]
        lax.fori_loop(0, 4, whole, 0)
        lax.fori_loop(4, 8, upper, 0)
        kv_wait(1)
        out_kv.append(keep(kv.at[:, :, :, pl.ds(128, 128), :], kv_hbm.at[:, :, :, pl.ds(128, 128), :], 9))
        lax.fori_loop(4, 8, rest, 0)
        wo_load.wait()
        ex = []
        for half in range(2):
            cols = slice(half * 768, (half + 1) * 768)
            acc[half, :, 0:768] = mm(low_ref[...], wo_ref[:, cols])
            ex.append(push(acc.at[half, :, pl.ds(0, 768)], got_br.at[half], partner()))
        for copy in ex:
            copy.wait()
        mid = t_ref[...].astype(F32) + jnp.concatenate([acc[h, :, 0:768] + got_br[h] for h in range(2)], axis=1)
        out_ref[...] = mid
        inv = lax.rsqrt(jnp.mean(mid * mid, axis=1, keepdims=True) + 1e-06)
        normed = (mid * inv * g_ref[1:2, :]).astype(BF16)
        norm_ref[...] = normed
        turned = normed.astype(F32).T
        for m in range(2):
            nt_ref[m] = in_order(turned, MLP_AXES[m][1:] + MLP_AXES[m][:1]).astype(BF16).reshape(4, 384, 128)
        own.append(keep(nt_ref.at[0], x0.at[:, :, pl.ds(0, 128)], 4))
        own.append(keep(nt_ref.at[1], x1.at[:, :, pl.ds(0, 128)], 5))
        half = pl.ds(2 * lax.axis_index("tensor"), 2)
        halves = {}
        for k in (1, 2, 3):
            for m, w in ((0, "z"), (1, "x")):
                halves[m, k] = push(nt_ref.at[m, half], xl.at[m, k - 1], peer(w, k))

        def pass_on():
            n = 11
            for (m, k), copy in halves.items():
                copy.wait()
                there = xs[m].at[half, :, pl.ds(k * 128, 128)]
                later.append(push(xl.at[m, k - 1], there, partner()))
                later.append(keep(xl.at[m, k - 1], there, n))
                n += 1

        lane = lax.broadcasted_iota(jnp.int32, (128, FC), 1)
        for j in range(4):
            b = j % 2
            d = (turn + j) % 4
            for copy in loads[j]:
                copy.wait()
            n = norm_ref[...]
            gate = mm(n, wg[b])
            up = mm(n, wu[b])
            gh = gh_ref[j]
            sig = 1.0 / (1.0 + jnp.exp(-gate))
            silu = gate * sig
            hidden = (silu * up).astype(BF16)
            g_gate = (gh * up * sig * (1.0 + gate * (1.0 - sig))).astype(BF16)
            g_up = (gh * silu).astype(BF16)
            vals = (g_gate, g_up, hidden)
            for m in range(3):
                act[m, j] = vals[m]
            twice = (lane < 128) & (d == 3)
            zero = jnp.zeros((128, FC), BF16)
            hidden, g_gate, g_up = (jnp.where(twice, zero, v) for v in (hidden, g_gate, g_up))
            add_g = nt(g_gate, wg[b]) + nt(g_up, wu[b])
            acc[1] = add_g if j == 0 else acc[1] + add_g
            if j == 3:
                ex = [push(acc.at[1], got.at[1], partner())]
            add_o = mm(hidden, wd[b])
            acc[0] = add_o if j == 0 else acc[0] + add_o
            if j + 2 < 4:
                loads.append(load(j + 2))
            if j == 2:
                pass_on()
            for m in range(3):
                w = MLP_AXES[m][0]
                k = (d + 4 - c[w]) % 4
                slot = pl.ds(pl.multiple_of(k * 128, 128), 128)

                @pl.when(k == 0)
                def _():
                    pltpu.make_async_copy(act.at[m, j], gs[m].at[pl.ds(0, 128), :], loc.at[m]).start()

                @pl.when(k != 0)
                def _():
                    remote(
                        act.at[m, j], gs[m].at[slot, :], send.at[96 + m * 4 + j], recv.at[96 + m * 4 + k], peer(w, k)
                    ).start()

        ex.append(push(acc.at[0], got.at[0], partner()))
        dn_ref[...] = jnp.sum(acc[1] * out_ref[...] * inv, axis=0, keepdims=True)
        cot_f = c_ref[...].astype(F32)
        ex[0].wait()
        gn = acc[1] + got[1]
        mid = out_ref[...]
        scaled = gn * g_ref[1:2, :]
        g_mid = cot_f + (inv * scaled - mid * (inv * inv * inv) * jnp.mean(scaled * mid, axis=1, keepdims=True))
        gmid_ref[...] = g_mid
        branch_low = g_mid.astype(BF16)
        bt_ref[...] = branch_low.T
        g_attn = nt(branch_low, wo_ref[...]).astype(BF16)
        for h in range(6):
            ga_ref[:, h * Q_BLK : (h + 1) * Q_BLK, :] = g_attn[:, h * 128 : (h + 1) * 128].reshape(8, Q_BLK, 128)
        for qb in range(8):
            delta_ref[qb] = jnp.sum((ga_ref[qb].astype(F32) * at_ref[qb]).T, axis=0, keepdims=True)
        ex[1].wait()
        out_ref[...] += acc[0] + got[0]
        for copy in later + own + out_kv + [own_q]:
            copy.wait()
        for m in range(3):
            w = MLP_AXES[m][0]
            pltpu.make_async_copy(act.at[m, 0], gs[m].at[pl.ds(0, 128), :], loc.at[m]).wait()
            for j in range(4):
                k = ((turn + j) % 4 + 4 - c[w]) % 4

                @pl.when(k != 0)
                def _():
                    slot = pl.ds(pl.multiple_of(k * 128, 128), 128)
                    remote(
                        act.at[m, j], gs[m].at[slot, :], send.at[96 + m * 4 + j], recv.at[96 + m * 4 + k], peer(w, k)
                    ).wait()

    f32 = lambda *s: jax.ShapeDtypeStruct(s, F32)
    b16 = lambda *s: jax.ShapeDtypeStruct(s, BF16)
    vm, sm, hbm = (pl.BlockSpec(memory_space=m) for m in (pltpu.VMEM, pltpu.SMEM, pl.ANY))
    held = [(6, 1536, 128, BF16), (8, 96, 128, F32), (4, 96, 1, F32), (4, 96, 1, F32), (4, 96, 128, F32)]
    held += [(4, 128, FC, F32), (768, 1536, BF16), (2, 1536, FC, BF16), (2, 1536, FC, BF16), (2, FC, 1536, BF16)]
    held += [(2, 128, 768, F32), (2, 128, 1536, F32), (2, 128, 1536, F32), (128, 1536, BF16)]
    held += [(2, 4, 384, 128, BF16), (4, 384, 128, BF16), (4, 384, 128, BF16), (2, 3, 2, 384, 128, BF16), (3, 4, 128, FC, BF16)]
    return pl.pallas_call(
        body,
        out_shape=(f32(128, 1536), f32(128, 1536), b16(1536, 128), b16(8, 96, 128), f32(8, 1, 96), f32(1, 1536))
        + (b16(8, 96, 128), f32(128, 128), f32(128, 128), b16(128, 768), f32(8, 1, 96))
        + (b16(4, 384, 512),) * 3
        + (b16(512, FC),) * 3
        + (b16(4, 4, 4, 256, 128), b16(4, 384, 512)),
        in_specs=[sm] + [vm] * 8 + [hbm] * 5,
        out_specs=(vm,) * 11 + (hbm,) * 8,
        scratch_shapes=[pltpu.VMEM((4, 4, 4, 256, 128), BF16)]
        + [pltpu.VMEM(v[:-1], v[-1]) for v in held]
        + [DMA((2, 3)), DMA((17,)), DMA((112,)), DMA((112,))],
        compiler_params=pltpu.CompilerParams(collective_id=4, has_side_effects=True, vmem_limit_bytes=VMEM_BYTES),
        name="forward",
    )(lengths, tokens, cot, gains, wk, wv, bq, bk, bv, wq, w_out, w_gate, w_up, w_down)


OUT_ORDERS = (("z", "x", "y"), ("x", "y", "z"), ("y", "z", "x"))
QKV_ORDERS = (("x", "y"), ("y", "x"))
SMALL = 40


def slab_products(buf, left, rhs, order):
    def blocks(v, places):
        return jnp.concatenate([v[o * 24 : (o + 1) * 24] for o in places], axis=0)

    if order[0] == "z":
        for z in range(4):
            buf[z] = mm(left[z * 384 : (z + 1) * 384, :], rhs).astype(BF16)
    elif order[0] == "x":
        for x in range(4):
            lhs = jnp.concatenate([left[z * 384 + x * 96 : z * 384 + (x + 1) * 96, :] for z in range(4)], axis=0)
            buf[x] = blocks(mm(lhs, rhs), [z * 4 + y for y in range(4) for z in range(4)]).astype(BF16)
    else:
        for z in range(4):
            v = blocks(mm(left[z * 384 : (z + 1) * 384, :], rhs), [x * 4 + y for y in range(4) for x in range(4)])
            v = v.astype(BF16)
            for y in range(4):
                buf[y, z * 96 : (z + 1) * 96] = v[y * 96 : (y + 1) * 96]


def near(u):
    return u + 1 - 2 * (u % 2)


def far(u):
    return 3 - u


def over(u):
    return (u + 2) % 4


class Halves:
    def __init__(self, push, axis, c, slab, got_first, got_second):
        self.push, self.slab, self.u = push, slab, c[axis]
        self.got_first, self.got_second = got_first, got_second
        self.to = lambda place: peer(axis, place + 4 - c[axis])
        self.one, self.two = {}, []

    def ready(self, which):
        u = self.u
        if which == "over":
            self.one[0, 0] = self.push(self.slab(over(u), 0), self.got_first(0, 0), self.to(near(u)))
            self.one[1, 0] = self.push(self.slab(over(u), 1), self.got_first(1, 0), self.to(far(u)))
        elif which == "near":
            self.one[0, 1] = self.push(self.slab(near(u), 0), self.got_first(0, 1), self.to(near(u)))
        elif which == "far":
            self.one[1, 1] = self.push(self.slab(far(u), 1), self.got_first(1, 1), self.to(far(u)))

    def first(self):
        for which in ("over", "near", "far"):
            self.ready(which)

    def second(self):
        u = self.u
        for h, place in ((0, far(u)), (1, near(u))):
            self.one[h, 0].wait()
            at = self.slab(place, h)
            at[...] = (at[...].astype(F32) + self.got_first(h, 0)[...].astype(F32)).astype(BF16)
            self.two.append(self.push(at, self.got_second(h), self.to(place)))

    def final(self):
        for h in range(2):
            self.one[h, 1].wait()
            self.two[h].wait()
            at = self.slab(self.u, h)
            at[...] = (
                at[...].astype(F32) + self.got_first(h, 1)[...].astype(F32) + self.got_second(h)[...].astype(F32)
            ).astype(BF16)


def sum_first(buf, got, copies, own):
    for copy in copies:
        copy.wait()
    total = buf[own].astype(F32)
    for k in range(3):
        total = total + got[k][...].astype(F32)
    buf[own] = total.astype(BF16)


def backward(xs_in, gs_in, q, g, kv, lse, delta, branch_t, attn_low, lengths,
             cos, sin, norm_shared, wq, wk, wv, tokens, gain, g_mid, d_norm2):
    n_late = 2

    def body(*refs):
        r = list(refs)
        take = lambda n: [r.pop(0) for _ in range(n)]
        (len_ref,), xs_hbm, gs_hbm, (kv_hbm, *w_hbm, xq_hbm), late = take(1), take(3), take(3), take(5), take(n_late)
        q_ref, g_ref, lse_ref, delta_ref, bt_ref, a_ref, cos_ref, sin_ref, gain_ref, dn2_ref = take(10)
        gt_ref, gqkv_ref, go_ref, s_out = take(4)
        m_outs = take(3)
        xs, gs, (dkv,), (t_ref,) = take(3), take(3), take(1), take(1)
        held = (t_ref, gt_ref)
        acc2, o_acc2, (dq_ref, own_ref) = take(3), take(3), take(2)
        sendbuf, r1, r2, t1, t2 = take(3), take(3), take(3), take(3), take(3)
        o_buf, o_r1, o_r2, o_got2 = take(1), take(3), take(3), take(3)
        kv1, kv1b, kv2, kv3 = take(6), take(6), take(6), take(6)
        m_got, o_got = take(3), take(3)
        q_got2, (q_acc2, q_got3) = take(2), take(2)
        o_buf = [xs[2].at[:, :, 0:256], xs[2].at[:, :, 256:512], o_buf[0]]
        q_left, q_right = xs[0], gs[0].at[:, 0:256]
        q_buf = [xs[1].at[:, :, 0:128], xs[1].at[:, :, 128:256]]
        q_got1 = [
            [gs[0].at[0:384, lo + k * 128 : lo + (k + 1) * 128] for k in range(3)] for lo in (256, 640)
        ]
        s_acc, s_got, gp_ref, part, got_part = take(5)
        loc, send, recv = take(3)
        c = coords()
        loads = [pltpu.make_async_copy(a, b, loc.at[i]) for i, (a, b) in enumerate(
            ((xs_hbm[0], xs[0]), (gs_hbm[0], gs[0]), (xs_hbm[2], xs[2]), (gs_hbm[2], gs[2]),
             (xs_hbm[1], xs[1]), (gs_hbm[1], gs[1]), (kv_hbm, dkv), *zip(late, held)))]
        for copy in loads:
            copy.start()
        barrier(core=True)
        sems = iter(range(256))

        def push(src, dst, device):
            n = next(sems)
            copy = remote(src, dst, send.at[n], recv.at[n], device)
            copy.start()
            return copy

        def mlp_slab(m):
            return lambda u, h: sendbuf[m].at[u, pl.ds(192 * h, 192), :]

        mlp_one = [
            Halves(push, MLP_AXES[m][1], c, mlp_slab(m), lambda h, i, m=m: r1[m].at[h, i], lambda h, m=m: r2[m].at[h])
            for m in range(3)
        ]

        def mlp_rows(m):
            own = sendbuf[m].at[c[MLP_AXES[m][1]]]
            return lambda u, h: own.at[pl.ds(pl.multiple_of(u * 96 + h * 48, 16), 48), :]

        mlp_two = [
            Halves(push, MLP_AXES[m][2], c, mlp_rows(m), lambda h, i, m=m: t1[m].at[h, i], lambda h, m=m: t2[m].at[h])
            for m in range(3)
        ]

        for name, place in (("over", over), ("near", near), ("far", far), ("own", lambda v: v)):
            for i, m in enumerate((0, 2, 1)):
                if name == "over":
                    loads[2 * i].wait()
                    loads[2 * i + 1].wait()
                u = place(c[MLP_AXES[m][1]])
                x = xs[m][u]
                sendbuf[m][u] = mm(x, gs[m][...]).astype(BF16)
                mlp_one[m].ready(name)

        def buf_slab(buf):
            return lambda u, h: buf.at[u, pl.ds(192 * h, 192), :]

        out_one = [
            Halves(push, OUT_ORDERS[p][0], c, buf_slab(o_buf[p]), lambda h, i, p=p: o_r1[p].at[h, i], lambda h, p=p: o_r2[p].at[h])
            for p in range(3)
        ]
        o_second = [[], [], []]

        def out_second(p):
            order = OUT_ORDERS[p]
            out_one[p].final()
            for k in (1, 2, 3):
                rows = pl.ds(pl.multiple_of(((c[order[1]] + k) % 4) * 96, 32), 96)
                o_second[p].append(push(o_buf[p].at[c[order[0]], rows, :], o_got2[p].at[k - 1], peer(order[1], k)))

        def out_sum(p):
            order = OUT_ORDERS[p]
            for copy in o_second[p]:
                copy.wait()
            rows = pl.ds(pl.multiple_of(c[order[1]] * 96, 32), 96)
            total = o_buf[p][c[order[0]], rows, :].astype(F32)
            for k in range(3):
                total = total + o_got2[p][k].astype(F32)
            o_acc2[p][...] = total

        loads[6].wait()
        dev = lax.axis_index("seq")
        row = lax.broadcasted_iota(jnp.int32, (BLK, 96), 0)
        key_off = (row % Q_BLK) * 64 + row // Q_BLK
        q_off = (lax.broadcasted_iota(jnp.int32, (1, 96), 1) % Q_BLK) * 64 + dev
        dq_ref[...] = jnp.zeros_like(dq_ref)

        def k_step(kb, _):
            k_blk = dkv[:, :, :, kv_rows(kb, 0), :].reshape(BLK, 128)
            v_blk = dkv[:, :, :, kv_rows(kb, 1), :].reshape(BLK, 128)
            k_t = k_blk.T
            pos_k = key_off + kb * BLK

            def pair(qb, carry, causal):
                dk, dv = carry
                q_blk, g_blk = q_ref[qb], g_ref[qb]
                pos_q = q_off + qb * BLK
                vis = pos_k >= doc_bounds(pos_q, len_ref)
                if causal:
                    vis = vis & (pos_k <= pos_q)
                s = nt(k_blk, q_blk)
                p = jnp.where(vis, jnp.exp2(s * SCALE2 - lse_ref[qb]), 0.0)
                gp = nt(v_blk, g_blk)
                ds = (p * (gp - delta_ref[qb])).astype(BF16)
                dq_ref[qb] += mm(k_t, ds)
                dk = dk + mm(ds, q_blk)
                dv = dv + mm(p.astype(BF16), g_blk)
                return dk, dv

            zero = jnp.zeros((BLK, 128), F32)
            carry = pair(kb, (zero, zero), True)
            dk, dv = lax.fori_loop(kb + 1, 8, lambda qb, carry: pair(qb, carry, False), carry)
            dkv[:, :, :, kv_rows(kb, 0), :] = (dk * SCALE).astype(BF16).reshape(4, 4, 4, Q_BLK, 128)
            dkv[:, :, :, kv_rows(kb, 1), :] = dv.astype(BF16).reshape(4, 4, 4, Q_BLK, 128)
            return 0

        kv_pending = [[] for _ in range(6)]
        kv_parts = [(r0 + 128 * chunk, rn, order) for chunk in range(2) for r0, rn, order in KV_CHUNK]

        def kv_slab(p):
            r0, rn, order = kv_parts[p]
            rest = [a for a in AXES if a != order[0]]

            def slab(u, h):
                where = {order[0]: u, rest[0]: pl.ds(2 * h, 2), rest[1]: slice(None)}
                return dkv.at[where["z"], where["x"], where["y"], pl.ds(r0, rn), :]

            return slab

        kv_one = [
            Halves(push, kv_parts[p][2][0], c, kv_slab(p), lambda h, i, p=p: kv1[p].at[h, i], lambda h, p=p: kv1b[p].at[h])
            for p in range(6)
        ]

        def kv_halves(chunk, step):
            for p in range(chunk * 3, chunk * 3 + 3):
                getattr(kv_one[p], step)()

        def kv_stage(chunk, stage):
            got = (None, kv2, kv3)
            for p in range(chunk * 3, chunk * 3 + 3):
                r0, rn, order = kv_parts[p]
                if stage == 1:
                    kv_one[p].final()
                else:
                    for copy in kv_pending[p]:
                        copy.wait()
                    kv_pending[p] = []
                    mine = kv_index(order[stage:], c, r0, rn)
                    own = dkv[mine].astype(F32)
                    for k in range(3):
                        own = own + got[stage - 1][p][k].astype(F32)
                    if stage == 3:
                        own_ref[pl.ds(r0, rn), :] = own
                        continue
                    dkv[mine] = own.astype(BF16)
                for k in (1, 2, 3):
                    cc = dict(c)
                    cc[order[stage]] = (c[order[stage]] + k) % 4
                    src = dkv.at[kv_index(order[stage + 1 :], cc, r0, rn)]
                    kv_pending[p].append(push(src, got[stage][p].at[k - 1], peer(order[stage], k)))

        def share(acc, got, axis):
            copies = []
            for k in (1, 2, 3):
                rows = pl.ds(pl.multiple_of(((c[axis] + k) % 4) * 24, 8), 24)
                copies.append(push(acc.at[rows, :], got.at[k - 1], peer(axis, k)))
            return copies

        q_copies = [[], []]

        def qkv_share():
            mine = pl.ds(pl.multiple_of(c["z"] * 256, 256), 256)
            copies = []
            for k in (1, 2, 3):
                cols = pl.ds(pl.multiple_of((c["z"] + k) % 4 * 256, 256), 256)
                copies.append(push(gp_ref.at[:, cols], q_right.at[k * 128 : (k + 1) * 128, :], peer("z", k)))
            q_right[0:128, :] = gp_ref[:, mine]
            return copies

        def qkv_first():
            for k in (2, 1, 3, 0):
                for p, (one, _) in enumerate(QKV_ORDERS):
                    u = (c[one] + k) % 4
                    if p == 0:
                        left = q_left[u]
                    else:
                        rows = pl.ds(pl.multiple_of(u * 96, 32), 96)
                        left = jnp.concatenate([q_left[x, rows, :] for x in range(4)], axis=0)
                    q_buf[p][u] = mm(left, q_right[:, p * 128 : (p + 1) * 128]).astype(BF16)
                    if k:
                        q_copies[p].append(push(q_buf[p].at[u], q_got1[p][k - 1], peer(one, k)))

        def qkv_second():
            for p, (one, two) in enumerate(QKV_ORDERS):
                sum_first(q_buf[p], q_got1[p], q_copies[p], c[one])
                q_copies[p] = []
                for k in (1, 2, 3):
                    rows = pl.ds(pl.multiple_of(((c[two] + k) % 4) * 96, 32), 96)
                    q_copies[p].append(push(q_buf[p].at[c[one], rows, :], q_got2[p].at[k - 1], peer(two, k)))

        def qkv_third():
            for p in range(2):
                one, two = QKV_ORDERS[p]
                for copy in q_copies[p]:
                    copy.wait()
                rows = pl.ds(pl.multiple_of(c[two] * 96, 32), 96)
                total = q_buf[p][c[one], rows, :].astype(F32)
                for k in range(3):
                    total = total + q_got2[p][k].astype(F32)
                q_acc2[:, p * 128 : (p + 1) * 128] = total
            return share(q_acc2, q_got3, "z")

        def qkv_out(copies):
            for copy in copies:
                copy.wait()
            for k in range(4):
                v = q_acc2[pl.ds(pl.multiple_of(c["z"] * 24, 8), 24), :] if k == 0 else q_got3[k - 1]
                block = (c["z"] + 4 - k) % 4
                gqkv_ref[2 * block] = v[:, :128]
                gqkv_ref[2 * block + 1] = v[:, 128:]

        m_copies = [None] * 3

        def mlp_third(m):
            mlp_two[m].final()
            rows = pl.ds(pl.multiple_of(c[MLP_AXES[m][2]] * 96, 32), 96)
            acc2[m][...] = sendbuf[m][c[MLP_AXES[m][1]], rows, :].astype(F32)
            m_copies[m] = share(acc2[m], m_got[m], MLP_AXES[m][0])

        weights = (0, 2, 1)
        lax.fori_loop(4, 6, k_step, 0)
        for m in weights:
            mlp_one[m].second()
        lax.fori_loop(6, 8, k_step, 0)
        kv_halves(1, "first")
        lax.fori_loop(0, 1, k_step, 0)
        kv_halves(1, "second")
        lax.fori_loop(1, 2, k_step, 0)
        for m in weights:
            mlp_one[m].final()
            mlp_two[m].first()
        for p, order in enumerate(OUT_ORDERS):
            slab_products(o_buf[p], bt_ref, a_ref[:, p * 256 : (p + 1) * 256], order)
            out_one[p].first()
        lax.fori_loop(2, 3, k_step, 0)
        for m in weights:
            mlp_two[m].second()
        kv_stage(1, 1)
        lax.fori_loop(3, 4, k_step, 0)
        kv_halves(0, "first")

        cos_t, sin_t = cos_ref[...], sin_ref[...]
        for qb in range(8):
            dq = dq_ref[qb].T * SCALE
            rows = slice(qb * Q_BLK, (qb + 1) * Q_BLK)
            cs, sn = cos_t[rows], sin_t[rows]
            for h in range(6):
                v = dq[h * Q_BLK : (h + 1) * Q_BLK]
                gp_ref[rows, h * 128 : (h + 1) * 128] = (v * cs - swap_halves(v) * sn).astype(BF16)
        kv_halves(0, "second")
        for p in range(3):
            out_one[p].second()
        q_load = pltpu.make_async_copy(xq_hbm, q_left, loc.at[7 + n_late + 8])
        q_load.start()
        kv_stage(1, 2)
        kv_stage(0, 1)
        kv_stage(0, 2)
        for m in (0, 2, 1):
            mlp_third(m)
        w_ref = [sendbuf[0].at[:, :, h * 128 : (h + 1) * 128] for h in range(8)]
        w_from = [w_hbm[0].at[h] for h in range(6)] + [w_hbm[1], w_hbm[2]]
        w_loads = [pltpu.make_async_copy(w_from[h], w_ref[h], loc.at[7 + n_late + h]) for h in range(8)]
        for copy in w_loads:
            copy.start()

        def back_through(lo, hi):
            total = nt(gp_ref[:, lo * 128 : (lo + 1) * 128], w_ref[lo][...].reshape(1536, 128))
            for h in range(lo + 1, hi):
                total = total + nt(gp_ref[:, h * 128 : (h + 1) * 128], w_ref[h][...].reshape(1536, 128))
            return total

        kv_stage(1, 3)
        kv_stage(0, 3)

        dk = jnp.concatenate([own_ref[0:64, :], own_ref[128:192, :]], axis=0)
        gp_ref[:, 768:896] = (dk * cos_t - swap_halves(dk) * sin_t).astype(BF16)
        gp_ref[:, 896:] = jnp.concatenate([own_ref[64:128, :], own_ref[192:256, :]], axis=0).astype(BF16)
        shared = qkv_share()
        for p in range(3):
            out_second(p)
        for copy in loads[7:] + w_loads:
            copy.wait()
        part[...] = back_through(0, 8)
        swap = push(part, got_part, partner())
        q_load.wait()
        for copy in shared:
            copy.wait()
        qkv_first()

        inputs = t_ref[...].astype(F32)
        inv = lax.rsqrt(jnp.mean(inputs * inputs, axis=1, keepdims=True) + 1e-06)
        d_norm1 = jnp.sum(part[...] * inputs * inv, axis=0, keepdims=True)
        d_bias = jnp.sum(gp_ref[...].astype(F32), axis=0, keepdims=True)
        core = lax.axis_index("tensor")
        for j in range(12):
            s_acc[0, j : j + 1, :] = d_norm1[:, j * 128 : (j + 1) * 128]
            s_acc[0, 12 + j : 13 + j, :] = dn2_ref[:, j * 128 : (j + 1) * 128]
        for j in range(8):
            v = d_bias[:, j * 128 : (j + 1) * 128]
            s_acc[0, 24 + j : 25 + j, :] = jnp.where(core == 0, v, 0.0)
            s_acc[0, 32 + j : 33 + j, :] = jnp.where(core == 1, v, 0.0)
        s_pending = []

        def send_small(stage):
            peers = [partner()] if stage == 0 else [peer(AXES[stage - 1], k) for k in (1, 2, 3)]
            for i, d in enumerate(peers):
                s_pending.append(push(s_acc.at[stage], s_got.at[stage * 3 + i], d))

        def sum_small(stage):
            for copy in s_pending:
                copy.wait()
            s_pending.clear()
            if stage == 0:
                return s_acc[0] + s_got[0]
            axis = AXES[stage - 1]
            parts = [s_acc[stage]] + [s_got[stage * 3 + k] for k in range(3)]
            total = jnp.zeros_like(parts[0])
            for w in range(4):
                term = jnp.zeros_like(total)
                for k in range(4):
                    term = jnp.where((c[axis] + 4 - k) % 4 == w, parts[k], term)
                total = total + term
            return total

        send_small(0)
        qkv_second()
        o_copies = [None] * 3
        for p in range(3):
            out_sum(p)
            o_copies[p] = share(o_acc2[p], o_got[p], OUT_ORDERS[p][2])
        s_acc[1] = sum_small(0)
        send_small(1)
        swap.wait()
        g_norm = part[...] + got_part[...]
        scaled = g_norm * gain_ref[0:1, :]
        gt_ref[...] += (
            inv * scaled - inputs * (inv * inv * inv) * jnp.mean(scaled * inputs, axis=1, keepdims=True)
        )
        s_acc[2] = sum_small(1)
        send_small(2)
        q_out = qkv_third()
        for p in range(3):
            for copy in o_copies[p]:
                copy.wait()
            rows = pl.ds(pl.multiple_of(c[OUT_ORDERS[p][2]] * 24, 8), 24)
            total = o_acc2[p][rows, :]
            for k in range(3):
                total = total + o_got[p][k]
            for j in range(2):
                go_ref[p * 2 + j] = total[:, j * 128 : (j + 1) * 128]
        for m in range(3):
            for copy in m_copies[m]:
                copy.wait()
            here = c[MLP_AXES[m][0]]
            m_outs[m][:, pl.ds(col_start(here), FC)] = acc2[m][pl.ds(pl.multiple_of(here * 24, 8), 24), :]
            for k in (1, 2, 3):
                m_outs[m][:, pl.ds(col_start((here + 4 - k) % 4), FC)] = m_got[m][k - 1]
        s_acc[3] = sum_small(2)
        send_small(3)
        qkv_out(q_out)
        s_out[...] = sum_small(3)

    rows = [rn for _, rn, _ in KV_CHUNK] * 2
    late = (tokens, g_mid)
    scratch = (
        [pltpu.VMEM((4, 384, 512), BF16)] * 3
        + [pltpu.VMEM((512, FC), BF16)] * 3
        + [pltpu.VMEM((4, 4, 4, 256, 128), BF16)]
        + [pltpu.VMEM((128, 1536), BF16)]
        + [pltpu.VMEM((96, FC), F32)] * 3
        + [pltpu.VMEM((96, 256), F32)] * 3
        + [pltpu.VMEM((8, 128, 96), F32), pltpu.VMEM((256, 128), F32)]
        + [pltpu.VMEM((4, 384, FC), BF16)] * 3
        + [pltpu.VMEM((2, 2, 192, FC), BF16)] * 3
        + [pltpu.VMEM((2, 192, FC), BF16)] * 3
        + [pltpu.VMEM((2, 2, 48, FC), BF16)] * 3
        + [pltpu.VMEM((2, 48, FC), BF16)] * 3
        + [pltpu.VMEM((4, 384, 256), BF16)]
        + [pltpu.VMEM((2, 2, 192, 256), BF16)] * 3
        + [pltpu.VMEM((2, 192, 256), BF16)] * 3
        + [pltpu.VMEM((3, 96, 256), BF16)] * 3
        + [pltpu.VMEM((2, 2, 2, 4, r, 128), BF16) for r in rows]
        + [pltpu.VMEM((2, 2, 4, r, 128), BF16) for r in rows]
        + [pltpu.VMEM((3, 4, r, 128), BF16) for r in rows]
        + [pltpu.VMEM((3, r, 128), BF16) for r in rows]
        + [pltpu.VMEM((3, 24, FC), F32)] * 3
        + [pltpu.VMEM((3, 24, 256), F32)] * 3
        + [pltpu.VMEM((3, 96, 128), BF16)] * 2
        + [pltpu.VMEM((96, 256), F32), pltpu.VMEM((3, 24, 256), F32)]
        + [
            pltpu.VMEM((4, SMALL, 128), F32),
            pltpu.VMEM((12, SMALL, 128), F32),
            pltpu.VMEM((128, 1024), BF16),
            pltpu.VMEM((128, 1536), F32),
            pltpu.VMEM((128, 1536), F32),
            DMA((7 + n_late + 9,)),
            DMA((224,)),
            DMA((224,)),
        ]
    )
    vm, sm, hbm = (pl.BlockSpec(memory_space=m) for m in (pltpu.VMEM, pltpu.SMEM, pl.ANY))
    f32 = lambda *s: jax.ShapeDtypeStruct(s, F32)
    shape = (f32(128, 1536), f32(8, 24, 128), f32(6, 24, 128), f32(SMALL, 128))
    shape = shape + (f32(24, 4480),) * 3
    return pl.pallas_call(
        body,
        out_shape=shape,
        in_specs=[sm] + [hbm] * (11 + n_late) + [vm] * 10,
        out_specs=(vm,) * 7,
        scratch_shapes=scratch,
        compiler_params=pltpu.CompilerParams(collective_id=2, has_side_effects=True, vmem_limit_bytes=VMEM_BYTES),
        name="backward",
    )(lengths, *xs_in, *gs_in, kv, wq.reshape(6, 4, 384, 128), wk.reshape(4, 384, 128), wv.reshape(4, 384, 128), norm_shared, *late, q, g, lse, delta, branch_t, attn_low, cos, sin, gain, d_norm2)


def hand_out(qkv, *arrays):
    n = len(arrays)

    def body(*refs):
        ins, outs, held, sem = refs[: n + 1], refs[n + 1 : 2 * n + 4], refs[2 * n + 4 : 3 * n + 5], refs[3 * n + 5]
        to = [pltpu.make_async_copy(a, b, sem.at[i]) for i, (a, b) in enumerate(zip(ins, held))]
        pieces = [[(held[0].at[pl.ds(0, 6)], outs[0]), (held[0].at[6], outs[1]), (held[0].at[7], outs[2])]]
        pieces += [[(held[i], outs[i + 2])] for i in range(1, n + 1)]
        for copy in to:
            copy.start()
        back = []
        for i in range(n + 1):
            to[i].wait()
            for a, b in pieces[i]:
                copy = pltpu.make_async_copy(a, b, sem.at[n + 1 + len(back)])
                copy.start()
                back.append(copy)
        for copy in back:
            copy.wait()

    hbm = pl.BlockSpec(memory_space=pl.ANY)
    f32 = lambda *s: jax.ShapeDtypeStruct(s, F32)
    return pl.pallas_call(
        body,
        out_shape=(f32(6, 24, 128), f32(24, 128), f32(24, 128)) + tuple(f32(*v.shape) for v in arrays),
        in_specs=[hbm] * (n + 1),
        out_specs=(hbm,) * (n + 3),
        scratch_shapes=[pltpu.VMEM(v.shape, v.dtype) for v in (qkv, *arrays)] + [DMA((2 * n + 4,))],
        compiler_params=pltpu.CompilerParams(vmem_limit_bytes=VMEM_BYTES),
        name="hand_out",
    )(qkv, *arrays)


def local(
    tokens, cotangent, lengths, norm1_gain, w_query, b_query, w_key, b_key, w_value, b_value, w_out,
    norm2_gain, w_gate, w_up, w_down,
):
    device = lax.axis_index("seq")
    core = lax.axis_index("tensor")
    wq = w_query.transpose(1, 0, 2)
    wk, wv = w_key.reshape(1536, 128), w_value.reshape(1536, 128)
    wo = w_out.reshape(768, 1536)
    gains = jnp.stack([norm1_gain, norm2_gain])

    (output, g_mid, branch_t, g_attn, delta, d_norm2, q, cos, sin, attn_low, lse, *shared, kv, norm_shared) = forward(
        tokens, cotangent, lengths, gains, wq, wk, wv, b_query, b_key, b_value, wo, w_gate, w_up, w_down
    )
    grad_tokens, grad_qkv, grad_wo, sums, grad_gate, grad_up, grad_down = backward(
        shared[:3], shared[3:], q, g_attn, kv, lse, delta, branch_t, attn_low, lengths,
        cos, sin, norm_shared, wq, wk, wv, tokens, gains, g_mid, d_norm2,
    )
    grad_wq, grad_wk, grad_wv, output, grad_tokens, grad_wo, grad_gate, grad_up, grad_down = hand_out(
        grad_qkv, output, grad_tokens, grad_wo, grad_gate, grad_up, grad_down
    )
    sums = sums.reshape(-1)
    grad_norm1 = lax.dynamic_slice(sums, (device * 24,), (24,))
    grad_norm2 = lax.dynamic_slice(sums, (1536 + device * 24,), (24,))
    bias = lax.dynamic_slice(sums.reshape(SMALL, 128), (24 + core * 8, device * 2), (8, 2))
    return (
        output,
        grad_tokens,
        grad_norm1,
        grad_wq.transpose(1, 0, 2),
        bias[:6],
        grad_wk.reshape(24, 1, 128),
        bias[6:7],
        grad_wv.reshape(24, 1, 128),
        bias[7:8],
        grad_wo.transpose(0, 2, 1),
        grad_norm2,
        grad_gate,
        grad_up,
        grad_down.T,
    )


def solution(mesh):
    in_specs = (
        P("seq", None), P("seq", None), P(), P(), P(None, "tensor", None), P("tensor", None),
        P(None, "tensor", None), P("tensor", None), P(None, "tensor", None), P("tensor", None),
        P("tensor", None, None), P(), P(None, "tensor"), P(None, "tensor"), P("tensor", None),
    )
    out_specs = (
        P("seq", None), P("seq", None), P("seq"), P("seq", "tensor", None), P("tensor", "seq"),
        P("seq", "tensor", None), P("tensor", "seq"), P("seq", "tensor", None), P("tensor", "seq"),
        P("tensor", None, "seq"), P("seq"), P("seq", "tensor"), P("seq", "tensor"), P("tensor", "seq"),
    )
    return jax.shard_map(local, mesh=mesh, in_specs=in_specs, out_specs=out_specs, check_vma=False)
```
